32 devices in a mesh: depth: 8 (over y, x, core), rows: 4 (over z).
Axes of the slice: x: 2, y: 2, z: 4, core: 2. Of those that a mesh axis runs over, the one named last changes fastest.
Arguments:
- volume: int32 [2, 64, 128, 1024], P(None, 'depth', 'rows'), may hold values from 0 to 255
- color_map: int32 [3, 256], replicated, may hold values from 0 to 255
- alpha_map: int32 [256], replicated, may hold values from 0 to 255
Outputs:
- image: float32 [4, 128, 1024], P(None, ('rows', 'depth'))
The draws below stay inside these ranges and needn't reach their ends.
All inputs are finite; a program needn't handle non-finite values.
Results may differ from the reference program's by a relative error of at most 0.003.
Values may be sent and summed in bfloat16 or wider, within the bound.
No kernel may reach another device: no remote copies, remote signals or barrier semaphores. Data moves between devices by JAX's collectives and lax.ppermute only.
A program may use at most 64 MiB of HBM per device.

```python
import jax
import jax.numpy as jnp
from jax import lax

NZ = 1024
LEVELS = 256
NX = 64
NY = 128


def set_ends(values, key, least, top_value):
    dims = values.shape
    place = [jax.random.randint(jax.random.fold_in(key, axis), (), 0, dims[axis]) for axis in range(len(dims))]
    values = values.at[tuple(place)].set(least)
    longest = dims.index(max(dims))
    place[longest] = (place[longest] + 1) % dims[longest]
    return values.at[tuple(place)].set(top_value)


def setup_inputs(seed: int = 0) -> dict:
    arg_keys = jax.random.split(jax.random.key(seed), 4)
    return {
        "volume": set_ends(jax.random.randint(arg_keys[0], (2, NX, NY, NZ), 0, LEVELS), jax.random.fold_in(arg_keys[0], 1), 0, LEVELS - 1).astype(jnp.int32),
        "color_map": set_ends(jax.random.randint(arg_keys[1], (3, LEVELS), 0, 256), jax.random.fold_in(arg_keys[1], 1), 0, 255).astype(jnp.int32),
        "alpha_map": set_ends(jax.random.randint(arg_keys[2], (LEVELS,), 0, 256), jax.random.fold_in(arg_keys[2], 1), 0, 255).astype(jnp.int32),
    }


LIGHT_DEPTH = 0.48
LIGHT_ROWS = 0.6
LIGHT_COLS = 0.64
OPACITY = 4.0

def sample_slice(values, position):
    inside = (position >= 0) & (position < values.shape[0])
    clamped = jnp.clip(position, 0, values.shape[0] - 1).astype(jnp.int32)
    taken = lax.dynamic_index_in_dim(values, clamped, 0, keepdims=False)
    return jnp.where(inside, taken.astype(jnp.float32), jnp.float32(0.0))

def reference(volume, color_map, alpha_map):
    primary = volume[0]
    secondary = volume[1]
    color_table = color_map.astype(jnp.float32) / 255.0
    alpha_table = alpha_map.astype(jnp.float32) * (OPACITY / (255.0 * NX))

    def march_slice(running, position):
        color_sum, alpha_sum = running
        ahead = sample_slice(primary, position + 1)
        behind = sample_slice(primary, position - 1)
        current = sample_slice(primary, position)
        padded = jnp.pad(current, 1)
        grad_depth = 0.5 * (ahead - behind)
        grad_rows = 0.5 * (padded[2:, 1:-1] - padded[:-2, 1:-1])
        grad_cols = 0.5 * (padded[1:-1, 2:] - padded[1:-1, :-2])
        magnitude = jnp.sqrt(grad_depth * grad_depth + grad_rows * grad_rows + grad_cols * grad_cols)
        facing = LIGHT_DEPTH * grad_depth + LIGHT_ROWS * grad_rows + LIGHT_COLS * grad_cols
        shading = 0.3 + 0.7 * jnp.abs(facing) / jnp.maximum(magnitude, 1.0)
        primary_level = lax.dynamic_index_in_dim(primary, position, 0, keepdims=False)
        secondary_level = lax.dynamic_index_in_dim(secondary, position, 0, keepdims=False)
        emitted = jnp.take(color_table, primary_level, axis=1)
        opacity = jnp.take(alpha_table, secondary_level)
        weight = 1.0 - alpha_sum
        color_sum = color_sum + weight[None] * emitted * (opacity * shading)[None]
        alpha_sum = alpha_sum + weight * opacity
        return ((color_sum, alpha_sum), None)
    starting = (jnp.zeros((3, NY, NZ), jnp.float32), jnp.zeros((NY, NZ), jnp.float32))
    (color_sum, alpha_sum), _ = lax.scan(march_slice, starting, jnp.arange(NX, dtype=jnp.int32))
    return jnp.concatenate([color_sum, alpha_sum[None]], axis=0)
```

```python
import functools

import jax
import jax.numpy as jnp
from jax import lax
from jax.experimental import pallas as pl
from jax.experimental.pallas import tpu as pltpu
from jax.sharding import PartitionSpec as P

LIGHT_DEPTH = 0.48
LIGHT_ROWS = 0.6
LIGHT_COLS = 0.64
OPACITY = 4.0
LANES = 128
SUBLANES = 8


def edges_kernel(first_ref, last_ref, top_ref, bottom_ref, first_out, last_out, top_out, bottom_out):
    first_out[...] = first_ref[0, 0].astype(jnp.float32).astype(jnp.bfloat16)
    last_out[...] = last_ref[0, 0].astype(jnp.float32).astype(jnp.bfloat16)
    top_out[...] = top_ref[0, :, 0, :].astype(jnp.float32).astype(jnp.bfloat16)
    bottom_out[...] = bottom_ref[0, :, SUBLANES - 1, :].astype(jnp.float32).astype(jnp.bfloat16)


def cut_edges(volume):
    _, slices, height, columns = volume.shape
    plane = jax.ShapeDtypeStruct((height, columns), jnp.bfloat16)
    strip = jax.ShapeDtypeStruct((slices, columns), jnp.bfloat16)
    tiles = height // SUBLANES
    return pl.pallas_call(
        edges_kernel,
        grid=(1,),
        in_specs=[
            pl.BlockSpec((1, 1, height, columns), lambda i: (0, 0, 0, 0)),
            pl.BlockSpec((1, 1, height, columns), lambda i: (0, slices - 1, 0, 0)),
            pl.BlockSpec((1, slices, SUBLANES, columns), lambda i: (0, 0, 0, 0)),
            pl.BlockSpec((1, slices, SUBLANES, columns), lambda i: (0, 0, tiles - 1, 0)),
        ],
        out_specs=[
            pl.BlockSpec((height, columns), lambda i: (0, 0)),
            pl.BlockSpec((height, columns), lambda i: (0, 0)),
            pl.BlockSpec((slices, columns), lambda i: (0, 0)),
            pl.BlockSpec((slices, columns), lambda i: (0, 0)),
        ],
        out_shape=[plane, plane, strip, strip],
    )(volume, volume, volume, volume)


def to_level(values):
    return values.astype(jnp.float32).astype(jnp.int32)


def march_kernel(opacity_scale, share, volume_ref, before_ref, after_ref, above_ref, below_ref, color_ref, alpha_ref, out_ref):
    _, slices, height, columns = volume_ref.shape
    tiles = height // SUBLANES
    chunks = columns // LANES
    tile = (SUBLANES, LANES)

    def table(rows):
        return jnp.broadcast_to(rows, tile)

    packed = color_ref[0:1, :] + color_ref[1:2, :] * 256 + color_ref[2:3, :] * 65536
    color_low = table(packed[:, :LANES])
    color_high = table(packed[:, LANES:])
    alpha_both = table(alpha_ref[0:1, :LANES] + alpha_ref[0:1, LANES:] * 256)

    def pick(entries, places):
        return jnp.take_along_axis(entries, places, axis=1, mode="promise_in_bounds")

    lane = lax.broadcasted_iota(jnp.int32, tile, 1)
    row = lax.broadcasted_iota(jnp.int32, tile, 0)
    first_lane, last_lane = lane == 0, lane == LANES - 1
    first_row, last_row = row == 0, row == SUBLANES - 1

    def chunk(j, carry):
        here = pl.ds(pl.multiple_of(j * LANES, LANES), LANES)
        left = pl.ds(pl.multiple_of(jnp.maximum(j - 1, 0) * LANES, LANES), LANES)
        right = pl.ds(pl.multiple_of(jnp.minimum(j + 1, chunks - 1) * LANES, LANES), LANES)
        take_left = last_lane & (j > 0)
        take_right = first_lane & (j < chunks - 1)
        zero_left = last_lane & (j == 0)
        zero_right = first_lane & (j == chunks - 1)
        above = to_level(above_ref[:, here])
        below = to_level(below_ref[:, here])
        before = to_level(before_ref[:, here])
        after = to_level(after_ref[:, here])
        for r in range(tiles):
            rows = slice(r * SUBLANES, (r + 1) * SUBLANES)
            values = [before[rows]]
            values += [volume_ref[0, s, rows, here] for s in range(slices)]
            values += [after[rows]]
            remaining = jnp.ones(tile, jnp.float32)
            sums = [jnp.zeros(tile, jnp.float32) for _ in range(3)]
            for s in range(slices):
                value = values[s + 1]
                if r > 0:
                    up = volume_ref[0, s, (r - 1) * SUBLANES : r * SUBLANES, here]
                else:
                    up = jnp.broadcast_to(above[s : s + 1], tile)
                if r < tiles - 1:
                    down = volume_ref[0, s, (r + 1) * SUBLANES : (r + 2) * SUBLANES, here]
                else:
                    down = jnp.broadcast_to(below[s : s + 1], tile)
                up = pltpu.roll(jnp.where(last_row, up, value), 1, 0)
                down = pltpu.roll(jnp.where(first_row, down, value), SUBLANES - 1, 0)
                west = jnp.where(take_left, volume_ref[0, s, rows, left], value)
                west = pltpu.roll(jnp.where(zero_left, 0, west), 1, 1)
                east = jnp.where(take_right, volume_ref[0, s, rows, right], value)
                east = pltpu.roll(jnp.where(zero_right, 0, east), LANES - 1, 1)
                grad_depth = (values[s + 2] - values[s]).astype(jnp.float32)
                grad_rows = (down - up).astype(jnp.float32)
                grad_cols = (east - west).astype(jnp.float32)
                squares = grad_depth * grad_depth + grad_rows * grad_rows + grad_cols * grad_cols
                facing = (
                    (0.7 * LIGHT_DEPTH) * grad_depth
                    + (0.7 * LIGHT_ROWS) * grad_rows
                    + (0.7 * LIGHT_COLS) * grad_cols
                )
                shading = 0.3 + jnp.abs(facing) * lax.rsqrt(jnp.maximum(squares, 4.0))
                place = value & (LANES - 1)
                color = jnp.where(value < LANES, pick(color_low, place), pick(color_high, place))
                level = volume_ref[1, s, rows, here]
                entry = pick(alpha_both, level & (LANES - 1))
                entry = lax.shift_right_logical(entry, lax.shift_right_logical(level & LANES, 4)) & 255
                weight = remaining * (entry.astype(jnp.float32) * opacity_scale)
                remaining = remaining - weight
                lit = weight * shading
                for c in range(3):
                    part = lax.shift_right_logical(color, 8 * c) if c else color
                    if c < 2:
                        part = part & 255
                    sums[c] = sums[c] + part.astype(jnp.float32) * lit
            planes = [total * (1.0 / 255.0) for total in sums] + [1.0 - remaining]
            for first in range(0, SUBLANES, share):
                rows_out = jnp.concatenate([plane[first : first + share] for plane in planes], axis=0)
                out_ref[(r * SUBLANES + first) // share, :, here] = rows_out.astype(jnp.bfloat16)
        return carry

    lax.fori_loop(0, chunks, chunk, 0)


def march(volume, before, after, above, below, color_map, alpha_map, depth_count):
    _, slices, height, columns = volume.shape
    share = height // depth_count
    opacity_scale = OPACITY / (255.0 * slices * depth_count)
    whole = pl.BlockSpec(memory_space=pltpu.VMEM)
    return pl.pallas_call(
        functools.partial(march_kernel, opacity_scale, share),
        in_specs=[whole] * 7,
        out_specs=whole,
        out_shape=jax.ShapeDtypeStruct((depth_count, 4 * share, columns), jnp.bfloat16),
        compiler_params=pltpu.CompilerParams(vmem_limit_bytes=16 * 1024 * 1024),
    )(volume, before, after, above, below, color_map, alpha_map.reshape(1, -1))


def finish_kernel(parts_ref, out_ref):
    count = parts_ref.shape[0]
    _, share, columns = out_ref.shape
    remaining = jnp.ones((share, columns), jnp.float32)
    sums = [jnp.zeros((share, columns), jnp.float32) for _ in range(3)]
    for k in range(count):
        part = parts_ref[k].astype(jnp.float32)
        for c in range(3):
            sums[c] = sums[c] + remaining * part[c * share : (c + 1) * share]
        remaining = remaining - remaining * part[3 * share :]
    for c in range(3):
        out_ref[c] = sums[c]
    out_ref[3] = 1.0 - remaining


def finish(parts, share):
    columns = parts.shape[2]
    whole = pl.BlockSpec(memory_space=pltpu.VMEM)
    return pl.pallas_call(
        finish_kernel,
        in_specs=[whole],
        out_specs=whole,
        out_shape=jax.ShapeDtypeStruct((4, share, columns), jnp.float32),
    )(parts)


def shifted(values, axis, step):
    size = lax.axis_size(axis)
    pairs = [(i, i + step) for i in range(size) if 0 <= i + step < size]
    return lax.ppermute(values, axis, pairs)


def body(volume, color_map, alpha_map):
    depth_count = lax.axis_size("depth")
    share = volume.shape[2] // depth_count
    first, last, top, bottom = cut_edges(volume)
    before = shifted(last, "depth", 1)
    after = shifted(first, "depth", -1)
    above = shifted(bottom, "rows", 1)
    below = shifted(top, "rows", -1)
    parts = march(volume, before, after, above, below, color_map, alpha_map, depth_count)
    parts = lax.all_to_all(parts, "depth", 0, 0, tiled=True)
    return finish(parts, share)


def solution(mesh):
    in_specs = (P(None, "depth", "rows", None), P(), P())
    out_specs = P(None, ("rows", "depth"), None)
    return jax.shard_map(body, mesh=mesh, in_specs=in_specs, out_specs=out_specs, check_vma=False)
```

```python
import functools

import jax
import jax.numpy as jnp
from jax import lax
from jax.experimental import pallas as pl
from jax.experimental.pallas import tpu as pltpu
from jax.sharding import PartitionSpec as P

AMBIENT = 0.3
DIFFUSE = 0.7
LIGHT_DEPTH = 0.48 * DIFFUSE
LIGHT_ROWS = 0.6 * DIFFUSE
LIGHT_COLS = 0.64 * DIFFUSE
OPACITY = 4.0
LANES = 128
SUBLANES = 8
WHOLE = pl.BlockSpec(memory_space=pltpu.VMEM)


def edges_kernel(volume_ref, first_out, last_out, top_out, bottom_out):
    _, slices, height, _ = volume_ref.shape

    def narrow(values):
        return values.astype(jnp.float32).astype(jnp.bfloat16)

    last_out[...] = narrow(volume_ref[0, slices - 1])
    first_out[...] = narrow(volume_ref[0, 0])
    bottom_out[...] = narrow(volume_ref[0, :, height - 1, :])
    top_out[...] = narrow(volume_ref[0, :, 0, :])


def cut_edges(volume):
    _, slices, height, columns = volume.shape
    plane = jax.ShapeDtypeStruct((height, columns), jnp.bfloat16)
    strip = jax.ShapeDtypeStruct((slices, columns), jnp.bfloat16)
    return pl.pallas_call(
        edges_kernel,
        in_specs=[WHOLE],
        out_specs=[WHOLE] * 4,
        out_shape=[plane, plane, strip, strip],
    )(volume)


def pick(entries, places):
    return jnp.take_along_axis(entries, places, axis=1, mode="promise_in_bounds")


def shade(grad_depth, facing, squares):
    facing = facing + LIGHT_DEPTH * grad_depth
    squares = squares + grad_depth * grad_depth
    return AMBIENT + jnp.abs(facing) * lax.rsqrt(jnp.maximum(squares, 4.0))


def interior_kernel(
    opacity_scale, volume_ref, color_ref, alpha_ref, base_ref, face_ref, square_ref, lit_ref, grad_ref, strip_ref, held_ref
):
    _, slices, height, columns = volume_ref.shape
    tiles = height // SUBLANES
    chunks = columns // LANES
    tile = (SUBLANES, LANES)
    strip = (slices, LANES)

    packed = color_ref[0:1, :] + color_ref[1:2, :] * 256 + color_ref[2:3, :] * 65536
    color_low, color_high = packed[:, :LANES], packed[:, LANES:]
    alpha_both = alpha_ref[0:1, :LANES] + alpha_ref[0:1, LANES:] * 256

    def colors(value, tables):
        low, high = tables
        place = value & (LANES - 1)
        color = jnp.where(value < LANES, pick(low, place), pick(high, place))
        parts = (color & 255, lax.shift_right_logical(color, 8) & 255, lax.shift_right_logical(color, 16))
        return [part.astype(jnp.float32) for part in parts]

    def opacity(level, table):
        entry = pick(table, level & (LANES - 1))
        entry = lax.shift_right_logical(entry, lax.shift_right_logical(level & LANES, 4)) & 255
        return entry.astype(jnp.float32) * opacity_scale

    tile_colors = [jnp.broadcast_to(t, tile) for t in (color_low, color_high)]
    tile_alpha = jnp.broadcast_to(alpha_both, tile)
    strip_colors = [jnp.broadcast_to(t, strip) for t in (color_low, color_high)]

    def masks(shape):
        lane = lax.broadcasted_iota(jnp.int32, shape, 1)
        row = lax.broadcasted_iota(jnp.int32, shape, 0)
        return lane == 0, lane == LANES - 1, row == 0, row == shape[0] - 1

    first_lane, last_lane, first_row, last_row = masks(tile)
    strip_first_lane, strip_last_lane, front, back = masks(strip)

    def chunk(j, carry):
        here = pl.ds(pl.multiple_of(j * LANES, LANES), LANES)
        left = pl.ds(pl.multiple_of(jnp.maximum(j - 1, 0) * LANES, LANES), LANES)
        right = pl.ds(pl.multiple_of(jnp.minimum(j + 1, chunks - 1) * LANES, LANES), LANES)

        def across(value, left_value, right_value, first, last):
            west = jnp.where(last & (j > 0), left_value, value)
            west = pltpu.roll(jnp.where(last & (j == 0), 0, west), 1, 1)
            east = jnp.where(first & (j < chunks - 1), right_value, value)
            east = pltpu.roll(jnp.where(first & (j == chunks - 1), 0, east), LANES - 1, 1)
            return (east - west).astype(jnp.float32)

        for r in range(tiles):
            rows = slice(r * SUBLANES, (r + 1) * SUBLANES)
            values = [volume_ref[0, s, rows, here] for s in range(slices)]
            remaining = jnp.ones(tile, jnp.float32)
            sums = [jnp.zeros(tile, jnp.float32) for _ in range(3)]
            for s in range(slices):
                value = values[s]
                up = volume_ref[0, s, (r - 1) * SUBLANES : r * SUBLANES, here] if r > 0 else value
                down = volume_ref[0, s, (r + 1) * SUBLANES : (r + 2) * SUBLANES, here] if r < tiles - 1 else value
                up = pltpu.roll(jnp.where(last_row, up, value), 1, 0)
                down = pltpu.roll(jnp.where(first_row, down, value), SUBLANES - 1, 0)
                grad_rows = (down - up).astype(jnp.float32)
                grad_cols = across(
                    value, volume_ref[0, s, rows, left], volume_ref[0, s, rows, right], first_lane, last_lane
                )
                squares = grad_rows * grad_rows + grad_cols * grad_cols
                facing = LIGHT_ROWS * grad_rows + LIGHT_COLS * grad_cols
                weight = remaining * opacity(volume_ref[1, s, rows, here], tile_alpha)
                remaining = remaining - weight
                if r == 0:
                    held_ref[0, s : s + 1, :] = weight[:1]
                    weight = jnp.where(first_row, 0.0, weight)
                if r == tiles - 1:
                    held_ref[1, s : s + 1, :] = weight[SUBLANES - 1 :]
                    weight = jnp.where(last_row, 0.0, weight)
                emitted = colors(value, tile_colors)
                if 0 < s < slices - 1:
                    grad_depth = (values[s + 1] - values[s - 1]).astype(jnp.float32)
                    weight = weight * shade(grad_depth, facing, squares)
                    for c in range(3):
                        sums[c] = sums[c] + emitted[c] * weight
                else:
                    end = int(s > 0)
                    face_ref[end, rows, here] = facing
                    square_ref[end, rows, here] = squares
                    weight = weight * (1.0 / 255.0)
                    for c in range(3):
                        lit_ref[end, c, rows, here] = emitted[c] * weight
            for c in range(3):
                base_ref[c, rows, here] = sums[c] * (1.0 / 255.0)
            base_ref[3, rows, here] = 1.0 - remaining

        for q, (edge, inner) in enumerate(((0, 1), (height - 1, height - 2))):
            value = volume_ref[0, :, edge, here]
            behind = pltpu.roll(jnp.where(back, 0, value), 1, 0)
            ahead = pltpu.roll(jnp.where(front, 0, value), slices - 1, 0)
            grad_ref[q, 0, :, here] = (ahead - behind).astype(jnp.float32)
            grad_ref[q, 1, :, here] = volume_ref[0, :, inner, here].astype(jnp.float32)
            grad_ref[q, 2, :, here] = across(
                value, volume_ref[0, :, edge, left], volume_ref[0, :, edge, right], strip_first_lane, strip_last_lane
            )
            weight = held_ref[q] * (1.0 / 255.0)
            emitted = colors(value, strip_colors)
            for c in range(3):
                strip_ref[q, c, :, here] = emitted[c] * weight
        return carry

    lax.fori_loop(0, chunks, chunk, 0)


def march_interior(volume, color_map, alpha_map, depth_count):
    _, slices, height, columns = volume.shape
    opacity_scale = OPACITY / (255.0 * slices * depth_count)
    shapes = [
        (4, height, columns),
        (2, height, columns),
        (2, height, columns),
        (2, 3, height, columns),
        (2, 3, slices, columns),
        (2, 3, slices, columns),
    ]
    voxels = slices * height * columns
    return pl.pallas_call(
        functools.partial(interior_kernel, opacity_scale),
        in_specs=[WHOLE] * 3,
        out_specs=[WHOLE] * len(shapes),
        out_shape=[jax.ShapeDtypeStruct(shape, jnp.float32) for shape in shapes],
        scratch_shapes=[pltpu.VMEM((2, slices, LANES), jnp.float32)],
        compiler_params=pltpu.CompilerParams(vmem_limit_bytes=24 * 1024 * 1024),
        cost_estimate=pl.CostEstimate(flops=voxels * 80, bytes_accessed=voxels * 20, transcendentals=voxels),
    )(volume, color_map, alpha_map.reshape(1, -1))


def edge_kernel(
    share, volume_ref, base_ref, face_ref, square_ref, lit_ref, grad_ref, strip_ref, before_ref, after_ref, above_ref, below_ref, out_ref
):
    _, slices, height, columns = volume_ref.shape
    tiles = height // SUBLANES
    tile = (SUBLANES, LANES)
    row = lax.broadcasted_iota(jnp.int32, tile, 0)
    first_row, last_row = row == 0, row == SUBLANES - 1
    level = lax.broadcasted_iota(jnp.int32, (slices, LANES), 0)
    front, back = level == 0, level == slices - 1

    def chunk(j, carry):
        here = pl.ds(pl.multiple_of(j * LANES, LANES), LANES)
        before = before_ref[:, here].astype(jnp.float32)
        after = after_ref[:, here].astype(jnp.float32)
        above = above_ref[:, here].astype(jnp.float32)
        below = below_ref[:, here].astype(jnp.float32)
        extra = []
        for q, edge in enumerate((0, height - 1)):
            inner = grad_ref[q, 1, :, here]
            grad_rows = below - inner if q else inner - above
            grad_cols = grad_ref[q, 2, :, here]
            grad_depth = grad_ref[q, 0, :, here] + jnp.where(
                back, after[edge : edge + 1], jnp.where(front, -before[edge : edge + 1], 0.0)
            )
            shading = shade(
                grad_depth,
                LIGHT_ROWS * grad_rows + LIGHT_COLS * grad_cols,
                grad_rows * grad_rows + grad_cols * grad_cols,
            )
            extra.append([jnp.sum(strip_ref[q, c, :, here] * shading, axis=0, keepdims=True) for c in range(3)])
        for r in range(tiles):
            rows = slice(r * SUBLANES, (r + 1) * SUBLANES)
            planes = [base_ref[c, rows, here] for c in range(4)]
            for end in range(2):
                if end:
                    grad_depth = after[rows] - volume_ref[0, slices - 2, rows, here].astype(jnp.float32)
                else:
                    grad_depth = volume_ref[0, 1, rows, here].astype(jnp.float32) - before[rows]
                shading = shade(grad_depth, face_ref[end, rows, here], square_ref[end, rows, here])
                for c in range(3):
                    planes[c] = planes[c] + lit_ref[end, c, rows, here] * shading
            for c in range(3):
                if r == 0:
                    planes[c] = planes[c] + jnp.where(first_row, extra[0][c], 0.0)
                if r == tiles - 1:
                    planes[c] = planes[c] + jnp.where(last_row, extra[1][c], 0.0)
            for first in range(0, SUBLANES, share):
                block = jnp.concatenate([plane[first : first + share] for plane in planes], axis=0)
                out_ref[(r * SUBLANES + first) // share, :, here] = block.astype(jnp.bfloat16)
        return carry

    lax.fori_loop(0, columns // LANES, chunk, 0)


def add_edges(volume, interior, halos, depth_count):
    _, slices, height, columns = volume.shape
    share = height // depth_count
    return pl.pallas_call(
        functools.partial(edge_kernel, share),
        in_specs=[WHOLE] * 11,
        out_specs=WHOLE,
        out_shape=jax.ShapeDtypeStruct((depth_count, 4 * share, columns), jnp.bfloat16),
        compiler_params=pltpu.CompilerParams(vmem_limit_bytes=24 * 1024 * 1024),
    )(volume, *interior, *halos)


def finish_kernel(parts_ref, out_ref):
    count = parts_ref.shape[0]
    _, share, columns = out_ref.shape
    remaining = jnp.ones((share, columns), jnp.float32)
    sums = [jnp.zeros((share, columns), jnp.float32) for _ in range(3)]
    for k in range(count):
        part = parts_ref[k].astype(jnp.float32)
        for c in range(3):
            sums[c] = sums[c] + remaining * part[c * share : (c + 1) * share]
        remaining = remaining - remaining * part[3 * share :]
    for c in range(3):
        out_ref[c] = sums[c]
    out_ref[3] = 1.0 - remaining


def finish(parts, share):
    columns = parts.shape[2]
    return pl.pallas_call(
        finish_kernel,
        in_specs=[WHOLE],
        out_specs=WHOLE,
        out_shape=jax.ShapeDtypeStruct((4, share, columns), jnp.float32),
    )(parts)


def shifted(values, axis, step):
    size = lax.axis_size(axis)
    pairs = [(i, i + step) for i in range(size) if 0 <= i + step < size]
    return lax.ppermute(values, axis, pairs)


def body(volume, color_map, alpha_map):
    depth_count = lax.axis_size("depth")
    share = volume.shape[2] // depth_count
    first, last, top, bottom = cut_edges(volume)
    before = shifted(last, "depth", 1)
    after = shifted(first, "depth", -1)
    above = shifted(bottom, "rows", 1)
    below = shifted(top, "rows", -1)
    interior = march_interior(volume, color_map, alpha_map, depth_count)
    parts = add_edges(volume, interior, (before, after, above, below), depth_count)
    parts = lax.all_to_all(parts, "depth", 0, 0, tiled=True)
    return finish(parts, share)


def solution(mesh):
    in_specs = (P(None, "depth", "rows", None), P(), P())
    out_specs = P(None, ("rows", "depth"), None)
    return jax.shard_map(body, mesh=mesh, in_specs=in_specs, out_specs=out_specs, check_vma=False)
```

```python
import functools

import jax
import jax.numpy as jnp
from jax import lax
from jax.experimental import pallas as pl
from jax.experimental.pallas import tpu as pltpu
from jax.sharding import PartitionSpec as P

AMBIENT = 0.3
DIFFUSE = 0.7
LIGHT_DEPTH = 0.48 * DIFFUSE
LIGHT_ROWS = 0.6 * DIFFUSE
LIGHT_COLS = 0.64 * DIFFUSE
OPACITY = 4.0
LANES = 128
SUBLANES = 8
WHOLE = pl.BlockSpec(memory_space=pltpu.VMEM)


def parity():
    return lax.axis_index("depth") % 2


def edges_kernel(volume_ref, across_out, beside_out, top_out, bottom_out, plane_ref, strip_ref, sems):
    _, slices, height, _ = volume_ref.shape
    odd = parity()
    copies = [
        pltpu.make_async_copy(volume_ref.at[0, odd * (slices - 1)], plane_ref.at[0], sems.at[0]),
        pltpu.make_async_copy(volume_ref.at[0, (1 - odd) * (slices - 1)], plane_ref.at[1], sems.at[1]),
        pltpu.make_async_copy(volume_ref.at[0, :, pl.ds(height - SUBLANES, SUBLANES)], strip_ref.at[0], sems.at[2]),
        pltpu.make_async_copy(volume_ref.at[0, :, pl.ds(0, SUBLANES)], strip_ref.at[1], sems.at[3]),
    ]
    for copy in copies:
        copy.start()

    def narrow(values):
        return values.astype(jnp.float32).astype(jnp.bfloat16)

    copies[0].wait()
    across_out[...] = narrow(plane_ref[0])
    copies[1].wait()
    beside_out[...] = narrow(plane_ref[1])
    copies[2].wait()
    bottom_out[...] = narrow(strip_ref[0, :, SUBLANES - 1, :])
    copies[3].wait()
    top_out[...] = narrow(strip_ref[1, :, 0, :])


def cut_edges(volume):
    _, slices, height, columns = volume.shape
    plane = jax.ShapeDtypeStruct((height, columns), jnp.bfloat16)
    strip = jax.ShapeDtypeStruct((slices, columns), jnp.bfloat16)
    return pl.pallas_call(
        edges_kernel,
        in_specs=[pl.BlockSpec(memory_space=pl.ANY)],
        out_specs=[WHOLE] * 4,
        out_shape=[plane, plane, strip, strip],
        scratch_shapes=[
            pltpu.VMEM((2, height, columns), jnp.int32),
            pltpu.VMEM((2, slices, SUBLANES, columns), jnp.int32),
            pltpu.SemaphoreType.DMA((4,)),
        ],
    )(volume)


def pick(entries, places):
    return jnp.take_along_axis(entries, places, axis=1, mode="promise_in_bounds")


def shade(grad_depth, facing, squares):
    facing = facing + LIGHT_DEPTH * grad_depth
    squares = squares + grad_depth * grad_depth
    return AMBIENT + jnp.abs(facing) * lax.rsqrt(jnp.maximum(squares, 4.0))


def interior_kernel(
    opacity_scale, volume_ref, color_ref, alpha_ref, base_ref, face_ref, square_ref, lit_ref, grad_ref, strip_ref, held_ref
):
    _, slices, height, columns = volume_ref.shape
    tiles = height // SUBLANES
    chunks = columns // LANES
    tile = (SUBLANES, LANES)
    strip = (slices, LANES)

    packed = color_ref[0:1, :] + color_ref[1:2, :] * 256 + color_ref[2:3, :] * 65536
    color_low, color_high = packed[:, :LANES], packed[:, LANES:]
    alpha_both = alpha_ref[0:1, :LANES] + alpha_ref[0:1, LANES:] * 256

    def colors(value, tables):
        low, high = tables
        place = value & (LANES - 1)
        color = jnp.where(value < LANES, pick(low, place), pick(high, place))
        parts = (color & 255, lax.shift_right_logical(color, 8) & 255, lax.shift_right_logical(color, 16))
        return [part.astype(jnp.float32) for part in parts]

    def opacity(level, table):
        entry = pick(table, level & (LANES - 1))
        entry = lax.shift_right_logical(entry, lax.shift_right_logical(level & LANES, 4)) & 255
        return entry.astype(jnp.float32) * opacity_scale

    tile_colors = [jnp.broadcast_to(t, tile) for t in (color_low, color_high)]
    tile_alpha = jnp.broadcast_to(alpha_both, tile)
    strip_colors = [jnp.broadcast_to(t, strip) for t in (color_low, color_high)]

    def masks(shape):
        lane = lax.broadcasted_iota(jnp.int32, shape, 1)
        row = lax.broadcasted_iota(jnp.int32, shape, 0)
        return lane == 0, lane == LANES - 1, row == 0, row == shape[0] - 1

    first_lane, last_lane, first_row, last_row = masks(tile)
    strip_first_lane, strip_last_lane, front, back = masks(strip)

    def chunk(j, carry):
        here = pl.ds(pl.multiple_of(j * LANES, LANES), LANES)
        left = pl.ds(pl.multiple_of(jnp.maximum(j - 1, 0) * LANES, LANES), LANES)
        right = pl.ds(pl.multiple_of(jnp.minimum(j + 1, chunks - 1) * LANES, LANES), LANES)

        def across(value, left_value, right_value, first, last):
            west = jnp.where(last & (j > 0), left_value, value)
            west = pltpu.roll(jnp.where(last & (j == 0), 0, west), 1, 1)
            east = jnp.where(first & (j < chunks - 1), right_value, value)
            east = pltpu.roll(jnp.where(first & (j == chunks - 1), 0, east), LANES - 1, 1)
            return (east - west).astype(jnp.float32)

        for r in range(tiles):
            rows = slice(r * SUBLANES, (r + 1) * SUBLANES)
            values = [volume_ref[0, s, rows, here] for s in range(slices)]
            remaining = jnp.ones(tile, jnp.float32)
            sums = [jnp.zeros(tile, jnp.float32) for _ in range(3)]
            for s in range(slices):
                value = values[s]
                up = volume_ref[0, s, (r - 1) * SUBLANES : r * SUBLANES, here] if r > 0 else value
                down = volume_ref[0, s, (r + 1) * SUBLANES : (r + 2) * SUBLANES, here] if r < tiles - 1 else value
                up = pltpu.roll(jnp.where(last_row, up, value), 1, 0)
                down = pltpu.roll(jnp.where(first_row, down, value), SUBLANES - 1, 0)
                grad_rows = (down - up).astype(jnp.float32)
                grad_cols = across(
                    value, volume_ref[0, s, rows, left], volume_ref[0, s, rows, right], first_lane, last_lane
                )
                squares = grad_rows * grad_rows + grad_cols * grad_cols
                facing = LIGHT_ROWS * grad_rows + LIGHT_COLS * grad_cols
                weight = remaining * opacity(volume_ref[1, s, rows, here], tile_alpha)
                remaining = remaining - weight
                if r == 0:
                    held_ref[0, s : s + 1, :] = weight[:1]
                    weight = jnp.where(first_row, 0.0, weight)
                if r == tiles - 1:
                    held_ref[1, s : s + 1, :] = weight[SUBLANES - 1 :]
                    weight = jnp.where(last_row, 0.0, weight)
                emitted = colors(value, tile_colors)
                if 0 < s < slices - 1:
                    grad_depth = (values[s + 1] - values[s - 1]).astype(jnp.float32)
                    weight = weight * shade(grad_depth, facing, squares)
                    for c in range(3):
                        sums[c] = sums[c] + emitted[c] * weight
                else:
                    end = int(s > 0)
                    face_ref[end, rows, here] = facing
                    square_ref[end, rows, here] = squares
                    weight = weight * (1.0 / 255.0)
                    for c in range(3):
                        lit_ref[end, c, rows, here] = emitted[c] * weight
            for c in range(3):
                base_ref[c, rows, here] = sums[c] * (1.0 / 255.0)
            base_ref[3, rows, here] = 1.0 - remaining

        for q, (edge, inner) in enumerate(((0, 1), (height - 1, height - 2))):
            value = volume_ref[0, :, edge, here]
            behind = pltpu.roll(jnp.where(back, 0, value), 1, 0)
            ahead = pltpu.roll(jnp.where(front, 0, value), slices - 1, 0)
            grad_ref[q, 0, :, here] = (ahead - behind).astype(jnp.float32)
            grad_ref[q, 1, :, here] = volume_ref[0, :, inner, here].astype(jnp.float32)
            grad_ref[q, 2, :, here] = across(
                value, volume_ref[0, :, edge, left], volume_ref[0, :, edge, right], strip_first_lane, strip_last_lane
            )
            weight = held_ref[q] * (1.0 / 255.0)
            emitted = colors(value, strip_colors)
            for c in range(3):
                strip_ref[q, c, :, here] = emitted[c] * weight
        return carry

    lax.fori_loop(0, chunks, chunk, 0)


def march_interior(volume, color_map, alpha_map, depth_count):
    _, slices, height, columns = volume.shape
    opacity_scale = OPACITY / (255.0 * slices * depth_count)
    shapes = [
        (4, height, columns),
        (2, height, columns),
        (2, height, columns),
        (2, 3, height, columns),
        (2, 3, slices, columns),
        (2, 3, slices, columns),
    ]
    voxels = slices * height * columns
    return pl.pallas_call(
        functools.partial(interior_kernel, opacity_scale),
        in_specs=[WHOLE] * 3,
        out_specs=[WHOLE] * len(shapes),
        out_shape=[jax.ShapeDtypeStruct(shape, jnp.float32) for shape in shapes],
        scratch_shapes=[pltpu.VMEM((2, slices, LANES), jnp.float32)],
        compiler_params=pltpu.CompilerParams(vmem_limit_bytes=24 * 1024 * 1024),
        cost_estimate=pl.CostEstimate(flops=voxels * 80, bytes_accessed=voxels * 20, transcendentals=voxels),
    )(volume, color_map, alpha_map.reshape(1, -1))


def edge_kernel(
    share, volume_ref, base_ref, face_ref, square_ref, lit_ref, grad_ref, strip_ref, across_ref, beside_ref, above_ref, below_ref, out_ref
):
    _, slices, height, columns = volume_ref.shape
    tiles = height // SUBLANES
    tile = (SUBLANES, LANES)
    row = lax.broadcasted_iota(jnp.int32, tile, 0)
    first_row, last_row = row == 0, row == SUBLANES - 1
    level = lax.broadcasted_iota(jnp.int32, (slices, LANES), 0)
    front, back = level == 0, level == slices - 1
    odd = parity() == 1

    def chunk(j, carry):
        here = pl.ds(pl.multiple_of(j * LANES, LANES), LANES)
        across = across_ref[:, here].astype(jnp.float32)
        beside = beside_ref[:, here].astype(jnp.float32)
        before = jnp.where(odd, beside, across)
        after = jnp.where(odd, across, beside)
        above = above_ref[:, here].astype(jnp.float32)
        below = below_ref[:, here].astype(jnp.float32)
        extra = []
        for q, edge in enumerate((0, height - 1)):
            inner = grad_ref[q, 1, :, here]
            grad_rows = below - inner if q else inner - above
            grad_cols = grad_ref[q, 2, :, here]
            grad_depth = grad_ref[q, 0, :, here] + jnp.where(
                back, after[edge : edge + 1], jnp.where(front, -before[edge : edge + 1], 0.0)
            )
            shading = shade(
                grad_depth,
                LIGHT_ROWS * grad_rows + LIGHT_COLS * grad_cols,
                grad_rows * grad_rows + grad_cols * grad_cols,
            )
            extra.append([jnp.sum(strip_ref[q, c, :, here] * shading, axis=0, keepdims=True) for c in range(3)])
        for r in range(tiles):
            rows = slice(r * SUBLANES, (r + 1) * SUBLANES)
            planes = [base_ref[c, rows, here] for c in range(4)]
            for end in range(2):
                if end:
                    grad_depth = after[rows] - volume_ref[0, slices - 2, rows, here].astype(jnp.float32)
                else:
                    grad_depth = volume_ref[0, 1, rows, here].astype(jnp.float32) - before[rows]
                shading = shade(grad_depth, face_ref[end, rows, here], square_ref[end, rows, here])
                for c in range(3):
                    planes[c] = planes[c] + lit_ref[end, c, rows, here] * shading
            for c in range(3):
                if r == 0:
                    planes[c] = planes[c] + jnp.where(first_row, extra[0][c], 0.0)
                if r == tiles - 1:
                    planes[c] = planes[c] + jnp.where(last_row, extra[1][c], 0.0)
            for first in range(0, SUBLANES, share):
                block = jnp.concatenate([plane[first : first + share] for plane in planes], axis=0)
                out_ref[(r * SUBLANES + first) // share, :, here] = block.astype(jnp.bfloat16)
        return carry

    lax.fori_loop(0, columns // LANES, chunk, 0)


def add_edges(volume, interior, halos, depth_count):
    _, slices, height, columns = volume.shape
    share = height // depth_count
    return pl.pallas_call(
        functools.partial(edge_kernel, share),
        in_specs=[WHOLE] * 11,
        out_specs=WHOLE,
        out_shape=jax.ShapeDtypeStruct((depth_count, 4 * share, columns), jnp.bfloat16),
        compiler_params=pltpu.CompilerParams(vmem_limit_bytes=24 * 1024 * 1024),
    )(volume, *interior, *halos)


def finish_kernel(parts_ref, out_ref):
    count = parts_ref.shape[0]
    _, share, columns = out_ref.shape
    remaining = jnp.ones((share, columns), jnp.float32)
    sums = [jnp.zeros((share, columns), jnp.float32) for _ in range(3)]
    for k in range(count):
        part = parts_ref[k].astype(jnp.float32)
        for c in range(3):
            sums[c] = sums[c] + remaining * part[c * share : (c + 1) * share]
        remaining = remaining - remaining * part[3 * share :]
    for c in range(3):
        out_ref[c] = sums[c]
    out_ref[3] = 1.0 - remaining


def finish(parts, share):
    columns = parts.shape[2]
    return pl.pallas_call(
        finish_kernel,
        in_specs=[WHOLE],
        out_specs=WHOLE,
        out_shape=jax.ShapeDtypeStruct((4, share, columns), jnp.float32),
    )(parts)


def shifted(values, axis, step):
    size = lax.axis_size(axis)
    pairs = [(i, i + step) for i in range(size) if 0 <= i + step < size]
    return lax.ppermute(values, axis, pairs)


def swapped(values, axis, start):
    pairs = [(i, i + 1) for i in range(start, lax.axis_size(axis) - 1, 2)]
    return lax.ppermute(values, axis, pairs + [(j, i) for i, j in pairs])


def body(volume, color_map, alpha_map):
    depth_count = lax.axis_size("depth")
    share = volume.shape[2] // depth_count
    across, beside, top, bottom = cut_edges(volume)
    volume, across = lax.optimization_barrier((volume, across))
    across = swapped(across, "depth", 1)
    beside = swapped(beside, "depth", 0)
    above = shifted(bottom, "rows", 1)
    below = shifted(top, "rows", -1)
    interior = march_interior(volume, color_map, alpha_map, depth_count)
    parts = add_edges(volume, interior, (across, beside, above, below), depth_count)
    parts = lax.all_to_all(parts, "depth", 0, 0, tiled=True)
    return finish(parts, share)


def solution(mesh):
    in_specs = (P(None, "depth", "rows", None), P(), P())
    out_specs = P(None, ("rows", "depth"), None)
    return jax.shard_map(body, mesh=mesh, in_specs=in_specs, out_specs=out_specs, check_vma=False)
```

```python
import functools

import jax
import jax.numpy as jnp
from jax import lax
from jax.experimental import pallas as pl
from jax.experimental.pallas import tpu as pltpu
from jax.sharding import PartitionSpec as P

AMBIENT = 0.3
DIFFUSE = 0.7
LIGHT_DEPTH = 0.48 * DIFFUSE
LIGHT_ROWS = 0.6 * DIFFUSE
LIGHT_COLS = 0.64 * DIFFUSE
OPACITY = 4.0
LANES = 128
SUBLANES = 8
WHOLE = pl.BlockSpec(memory_space=pltpu.VMEM)


def parity(axis):
    return lax.axis_index(axis) % 2


def edges_kernel(volume_ref, rows_near_out, rows_far_out, far_out, near_out, strip_ref, plane_ref, sems):
    _, slices, height, _ = volume_ref.shape
    odd, odd_row = parity("depth"), parity("rows")
    last_tile = height // SUBLANES - 1

    def tile(i):
        return pl.ds(pl.multiple_of(i * SUBLANES, SUBLANES), SUBLANES)

    copies = [
        pltpu.make_async_copy(volume_ref.at[0, :, tile((1 - odd_row) * last_tile)], strip_ref.at[0], sems.at[0]),
        pltpu.make_async_copy(volume_ref.at[0, :, tile(odd_row * last_tile)], strip_ref.at[1], sems.at[1]),
        pltpu.make_async_copy(volume_ref.at[0, odd * (slices - 1)], plane_ref.at[0], sems.at[2]),
        pltpu.make_async_copy(volume_ref.at[0, (1 - odd) * (slices - 1)], plane_ref.at[1], sems.at[3]),
    ]
    for copy in copies:
        copy.start()

    def narrow(values):
        return values.astype(jnp.float32).astype(jnp.bfloat16)

    copies[0].wait()
    rows_near_out[...] = narrow(jnp.where(odd_row == 1, strip_ref[0, :, 0, :], strip_ref[0, :, SUBLANES - 1, :]))
    copies[1].wait()
    rows_far_out[...] = narrow(jnp.where(odd_row == 1, strip_ref[1, :, SUBLANES - 1, :], strip_ref[1, :, 0, :]))
    copies[2].wait()
    far_out[...] = narrow(plane_ref[0])
    copies[3].wait()
    near_out[...] = narrow(plane_ref[1])


def cut_edges(volume):
    _, slices, height, columns = volume.shape
    plane = jax.ShapeDtypeStruct((height, columns), jnp.bfloat16)
    strip = jax.ShapeDtypeStruct((slices, columns), jnp.bfloat16)
    return pl.pallas_call(
        edges_kernel,
        in_specs=[pl.BlockSpec(memory_space=pl.ANY)],
        out_specs=[WHOLE] * 4,
        out_shape=[strip, strip, plane, plane],
        scratch_shapes=[
            pltpu.VMEM((2, slices, SUBLANES, columns), jnp.int32),
            pltpu.VMEM((2, height, columns), jnp.int32),
            pltpu.SemaphoreType.DMA((4,)),
        ],
    )(volume)


def pick(entries, places):
    return jnp.take_along_axis(entries, places, axis=1, mode="promise_in_bounds")


def shade(grad_depth, facing, squares):
    facing = facing + LIGHT_DEPTH * grad_depth
    squares = squares + grad_depth * grad_depth
    return AMBIENT + jnp.abs(facing) * lax.rsqrt(jnp.maximum(squares, 4.0))


def interior_kernel(
    opacity_scale, volume_ref, color_ref, alpha_ref, base_ref, face_ref, square_ref, lit_ref, grad_ref, strip_ref, held_ref
):
    _, slices, height, columns = volume_ref.shape
    tiles = height // SUBLANES
    chunks = columns // LANES
    tile = (SUBLANES, LANES)
    strip = (slices, LANES)

    packed = color_ref[0:1, :] + color_ref[1:2, :] * 256 + color_ref[2:3, :] * 65536
    color_low, color_high = packed[:, :LANES], packed[:, LANES:]
    alpha_both = alpha_ref[0:1, :LANES] + alpha_ref[0:1, LANES:] * 256

    def colors(value, tables):
        low, high = tables
        place = value & (LANES - 1)
        color = jnp.where(value < LANES, pick(low, place), pick(high, place))
        parts = (color & 255, lax.shift_right_logical(color, 8) & 255, lax.shift_right_logical(color, 16))
        return [part.astype(jnp.float32) for part in parts]

    def opacity(level, table):
        entry = pick(table, level & (LANES - 1))
        entry = lax.shift_right_logical(entry, lax.shift_right_logical(level & LANES, 4)) & 255
        return entry.astype(jnp.float32) * opacity_scale

    tile_colors = [jnp.broadcast_to(t, tile) for t in (color_low, color_high)]
    tile_alpha = jnp.broadcast_to(alpha_both, tile)
    strip_colors = [jnp.broadcast_to(t, strip) for t in (color_low, color_high)]

    def masks(shape):
        lane = lax.broadcasted_iota(jnp.int32, shape, 1)
        row = lax.broadcasted_iota(jnp.int32, shape, 0)
        return lane == 0, lane == LANES - 1, row == 0, row == shape[0] - 1

    first_lane, last_lane, first_row, last_row = masks(tile)
    strip_first_lane, strip_last_lane, front, back = masks(strip)

    def chunk(j, carry):
        here = pl.ds(pl.multiple_of(j * LANES, LANES), LANES)
        left = pl.ds(pl.multiple_of(jnp.maximum(j - 1, 0) * LANES, LANES), LANES)
        right = pl.ds(pl.multiple_of(jnp.minimum(j + 1, chunks - 1) * LANES, LANES), LANES)

        def across(value, left_value, right_value, first, last):
            west = jnp.where(last & (j > 0), left_value, value)
            west = pltpu.roll(jnp.where(last & (j == 0), 0, west), 1, 1)
            east = jnp.where(first & (j < chunks - 1), right_value, value)
            east = pltpu.roll(jnp.where(first & (j == chunks - 1), 0, east), LANES - 1, 1)
            return (east - west).astype(jnp.float32)

        for r in range(tiles):
            rows = slice(r * SUBLANES, (r + 1) * SUBLANES)
            values = [volume_ref[0, s, rows, here] for s in range(slices)]
            remaining = jnp.ones(tile, jnp.float32)
            sums = [jnp.zeros(tile, jnp.float32) for _ in range(3)]
            for s in range(slices):
                value = values[s]
                up = volume_ref[0, s, (r - 1) * SUBLANES : r * SUBLANES, here] if r > 0 else value
                down = volume_ref[0, s, (r + 1) * SUBLANES : (r + 2) * SUBLANES, here] if r < tiles - 1 else value
                up = pltpu.roll(jnp.where(last_row, up, value), 1, 0)
                down = pltpu.roll(jnp.where(first_row, down, value), SUBLANES - 1, 0)
                grad_rows = (down - up).astype(jnp.float32)
                grad_cols = across(
                    value, volume_ref[0, s, rows, left], volume_ref[0, s, rows, right], first_lane, last_lane
                )
                squares = grad_rows * grad_rows + grad_cols * grad_cols
                facing = LIGHT_ROWS * grad_rows + LIGHT_COLS * grad_cols
                weight = remaining * opacity(volume_ref[1, s, rows, here], tile_alpha)
                remaining = remaining - weight
                if r == 0:
                    held_ref[0, s : s + 1, :] = weight[:1]
                    weight = jnp.where(first_row, 0.0, weight)
                if r == tiles - 1:
                    held_ref[1, s : s + 1, :] = weight[SUBLANES - 1 :]
                    weight = jnp.where(last_row, 0.0, weight)
                emitted = colors(value, tile_colors)
                if 0 < s < slices - 1:
                    grad_depth = (values[s + 1] - values[s - 1]).astype(jnp.float32)
                    weight = weight * shade(grad_depth, facing, squares)
                    for c in range(3):
                        sums[c] = sums[c] + emitted[c] * weight
                else:
                    end = int(s > 0)
                    face_ref[end, rows, here] = facing
                    square_ref[end, rows, here] = squares
                    weight = weight * (1.0 / 255.0)
                    for c in range(3):
                        lit_ref[end, c, rows, here] = emitted[c] * weight
            for c in range(3):
                base_ref[c, rows, here] = sums[c] * (1.0 / 255.0)
            base_ref[3, rows, here] = 1.0 - remaining

        for q, (edge, inner) in enumerate(((0, 1), (height - 1, height - 2))):
            value = volume_ref[0, :, edge, here]
            behind = pltpu.roll(jnp.where(back, 0, value), 1, 0)
            ahead = pltpu.roll(jnp.where(front, 0, value), slices - 1, 0)
            grad_ref[q, 0, :, here] = (ahead - behind).astype(jnp.float32)
            grad_ref[q, 1, :, here] = volume_ref[0, :, inner, here].astype(jnp.float32)
            grad_ref[q, 2, :, here] = across(
                value, volume_ref[0, :, edge, left], volume_ref[0, :, edge, right], strip_first_lane, strip_last_lane
            )
            weight = held_ref[q] * (1.0 / 255.0)
            emitted = colors(value, strip_colors)
            for c in range(3):
                strip_ref[q, c, :, here] = emitted[c] * weight
        return carry

    lax.fori_loop(0, chunks, chunk, 0)


def march_interior(volume, color_map, alpha_map, depth_count):
    _, slices, height, columns = volume.shape
    opacity_scale = OPACITY / (255.0 * slices * depth_count)
    shapes = [
        (4, height, columns),
        (2, height, columns),
        (2, height, columns),
        (2, 3, height, columns),
        (2, 3, slices, columns),
        (2, 3, slices, columns),
    ]
    voxels = slices * height * columns
    return pl.pallas_call(
        functools.partial(interior_kernel, opacity_scale),
        in_specs=[WHOLE] * 3,
        out_specs=[WHOLE] * len(shapes),
        out_shape=[jax.ShapeDtypeStruct(shape, jnp.float32) for shape in shapes],
        scratch_shapes=[pltpu.VMEM((2, slices, LANES), jnp.float32)],
        compiler_params=pltpu.CompilerParams(vmem_limit_bytes=24 * 1024 * 1024),
        cost_estimate=pl.CostEstimate(flops=voxels * 80, bytes_accessed=voxels * 20, transcendentals=voxels),
    )(volume, color_map, alpha_map.reshape(1, -1))


def edge_kernel(
    share, volume_ref, base_ref, face_ref, square_ref, lit_ref, grad_ref, strip_ref, rows_near_ref, rows_far_ref, far_ref, near_ref, out_ref
):
    _, slices, height, columns = volume_ref.shape
    tiles = height // SUBLANES
    tile = (SUBLANES, LANES)
    row = lax.broadcasted_iota(jnp.int32, tile, 0)
    first_row, last_row = row == 0, row == SUBLANES - 1
    level = lax.broadcasted_iota(jnp.int32, (slices, LANES), 0)
    front, back = level == 0, level == slices - 1
    odd, odd_row = parity("depth") == 1, parity("rows") == 1

    def chunk(j, carry):
        here = pl.ds(pl.multiple_of(j * LANES, LANES), LANES)
        rows_near = rows_near_ref[:, here].astype(jnp.float32)
        rows_far = rows_far_ref[:, here].astype(jnp.float32)
        above = jnp.where(odd_row, rows_near, rows_far)
        below = jnp.where(odd_row, rows_far, rows_near)
        far = far_ref[:, here].astype(jnp.float32)
        near = near_ref[:, here].astype(jnp.float32)
        before = jnp.where(odd, near, far)
        after = jnp.where(odd, far, near)
        extra = []
        for q, edge in enumerate((0, height - 1)):
            inner = grad_ref[q, 1, :, here]
            grad_rows = below - inner if q else inner - above
            grad_cols = grad_ref[q, 2, :, here]
            grad_depth = grad_ref[q, 0, :, here] + jnp.where(
                back, after[edge : edge + 1], jnp.where(front, -before[edge : edge + 1], 0.0)
            )
            shading = shade(
                grad_depth,
                LIGHT_ROWS * grad_rows + LIGHT_COLS * grad_cols,
                grad_rows * grad_rows + grad_cols * grad_cols,
            )
            extra.append([jnp.sum(strip_ref[q, c, :, here] * shading, axis=0, keepdims=True) for c in range(3)])
        for r in range(tiles):
            rows = slice(r * SUBLANES, (r + 1) * SUBLANES)
            planes = [base_ref[c, rows, here] for c in range(4)]
            for end in range(2):
                if end:
                    grad_depth = after[rows] - volume_ref[0, slices - 2, rows, here].astype(jnp.float32)
                else:
                    grad_depth = volume_ref[0, 1, rows, here].astype(jnp.float32) - before[rows]
                shading = shade(grad_depth, face_ref[end, rows, here], square_ref[end, rows, here])
                for c in range(3):
                    planes[c] = planes[c] + lit_ref[end, c, rows, here] * shading
            for c in range(3):
                if r == 0:
                    planes[c] = planes[c] + jnp.where(first_row, extra[0][c], 0.0)
                if r == tiles - 1:
                    planes[c] = planes[c] + jnp.where(last_row, extra[1][c], 0.0)
            for first in range(0, SUBLANES, share):
                block = jnp.concatenate([plane[first : first + share] for plane in planes], axis=0)
                out_ref[(r * SUBLANES + first) // share, :, here] = block.astype(jnp.bfloat16)
        return carry

    lax.fori_loop(0, columns // LANES, chunk, 0)


def add_edges(volume, interior, halos, depth_count):
    _, slices, height, columns = volume.shape
    share = height // depth_count
    return pl.pallas_call(
        functools.partial(edge_kernel, share),
        in_specs=[WHOLE] * 11,
        out_specs=WHOLE,
        out_shape=jax.ShapeDtypeStruct((depth_count, 4 * share, columns), jnp.bfloat16),
        compiler_params=pltpu.CompilerParams(vmem_limit_bytes=24 * 1024 * 1024),
    )(volume, *interior, *halos)


def finish_kernel(parts_ref, out_ref):
    count = parts_ref.shape[0]
    _, share, columns = out_ref.shape
    remaining = jnp.ones((share, columns), jnp.float32)
    sums = [jnp.zeros((share, columns), jnp.float32) for _ in range(3)]
    for k in range(count):
        part = parts_ref[k].astype(jnp.float32)
        for c in range(3):
            sums[c] = sums[c] + remaining * part[c * share : (c + 1) * share]
        remaining = remaining - remaining * part[3 * share :]
    for c in range(3):
        out_ref[c] = sums[c]
    out_ref[3] = 1.0 - remaining


def finish(parts, share):
    columns = parts.shape[2]
    return pl.pallas_call(
        finish_kernel,
        in_specs=[WHOLE],
        out_specs=WHOLE,
        out_shape=jax.ShapeDtypeStruct((4, share, columns), jnp.float32),
    )(parts)


def swapped(values, axis, start):
    pairs = [(i, i + 1) for i in range(start, lax.axis_size(axis) - 1, 2)]
    return lax.ppermute(values, axis, pairs + [(j, i) for i, j in pairs])


def body(volume, color_map, alpha_map):
    depth_count = lax.axis_size("depth")
    share = volume.shape[2] // depth_count
    rows_near, rows_far, far, near = cut_edges(volume)
    rows_near = swapped(rows_near, "rows", 0)
    rows_far = swapped(rows_far, "rows", 1)
    far = swapped(far, "depth", 1)
    near = swapped(near, "depth", 0)
    interior = march_interior(volume, color_map, alpha_map, depth_count)
    parts = add_edges(volume, interior, (rows_near, rows_far, far, near), depth_count)
    parts = lax.all_to_all(parts, "depth", 0, 0, tiled=True)
    return finish(parts, share)


def solution(mesh):
    in_specs = (P(None, "depth", "rows", None), P(), P())
    out_specs = P(None, ("rows", "depth"), None)
    return jax.shard_map(body, mesh=mesh, in_specs=in_specs, out_specs=out_specs, check_vma=False)
```

```python
import functools

import jax
import jax.numpy as jnp
from jax import lax
from jax.experimental import pallas as pl
from jax.experimental.pallas import tpu as pltpu
from jax.sharding import PartitionSpec as P

AMBIENT = 0.3
DIFFUSE = 0.7
LIGHT_DEPTH = 0.48 * DIFFUSE
LIGHT_ROWS = 0.6 * DIFFUSE
LIGHT_COLS = 0.64 * DIFFUSE
OPACITY = 4.0
LANES = 128
SUBLANES = 8
WHOLE = pl.BlockSpec(memory_space=pltpu.VMEM)


def parity(axis):
    return lax.axis_index(axis) % 2


def ends(axis):
    position = lax.axis_index(axis)
    return position == 0, position == lax.axis_size(axis) - 1


def edges_kernel(volume_ref, rows_near_out, rows_far_out, far_out, near_out, strip_ref, plane_ref, sems):
    _, slices, height, _ = volume_ref.shape
    odd, odd_row = parity("depth"), parity("rows")
    last_tile = height // SUBLANES - 1

    def tile(i):
        return pl.ds(pl.multiple_of(i * SUBLANES, SUBLANES), SUBLANES)

    copies = [
        pltpu.make_async_copy(volume_ref.at[0, :, tile((1 - odd_row) * last_tile)], strip_ref.at[0], sems.at[0]),
        pltpu.make_async_copy(volume_ref.at[0, :, tile(odd_row * last_tile)], strip_ref.at[1], sems.at[1]),
        pltpu.make_async_copy(volume_ref.at[0, odd * (slices - 1)], plane_ref.at[0], sems.at[2]),
        pltpu.make_async_copy(volume_ref.at[0, (1 - odd) * (slices - 1)], plane_ref.at[1], sems.at[3]),
    ]
    for copy in copies:
        copy.start()

    def narrow(values):
        return values.astype(jnp.float32).astype(jnp.bfloat16)

    copies[0].wait()
    rows_near_out[...] = narrow(jnp.where(odd_row == 1, strip_ref[0, :, 0, :], strip_ref[0, :, SUBLANES - 1, :]))
    copies[1].wait()
    rows_far_out[...] = narrow(jnp.where(odd_row == 1, strip_ref[1, :, SUBLANES - 1, :], strip_ref[1, :, 0, :]))
    copies[2].wait()
    far_out[...] = narrow(plane_ref[0])
    copies[3].wait()
    near_out[...] = narrow(plane_ref[1])


def cut_edges(volume):
    _, slices, height, columns = volume.shape
    plane = jax.ShapeDtypeStruct((height, columns), jnp.bfloat16)
    strip = jax.ShapeDtypeStruct((slices, columns), jnp.bfloat16)
    return pl.pallas_call(
        edges_kernel,
        in_specs=[pl.BlockSpec(memory_space=pl.ANY)],
        out_specs=[WHOLE] * 4,
        out_shape=[strip, strip, plane, plane],
        scratch_shapes=[
            pltpu.VMEM((2, slices, SUBLANES, columns), jnp.int32),
            pltpu.VMEM((2, height, columns), jnp.int32),
            pltpu.SemaphoreType.DMA((4,)),
        ],
    )(volume)


def pick(entries, places):
    return jnp.take_along_axis(entries, places, axis=1, mode="promise_in_bounds")


def shade(grad_depth, facing, squares):
    facing = facing + LIGHT_DEPTH * grad_depth
    squares = squares + grad_depth * grad_depth
    return AMBIENT + jnp.abs(facing) * lax.rsqrt(jnp.maximum(squares, 4.0))


def interior_kernel(
    opacity_scale, volume_ref, color_ref, alpha_ref, base_ref, face_ref, square_ref, lit_ref, grad_ref, strip_ref, held_ref
):
    _, slices, height, columns = volume_ref.shape
    tiles = height // SUBLANES
    chunks = columns // LANES
    tile = (SUBLANES, LANES)
    strip = (slices, LANES)

    packed = color_ref[0:1, :] + color_ref[1:2, :] * 256 + color_ref[2:3, :] * 65536
    color_low, color_high = packed[:, :LANES], packed[:, LANES:]
    alpha_both = alpha_ref[0:1, :LANES] + alpha_ref[0:1, LANES:] * 256

    def colors(value, tables):
        low, high = tables
        place = value & (LANES - 1)
        color = jnp.where(value < LANES, pick(low, place), pick(high, place))
        parts = (color & 255, lax.shift_right_logical(color, 8) & 255, lax.shift_right_logical(color, 16))
        return [part.astype(jnp.float32) for part in parts]

    def opacity(level, table):
        entry = pick(table, level & (LANES - 1))
        entry = lax.shift_right_logical(entry, lax.shift_right_logical(level & LANES, 4)) & 255
        return entry.astype(jnp.float32) * opacity_scale

    tile_colors = [jnp.broadcast_to(t, tile) for t in (color_low, color_high)]
    tile_alpha = jnp.broadcast_to(alpha_both, tile)
    strip_colors = [jnp.broadcast_to(t, strip) for t in (color_low, color_high)]

    def masks(shape):
        lane = lax.broadcasted_iota(jnp.int32, shape, 1)
        row = lax.broadcasted_iota(jnp.int32, shape, 0)
        return lane == 0, lane == LANES - 1, row == 0, row == shape[0] - 1

    first_lane, last_lane, first_row, last_row = masks(tile)
    strip_first_lane, strip_last_lane, front, back = masks(strip)

    def chunk(j, carry):
        here = pl.ds(pl.multiple_of(j * LANES, LANES), LANES)
        left = pl.ds(pl.multiple_of(jnp.maximum(j - 1, 0) * LANES, LANES), LANES)
        right = pl.ds(pl.multiple_of(jnp.minimum(j + 1, chunks - 1) * LANES, LANES), LANES)

        def across(value, left_value, right_value, first, last):
            west = jnp.where(last & (j > 0), left_value, value)
            west = pltpu.roll(jnp.where(last & (j == 0), 0, west), 1, 1)
            east = jnp.where(first & (j < chunks - 1), right_value, value)
            east = pltpu.roll(jnp.where(first & (j == chunks - 1), 0, east), LANES - 1, 1)
            return (east - west).astype(jnp.float32)

        for r in range(tiles):
            rows = slice(r * SUBLANES, (r + 1) * SUBLANES)
            values = [volume_ref[0, s, rows, here] for s in range(slices)]
            remaining = jnp.ones(tile, jnp.float32)
            sums = [jnp.zeros(tile, jnp.float32) for _ in range(3)]
            for s in range(slices):
                value = values[s]
                up = volume_ref[0, s, (r - 1) * SUBLANES : r * SUBLANES, here] if r > 0 else value
                down = volume_ref[0, s, (r + 1) * SUBLANES : (r + 2) * SUBLANES, here] if r < tiles - 1 else value
                up = pltpu.roll(jnp.where(last_row, up, value), 1, 0)
                down = pltpu.roll(jnp.where(first_row, down, value), SUBLANES - 1, 0)
                grad_rows = (down - up).astype(jnp.float32)
                grad_cols = across(
                    value, volume_ref[0, s, rows, left], volume_ref[0, s, rows, right], first_lane, last_lane
                )
                squares = grad_rows * grad_rows + grad_cols * grad_cols
                facing = LIGHT_ROWS * grad_rows + LIGHT_COLS * grad_cols
                weight = remaining * opacity(volume_ref[1, s, rows, here], tile_alpha)
                remaining = remaining - weight
                if r == 0:
                    held_ref[0, s : s + 1, :] = weight[:1]
                    weight = jnp.where(first_row, 0.0, weight)
                if r == tiles - 1:
                    held_ref[1, s : s + 1, :] = weight[SUBLANES - 1 :]
                    weight = jnp.where(last_row, 0.0, weight)
                emitted = colors(value, tile_colors)
                if 0 < s < slices - 1:
                    grad_depth = (values[s + 1] - values[s - 1]).astype(jnp.float32)
                    weight = weight * shade(grad_depth, facing, squares)
                    for c in range(3):
                        sums[c] = sums[c] + emitted[c] * weight
                else:
                    end = int(s > 0)
                    face_ref[end, rows, here] = facing
                    square_ref[end, rows, here] = squares
                    weight = weight * (1.0 / 255.0)
                    for c in range(3):
                        lit_ref[end, c, rows, here] = emitted[c] * weight
            for c in range(3):
                base_ref[c, rows, here] = sums[c] * (1.0 / 255.0)
            base_ref[3, rows, here] = 1.0 - remaining

        for q, (edge, inner) in enumerate(((0, 1), (height - 1, height - 2))):
            value = volume_ref[0, :, edge, here]
            behind = pltpu.roll(jnp.where(back, 0, value), 1, 0)
            ahead = pltpu.roll(jnp.where(front, 0, value), slices - 1, 0)
            grad_ref[q, 0, :, here] = (ahead - behind).astype(jnp.float32)
            grad_ref[q, 1, :, here] = volume_ref[0, :, inner, here].astype(jnp.float32)
            grad_ref[q, 2, :, here] = across(
                value, volume_ref[0, :, edge, left], volume_ref[0, :, edge, right], strip_first_lane, strip_last_lane
            )
            weight = held_ref[q] * (1.0 / 255.0)
            emitted = colors(value, strip_colors)
            for c in range(3):
                strip_ref[q, c, :, here] = emitted[c] * weight
        return carry

    lax.fori_loop(0, chunks, chunk, 0)


def march_interior(volume, color_map, alpha_map, depth_count):
    _, slices, height, columns = volume.shape
    opacity_scale = OPACITY / (255.0 * slices * depth_count)
    shapes = [
        (4, height, columns),
        (2, height, columns),
        (2, height, columns),
        (2, 3, height, columns),
        (2, 3, slices, columns),
        (2, 3, slices, columns),
    ]
    voxels = slices * height * columns
    return pl.pallas_call(
        functools.partial(interior_kernel, opacity_scale),
        in_specs=[WHOLE] * 3,
        out_specs=[WHOLE] * len(shapes),
        out_shape=[jax.ShapeDtypeStruct(shape, jnp.float32) for shape in shapes],
        scratch_shapes=[pltpu.VMEM((2, slices, LANES), jnp.float32)],
        compiler_params=pltpu.CompilerParams(vmem_limit_bytes=24 * 1024 * 1024),
        cost_estimate=pl.CostEstimate(flops=voxels * 80, bytes_accessed=voxels * 20, transcendentals=voxels),
    )(volume, color_map, alpha_map.reshape(1, -1))


def edge_kernel(
    share, volume_ref, base_ref, face_ref, square_ref, lit_ref, grad_ref, strip_ref, rows_near_ref, rows_far_ref, far_ref, near_ref, out_ref
):
    _, slices, height, columns = volume_ref.shape
    tiles = height // SUBLANES
    tile = (SUBLANES, LANES)
    row = lax.broadcasted_iota(jnp.int32, tile, 0)
    first_row, last_row = row == 0, row == SUBLANES - 1
    level = lax.broadcasted_iota(jnp.int32, (slices, LANES), 0)
    front, back = level == 0, level == slices - 1
    odd, odd_row = parity("depth") == 1, parity("rows") == 1
    front_end, back_end = ends("depth")
    top_end, bottom_end = ends("rows")

    def chunk(j, carry):
        here = pl.ds(pl.multiple_of(j * LANES, LANES), LANES)
        rows_near = rows_near_ref[:, here].astype(jnp.float32)
        rows_far = rows_far_ref[:, here].astype(jnp.float32)
        above = jnp.where(top_end, 0.0, jnp.where(odd_row, rows_near, rows_far))
        below = jnp.where(bottom_end, 0.0, jnp.where(odd_row, rows_far, rows_near))
        far = far_ref[:, here].astype(jnp.float32)
        near = near_ref[:, here].astype(jnp.float32)
        before = jnp.where(front_end, 0.0, jnp.where(odd, near, far))
        after = jnp.where(back_end, 0.0, jnp.where(odd, far, near))
        extra = []
        for q, edge in enumerate((0, height - 1)):
            inner = grad_ref[q, 1, :, here]
            grad_rows = below - inner if q else inner - above
            grad_cols = grad_ref[q, 2, :, here]
            grad_depth = grad_ref[q, 0, :, here] + jnp.where(
                back, after[edge : edge + 1], jnp.where(front, -before[edge : edge + 1], 0.0)
            )
            shading = shade(
                grad_depth,
                LIGHT_ROWS * grad_rows + LIGHT_COLS * grad_cols,
                grad_rows * grad_rows + grad_cols * grad_cols,
            )
            extra.append([jnp.sum(strip_ref[q, c, :, here] * shading, axis=0, keepdims=True) for c in range(3)])
        for r in range(tiles):
            rows = slice(r * SUBLANES, (r + 1) * SUBLANES)
            planes = [base_ref[c, rows, here] for c in range(4)]
            for end in range(2):
                if end:
                    grad_depth = after[rows] - volume_ref[0, slices - 2, rows, here].astype(jnp.float32)
                else:
                    grad_depth = volume_ref[0, 1, rows, here].astype(jnp.float32) - before[rows]
                shading = shade(grad_depth, face_ref[end, rows, here], square_ref[end, rows, here])
                for c in range(3):
                    planes[c] = planes[c] + lit_ref[end, c, rows, here] * shading
            for c in range(3):
                if r == 0:
                    planes[c] = planes[c] + jnp.where(first_row, extra[0][c], 0.0)
                if r == tiles - 1:
                    planes[c] = planes[c] + jnp.where(last_row, extra[1][c], 0.0)
            for first in range(0, SUBLANES, share):
                block = jnp.concatenate([plane[first : first + share] for plane in planes], axis=0)
                out_ref[(r * SUBLANES + first) // share, :, here] = block.astype(jnp.bfloat16)
        return carry

    lax.fori_loop(0, columns // LANES, chunk, 0)


def add_edges(volume, interior, halos, depth_count):
    _, slices, height, columns = volume.shape
    share = height // depth_count
    return pl.pallas_call(
        functools.partial(edge_kernel, share),
        in_specs=[WHOLE] * 11,
        out_specs=WHOLE,
        out_shape=jax.ShapeDtypeStruct((depth_count, 4 * share, columns), jnp.bfloat16),
        compiler_params=pltpu.CompilerParams(vmem_limit_bytes=24 * 1024 * 1024),
    )(volume, *interior, *halos)


def finish_kernel(parts_ref, out_ref):
    count = parts_ref.shape[0]
    _, share, columns = out_ref.shape
    remaining = jnp.ones((share, columns), jnp.float32)
    sums = [jnp.zeros((share, columns), jnp.float32) for _ in range(3)]
    for k in range(count):
        part = parts_ref[k].astype(jnp.float32)
        for c in range(3):
            sums[c] = sums[c] + remaining * part[c * share : (c + 1) * share]
        remaining = remaining - remaining * part[3 * share :]
    for c in range(3):
        out_ref[c] = sums[c]
    out_ref[3] = 1.0 - remaining


def finish(parts, share):
    columns = parts.shape[2]
    return pl.pallas_call(
        finish_kernel,
        in_specs=[WHOLE],
        out_specs=WHOLE,
        out_shape=jax.ShapeDtypeStruct((4, share, columns), jnp.float32),
    )(parts)


def swapped(values, axis, start):
    size = lax.axis_size(axis)
    partner = list(range(size))
    for i in range(start, size - 1, 2):
        partner[i], partner[i + 1] = i + 1, i
    return lax.ppermute(values, axis, list(enumerate(partner)))


def body(volume, color_map, alpha_map):
    depth_count = lax.axis_size("depth")
    share = volume.shape[2] // depth_count
    rows_near, rows_far, far, near = cut_edges(volume)
    rows_far = swapped(rows_far, "rows", 1)
    rows_near = swapped(rows_near, "rows", 0)
    far = swapped(far, "depth", 1)
    near = swapped(near, "depth", 0)
    interior = march_interior(volume, color_map, alpha_map, depth_count)
    parts = add_edges(volume, interior, (rows_near, rows_far, far, near), depth_count)
    parts = lax.all_to_all(parts, "depth", 0, 0, tiled=True)
    return finish(parts, share)


def solution(mesh):
    in_specs = (P(None, "depth", "rows", None), P(), P())
    out_specs = P(None, ("rows", "depth"), None)
    return jax.shard_map(body, mesh=mesh, in_specs=in_specs, out_specs=out_specs, check_vma=False)
```

```python
import functools

import jax
import jax.numpy as jnp
from jax import lax
from jax.experimental import pallas as pl
from jax.experimental.pallas import tpu as pltpu
from jax.sharding import PartitionSpec as P

AMBIENT = 0.3
DIFFUSE = 0.7
LIGHT_DEPTH = 0.48 * DIFFUSE
LIGHT_ROWS = 0.6 * DIFFUSE
LIGHT_COLS = 0.64 * DIFFUSE
OPACITY = 4.0
LANES = 128
SUBLANES = 8
WHOLE = pl.BlockSpec(memory_space=pltpu.VMEM)


def parity(axis):
    return lax.axis_index(axis) % 2


def ends(axis):
    position = lax.axis_index(axis)
    return position == 0, position == lax.axis_size(axis) - 1


def edges_kernel(volume_ref, rows_far_out, rows_near_out, far_out, near_out, strip_ref, plane_ref, sems):
    _, slices, height, _ = volume_ref.shape
    odd, odd_row = parity("depth"), parity("rows")
    last_tile = height // SUBLANES - 1

    def tile(i):
        return pl.ds(pl.multiple_of(i * SUBLANES, SUBLANES), SUBLANES)

    copies = [
        pltpu.make_async_copy(volume_ref.at[0, :, tile((1 - odd_row) * last_tile)], strip_ref.at[0], sems.at[0]),
        pltpu.make_async_copy(volume_ref.at[0, :, tile(odd_row * last_tile)], strip_ref.at[1], sems.at[1]),
        pltpu.make_async_copy(volume_ref.at[0, odd * (slices - 1)], plane_ref.at[0], sems.at[2]),
        pltpu.make_async_copy(volume_ref.at[0, (1 - odd) * (slices - 1)], plane_ref.at[1], sems.at[3]),
    ]
    for copy in copies:
        copy.start()

    def narrow(values):
        return values.astype(jnp.float32).astype(jnp.bfloat16)

    copies[0].wait()
    rows_near_out[...] = narrow(jnp.where(odd_row == 1, strip_ref[0, :, 0, :], strip_ref[0, :, SUBLANES - 1, :]))
    copies[1].wait()
    rows_far_out[...] = narrow(jnp.where(odd_row == 1, strip_ref[1, :, SUBLANES - 1, :], strip_ref[1, :, 0, :]))
    copies[2].wait()
    far_out[...] = narrow(plane_ref[0])
    copies[3].wait()
    near_out[...] = narrow(plane_ref[1])


def cut_edges(volume):
    _, slices, height, columns = volume.shape
    plane = jax.ShapeDtypeStruct((height, columns), jnp.bfloat16)
    strip = jax.ShapeDtypeStruct((slices, columns), jnp.bfloat16)
    return pl.pallas_call(
        edges_kernel,
        in_specs=[pl.BlockSpec(memory_space=pl.ANY)],
        out_specs=[WHOLE] * 4,
        out_shape=[strip, strip, plane, plane],
        scratch_shapes=[
            pltpu.VMEM((2, slices, SUBLANES, columns), jnp.int32),
            pltpu.VMEM((2, height, columns), jnp.int32),
            pltpu.SemaphoreType.DMA((4,)),
        ],
    )(volume)


def pick(entries, places):
    return jnp.take_along_axis(entries, places, axis=1, mode="promise_in_bounds")


def shade(grad_depth, facing, squares):
    facing = facing + LIGHT_DEPTH * grad_depth
    squares = squares + grad_depth * grad_depth
    return AMBIENT + jnp.abs(facing) * lax.rsqrt(jnp.maximum(squares, 4.0))


def interior_kernel(
    opacity_scale, volume_ref, color_ref, alpha_ref, base_ref, face_ref, square_ref, lit_ref, grad_ref, strip_ref, held_ref
):
    _, slices, height, columns = volume_ref.shape
    tiles = height // SUBLANES
    chunks = columns // LANES
    tile = (SUBLANES, LANES)
    strip = (slices, LANES)

    packed = color_ref[0:1, :] + color_ref[1:2, :] * 256 + color_ref[2:3, :] * 65536
    color_low, color_high = packed[:, :LANES], packed[:, LANES:]
    alpha_both = alpha_ref[0:1, :LANES] + alpha_ref[0:1, LANES:] * 256

    def colors(value, tables):
        low, high = tables
        place = value & (LANES - 1)
        color = jnp.where(value < LANES, pick(low, place), pick(high, place))
        parts = (color & 255, lax.shift_right_logical(color, 8) & 255, lax.shift_right_logical(color, 16))
        return [part.astype(jnp.float32) for part in parts]

    def opacity(level, table):
        entry = pick(table, level & (LANES - 1))
        entry = lax.shift_right_logical(entry, lax.shift_right_logical(level & LANES, 4)) & 255
        return entry.astype(jnp.float32) * opacity_scale

    tile_colors = [jnp.broadcast_to(t, tile) for t in (color_low, color_high)]
    tile_alpha = jnp.broadcast_to(alpha_both, tile)
    strip_colors = [jnp.broadcast_to(t, strip) for t in (color_low, color_high)]

    def masks(shape):
        lane = lax.broadcasted_iota(jnp.int32, shape, 1)
        row = lax.broadcasted_iota(jnp.int32, shape, 0)
        return lane == 0, lane == LANES - 1, row == 0, row == shape[0] - 1

    first_lane, last_lane, first_row, last_row = masks(tile)
    strip_first_lane, strip_last_lane, front, back = masks(strip)

    def chunk(j, carry):
        here = pl.ds(pl.multiple_of(j * LANES, LANES), LANES)
        left = pl.ds(pl.multiple_of(jnp.maximum(j - 1, 0) * LANES, LANES), LANES)
        right = pl.ds(pl.multiple_of(jnp.minimum(j + 1, chunks - 1) * LANES, LANES), LANES)

        def across(value, left_value, right_value, first, last):
            west = jnp.where(last & (j > 0), left_value, value)
            west = pltpu.roll(jnp.where(last & (j == 0), 0, west), 1, 1)
            east = jnp.where(first & (j < chunks - 1), right_value, value)
            east = pltpu.roll(jnp.where(first & (j == chunks - 1), 0, east), LANES - 1, 1)
            return (east - west).astype(jnp.float32)

        for r in range(tiles):
            rows = slice(r * SUBLANES, (r + 1) * SUBLANES)
            values = [volume_ref[0, s, rows, here] for s in range(slices)]
            remaining = jnp.ones(tile, jnp.float32)
            sums = [jnp.zeros(tile, jnp.float32) for _ in range(3)]
            for s in range(slices):
                value = values[s]
                up = volume_ref[0, s, (r - 1) * SUBLANES : r * SUBLANES, here] if r > 0 else value
                down = volume_ref[0, s, (r + 1) * SUBLANES : (r + 2) * SUBLANES, here] if r < tiles - 1 else value
                up = pltpu.roll(jnp.where(last_row, up, value), 1, 0)
                down = pltpu.roll(jnp.where(first_row, down, value), SUBLANES - 1, 0)
                grad_rows = (down - up).astype(jnp.float32)
                grad_cols = across(
                    value, volume_ref[0, s, rows, left], volume_ref[0, s, rows, right], first_lane, last_lane
                )
                squares = grad_rows * grad_rows + grad_cols * grad_cols
                facing = LIGHT_ROWS * grad_rows + LIGHT_COLS * grad_cols
                weight = remaining * opacity(volume_ref[1, s, rows, here], tile_alpha)
                remaining = remaining - weight
                if r == 0:
                    held_ref[0, s : s + 1, :] = weight[:1]
                    weight = jnp.where(first_row, 0.0, weight)
                if r == tiles - 1:
                    held_ref[1, s : s + 1, :] = weight[SUBLANES - 1 :]
                    weight = jnp.where(last_row, 0.0, weight)
                emitted = colors(value, tile_colors)
                if 0 < s < slices - 1:
                    grad_depth = (values[s + 1] - values[s - 1]).astype(jnp.float32)
                    weight = weight * shade(grad_depth, facing, squares)
                    for c in range(3):
                        sums[c] = sums[c] + emitted[c] * weight
                else:
                    end = int(s > 0)
                    face_ref[end, rows, here] = facing
                    square_ref[end, rows, here] = squares
                    weight = weight * (1.0 / 255.0)
                    for c in range(3):
                        lit_ref[end, c, rows, here] = emitted[c] * weight
            for c in range(3):
                base_ref[c, rows, here] = sums[c] * (1.0 / 255.0)
            base_ref[3, rows, here] = 1.0 - remaining

        for q, (edge, inner) in enumerate(((0, 1), (height - 1, height - 2))):
            value = volume_ref[0, :, edge, here]
            behind = pltpu.roll(jnp.where(back, 0, value), 1, 0)
            ahead = pltpu.roll(jnp.where(front, 0, value), slices - 1, 0)
            grad_ref[q, 0, :, here] = (ahead - behind).astype(jnp.float32)
            grad_ref[q, 1, :, here] = volume_ref[0, :, inner, here].astype(jnp.float32)
            grad_ref[q, 2, :, here] = across(
                value, volume_ref[0, :, edge, left], volume_ref[0, :, edge, right], strip_first_lane, strip_last_lane
            )
            weight = held_ref[q] * (1.0 / 255.0)
            emitted = colors(value, strip_colors)
            for c in range(3):
                strip_ref[q, c, :, here] = emitted[c] * weight
        return carry

    lax.fori_loop(0, chunks, chunk, 0)


def march_interior(volume, color_map, alpha_map, depth_count):
    _, slices, height, columns = volume.shape
    opacity_scale = OPACITY / (255.0 * slices * depth_count)
    shapes = [
        (4, height, columns),
        (2, height, columns),
        (2, height, columns),
        (2, 3, height, columns),
        (2, 3, slices, columns),
        (2, 3, slices, columns),
    ]
    voxels = slices * height * columns
    return pl.pallas_call(
        functools.partial(interior_kernel, opacity_scale),
        in_specs=[WHOLE] * 3,
        out_specs=[WHOLE] * len(shapes),
        out_shape=[jax.ShapeDtypeStruct(shape, jnp.float32) for shape in shapes],
        scratch_shapes=[pltpu.VMEM((2, slices, LANES), jnp.float32)],
        compiler_params=pltpu.CompilerParams(vmem_limit_bytes=24 * 1024 * 1024),
        cost_estimate=pl.CostEstimate(flops=voxels * 80, bytes_accessed=voxels * 20, transcendentals=voxels),
    )(volume, color_map, alpha_map.reshape(1, -1))


def edge_kernel(
    share, volume_ref, base_ref, face_ref, square_ref, lit_ref, grad_ref, strip_ref, rows_far_ref, rows_near_ref, far_ref, near_ref, out_ref
):
    _, slices, height, columns = volume_ref.shape
    tiles = height // SUBLANES
    tile = (SUBLANES, LANES)
    row = lax.broadcasted_iota(jnp.int32, tile, 0)
    first_row, last_row = row == 0, row == SUBLANES - 1
    level = lax.broadcasted_iota(jnp.int32, (slices, LANES), 0)
    front, back = level == 0, level == slices - 1
    odd, odd_row = parity("depth") == 1, parity("rows") == 1
    front_end, back_end = ends("depth")
    top_end, bottom_end = ends("rows")

    def chunk(j, carry):
        here = pl.ds(pl.multiple_of(j * LANES, LANES), LANES)
        rows_near = rows_near_ref[:, here].astype(jnp.float32)
        rows_far = rows_far_ref[:, here].astype(jnp.float32)
        above = jnp.where(top_end, 0.0, jnp.where(odd_row, rows_near, rows_far))
        below = jnp.where(bottom_end, 0.0, jnp.where(odd_row, rows_far, rows_near))
        far = far_ref[:, here].astype(jnp.float32)
        near = near_ref[:, here].astype(jnp.float32)
        before = jnp.where(front_end, 0.0, jnp.where(odd, near, far))
        after = jnp.where(back_end, 0.0, jnp.where(odd, far, near))
        extra = []
        for q, edge in enumerate((0, height - 1)):
            inner = grad_ref[q, 1, :, here]
            grad_rows = below - inner if q else inner - above
            grad_cols = grad_ref[q, 2, :, here]
            grad_depth = grad_ref[q, 0, :, here] + jnp.where(
                back, after[edge : edge + 1], jnp.where(front, -before[edge : edge + 1], 0.0)
            )
            shading = shade(
                grad_depth,
                LIGHT_ROWS * grad_rows + LIGHT_COLS * grad_cols,
                grad_rows * grad_rows + grad_cols * grad_cols,
            )
            extra.append([jnp.sum(strip_ref[q, c, :, here] * shading, axis=0, keepdims=True) for c in range(3)])
        for r in range(tiles):
            rows = slice(r * SUBLANES, (r + 1) * SUBLANES)
            planes = [base_ref[c, rows, here] for c in range(4)]
            for end in range(2):
                if end:
                    grad_depth = after[rows] - volume_ref[0, slices - 2, rows, here].astype(jnp.float32)
                else:
                    grad_depth = volume_ref[0, 1, rows, here].astype(jnp.float32) - before[rows]
                shading = shade(grad_depth, face_ref[end, rows, here], square_ref[end, rows, here])
                for c in range(3):
                    planes[c] = planes[c] + lit_ref[end, c, rows, here] * shading
            for c in range(3):
                if r == 0:
                    planes[c] = planes[c] + jnp.where(first_row, extra[0][c], 0.0)
                if r == tiles - 1:
                    planes[c] = planes[c] + jnp.where(last_row, extra[1][c], 0.0)
            for first in range(0, SUBLANES, share):
                block = jnp.concatenate([plane[first : first + share] for plane in planes], axis=0)
                out_ref[(r * SUBLANES + first) // share, :, here] = block.astype(jnp.bfloat16)
        return carry

    lax.fori_loop(0, columns // LANES, chunk, 0)


def add_edges(volume, interior, halos, depth_count):
    _, slices, height, columns = volume.shape
    share = height // depth_count
    return pl.pallas_call(
        functools.partial(edge_kernel, share),
        in_specs=[WHOLE] * 11,
        out_specs=WHOLE,
        out_shape=jax.ShapeDtypeStruct((depth_count, 4 * share, columns), jnp.bfloat16),
        compiler_params=pltpu.CompilerParams(vmem_limit_bytes=24 * 1024 * 1024),
    )(volume, *interior, *halos)


def finish_kernel(parts_ref, out_ref):
    count = parts_ref.shape[0]
    _, share, columns = out_ref.shape
    remaining = jnp.ones((share, columns), jnp.float32)
    sums = [jnp.zeros((share, columns), jnp.float32) for _ in range(3)]
    for k in range(count):
        part = parts_ref[k].astype(jnp.float32)
        for c in range(3):
            sums[c] = sums[c] + remaining * part[c * share : (c + 1) * share]
        remaining = remaining - remaining * part[3 * share :]
    for c in range(3):
        out_ref[c] = sums[c]
    out_ref[3] = 1.0 - remaining


def finish(parts, share):
    columns = parts.shape[2]
    return pl.pallas_call(
        finish_kernel,
        in_specs=[WHOLE],
        out_specs=WHOLE,
        out_shape=jax.ShapeDtypeStruct((4, share, columns), jnp.float32),
    )(parts)


def swapped(values, axis, start):
    size = lax.axis_size(axis)
    pairs = [((i + start) % size, (i + 1 + start) % size) for i in range(0, size, 2)]
    return lax.ppermute(values, axis, pairs + [(j, i) for i, j in pairs])


def body(volume, color_map, alpha_map):
    depth_count = lax.axis_size("depth")
    share = volume.shape[2] // depth_count
    rows_far, rows_near, far, near = cut_edges(volume)
    rows_far = swapped(rows_far, "rows", 1)
    rows_near = swapped(rows_near, "rows", 0)
    far = swapped(far, "depth", 1)
    near = swapped(near, "depth", 0)
    interior = march_interior(volume, color_map, alpha_map, depth_count)
    parts = add_edges(volume, interior, (rows_far, rows_near, far, near), depth_count)
    parts = lax.all_to_all(parts, "depth", 0, 0, tiled=True)
    return finish(parts, share)


def solution(mesh):
    in_specs = (P(None, "depth", "rows", None), P(), P())
    out_specs = P(None, ("rows", "depth"), None)
    return jax.shard_map(body, mesh=mesh, in_specs=in_specs, out_specs=out_specs, check_vma=False)
```

```python
import functools

import jax
import jax.numpy as jnp
from jax import lax
from jax.experimental import pallas as pl
from jax.experimental.pallas import tpu as pltpu
from jax.sharding import PartitionSpec as P

AMBIENT = 0.3
DIFFUSE = 0.7
LIGHT_DEPTH = 0.48 * DIFFUSE
LIGHT_ROWS = 0.6 * DIFFUSE
LIGHT_COLS = 0.64 * DIFFUSE
OPACITY = 4.0
LANES = 128
SUBLANES = 8
WHOLE = pl.BlockSpec(memory_space=pltpu.VMEM)


def parity(axis):
    return lax.axis_index(axis) % 2


def ends(axis):
    position = lax.axis_index(axis)
    return position == 0, position == lax.axis_size(axis) - 1


def edges_kernel(volume_ref, rows_far_out, rows_near_out, far_out, near_out, strip_ref, plane_ref, sems):
    _, slices, height, _ = volume_ref.shape
    odd, odd_row = parity("depth"), parity("rows")
    last_tile = height // SUBLANES - 1

    def tile(i):
        return pl.ds(pl.multiple_of(i * SUBLANES, SUBLANES), SUBLANES)

    copies = [
        pltpu.make_async_copy(volume_ref.at[0, :, tile((1 - odd_row) * last_tile)], strip_ref.at[0], sems.at[0]),
        pltpu.make_async_copy(volume_ref.at[0, :, tile(odd_row * last_tile)], strip_ref.at[1], sems.at[1]),
        pltpu.make_async_copy(volume_ref.at[0, odd * (slices - 1)], plane_ref.at[0], sems.at[2]),
        pltpu.make_async_copy(volume_ref.at[0, (1 - odd) * (slices - 1)], plane_ref.at[1], sems.at[3]),
    ]
    for copy in copies:
        copy.start()

    def narrow(values):
        return values.astype(jnp.float32).astype(jnp.bfloat16)

    copies[0].wait()
    rows_near_out[...] = narrow(jnp.where(odd_row == 1, strip_ref[0, :, 0, :], strip_ref[0, :, SUBLANES - 1, :]))
    copies[1].wait()
    rows_far_out[...] = narrow(jnp.where(odd_row == 1, strip_ref[1, :, SUBLANES - 1, :], strip_ref[1, :, 0, :]))
    copies[2].wait()
    far_out[...] = narrow(plane_ref[0])
    copies[3].wait()
    near_out[...] = narrow(plane_ref[1])


def cut_edges(volume):
    _, slices, height, columns = volume.shape
    plane = jax.ShapeDtypeStruct((height, columns), jnp.bfloat16)
    strip = jax.ShapeDtypeStruct((slices, columns), jnp.bfloat16)
    return pl.pallas_call(
        edges_kernel,
        in_specs=[pl.BlockSpec(memory_space=pl.ANY)],
        out_specs=[WHOLE] * 4,
        out_shape=[strip, strip, plane, plane],
        scratch_shapes=[
            pltpu.VMEM((2, slices, SUBLANES, columns), jnp.int32),
            pltpu.VMEM((2, height, columns), jnp.int32),
            pltpu.SemaphoreType.DMA((4,)),
        ],
    )(volume)


def pick(entries, places):
    return jnp.take_along_axis(entries, places, axis=1, mode="promise_in_bounds")


def shade(grad_depth, facing, squares):
    facing = facing + LIGHT_DEPTH * grad_depth
    squares = squares + grad_depth * grad_depth
    return AMBIENT + jnp.abs(facing) * lax.rsqrt(jnp.maximum(squares, 4.0))


def interior_kernel(
    opacity_scale, volume_ref, color_ref, alpha_ref, base_ref, face_ref, square_ref, lit_ref, grad_ref, strip_ref, held_ref
):
    _, slices, height, columns = volume_ref.shape
    tiles = height // SUBLANES
    chunks = columns // LANES
    tile = (SUBLANES, LANES)
    strip = (slices, LANES)

    packed = color_ref[0:1, :] + color_ref[1:2, :] * 256 + color_ref[2:3, :] * 65536
    color_low, color_high = packed[:, :LANES], packed[:, LANES:]
    alpha_both = alpha_ref[0:1, :LANES] + alpha_ref[0:1, LANES:] * 256

    def colors(value, tables):
        low, high = tables
        place = value & (LANES - 1)
        color = jnp.where(value < LANES, pick(low, place), pick(high, place))
        parts = (color & 255, lax.shift_right_logical(color, 8) & 255, lax.shift_right_logical(color, 16))
        return [part.astype(jnp.float32) for part in parts]

    def opacity(level, table):
        entry = pick(table, level & (LANES - 1))
        entry = lax.shift_right_logical(entry, lax.shift_right_logical(level & LANES, 4)) & 255
        return entry.astype(jnp.float32) * opacity_scale

    tile_colors = [jnp.broadcast_to(t, tile) for t in (color_low, color_high)]
    tile_alpha = jnp.broadcast_to(alpha_both, tile)
    strip_colors = [jnp.broadcast_to(t, strip) for t in (color_low, color_high)]

    def masks(shape):
        lane = lax.broadcasted_iota(jnp.int32, shape, 1)
        row = lax.broadcasted_iota(jnp.int32, shape, 0)
        return lane == 0, lane == LANES - 1, row == 0, row == shape[0] - 1

    first_lane, last_lane, first_row, last_row = masks(tile)
    strip_first_lane, strip_last_lane, front, back = masks(strip)

    def chunk(j, carry):
        here = pl.ds(pl.multiple_of(j * LANES, LANES), LANES)
        left = pl.ds(pl.multiple_of(jnp.maximum(j - 1, 0) * LANES, LANES), LANES)
        right = pl.ds(pl.multiple_of(jnp.minimum(j + 1, chunks - 1) * LANES, LANES), LANES)

        def across(value, left_value, right_value, first, last):
            west = jnp.where(last & (j > 0), left_value, value)
            west = pltpu.roll(jnp.where(last & (j == 0), 0, west), 1, 1)
            east = jnp.where(first & (j < chunks - 1), right_value, value)
            east = pltpu.roll(jnp.where(first & (j == chunks - 1), 0, east), LANES - 1, 1)
            return (east - west).astype(jnp.float32)

        for r in range(tiles):
            rows = slice(r * SUBLANES, (r + 1) * SUBLANES)
            values = [volume_ref[0, s, rows, here] for s in range(slices)]
            remaining = jnp.ones(tile, jnp.float32)
            sums = [jnp.zeros(tile, jnp.float32) for _ in range(3)]
            for s in range(slices):
                value = values[s]
                up = volume_ref[0, s, (r - 1) * SUBLANES : r * SUBLANES, here] if r > 0 else value
                down = volume_ref[0, s, (r + 1) * SUBLANES : (r + 2) * SUBLANES, here] if r < tiles - 1 else value
                up = pltpu.roll(jnp.where(last_row, up, value), 1, 0)
                down = pltpu.roll(jnp.where(first_row, down, value), SUBLANES - 1, 0)
                grad_rows = (down - up).astype(jnp.float32)
                grad_cols = across(
                    value, volume_ref[0, s, rows, left], volume_ref[0, s, rows, right], first_lane, last_lane
                )
                squares = grad_rows * grad_rows + grad_cols * grad_cols
                facing = LIGHT_ROWS * grad_rows + LIGHT_COLS * grad_cols
                weight = remaining * opacity(volume_ref[1, s, rows, here], tile_alpha)
                remaining = remaining - weight
                if r == 0:
                    held_ref[0, s : s + 1, :] = weight[:1]
                    weight = jnp.where(first_row, 0.0, weight)
                if r == tiles - 1:
                    held_ref[1, s : s + 1, :] = weight[SUBLANES - 1 :]
                    weight = jnp.where(last_row, 0.0, weight)
                emitted = colors(value, tile_colors)
                if 0 < s < slices - 1:
                    grad_depth = (values[s + 1] - values[s - 1]).astype(jnp.float32)
                    weight = weight * shade(grad_depth, facing, squares)
                    for c in range(3):
                        sums[c] = sums[c] + emitted[c] * weight
                else:
                    end = int(s > 0)
                    face_ref[end, rows, here] = facing
                    square_ref[end, rows, here] = squares
                    weight = weight * (1.0 / 255.0)
                    for c in range(3):
                        lit_ref[end, c, rows, here] = emitted[c] * weight
            for c in range(3):
                base_ref[c, rows, here] = sums[c] * (1.0 / 255.0)
            base_ref[3, rows, here] = 1.0 - remaining

        for q, (edge, inner) in enumerate(((0, 1), (height - 1, height - 2))):
            value = volume_ref[0, :, edge, here]
            behind = pltpu.roll(jnp.where(back, 0, value), 1, 0)
            ahead = pltpu.roll(jnp.where(front, 0, value), slices - 1, 0)
            grad_ref[q, 0, :, here] = (ahead - behind).astype(jnp.float32)
            grad_ref[q, 1, :, here] = volume_ref[0, :, inner, here].astype(jnp.float32)
            grad_ref[q, 2, :, here] = across(
                value, volume_ref[0, :, edge, left], volume_ref[0, :, edge, right], strip_first_lane, strip_last_lane
            )
            weight = held_ref[q] * (1.0 / 255.0)
            emitted = colors(value, strip_colors)
            for c in range(3):
                strip_ref[q, c, :, here] = emitted[c] * weight
        return carry

    lax.fori_loop(0, chunks, chunk, 0)


def march_interior(volume, color_map, alpha_map, depth_count):
    _, slices, height, columns = volume.shape
    opacity_scale = OPACITY / (255.0 * slices * depth_count)
    shapes = [
        (4, height, columns),
        (2, height, columns),
        (2, height, columns),
        (2, 3, height, columns),
        (2, 3, slices, columns),
        (2, 3, slices, columns),
    ]
    voxels = slices * height * columns
    return pl.pallas_call(
        functools.partial(interior_kernel, opacity_scale),
        in_specs=[WHOLE] * 3,
        out_specs=[WHOLE] * len(shapes),
        out_shape=[jax.ShapeDtypeStruct(shape, jnp.float32) for shape in shapes],
        scratch_shapes=[pltpu.VMEM((2, slices, LANES), jnp.float32)],
        compiler_params=pltpu.CompilerParams(vmem_limit_bytes=24 * 1024 * 1024),
        cost_estimate=pl.CostEstimate(flops=voxels * 80, bytes_accessed=voxels * 20, transcendentals=voxels),
    )(volume, color_map, alpha_map.reshape(1, -1))


def edge_kernel(
    share, volume_ref, base_ref, face_ref, square_ref, lit_ref, grad_ref, strip_ref, rows_near_ref, rows_far_ref, far_ref, near_ref, out_ref
):
    _, slices, height, columns = volume_ref.shape
    tiles = height // SUBLANES
    tile = (SUBLANES, LANES)
    row = lax.broadcasted_iota(jnp.int32, tile, 0)
    first_row, last_row = row == 0, row == SUBLANES - 1
    level = lax.broadcasted_iota(jnp.int32, (slices, LANES), 0)
    front, back = level == 0, level == slices - 1
    odd, odd_row = parity("depth") == 1, parity("rows") == 1
    front_end, back_end = ends("depth")
    top_end, bottom_end = ends("rows")

    def chunk(j, carry):
        here = pl.ds(pl.multiple_of(j * LANES, LANES), LANES)
        rows_near = rows_near_ref[:, here].astype(jnp.float32)
        rows_far = rows_far_ref[:, here].astype(jnp.float32)
        above = jnp.where(top_end, 0.0, jnp.where(odd_row, rows_near, rows_far))
        below = jnp.where(bottom_end, 0.0, jnp.where(odd_row, rows_far, rows_near))
        far = far_ref[:, here].astype(jnp.float32)
        near = near_ref[:, here].astype(jnp.float32)
        before = jnp.where(front_end, 0.0, jnp.where(odd, near, far))
        after = jnp.where(back_end, 0.0, jnp.where(odd, far, near))
        extra = []
        for q, edge in enumerate((0, height - 1)):
            inner = grad_ref[q, 1, :, here]
            grad_rows = below - inner if q else inner - above
            grad_cols = grad_ref[q, 2, :, here]
            grad_depth = grad_ref[q, 0, :, here] + jnp.where(
                back, after[edge : edge + 1], jnp.where(front, -before[edge : edge + 1], 0.0)
            )
            shading = shade(
                grad_depth,
                LIGHT_ROWS * grad_rows + LIGHT_COLS * grad_cols,
                grad_rows * grad_rows + grad_cols * grad_cols,
            )
            extra.append([jnp.sum(strip_ref[q, c, :, here] * shading, axis=0, keepdims=True) for c in range(3)])
        for r in range(tiles):
            rows = slice(r * SUBLANES, (r + 1) * SUBLANES)
            planes = [base_ref[c, rows, here] for c in range(4)]
            for end in range(2):
                if end:
                    grad_depth = after[rows] - volume_ref[0, slices - 2, rows, here].astype(jnp.float32)
                else:
                    grad_depth = volume_ref[0, 1, rows, here].astype(jnp.float32) - before[rows]
                shading = shade(grad_depth, face_ref[end, rows, here], square_ref[end, rows, here])
                for c in range(3):
                    planes[c] = planes[c] + lit_ref[end, c, rows, here] * shading
            for c in range(3):
                if r == 0:
                    planes[c] = planes[c] + jnp.where(first_row, extra[0][c], 0.0)
                if r == tiles - 1:
                    planes[c] = planes[c] + jnp.where(last_row, extra[1][c], 0.0)
            for first in range(0, SUBLANES, share):
                block = jnp.concatenate([plane[first : first + share] for plane in planes], axis=0)
                out_ref[(r * SUBLANES + first) // share, :, here] = block.astype(jnp.bfloat16)
        return carry

    lax.fori_loop(0, columns // LANES, chunk, 0)


def add_edges(volume, interior, halos, depth_count):
    _, slices, height, columns = volume.shape
    share = height // depth_count
    return pl.pallas_call(
        functools.partial(edge_kernel, share),
        in_specs=[WHOLE] * 11,
        out_specs=WHOLE,
        out_shape=jax.ShapeDtypeStruct((depth_count, 4 * share, columns), jnp.bfloat16),
        compiler_params=pltpu.CompilerParams(vmem_limit_bytes=24 * 1024 * 1024),
    )(volume, *interior, *halos)


def finish_kernel(parts_ref, out_ref):
    count = parts_ref.shape[0]
    _, share, columns = out_ref.shape
    remaining = jnp.ones((share, columns), jnp.float32)
    sums = [jnp.zeros((share, columns), jnp.float32) for _ in range(3)]
    for k in range(count):
        part = parts_ref[k].astype(jnp.float32)
        for c in range(3):
            sums[c] = sums[c] + remaining * part[c * share : (c + 1) * share]
        remaining = remaining - remaining * part[3 * share :]
    for c in range(3):
        out_ref[c] = sums[c]
    out_ref[3] = 1.0 - remaining


def finish(parts, share):
    columns = parts.shape[2]
    return pl.pallas_call(
        finish_kernel,
        in_specs=[WHOLE],
        out_specs=WHOLE,
        out_shape=jax.ShapeDtypeStruct((4, share, columns), jnp.float32),
    )(parts)


def swapped(values, axis, start):
    depth_count, row_count = lax.axis_size("depth"), lax.axis_size("rows")
    size = lax.axis_size(axis)
    perm = []
    for d in range(depth_count):
        for r in range(row_count):
            i = d if axis == "depth" else r
            j = i + 1 if i % 2 == start else i - 1
            if 0 <= j < size:
                e, q = (j, r) if axis == "depth" else (d, j)
            elif axis == "depth":
                e, q = (size - 1 - d, r)
            else:
                e, q = (d ^ 1, r)
            perm.append((d * row_count + r, e * row_count + q))
    return lax.ppermute(values, ("depth", "rows"), perm)


def body(volume, color_map, alpha_map):
    depth_count = lax.axis_size("depth")
    share = volume.shape[2] // depth_count
    rows_far, rows_near, far, near = cut_edges(volume)
    rows_far = swapped(rows_far, "rows", 1)
    rows_near = swapped(rows_near, "rows", 0)
    far = swapped(far, "depth", 1)
    near = swapped(near, "depth", 0)
    interior = march_interior(volume, color_map, alpha_map, depth_count)
    parts = add_edges(volume, interior, (rows_near, rows_far, far, near), depth_count)
    parts = lax.all_to_all(parts, "depth", 0, 0, tiled=True)
    return finish(parts, share)


def solution(mesh):
    in_specs = (P(None, "depth", "rows", None), P(), P())
    out_specs = P(None, ("rows", "depth"), None)
    return jax.shard_map(body, mesh=mesh, in_specs=in_specs, out_specs=out_specs, check_vma=False)
```

```python
import functools

import jax
import jax.numpy as jnp
from jax import lax
from jax.experimental import pallas as pl
from jax.experimental.pallas import tpu as pltpu
from jax.sharding import PartitionSpec as P

AMBIENT = 0.3
DIFFUSE = 0.7
LIGHT_DEPTH = 0.48 * DIFFUSE
LIGHT_ROWS = 0.6 * DIFFUSE
LIGHT_COLS = 0.64 * DIFFUSE
OPACITY = 4.0
LANES = 128
SUBLANES = 8
WHOLE = pl.BlockSpec(memory_space=pltpu.VMEM)


def parity(axis):
    return lax.axis_index(axis) % 2


def ends(axis):
    position = lax.axis_index(axis)
    return position == 0, position == lax.axis_size(axis) - 1


def load_kernel(volume_ref, held_ref, rows_far_out, rows_near_out, far_out, near_out, strips_ref, planes_ref, in_sems, out_sems):
    _, slices, height, _ = volume_ref.shape
    loads = [
        pltpu.make_async_copy(volume_ref.at[0, s], held_ref.at[0, s], in_sems.at[s]) for s in range(slices)
    ] + [pltpu.make_async_copy(volume_ref.at[1], held_ref.at[1], in_sems.at[slices])]
    for s in (0, slices - 1, *range(1, slices - 1), slices):
        loads[s].start()

    def narrow(values):
        return values.astype(jnp.float32).astype(jnp.bfloat16)

    outs = [
        pltpu.make_async_copy(source, out, out_sems.at[i])
        for i, (source, out) in enumerate(
            (
                (planes_ref.at[0], far_out),
                (planes_ref.at[1], near_out),
                (strips_ref.at[0], rows_far_out),
                (strips_ref.at[1], rows_near_out),
            )
        )
    ]
    odd, odd_row = parity("depth") == 1, parity("rows") == 1
    loads[0].wait()
    loads[slices - 1].wait()
    first, last = narrow(held_ref[0, 0]), narrow(held_ref[0, slices - 1])
    planes_ref[0] = jnp.where(odd, last, first)
    outs[0].start()
    planes_ref[1] = jnp.where(odd, first, last)
    outs[1].start()
    for s in range(1, slices - 1):
        loads[s].wait()
    top, bottom = narrow(held_ref[0, :, 0, :]), narrow(held_ref[0, :, height - 1, :])
    strips_ref[0] = jnp.where(odd_row, bottom, top)
    outs[2].start()
    strips_ref[1] = jnp.where(odd_row, top, bottom)
    outs[3].start()
    loads[slices].wait()
    for out in outs:
        out.wait()


def load(volume):
    _, slices, height, columns = volume.shape
    plane = jax.ShapeDtypeStruct((height, columns), jnp.bfloat16)
    strip = jax.ShapeDtypeStruct((slices, columns), jnp.bfloat16)
    return pl.pallas_call(
        load_kernel,
        in_specs=[pl.BlockSpec(memory_space=pltpu.HBM)],
        out_specs=[WHOLE] + [pl.BlockSpec(memory_space=pl.ANY)] * 4,
        out_shape=[jax.ShapeDtypeStruct(volume.shape, volume.dtype), strip, strip, plane, plane],
        scratch_shapes=[
            pltpu.VMEM((2, slices, columns), jnp.bfloat16),
            pltpu.VMEM((2, height, columns), jnp.bfloat16),
            pltpu.SemaphoreType.DMA((slices + 1,)),
            pltpu.SemaphoreType.DMA((4,)),
        ],
    )(volume)


def pick(entries, places):
    return jnp.take_along_axis(entries, places, axis=1, mode="promise_in_bounds")


def shade(grad_depth, facing, squares):
    facing = facing + LIGHT_DEPTH * grad_depth
    squares = squares + grad_depth * grad_depth
    return AMBIENT + jnp.abs(facing) * lax.rsqrt(jnp.maximum(squares, 4.0))


def interior_kernel(
    opacity_scale, volume_ref, color_ref, alpha_ref, base_ref, face_ref, square_ref, lit_ref, grad_ref, strip_ref, held_ref
):
    _, slices, height, columns = volume_ref.shape
    tiles = height // SUBLANES
    chunks = columns // LANES
    tile = (SUBLANES, LANES)
    strip = (slices, LANES)

    packed = color_ref[0:1, :] + color_ref[1:2, :] * 256 + color_ref[2:3, :] * 65536
    color_low, color_high = packed[:, :LANES], packed[:, LANES:]
    alpha_both = alpha_ref[0:1, :LANES] + alpha_ref[0:1, LANES:] * 256

    def colors(value, tables):
        low, high = tables
        place = value & (LANES - 1)
        color = jnp.where(value < LANES, pick(low, place), pick(high, place))
        parts = (color & 255, lax.shift_right_logical(color, 8) & 255, lax.shift_right_logical(color, 16))
        return [part.astype(jnp.float32) for part in parts]

    def opacity(level, table):
        entry = pick(table, level & (LANES - 1))
        entry = lax.shift_right_logical(entry, lax.shift_right_logical(level & LANES, 4)) & 255
        return entry.astype(jnp.float32) * opacity_scale

    tile_colors = [jnp.broadcast_to(t, tile) for t in (color_low, color_high)]
    tile_alpha = jnp.broadcast_to(alpha_both, tile)
    strip_colors = [jnp.broadcast_to(t, strip) for t in (color_low, color_high)]

    def masks(shape):
        lane = lax.broadcasted_iota(jnp.int32, shape, 1)
        row = lax.broadcasted_iota(jnp.int32, shape, 0)
        return lane == 0, lane == LANES - 1, row == 0, row == shape[0] - 1

    first_lane, last_lane, first_row, last_row = masks(tile)
    strip_first_lane, strip_last_lane, front, back = masks(strip)

    def chunk(j, carry):
        here = pl.ds(pl.multiple_of(j * LANES, LANES), LANES)
        left = pl.ds(pl.multiple_of(jnp.maximum(j - 1, 0) * LANES, LANES), LANES)
        right = pl.ds(pl.multiple_of(jnp.minimum(j + 1, chunks - 1) * LANES, LANES), LANES)

        def across(value, left_value, right_value, first, last):
            west = jnp.where(last & (j > 0), left_value, value)
            west = pltpu.roll(jnp.where(last & (j == 0), 0, west), 1, 1)
            east = jnp.where(first & (j < chunks - 1), right_value, value)
            east = pltpu.roll(jnp.where(first & (j == chunks - 1), 0, east), LANES - 1, 1)
            return (east - west).astype(jnp.float32)

        for r in range(tiles):
            rows = slice(r * SUBLANES, (r + 1) * SUBLANES)
            values = [volume_ref[0, s, rows, here] for s in range(slices)]
            remaining = jnp.ones(tile, jnp.float32)
            sums = [jnp.zeros(tile, jnp.float32) for _ in range(3)]
            for s in range(slices):
                value = values[s]
                up = volume_ref[0, s, (r - 1) * SUBLANES : r * SUBLANES, here] if r > 0 else value
                down = volume_ref[0, s, (r + 1) * SUBLANES : (r + 2) * SUBLANES, here] if r < tiles - 1 else value
                up = pltpu.roll(jnp.where(last_row, up, value), 1, 0)
                down = pltpu.roll(jnp.where(first_row, down, value), SUBLANES - 1, 0)
                grad_rows = (down - up).astype(jnp.float32)
                grad_cols = across(
                    value, volume_ref[0, s, rows, left], volume_ref[0, s, rows, right], first_lane, last_lane
                )
                squares = grad_rows * grad_rows + grad_cols * grad_cols
                facing = LIGHT_ROWS * grad_rows + LIGHT_COLS * grad_cols
                weight = remaining * opacity(volume_ref[1, s, rows, here], tile_alpha)
                remaining = remaining - weight
                if r == 0:
                    held_ref[0, s : s + 1, :] = weight[:1]
                    weight = jnp.where(first_row, 0.0, weight)
                if r == tiles - 1:
                    held_ref[1, s : s + 1, :] = weight[SUBLANES - 1 :]
                    weight = jnp.where(last_row, 0.0, weight)
                emitted = colors(value, tile_colors)
                if 0 < s < slices - 1:
                    grad_depth = (values[s + 1] - values[s - 1]).astype(jnp.float32)
                    weight = weight * shade(grad_depth, facing, squares)
                    for c in range(3):
                        sums[c] = sums[c] + emitted[c] * weight
                else:
                    end = int(s > 0)
                    face_ref[end, rows, here] = facing
                    square_ref[end, rows, here] = squares
                    weight = weight * (1.0 / 255.0)
                    for c in range(3):
                        lit_ref[end, c, rows, here] = emitted[c] * weight
            for c in range(3):
                base_ref[c, rows, here] = sums[c] * (1.0 / 255.0)
            base_ref[3, rows, here] = 1.0 - remaining

        for q, (edge, inner) in enumerate(((0, 1), (height - 1, height - 2))):
            value = volume_ref[0, :, edge, here]
            behind = pltpu.roll(jnp.where(back, 0, value), 1, 0)
            ahead = pltpu.roll(jnp.where(front, 0, value), slices - 1, 0)
            grad_ref[q, 0, :, here] = (ahead - behind).astype(jnp.float32)
            grad_ref[q, 1, :, here] = volume_ref[0, :, inner, here].astype(jnp.float32)
            grad_ref[q, 2, :, here] = across(
                value, volume_ref[0, :, edge, left], volume_ref[0, :, edge, right], strip_first_lane, strip_last_lane
            )
            weight = held_ref[q] * (1.0 / 255.0)
            emitted = colors(value, strip_colors)
            for c in range(3):
                strip_ref[q, c, :, here] = emitted[c] * weight
        return carry

    lax.fori_loop(0, chunks, chunk, 0)


def march_interior(volume, color_map, alpha_map, depth_count):
    _, slices, height, columns = volume.shape
    opacity_scale = OPACITY / (255.0 * slices * depth_count)
    shapes = [
        (4, height, columns),
        (2, height, columns),
        (2, height, columns),
        (2, 3, height, columns),
        (2, 3, slices, columns),
        (2, 3, slices, columns),
    ]
    voxels = slices * height * columns
    return pl.pallas_call(
        functools.partial(interior_kernel, opacity_scale),
        in_specs=[WHOLE] * 3,
        out_specs=[WHOLE] * len(shapes),
        out_shape=[jax.ShapeDtypeStruct(shape, jnp.float32) for shape in shapes],
        scratch_shapes=[pltpu.VMEM((2, slices, LANES), jnp.float32)],
        compiler_params=pltpu.CompilerParams(vmem_limit_bytes=24 * 1024 * 1024),
        cost_estimate=pl.CostEstimate(flops=voxels * 80, bytes_accessed=voxels * 20, transcendentals=voxels),
    )(volume, color_map, alpha_map.reshape(1, -1))


def edge_kernel(
    share, volume_ref, base_ref, face_ref, square_ref, lit_ref, grad_ref, strip_ref, rows_near_ref, rows_far_ref, far_ref, near_ref, out_ref
):
    _, slices, height, columns = volume_ref.shape
    tiles = height // SUBLANES
    tile = (SUBLANES, LANES)
    row = lax.broadcasted_iota(jnp.int32, tile, 0)
    first_row, last_row = row == 0, row == SUBLANES - 1
    level = lax.broadcasted_iota(jnp.int32, (slices, LANES), 0)
    front, back = level == 0, level == slices - 1
    odd, odd_row = parity("depth") == 1, parity("rows") == 1
    front_end, back_end = ends("depth")
    top_end, bottom_end = ends("rows")

    def chunk(j, carry):
        here = pl.ds(pl.multiple_of(j * LANES, LANES), LANES)
        rows_near = rows_near_ref[:, here].astype(jnp.float32)
        rows_far = rows_far_ref[:, here].astype(jnp.float32)
        above = jnp.where(top_end, 0.0, jnp.where(odd_row, rows_near, rows_far))
        below = jnp.where(bottom_end, 0.0, jnp.where(odd_row, rows_far, rows_near))
        far = far_ref[:, here].astype(jnp.float32)
        near = near_ref[:, here].astype(jnp.float32)
        before = jnp.where(front_end, 0.0, jnp.where(odd, near, far))
        after = jnp.where(back_end, 0.0, jnp.where(odd, far, near))
        extra = []
        for q, edge in enumerate((0, height - 1)):
            inner = grad_ref[q, 1, :, here]
            grad_rows = below - inner if q else inner - above
            grad_cols = grad_ref[q, 2, :, here]
            grad_depth = grad_ref[q, 0, :, here] + jnp.where(
                back, after[edge : edge + 1], jnp.where(front, -before[edge : edge + 1], 0.0)
            )
            shading = shade(
                grad_depth,
                LIGHT_ROWS * grad_rows + LIGHT_COLS * grad_cols,
                grad_rows * grad_rows + grad_cols * grad_cols,
            )
            extra.append([jnp.sum(strip_ref[q, c, :, here] * shading, axis=0, keepdims=True) for c in range(3)])
        for r in range(tiles):
            rows = slice(r * SUBLANES, (r + 1) * SUBLANES)
            planes = [base_ref[c, rows, here] for c in range(4)]
            for end in range(2):
                if end:
                    grad_depth = after[rows] - volume_ref[0, slices - 2, rows, here].astype(jnp.float32)
                else:
                    grad_depth = volume_ref[0, 1, rows, here].astype(jnp.float32) - before[rows]
                shading = shade(grad_depth, face_ref[end, rows, here], square_ref[end, rows, here])
                for c in range(3):
                    planes[c] = planes[c] + lit_ref[end, c, rows, here] * shading
            for c in range(3):
                if r == 0:
                    planes[c] = planes[c] + jnp.where(first_row, extra[0][c], 0.0)
                if r == tiles - 1:
                    planes[c] = planes[c] + jnp.where(last_row, extra[1][c], 0.0)
            for first in range(0, SUBLANES, share):
                block = jnp.concatenate([plane[first : first + share] for plane in planes], axis=0)
                out_ref[(r * SUBLANES + first) // share, :, here] = block.astype(jnp.bfloat16)
        return carry

    lax.fori_loop(0, columns // LANES, chunk, 0)


def add_edges(volume, interior, halos, depth_count):
    _, slices, height, columns = volume.shape
    share = height // depth_count
    return pl.pallas_call(
        functools.partial(edge_kernel, share),
        in_specs=[WHOLE] * 11,
        out_specs=WHOLE,
        out_shape=jax.ShapeDtypeStruct((depth_count, 4 * share, columns), jnp.bfloat16),
        compiler_params=pltpu.CompilerParams(vmem_limit_bytes=24 * 1024 * 1024),
    )(volume, *interior, *halos)


def finish_kernel(parts_ref, out_ref):
    count = parts_ref.shape[0]
    _, share, columns = out_ref.shape
    remaining = jnp.ones((share, columns), jnp.float32)
    sums = [jnp.zeros((share, columns), jnp.float32) for _ in range(3)]
    for k in range(count):
        part = parts_ref[k].astype(jnp.float32)
        for c in range(3):
            sums[c] = sums[c] + remaining * part[c * share : (c + 1) * share]
        remaining = remaining - remaining * part[3 * share :]
    for c in range(3):
        out_ref[c] = sums[c]
    out_ref[3] = 1.0 - remaining


def finish(parts, share):
    columns = parts.shape[2]
    return pl.pallas_call(
        finish_kernel,
        in_specs=[WHOLE],
        out_specs=WHOLE,
        out_shape=jax.ShapeDtypeStruct((4, share, columns), jnp.float32),
    )(parts)


def swapped(values, axis, start):
    depth_count, row_count = lax.axis_size("depth"), lax.axis_size("rows")
    size = lax.axis_size(axis)
    perm = []
    for d in range(depth_count):
        for r in range(row_count):
            i = d if axis == "depth" else r
            j = i + 1 if i % 2 == start else i - 1
            if 0 <= j < size:
                e, q = (j, r) if axis == "depth" else (d, j)
            elif axis == "depth":
                e, q = (size - 1 - d, r)
            else:
                e, q = (d ^ 1, r)
            perm.append((d * row_count + r, e * row_count + q))
    return lax.ppermute(values, ("depth", "rows"), perm)


def body(volume, color_map, alpha_map):
    depth_count = lax.axis_size("depth")
    share = volume.shape[2] // depth_count
    volume, rows_far, rows_near, far, near = load(volume)
    rows_far = swapped(rows_far, "rows", 1)
    rows_near = swapped(rows_near, "rows", 0)
    far = swapped(far, "depth", 1)
    near = swapped(near, "depth", 0)
    interior = march_interior(volume, color_map, alpha_map, depth_count)
    parts = add_edges(volume, interior, (rows_near, rows_far, far, near), depth_count)
    parts = lax.all_to_all(parts, "depth", 0, 0, tiled=True)
    return finish(parts, share)


def solution(mesh):
    in_specs = (P(None, "depth", "rows", None), P(), P())
    out_specs = P(None, ("rows", "depth"), None)
    return jax.shard_map(body, mesh=mesh, in_specs=in_specs, out_specs=out_specs, check_vma=False)
```

```python
import functools

import jax
import jax.numpy as jnp
from jax import lax
from jax.experimental import pallas as pl
from jax.experimental.pallas import tpu as pltpu
from jax.sharding import PartitionSpec as P

AMBIENT = 0.3
DIFFUSE = 0.7
LIGHT_DEPTH = 0.48 * DIFFUSE
LIGHT_ROWS = 0.6 * DIFFUSE
LIGHT_COLS = 0.64 * DIFFUSE
OPACITY = 4.0
LANES = 128
SUBLANES = 8
WHOLE = pl.BlockSpec(memory_space=pltpu.VMEM)


def parity(axis):
    return lax.axis_index(axis) % 2


def ends(axis):
    position = lax.axis_index(axis)
    return position == 0, position == lax.axis_size(axis) - 1


def edges_kernel(volume_ref, rows_far_out, rows_near_out, far_out, near_out, strip_ref, plane_ref, sems):
    _, slices, height, _ = volume_ref.shape
    odd, odd_row = parity("depth"), parity("rows")
    last_tile = height // SUBLANES - 1

    def tile(i):
        return pl.ds(pl.multiple_of(i * SUBLANES, SUBLANES), SUBLANES)

    copies = [
        pltpu.make_async_copy(volume_ref.at[0, :, tile((1 - odd_row) * last_tile)], strip_ref.at[0], sems.at[0]),
        pltpu.make_async_copy(volume_ref.at[0, :, tile(odd_row * last_tile)], strip_ref.at[1], sems.at[1]),
        pltpu.make_async_copy(volume_ref.at[0, odd * (slices - 1)], plane_ref.at[0], sems.at[2]),
        pltpu.make_async_copy(volume_ref.at[0, (1 - odd) * (slices - 1)], plane_ref.at[1], sems.at[3]),
    ]
    for copy in copies:
        copy.start()

    def narrow(values):
        return values.astype(jnp.float32).astype(jnp.bfloat16)

    copies[0].wait()
    rows_near_out[...] = narrow(jnp.where(odd_row == 1, strip_ref[0, :, 0, :], strip_ref[0, :, SUBLANES - 1, :]))
    copies[1].wait()
    rows_far_out[...] = narrow(jnp.where(odd_row == 1, strip_ref[1, :, SUBLANES - 1, :], strip_ref[1, :, 0, :]))
    copies[2].wait()
    far_out[...] = narrow(plane_ref[0])
    copies[3].wait()
    near_out[...] = narrow(plane_ref[1])


def cut_edges(volume):
    _, slices, height, columns = volume.shape
    plane = jax.ShapeDtypeStruct((height, columns), jnp.bfloat16)
    strip = jax.ShapeDtypeStruct((slices, columns), jnp.bfloat16)
    return pl.pallas_call(
        edges_kernel,
        in_specs=[pl.BlockSpec(memory_space=pl.ANY)],
        out_specs=[WHOLE] * 4,
        out_shape=[strip, strip, plane, plane],
        scratch_shapes=[
            pltpu.VMEM((2, slices, SUBLANES, columns), jnp.int32),
            pltpu.VMEM((2, height, columns), jnp.int32),
            pltpu.SemaphoreType.DMA((4,)),
        ],
    )(volume)


def pick(entries, places):
    return jnp.take_along_axis(entries, places, axis=1, mode="promise_in_bounds")


def shade(grad_depth, facing, squares):
    facing = facing + LIGHT_DEPTH * grad_depth
    squares = squares + grad_depth * grad_depth
    return AMBIENT + jnp.abs(facing) * lax.rsqrt(jnp.maximum(squares, 4.0))


def interior_kernel(
    opacity_scale,
    volume_ref,
    color_ref,
    alpha_ref,
    base_ref,
    face_ref,
    square_ref,
    lit_ref,
    inner_ref,
    grad_ref,
    strip_ref,
    first_ref,
    second_ref,
    held_ref,
    sems,
):
    _, slices, height, columns = volume_ref.shape
    tiles = height // SUBLANES
    chunks = columns // LANES
    tile = (SUBLANES, LANES)
    strip = (slices, LANES)
    top = SUBLANES

    def load_first(j):
        source = volume_ref.at[0, :, :, pl.ds(pl.multiple_of(j * LANES, LANES), LANES)]
        return pltpu.make_async_copy(source, first_ref.at[j + 1, :, pl.ds(top, height), :], sems.at[0, j])

    def load_second(j):
        source = volume_ref.at[1, :, :, pl.ds(pl.multiple_of(j * LANES, LANES), LANES)]
        return pltpu.make_async_copy(source, second_ref.at[j], sems.at[1, j])

    for j in range(chunks):
        load_first(j).start()
        load_second(j).start()

    blank = jnp.zeros((slices, height, LANES), jnp.int32)
    first_ref[0, :, top : top + height] = blank
    first_ref[chunks + 1, :, top : top + height] = blank
    margin = jnp.zeros((slices, SUBLANES, LANES), jnp.int32)
    for j in range(chunks):
        first_ref[j + 1, :, :top] = margin
        first_ref[j + 1, :, top + height :] = margin

    packed = color_ref[0:1, :] + color_ref[1:2, :] * 256 + color_ref[2:3, :] * 65536
    color_low, color_high = packed[:, :LANES], packed[:, LANES:]
    opacities = alpha_ref[0:1, :].astype(jnp.float32) * opacity_scale

    def choose(value, tables):
        low, high = tables
        place = value & (LANES - 1)
        return jnp.where(value < LANES, pick(low, place), pick(high, place))

    def colors(value, tables):
        color = choose(value, tables)
        parts = (color & 255, lax.shift_right_logical(color, 8) & 255, lax.shift_right_logical(color, 16))
        return [part.astype(jnp.float32) for part in parts]

    tile_colors = [jnp.broadcast_to(t, tile) for t in (color_low, color_high)]
    tile_opacities = [jnp.broadcast_to(t, tile) for t in (opacities[:, :LANES], opacities[:, LANES:])]
    strip_colors = [jnp.broadcast_to(t, strip) for t in (color_low, color_high)]

    def masks(shape):
        lane = lax.broadcasted_iota(jnp.int32, shape, 1)
        row = lax.broadcasted_iota(jnp.int32, shape, 0)
        return lane == 0, lane == LANES - 1, row == 0, row == shape[0] - 1

    first_lane, last_lane, first_row, last_row = masks(tile)
    strip_first_lane, strip_last_lane, front, back = masks(strip)

    def across(left_value, value, right_value, first, last):
        west = pltpu.roll(jnp.where(last, left_value, value), 1, 1)
        east = pltpu.roll(jnp.where(first, right_value, value), LANES - 1, 1)
        return (east - west).astype(jnp.float32)

    load_first(0).wait()

    def chunk(j, carry):
        here = pl.ds(pl.multiple_of(j * LANES, LANES), LANES)

        @pl.when(j < chunks - 1)
        def _():
            load_first(j + 1).wait()

        load_second(j).wait()

        for r in range(tiles):
            rows = slice(r * SUBLANES, (r + 1) * SUBLANES)

            def shifted_rows(c, s, offset=0):
                return first_ref[c, s, top + r * SUBLANES + offset : top + (r + 1) * SUBLANES + offset, :]

            values = [shifted_rows(j + 1, s) for s in range(slices)]
            remaining = jnp.ones(tile, jnp.float32)
            sums = [jnp.zeros(tile, jnp.float32) for _ in range(3)]
            for s in range(slices):
                value = values[s]
                grad_rows = (shifted_rows(j + 1, s, 1) - shifted_rows(j + 1, s, -1)).astype(jnp.float32)
                grad_cols = across(shifted_rows(j, s), value, shifted_rows(j + 2, s), first_lane, last_lane)
                squares = grad_rows * grad_rows + grad_cols * grad_cols
                facing = LIGHT_ROWS * grad_rows + LIGHT_COLS * grad_cols
                weight = remaining * choose(second_ref[j, s, rows, :], tile_opacities)
                remaining = remaining - weight
                if r == 0:
                    held_ref[0, s : s + 1, :] = weight[:1]
                    weight = jnp.where(first_row, 0.0, weight)
                if r == tiles - 1:
                    held_ref[1, s : s + 1, :] = weight[SUBLANES - 1 :]
                    weight = jnp.where(last_row, 0.0, weight)
                emitted = colors(value, tile_colors)
                if 0 < s < slices - 1:
                    grad_depth = (values[s + 1] - values[s - 1]).astype(jnp.float32)
                    weight = weight * shade(grad_depth, facing, squares)
                    for c in range(3):
                        sums[c] = sums[c] + emitted[c] * weight
                else:
                    end = int(s > 0)
                    face_ref[end, rows, here] = facing
                    square_ref[end, rows, here] = squares
                    inner_ref[end, rows, here] = values[slices - 2 if end else 1].astype(jnp.float32)
                    weight = weight * (1.0 / 255.0)
                    for c in range(3):
                        lit_ref[end, c, rows, here] = emitted[c] * weight
            for c in range(3):
                base_ref[c, rows, here] = sums[c] * (1.0 / 255.0)
            base_ref[3, rows, here] = 1.0 - remaining

        for q, (edge, inner) in enumerate(((top, top + 1), (top + height - 1, top + height - 2))):
            value = first_ref[j + 1, :, edge, :]
            behind = pltpu.roll(jnp.where(back, 0, value), 1, 0)
            ahead = pltpu.roll(jnp.where(front, 0, value), slices - 1, 0)
            grad_ref[q, 0, :, here] = (ahead - behind).astype(jnp.float32)
            grad_ref[q, 1, :, here] = first_ref[j + 1, :, inner, :].astype(jnp.float32)
            grad_ref[q, 2, :, here] = across(
                first_ref[j, :, edge, :], value, first_ref[j + 2, :, edge, :], strip_first_lane, strip_last_lane
            )
            weight = held_ref[q] * (1.0 / 255.0)
            emitted = colors(value, strip_colors)
            for c in range(3):
                strip_ref[q, c, :, here] = emitted[c] * weight
        return carry

    lax.fori_loop(0, chunks, chunk, 0)


def march_interior(volume, color_map, alpha_map, depth_count):
    _, slices, height, columns = volume.shape
    chunks = columns // LANES
    opacity_scale = OPACITY / (255.0 * slices * depth_count)
    shapes = [
        (4, height, columns),
        (2, height, columns),
        (2, height, columns),
        (2, 3, height, columns),
        (2, height, columns),
        (2, 3, slices, columns),
        (2, 3, slices, columns),
    ]
    voxels = slices * height * columns
    return pl.pallas_call(
        functools.partial(interior_kernel, opacity_scale),
        in_specs=[pl.BlockSpec(memory_space=pltpu.HBM), WHOLE, WHOLE],
        out_specs=[WHOLE] * len(shapes),
        out_shape=[jax.ShapeDtypeStruct(shape, jnp.float32) for shape in shapes],
        scratch_shapes=[
            pltpu.VMEM((chunks + 2, slices, height + 2 * SUBLANES, LANES), jnp.int32),
            pltpu.VMEM((chunks, slices, height, LANES), jnp.int32),
            pltpu.VMEM((2, slices, LANES), jnp.float32),
            pltpu.SemaphoreType.DMA((2, chunks)),
        ],
        compiler_params=pltpu.CompilerParams(vmem_limit_bytes=24 * 1024 * 1024),
        cost_estimate=pl.CostEstimate(flops=voxels * 80, bytes_accessed=voxels * 20, transcendentals=voxels),
    )(volume, color_map, alpha_map.reshape(1, -1))


def edge_kernel(
    share, base_ref, face_ref, square_ref, lit_ref, inner_ref, grad_ref, strip_ref, rows_near_ref, rows_far_ref, far_ref, near_ref, out_ref
):
    _, height, columns = base_ref.shape
    slices = strip_ref.shape[2]
    tiles = height // SUBLANES
    tile = (SUBLANES, LANES)
    row = lax.broadcasted_iota(jnp.int32, tile, 0)
    first_row, last_row = row == 0, row == SUBLANES - 1
    level = lax.broadcasted_iota(jnp.int32, (slices, LANES), 0)
    front, back = level == 0, level == slices - 1
    odd, odd_row = parity("depth") == 1, parity("rows") == 1
    front_end, back_end = ends("depth")
    top_end, bottom_end = ends("rows")

    def chunk(j, carry):
        here = pl.ds(pl.multiple_of(j * LANES, LANES), LANES)
        rows_near = rows_near_ref[:, here].astype(jnp.float32)
        rows_far = rows_far_ref[:, here].astype(jnp.float32)
        above = jnp.where(top_end, 0.0, jnp.where(odd_row, rows_near, rows_far))
        below = jnp.where(bottom_end, 0.0, jnp.where(odd_row, rows_far, rows_near))
        far = far_ref[:, here].astype(jnp.float32)
        near = near_ref[:, here].astype(jnp.float32)
        before = jnp.where(front_end, 0.0, jnp.where(odd, near, far))
        after = jnp.where(back_end, 0.0, jnp.where(odd, far, near))
        extra = []
        for q, edge in enumerate((0, height - 1)):
            inner = grad_ref[q, 1, :, here]
            grad_rows = below - inner if q else inner - above
            grad_cols = grad_ref[q, 2, :, here]
            grad_depth = grad_ref[q, 0, :, here] + jnp.where(
                back, after[edge : edge + 1], jnp.where(front, -before[edge : edge + 1], 0.0)
            )
            shading = shade(
                grad_depth,
                LIGHT_ROWS * grad_rows + LIGHT_COLS * grad_cols,
                grad_rows * grad_rows + grad_cols * grad_cols,
            )
            extra.append([jnp.sum(strip_ref[q, c, :, here] * shading, axis=0, keepdims=True) for c in range(3)])
        for r in range(tiles):
            rows = slice(r * SUBLANES, (r + 1) * SUBLANES)
            planes = [base_ref[c, rows, here] for c in range(4)]
            for end in range(2):
                if end:
                    grad_depth = after[rows] - inner_ref[1, rows, here]
                else:
                    grad_depth = inner_ref[0, rows, here] - before[rows]
                shading = shade(grad_depth, face_ref[end, rows, here], square_ref[end, rows, here])
                for c in range(3):
                    planes[c] = planes[c] + lit_ref[end, c, rows, here] * shading
            for c in range(3):
                if r == 0:
                    planes[c] = planes[c] + jnp.where(first_row, extra[0][c], 0.0)
                if r == tiles - 1:
                    planes[c] = planes[c] + jnp.where(last_row, extra[1][c], 0.0)
            for first in range(0, SUBLANES, share):
                block = jnp.concatenate([plane[first : first + share] for plane in planes], axis=0)
                out_ref[(r * SUBLANES + first) // share, :, here] = block.astype(jnp.bfloat16)
        return carry

    lax.fori_loop(0, columns // LANES, chunk, 0)


def add_edges(interior, halos, depth_count):
    _, height, columns = interior[0].shape
    share = height // depth_count
    return pl.pallas_call(
        functools.partial(edge_kernel, share),
        in_specs=[WHOLE] * 11,
        out_specs=WHOLE,
        out_shape=jax.ShapeDtypeStruct((depth_count, 4 * share, columns), jnp.bfloat16),
        compiler_params=pltpu.CompilerParams(vmem_limit_bytes=24 * 1024 * 1024),
    )(*interior, *halos)


def finish_kernel(parts_ref, out_ref):
    count = parts_ref.shape[0]
    _, share, columns = out_ref.shape
    remaining = jnp.ones((share, columns), jnp.float32)
    sums = [jnp.zeros((share, columns), jnp.float32) for _ in range(3)]
    for k in range(count):
        part = parts_ref[k].astype(jnp.float32)
        for c in range(3):
            sums[c] = sums[c] + remaining * part[c * share : (c + 1) * share]
        remaining = remaining - remaining * part[3 * share :]
    for c in range(3):
        out_ref[c] = sums[c]
    out_ref[3] = 1.0 - remaining


def finish(parts, share):
    columns = parts.shape[2]
    return pl.pallas_call(
        finish_kernel,
        in_specs=[WHOLE],
        out_specs=WHOLE,
        out_shape=jax.ShapeDtypeStruct((4, share, columns), jnp.float32),
    )(parts)


def swapped(values, axis, start):
    depth_count, row_count = lax.axis_size("depth"), lax.axis_size("rows")
    size = lax.axis_size(axis)
    perm = []
    for d in range(depth_count):
        for r in range(row_count):
            i = d if axis == "depth" else r
            j = i + 1 if i % 2 == start else i - 1
            if 0 <= j < size:
                e, q = (j, r) if axis == "depth" else (d, j)
            elif axis == "depth":
                e, q = (size - 1 - d, r)
            else:
                e, q = (d ^ 1, r)
            perm.append((d * row_count + r, e * row_count + q))
    return lax.ppermute(values, ("depth", "rows"), perm)


def body(volume, color_map, alpha_map):
    depth_count = lax.axis_size("depth")
    share = volume.shape[2] // depth_count
    rows_far, rows_near, far, near = cut_edges(volume)
    rows_far = swapped(rows_far, "rows", 1)
    rows_near = swapped(rows_near, "rows", 0)
    far = swapped(far, "depth", 1)
    near = swapped(near, "depth", 0)
    interior = march_interior(volume, color_map, alpha_map, depth_count)
    parts = add_edges(interior, (rows_near, rows_far, far, near), depth_count)
    parts = lax.all_to_all(parts, "depth", 0, 0, tiled=True)
    return finish(parts, share)


def solution(mesh):
    in_specs = (P(None, "depth", "rows", None), P(), P())
    out_specs = P(None, ("rows", "depth"), None)
    return jax.shard_map(body, mesh=mesh, in_specs=in_specs, out_specs=out_specs, check_vma=False)
```

```python
import functools

import jax
import jax.numpy as jnp
from jax import lax
from jax.experimental import pallas as pl
from jax.experimental.pallas import tpu as pltpu
from jax.sharding import PartitionSpec as P

AMBIENT = 0.3
DIFFUSE = 0.7
LIGHT_DEPTH = 0.48 * DIFFUSE
LIGHT_ROWS = 0.6 * DIFFUSE
LIGHT_COLS = 0.64 * DIFFUSE
OPACITY = 4.0
LANES = 128
SUBLANES = 8
WHOLE = pl.BlockSpec(memory_space=pltpu.VMEM)


def parity(axis):
    return lax.axis_index(axis) % 2


def ends(axis):
    position = lax.axis_index(axis)
    return position == 0, position == lax.axis_size(axis) - 1


def edges_kernel(volume_ref, rows_far_out, rows_near_out, far_out, near_out, strip_ref, plane_ref, sems):
    _, slices, height, _ = volume_ref.shape
    odd, odd_row = parity("depth"), parity("rows")
    last_tile = height // SUBLANES - 1

    def tile(i):
        return pl.ds(pl.multiple_of(i * SUBLANES, SUBLANES), SUBLANES)

    copies = [
        pltpu.make_async_copy(volume_ref.at[0, :, tile((1 - odd_row) * last_tile)], strip_ref.at[0], sems.at[0]),
        pltpu.make_async_copy(volume_ref.at[0, :, tile(odd_row * last_tile)], strip_ref.at[1], sems.at[1]),
        pltpu.make_async_copy(volume_ref.at[0, odd * (slices - 1)], plane_ref.at[0], sems.at[2]),
        pltpu.make_async_copy(volume_ref.at[0, (1 - odd) * (slices - 1)], plane_ref.at[1], sems.at[3]),
    ]
    for copy in copies:
        copy.start()

    def narrow(values):
        return values.astype(jnp.float32).astype(jnp.bfloat16)

    copies[0].wait()
    rows_near_out[...] = narrow(jnp.where(odd_row == 1, strip_ref[0, :, 0, :], strip_ref[0, :, SUBLANES - 1, :]))
    copies[1].wait()
    rows_far_out[...] = narrow(jnp.where(odd_row == 1, strip_ref[1, :, SUBLANES - 1, :], strip_ref[1, :, 0, :]))
    copies[2].wait()
    far_out[...] = narrow(plane_ref[0])
    copies[3].wait()
    near_out[...] = narrow(plane_ref[1])


def cut_edges(volume):
    _, slices, height, columns = volume.shape
    plane = jax.ShapeDtypeStruct((height, columns), jnp.bfloat16)
    strip = jax.ShapeDtypeStruct((slices, columns), jnp.bfloat16)
    return pl.pallas_call(
        edges_kernel,
        in_specs=[pl.BlockSpec(memory_space=pl.ANY)],
        out_specs=[WHOLE] * 4,
        out_shape=[strip, strip, plane, plane],
        scratch_shapes=[
            pltpu.VMEM((2, slices, SUBLANES, columns), jnp.int32),
            pltpu.VMEM((2, height, columns), jnp.int32),
            pltpu.SemaphoreType.DMA((4,)),
        ],
        compiler_params=pltpu.CompilerParams(vmem_limit_bytes=4 * 1024 * 1024),
    )(volume)


def pick(entries, places):
    return jnp.take_along_axis(entries, places, axis=1, mode="promise_in_bounds")


def shade(grad_depth, facing, squares):
    facing = facing + LIGHT_DEPTH * grad_depth
    squares = squares + grad_depth * grad_depth
    return AMBIENT + jnp.abs(facing) * lax.rsqrt(jnp.maximum(squares, 4.0))


def interior_kernel(
    opacity_scale, volume_ref, color_ref, alpha_ref, base_ref, face_ref, square_ref, lit_ref, grad_ref, strip_ref, held_ref
):
    _, slices, height, columns = volume_ref.shape
    tiles = height // SUBLANES
    chunks = columns // LANES
    tile = (SUBLANES, LANES)
    strip = (slices, LANES)

    packed = color_ref[0:1, :] + color_ref[1:2, :] * 256 + color_ref[2:3, :] * 65536
    color_low, color_high = packed[:, :LANES], packed[:, LANES:]
    alpha_both = alpha_ref[0:1, :LANES] + alpha_ref[0:1, LANES:] * 256

    def colors(value, tables):
        low, high = tables
        place = value & (LANES - 1)
        color = jnp.where(value < LANES, pick(low, place), pick(high, place))
        parts = (color & 255, lax.shift_right_logical(color, 8) & 255, lax.shift_right_logical(color, 16))
        return [part.astype(jnp.float32) for part in parts]

    def opacity(level, table):
        entry = pick(table, level & (LANES - 1))
        entry = lax.shift_right_logical(entry, lax.shift_right_logical(level & LANES, 4)) & 255
        return entry.astype(jnp.float32) * opacity_scale

    tile_colors = [jnp.broadcast_to(t, tile) for t in (color_low, color_high)]
    tile_alpha = jnp.broadcast_to(alpha_both, tile)
    strip_colors = [jnp.broadcast_to(t, strip) for t in (color_low, color_high)]

    def masks(shape):
        lane = lax.broadcasted_iota(jnp.int32, shape, 1)
        row = lax.broadcasted_iota(jnp.int32, shape, 0)
        return lane == 0, lane == LANES - 1, row == 0, row == shape[0] - 1

    first_lane, last_lane, first_row, last_row = masks(tile)
    strip_first_lane, strip_last_lane, front, back = masks(strip)

    def chunk(j, carry):
        here = pl.ds(pl.multiple_of(j * LANES, LANES), LANES)
        left = pl.ds(pl.multiple_of(jnp.maximum(j - 1, 0) * LANES, LANES), LANES)
        right = pl.ds(pl.multiple_of(jnp.minimum(j + 1, chunks - 1) * LANES, LANES), LANES)

        def across(value, left_value, right_value, first, last):
            west = jnp.where(last & (j > 0), left_value, value)
            west = pltpu.roll(jnp.where(last & (j == 0), 0, west), 1, 1)
            east = jnp.where(first & (j < chunks - 1), right_value, value)
            east = pltpu.roll(jnp.where(first & (j == chunks - 1), 0, east), LANES - 1, 1)
            return (east - west).astype(jnp.float32)

        for r in range(tiles):
            rows = slice(r * SUBLANES, (r + 1) * SUBLANES)
            values = [volume_ref[0, s, rows, here] for s in range(slices)]
            remaining = jnp.ones(tile, jnp.float32)
            sums = [jnp.zeros(tile, jnp.float32) for _ in range(3)]
            for s in range(slices):
                value = values[s]
                up = volume_ref[0, s, (r - 1) * SUBLANES : r * SUBLANES, here] if r > 0 else value
                down = volume_ref[0, s, (r + 1) * SUBLANES : (r + 2) * SUBLANES, here] if r < tiles - 1 else value
                up = pltpu.roll(jnp.where(last_row, up, value), 1, 0)
                down = pltpu.roll(jnp.where(first_row, down, value), SUBLANES - 1, 0)
                grad_rows = (down - up).astype(jnp.float32)
                grad_cols = across(
                    value, volume_ref[0, s, rows, left], volume_ref[0, s, rows, right], first_lane, last_lane
                )
                squares = grad_rows * grad_rows + grad_cols * grad_cols
                facing = LIGHT_ROWS * grad_rows + LIGHT_COLS * grad_cols
                weight = remaining * opacity(volume_ref[1, s, rows, here], tile_alpha)
                remaining = remaining - weight
                if r == 0:
                    held_ref[0, s : s + 1, :] = weight[:1]
                    weight = jnp.where(first_row, 0.0, weight)
                if r == tiles - 1:
                    held_ref[1, s : s + 1, :] = weight[SUBLANES - 1 :]
                    weight = jnp.where(last_row, 0.0, weight)
                emitted = colors(value, tile_colors)
                if 0 < s < slices - 1:
                    grad_depth = (values[s + 1] - values[s - 1]).astype(jnp.float32)
                    weight = weight * shade(grad_depth, facing, squares)
                    for c in range(3):
                        sums[c] = sums[c] + emitted[c] * weight
                else:
                    end = int(s > 0)
                    face_ref[end, rows, here] = facing
                    square_ref[end, rows, here] = squares
                    weight = weight * (1.0 / 255.0)
                    for c in range(3):
                        lit_ref[end, c, rows, here] = emitted[c] * weight
            for c in range(3):
                base_ref[c, rows, here] = sums[c] * (1.0 / 255.0)
            base_ref[3, rows, here] = 1.0 - remaining

        for q, (edge, inner) in enumerate(((0, 1), (height - 1, height - 2))):
            value = volume_ref[0, :, edge, here]
            behind = pltpu.roll(jnp.where(back, 0, value), 1, 0)
            ahead = pltpu.roll(jnp.where(front, 0, value), slices - 1, 0)
            grad_ref[q, 0, :, here] = (ahead - behind).astype(jnp.float32)
            grad_ref[q, 1, :, here] = volume_ref[0, :, inner, here].astype(jnp.float32)
            grad_ref[q, 2, :, here] = across(
                value, volume_ref[0, :, edge, left], volume_ref[0, :, edge, right], strip_first_lane, strip_last_lane
            )
            weight = held_ref[q] * (1.0 / 255.0)
            emitted = colors(value, strip_colors)
            for c in range(3):
                strip_ref[q, c, :, here] = emitted[c] * weight
        return carry

    lax.fori_loop(0, chunks, chunk, 0)


def march_interior(volume, color_map, alpha_map, depth_count):
    _, slices, height, columns = volume.shape
    opacity_scale = OPACITY / (255.0 * slices * depth_count)
    shapes = [
        (4, height, columns),
        (2, height, columns),
        (2, height, columns),
        (2, 3, height, columns),
        (2, 3, slices, columns),
        (2, 3, slices, columns),
    ]
    voxels = slices * height * columns
    return pl.pallas_call(
        functools.partial(interior_kernel, opacity_scale),
        in_specs=[WHOLE] * 3,
        out_specs=[WHOLE] * len(shapes),
        out_shape=[jax.ShapeDtypeStruct(shape, jnp.float32) for shape in shapes],
        scratch_shapes=[pltpu.VMEM((2, slices, LANES), jnp.float32)],
        compiler_params=pltpu.CompilerParams(vmem_limit_bytes=24 * 1024 * 1024),
        cost_estimate=pl.CostEstimate(flops=voxels * 80, bytes_accessed=voxels * 20, transcendentals=voxels),
    )(volume, color_map, alpha_map.reshape(1, -1))


def edge_kernel(
    share, volume_ref, base_ref, face_ref, square_ref, lit_ref, grad_ref, strip_ref, rows_near_ref, rows_far_ref, far_ref, near_ref, out_ref
):
    _, slices, height, columns = volume_ref.shape
    tiles = height // SUBLANES
    tile = (SUBLANES, LANES)
    row = lax.broadcasted_iota(jnp.int32, tile, 0)
    first_row, last_row = row == 0, row == SUBLANES - 1
    level = lax.broadcasted_iota(jnp.int32, (slices, LANES), 0)
    front, back = level == 0, level == slices - 1
    odd, odd_row = parity("depth") == 1, parity("rows") == 1
    front_end, back_end = ends("depth")
    top_end, bottom_end = ends("rows")

    def chunk(j, carry):
        here = pl.ds(pl.multiple_of(j * LANES, LANES), LANES)
        rows_near = rows_near_ref[:, here].astype(jnp.float32)
        rows_far = rows_far_ref[:, here].astype(jnp.float32)
        above = jnp.where(top_end, 0.0, jnp.where(odd_row, rows_near, rows_far))
        below = jnp.where(bottom_end, 0.0, jnp.where(odd_row, rows_far, rows_near))
        far = far_ref[:, here].astype(jnp.float32)
        near = near_ref[:, here].astype(jnp.float32)
        before = jnp.where(front_end, 0.0, jnp.where(odd, near, far))
        after = jnp.where(back_end, 0.0, jnp.where(odd, far, near))
        extra = []
        for q, edge in enumerate((0, height - 1)):
            inner = grad_ref[q, 1, :, here]
            grad_rows = below - inner if q else inner - above
            grad_cols = grad_ref[q, 2, :, here]
            grad_depth = grad_ref[q, 0, :, here] + jnp.where(
                back, after[edge : edge + 1], jnp.where(front, -before[edge : edge + 1], 0.0)
            )
            shading = shade(
                grad_depth,
                LIGHT_ROWS * grad_rows + LIGHT_COLS * grad_cols,
                grad_rows * grad_rows + grad_cols * grad_cols,
            )
            extra.append([jnp.sum(strip_ref[q, c, :, here] * shading, axis=0, keepdims=True) for c in range(3)])
        for r in range(tiles):
            rows = slice(r * SUBLANES, (r + 1) * SUBLANES)
            planes = [base_ref[c, rows, here] for c in range(4)]
            for end in range(2):
                if end:
                    grad_depth = after[rows] - volume_ref[0, slices - 2, rows, here].astype(jnp.float32)
                else:
                    grad_depth = volume_ref[0, 1, rows, here].astype(jnp.float32) - before[rows]
                shading = shade(grad_depth, face_ref[end, rows, here], square_ref[end, rows, here])
                for c in range(3):
                    planes[c] = planes[c] + lit_ref[end, c, rows, here] * shading
            for c in range(3):
                if r == 0:
                    planes[c] = planes[c] + jnp.where(first_row, extra[0][c], 0.0)
                if r == tiles - 1:
                    planes[c] = planes[c] + jnp.where(last_row, extra[1][c], 0.0)
            for first in range(0, SUBLANES, share):
                block = jnp.concatenate([plane[first : first + share] for plane in planes], axis=0)
                out_ref[(r * SUBLANES + first) // share, :, here] = block.astype(jnp.bfloat16)
        return carry

    lax.fori_loop(0, columns // LANES, chunk, 0)


def add_edges(volume, interior, halos, depth_count):
    _, slices, height, columns = volume.shape
    share = height // depth_count
    return pl.pallas_call(
        functools.partial(edge_kernel, share),
        in_specs=[WHOLE] * 11,
        out_specs=WHOLE,
        out_shape=jax.ShapeDtypeStruct((depth_count, 4 * share, columns), jnp.bfloat16),
        compiler_params=pltpu.CompilerParams(vmem_limit_bytes=24 * 1024 * 1024),
    )(volume, *interior, *halos)


def finish_kernel(parts_ref, out_ref):
    count = parts_ref.shape[0]
    _, share, columns = out_ref.shape
    remaining = jnp.ones((share, columns), jnp.float32)
    sums = [jnp.zeros((share, columns), jnp.float32) for _ in range(3)]
    for k in range(count):
        part = parts_ref[k].astype(jnp.float32)
        for c in range(3):
            sums[c] = sums[c] + remaining * part[c * share : (c + 1) * share]
        remaining = remaining - remaining * part[3 * share :]
    for c in range(3):
        out_ref[c] = sums[c]
    out_ref[3] = 1.0 - remaining


def finish(parts, share):
    columns = parts.shape[2]
    return pl.pallas_call(
        finish_kernel,
        in_specs=[WHOLE],
        out_specs=WHOLE,
        out_shape=jax.ShapeDtypeStruct((4, share, columns), jnp.float32),
        compiler_params=pltpu.CompilerParams(vmem_limit_bytes=4 * 1024 * 1024),
    )(parts)


def swapped(values, axis, start):
    depth_count, row_count = lax.axis_size("depth"), lax.axis_size("rows")
    size = lax.axis_size(axis)
    perm = []
    for d in range(depth_count):
        for r in range(row_count):
            i = d if axis == "depth" else r
            j = i + 1 if i % 2 == start else i - 1
            if 0 <= j < size:
                e, q = (j, r) if axis == "depth" else (d, j)
            elif axis == "depth":
                e, q = (size - 1 - d, r)
            else:
                e, q = (d ^ 1, r)
            perm.append((d * row_count + r, e * row_count + q))
    return lax.ppermute(values, ("depth", "rows"), perm)


def body(volume, color_map, alpha_map):
    depth_count = lax.axis_size("depth")
    share = volume.shape[2] // depth_count
    rows_far, rows_near, far, near = cut_edges(volume)
    rows_far = swapped(rows_far, "rows", 1)
    rows_near = swapped(rows_near, "rows", 0)
    far = swapped(far, "depth", 1)
    near = swapped(near, "depth", 0)
    interior = march_interior(volume, color_map, alpha_map, depth_count)
    parts = add_edges(volume, interior, (rows_near, rows_far, far, near), depth_count)
    parts = lax.all_to_all(parts, "depth", 0, 0, tiled=True)
    return finish(parts, share)


def solution(mesh):
    in_specs = (P(None, "depth", "rows", None), P(), P())
    out_specs = P(None, ("rows", "depth"), None)
    return jax.shard_map(body, mesh=mesh, in_specs=in_specs, out_specs=out_specs, check_vma=False)
```

```python
import functools

import jax
import jax.numpy as jnp
from jax import lax
from jax.experimental import pallas as pl
from jax.experimental.pallas import tpu as pltpu
from jax.sharding import PartitionSpec as P

AMBIENT = 0.3
DIFFUSE = 0.7
LIGHT_DEPTH = 0.48 * DIFFUSE
LIGHT_ROWS = 0.6 * DIFFUSE
LIGHT_COLS = 0.64 * DIFFUSE
OPACITY = 4.0
LANES = 128
SUBLANES = 8
WHOLE = pl.BlockSpec(memory_space=pltpu.VMEM)


def parity(axis):
    return lax.axis_index(axis) % 2


def ends(axis):
    position = lax.axis_index(axis)
    return position == 0, position == lax.axis_size(axis) - 1


def edges_kernel(volume_ref, rows_far_out, rows_near_out, far_out, near_out, strip_ref, plane_ref, sems):
    _, slices, height, _ = volume_ref.shape
    odd, odd_row = parity("depth"), parity("rows")
    last_tile = height // SUBLANES - 1

    def tile(i):
        return pl.ds(pl.multiple_of(i * SUBLANES, SUBLANES), SUBLANES)

    copies = [
        pltpu.make_async_copy(volume_ref.at[0, :, tile((1 - odd_row) * last_tile)], strip_ref.at[0], sems.at[0]),
        pltpu.make_async_copy(volume_ref.at[0, :, tile(odd_row * last_tile)], strip_ref.at[1], sems.at[1]),
        pltpu.make_async_copy(volume_ref.at[0, odd * (slices - 1)], plane_ref.at[0], sems.at[2]),
        pltpu.make_async_copy(volume_ref.at[0, (1 - odd) * (slices - 1)], plane_ref.at[1], sems.at[3]),
    ]
    for copy in copies:
        copy.start()

    def narrow(values):
        return values.astype(jnp.float32).astype(jnp.bfloat16)

    copies[0].wait()
    rows_near_out[...] = narrow(jnp.where(odd_row == 1, strip_ref[0, :, 0, :], strip_ref[0, :, SUBLANES - 1, :]))
    copies[1].wait()
    rows_far_out[...] = narrow(jnp.where(odd_row == 1, strip_ref[1, :, SUBLANES - 1, :], strip_ref[1, :, 0, :]))
    copies[2].wait()
    far_out[...] = narrow(plane_ref[0])
    copies[3].wait()
    near_out[...] = narrow(plane_ref[1])


def cut_edges(volume):
    _, slices, height, columns = volume.shape
    plane = jax.ShapeDtypeStruct((height, columns), jnp.bfloat16)
    strip = jax.ShapeDtypeStruct((slices, columns), jnp.bfloat16)
    return pl.pallas_call(
        edges_kernel,
        in_specs=[pl.BlockSpec(memory_space=pl.ANY)],
        out_specs=[WHOLE] * 4,
        out_shape=[strip, strip, plane, plane],
        scratch_shapes=[
            pltpu.VMEM((2, slices, SUBLANES, columns), jnp.int32),
            pltpu.VMEM((2, height, columns), jnp.int32),
            pltpu.SemaphoreType.DMA((4,)),
        ],
        compiler_params=pltpu.CompilerParams(vmem_limit_bytes=52 * 1024 * 1024),
    )(volume)


def pick(entries, places):
    return jnp.take_along_axis(entries, places, axis=1, mode="promise_in_bounds")


def shade(grad_depth, facing, squares):
    facing = facing + LIGHT_DEPTH * grad_depth
    squares = squares + grad_depth * grad_depth
    return AMBIENT + jnp.abs(facing) * lax.rsqrt(jnp.maximum(squares, 4.0))


def interior_kernel(
    opacity_scale, volume_ref, color_ref, alpha_ref, base_ref, face_ref, square_ref, lit_ref, grad_ref, strip_ref, held_ref
):
    _, slices, height, columns = volume_ref.shape
    tiles = height // SUBLANES
    chunks = columns // LANES
    tile = (SUBLANES, LANES)
    strip = (slices, LANES)

    packed = color_ref[0:1, :] + color_ref[1:2, :] * 256 + color_ref[2:3, :] * 65536
    color_low, color_high = packed[:, :LANES], packed[:, LANES:]
    alpha_both = alpha_ref[0:1, :LANES] + alpha_ref[0:1, LANES:] * 256

    def colors(value, tables):
        low, high = tables
        place = value & (LANES - 1)
        color = jnp.where(value < LANES, pick(low, place), pick(high, place))
        parts = (color & 255, lax.shift_right_logical(color, 8) & 255, lax.shift_right_logical(color, 16))
        return [part.astype(jnp.float32) for part in parts]

    def opacity(level, table):
        entry = pick(table, level & (LANES - 1))
        entry = lax.shift_right_logical(entry, lax.shift_right_logical(level & LANES, 4)) & 255
        return entry.astype(jnp.float32) * opacity_scale

    tile_colors = [jnp.broadcast_to(t, tile) for t in (color_low, color_high)]
    tile_alpha = jnp.broadcast_to(alpha_both, tile)
    strip_colors = [jnp.broadcast_to(t, strip) for t in (color_low, color_high)]

    def masks(shape):
        lane = lax.broadcasted_iota(jnp.int32, shape, 1)
        row = lax.broadcasted_iota(jnp.int32, shape, 0)
        return lane == 0, lane == LANES - 1, row == 0, row == shape[0] - 1

    first_lane, last_lane, first_row, last_row = masks(tile)
    strip_first_lane, strip_last_lane, front, back = masks(strip)

    def chunk(j, carry):
        here = pl.ds(pl.multiple_of(j * LANES, LANES), LANES)
        left = pl.ds(pl.multiple_of(jnp.maximum(j - 1, 0) * LANES, LANES), LANES)
        right = pl.ds(pl.multiple_of(jnp.minimum(j + 1, chunks - 1) * LANES, LANES), LANES)

        def across(value, left_value, right_value, first, last):
            west = jnp.where(last & (j > 0), left_value, value)
            west = pltpu.roll(jnp.where(last & (j == 0), 0, west), 1, 1)
            east = jnp.where(first & (j < chunks - 1), right_value, value)
            east = pltpu.roll(jnp.where(first & (j == chunks - 1), 0, east), LANES - 1, 1)
            return (east - west).astype(jnp.float32)

        for r in range(tiles):
            rows = slice(r * SUBLANES, (r + 1) * SUBLANES)
            values = [volume_ref[0, s, rows, here] for s in range(slices)]
            remaining = jnp.ones(tile, jnp.float32)
            sums = [jnp.zeros(tile, jnp.float32) for _ in range(3)]
            for s in range(slices):
                value = values[s]
                up = volume_ref[0, s, (r - 1) * SUBLANES : r * SUBLANES, here] if r > 0 else value
                down = volume_ref[0, s, (r + 1) * SUBLANES : (r + 2) * SUBLANES, here] if r < tiles - 1 else value
                up = pltpu.roll(jnp.where(last_row, up, value), 1, 0)
                down = pltpu.roll(jnp.where(first_row, down, value), SUBLANES - 1, 0)
                grad_rows = (down - up).astype(jnp.float32)
                grad_cols = across(
                    value, volume_ref[0, s, rows, left], volume_ref[0, s, rows, right], first_lane, last_lane
                )
                squares = grad_rows * grad_rows + grad_cols * grad_cols
                facing = LIGHT_ROWS * grad_rows + LIGHT_COLS * grad_cols
                weight = remaining * opacity(volume_ref[1, s, rows, here], tile_alpha)
                remaining = remaining - weight
                if r == 0:
                    held_ref[0, s : s + 1, :] = weight[:1]
                    weight = jnp.where(first_row, 0.0, weight)
                if r == tiles - 1:
                    held_ref[1, s : s + 1, :] = weight[SUBLANES - 1 :]
                    weight = jnp.where(last_row, 0.0, weight)
                emitted = colors(value, tile_colors)
                if 0 < s < slices - 1:
                    grad_depth = (values[s + 1] - values[s - 1]).astype(jnp.float32)
                    weight = weight * shade(grad_depth, facing, squares)
                    for c in range(3):
                        sums[c] = sums[c] + emitted[c] * weight
                else:
                    end = int(s > 0)
                    face_ref[end, rows, here] = facing
                    square_ref[end, rows, here] = squares
                    weight = weight * (1.0 / 255.0)
                    for c in range(3):
                        lit_ref[end, c, rows, here] = emitted[c] * weight
            for c in range(3):
                base_ref[c, rows, here] = sums[c] * (1.0 / 255.0)
            base_ref[3, rows, here] = 1.0 - remaining

        for q, (edge, inner) in enumerate(((0, 1), (height - 1, height - 2))):
            value = volume_ref[0, :, edge, here]
            behind = pltpu.roll(jnp.where(back, 0, value), 1, 0)
            ahead = pltpu.roll(jnp.where(front, 0, value), slices - 1, 0)
            grad_ref[q, 0, :, here] = (ahead - behind).astype(jnp.float32)
            grad_ref[q, 1, :, here] = volume_ref[0, :, inner, here].astype(jnp.float32)
            grad_ref[q, 2, :, here] = across(
                value, volume_ref[0, :, edge, left], volume_ref[0, :, edge, right], strip_first_lane, strip_last_lane
            )
            weight = held_ref[q] * (1.0 / 255.0)
            emitted = colors(value, strip_colors)
            for c in range(3):
                strip_ref[q, c, :, here] = emitted[c] * weight
        return carry

    lax.fori_loop(0, chunks, chunk, 0)


def march_interior(volume, color_map, alpha_map, depth_count):
    _, slices, height, columns = volume.shape
    opacity_scale = OPACITY / (255.0 * slices * depth_count)
    shapes = [
        (4, height, columns),
        (2, height, columns),
        (2, height, columns),
        (2, 3, height, columns),
        (2, 3, slices, columns),
        (2, 3, slices, columns),
    ]
    voxels = slices * height * columns
    return pl.pallas_call(
        functools.partial(interior_kernel, opacity_scale),
        in_specs=[WHOLE] * 3,
        out_specs=[WHOLE] * len(shapes),
        out_shape=[jax.ShapeDtypeStruct(shape, jnp.float32) for shape in shapes],
        scratch_shapes=[pltpu.VMEM((2, slices, LANES), jnp.float32)],
        compiler_params=pltpu.CompilerParams(vmem_limit_bytes=24 * 1024 * 1024),
        cost_estimate=pl.CostEstimate(flops=voxels * 80, bytes_accessed=voxels * 20, transcendentals=voxels),
    )(volume, color_map, alpha_map.reshape(1, -1))


def edge_kernel(
    share, volume_ref, base_ref, face_ref, square_ref, lit_ref, grad_ref, strip_ref, rows_near_ref, rows_far_ref, far_ref, near_ref, out_ref
):
    _, slices, height, columns = volume_ref.shape
    tiles = height // SUBLANES
    tile = (SUBLANES, LANES)
    row = lax.broadcasted_iota(jnp.int32, tile, 0)
    first_row, last_row = row == 0, row == SUBLANES - 1
    level = lax.broadcasted_iota(jnp.int32, (slices, LANES), 0)
    front, back = level == 0, level == slices - 1
    odd, odd_row = parity("depth") == 1, parity("rows") == 1
    front_end, back_end = ends("depth")
    top_end, bottom_end = ends("rows")

    def chunk(j, carry):
        here = pl.ds(pl.multiple_of(j * LANES, LANES), LANES)
        rows_near = rows_near_ref[:, here].astype(jnp.float32)
        rows_far = rows_far_ref[:, here].astype(jnp.float32)
        above = jnp.where(top_end, 0.0, jnp.where(odd_row, rows_near, rows_far))
        below = jnp.where(bottom_end, 0.0, jnp.where(odd_row, rows_far, rows_near))
        far = far_ref[:, here].astype(jnp.float32)
        near = near_ref[:, here].astype(jnp.float32)
        before = jnp.where(front_end, 0.0, jnp.where(odd, near, far))
        after = jnp.where(back_end, 0.0, jnp.where(odd, far, near))
        extra = []
        for q, edge in enumerate((0, height - 1)):
            inner = grad_ref[q, 1, :, here]
            grad_rows = below - inner if q else inner - above
            grad_cols = grad_ref[q, 2, :, here]
            grad_depth = grad_ref[q, 0, :, here] + jnp.where(
                back, after[edge : edge + 1], jnp.where(front, -before[edge : edge + 1], 0.0)
            )
            shading = shade(
                grad_depth,
                LIGHT_ROWS * grad_rows + LIGHT_COLS * grad_cols,
                grad_rows * grad_rows + grad_cols * grad_cols,
            )
            extra.append([jnp.sum(strip_ref[q, c, :, here] * shading, axis=0, keepdims=True) for c in range(3)])
        for r in range(tiles):
            rows = slice(r * SUBLANES, (r + 1) * SUBLANES)
            planes = [base_ref[c, rows, here] for c in range(4)]
            for end in range(2):
                if end:
                    grad_depth = after[rows] - volume_ref[0, slices - 2, rows, here].astype(jnp.float32)
                else:
                    grad_depth = volume_ref[0, 1, rows, here].astype(jnp.float32) - before[rows]
                shading = shade(grad_depth, face_ref[end, rows, here], square_ref[end, rows, here])
                for c in range(3):
                    planes[c] = planes[c] + lit_ref[end, c, rows, here] * shading
            for c in range(3):
                if r == 0:
                    planes[c] = planes[c] + jnp.where(first_row, extra[0][c], 0.0)
                if r == tiles - 1:
                    planes[c] = planes[c] + jnp.where(last_row, extra[1][c], 0.0)
            for first in range(0, SUBLANES, share):
                block = jnp.concatenate([plane[first : first + share] for plane in planes], axis=0)
                out_ref[(r * SUBLANES + first) // share, :, here] = block.astype(jnp.bfloat16)
        return carry

    lax.fori_loop(0, columns // LANES, chunk, 0)


def add_edges(volume, interior, halos, depth_count):
    _, slices, height, columns = volume.shape
    share = height // depth_count
    return pl.pallas_call(
        functools.partial(edge_kernel, share),
        in_specs=[WHOLE] * 11,
        out_specs=WHOLE,
        out_shape=jax.ShapeDtypeStruct((depth_count, 4 * share, columns), jnp.bfloat16),
        compiler_params=pltpu.CompilerParams(vmem_limit_bytes=24 * 1024 * 1024),
    )(volume, *interior, *halos)


def finish_kernel(parts_ref, out_ref):
    count = parts_ref.shape[0]
    _, share, columns = out_ref.shape
    remaining = jnp.ones((share, columns), jnp.float32)
    sums = [jnp.zeros((share, columns), jnp.float32) for _ in range(3)]
    for k in range(count):
        part = parts_ref[k].astype(jnp.float32)
        for c in range(3):
            sums[c] = sums[c] + remaining * part[c * share : (c + 1) * share]
        remaining = remaining - remaining * part[3 * share :]
    for c in range(3):
        out_ref[c] = sums[c]
    out_ref[3] = 1.0 - remaining


def finish(parts, share):
    columns = parts.shape[2]
    return pl.pallas_call(
        finish_kernel,
        in_specs=[WHOLE],
        out_specs=WHOLE,
        out_shape=jax.ShapeDtypeStruct((4, share, columns), jnp.float32),
        compiler_params=pltpu.CompilerParams(vmem_limit_bytes=4 * 1024 * 1024),
    )(parts)


def swapped(values, axis, start):
    depth_count, row_count = lax.axis_size("depth"), lax.axis_size("rows")
    size = lax.axis_size(axis)
    perm = []
    for d in range(depth_count):
        for r in range(row_count):
            i = d if axis == "depth" else r
            j = i + 1 if i % 2 == start else i - 1
            if 0 <= j < size:
                e, q = (j, r) if axis == "depth" else (d, j)
            elif axis == "depth":
                e, q = (size - 1 - d, r)
            else:
                e, q = (d ^ 1, r)
            perm.append((d * row_count + r, e * row_count + q))
    return lax.ppermute(values, ("depth", "rows"), perm)


def body(volume, color_map, alpha_map):
    depth_count = lax.axis_size("depth")
    share = volume.shape[2] // depth_count
    rows_far, rows_near, far, near = cut_edges(volume)
    rows_far = swapped(rows_far, "rows", 1)
    rows_near = swapped(rows_near, "rows", 0)
    far = swapped(far, "depth", 1)
    near = swapped(near, "depth", 0)
    interior = march_interior(volume, color_map, alpha_map, depth_count)
    parts = add_edges(volume, interior, (rows_near, rows_far, far, near), depth_count)
    parts = lax.all_to_all(parts, "depth", 0, 0, tiled=True)
    return finish(parts, share)


def solution(mesh):
    in_specs = (P(None, "depth", "rows", None), P(), P())
    out_specs = P(None, ("rows", "depth"), None)
    return jax.shard_map(body, mesh=mesh, in_specs=in_specs, out_specs=out_specs, check_vma=False)
```

```python
import functools

import jax
import jax.numpy as jnp
from jax import lax
from jax.experimental import pallas as pl
from jax.experimental.pallas import tpu as pltpu
from jax.sharding import PartitionSpec as P

AMBIENT = 0.3
DIFFUSE = 0.7
LIGHT_DEPTH = 0.48 * DIFFUSE
LIGHT_ROWS = 0.6 * DIFFUSE
LIGHT_COLS = 0.64 * DIFFUSE
OPACITY = 4.0
LANES = 128
SUBLANES = 8
WHOLE = pl.BlockSpec(memory_space=pltpu.VMEM)


def parity(axis):
    return lax.axis_index(axis) % 2


def ends(axis):
    position = lax.axis_index(axis)
    return position == 0, position == lax.axis_size(axis) - 1


def edges_kernel(volume_ref, rows_far_out, rows_near_out, far_out, near_out, strip_ref, plane_ref, sems):
    _, slices, height, _ = volume_ref.shape
    odd, odd_row = parity("depth"), parity("rows")
    last_tile = height // SUBLANES - 1

    def tile(i):
        return pl.ds(pl.multiple_of(i * SUBLANES, SUBLANES), SUBLANES)

    copies = [
        pltpu.make_async_copy(volume_ref.at[0, :, tile((1 - odd_row) * last_tile)], strip_ref.at[0], sems.at[0]),
        pltpu.make_async_copy(volume_ref.at[0, :, tile(odd_row * last_tile)], strip_ref.at[1], sems.at[1]),
        pltpu.make_async_copy(volume_ref.at[0, odd * (slices - 1)], plane_ref.at[0], sems.at[2]),
        pltpu.make_async_copy(volume_ref.at[0, (1 - odd) * (slices - 1)], plane_ref.at[1], sems.at[3]),
    ]
    for copy in copies:
        copy.start()

    def narrow(values):
        return values.astype(jnp.float32).astype(jnp.bfloat16)

    copies[0].wait()
    rows_near_out[...] = narrow(jnp.where(odd_row == 1, strip_ref[0, :, 0, :], strip_ref[0, :, SUBLANES - 1, :]))
    copies[1].wait()
    rows_far_out[...] = narrow(jnp.where(odd_row == 1, strip_ref[1, :, SUBLANES - 1, :], strip_ref[1, :, 0, :]))
    copies[2].wait()
    far_out[...] = narrow(plane_ref[0])
    copies[3].wait()
    near_out[...] = narrow(plane_ref[1])


def cut_edges(volume):
    _, slices, height, columns = volume.shape
    plane = jax.ShapeDtypeStruct((height, columns), jnp.bfloat16)
    strip = jax.ShapeDtypeStruct((slices, columns), jnp.bfloat16)
    return pl.pallas_call(
        edges_kernel,
        in_specs=[pl.BlockSpec(memory_space=pl.ANY)],
        out_specs=[WHOLE] * 4,
        out_shape=[strip, strip, plane, plane],
        scratch_shapes=[
            pltpu.VMEM((2, slices, SUBLANES, columns), jnp.int32),
            pltpu.VMEM((2, height, columns), jnp.int32),
            pltpu.SemaphoreType.DMA((4,)),
        ],
        compiler_params=pltpu.CompilerParams(vmem_limit_bytes=52 * 1024 * 1024),
    )(volume)


def pick(entries, places):
    return jnp.take_along_axis(entries, places, axis=1, mode="promise_in_bounds")


def shade(grad_depth, facing, squares):
    facing = facing + LIGHT_DEPTH * grad_depth
    squares = squares + grad_depth * grad_depth
    return AMBIENT + jnp.abs(facing) * lax.rsqrt(jnp.maximum(squares, 4.0))


def interior_kernel(
    opacity_scale,
    volume_ref,
    color_ref,
    alpha_ref,
    base_ref,
    face_ref,
    square_ref,
    lit_ref,
    grad_ref,
    strip_ref,
    held_ref,
    level_ref,
    down_ref,
    right_ref,
):
    _, slices, height, columns = volume_ref.shape
    tiles = height // SUBLANES
    chunks = columns // LANES
    tile = (SUBLANES, LANES)
    strip = (slices, LANES)

    packed = color_ref[0:1, :] + color_ref[1:2, :] * 256 + color_ref[2:3, :] * 65536
    color_low, color_high = packed[:, :LANES], packed[:, LANES:]
    alpha_both = alpha_ref[0:1, :LANES] + alpha_ref[0:1, LANES:] * 256

    def colors(value, tables):
        low, high = tables
        place = value & (LANES - 1)
        color = jnp.where(value < LANES, pick(low, place), pick(high, place))
        parts = (color & 255, lax.shift_right_logical(color, 8) & 255, lax.shift_right_logical(color, 16))
        return [part.astype(jnp.float32) for part in parts]

    def opacity(level, table):
        entry = pick(table, level & (LANES - 1))
        entry = lax.shift_right_logical(entry, lax.shift_right_logical(level & LANES, 4)) & 255
        return entry.astype(jnp.float32) * opacity_scale

    tile_colors = [jnp.broadcast_to(t, tile) for t in (color_low, color_high)]
    tile_alpha = jnp.broadcast_to(alpha_both, tile)
    strip_colors = [jnp.broadcast_to(t, strip) for t in (color_low, color_high)]

    def rows_of(shape):
        row = lax.broadcasted_iota(jnp.int32, shape, 0)
        return row == 0, row == shape[0] - 1

    first_row, last_row = rows_of(tile)
    front, back = rows_of(strip)

    voxel_rows = slices * height
    level_ref[:, :LANES] = jnp.zeros((voxel_rows, LANES), jnp.bfloat16)
    level_ref[:, LANES + columns :] = jnp.zeros((voxel_rows, LANES), jnp.bfloat16)
    for s in range(slices):
        level_ref[s * height : (s + 1) * height, LANES : LANES + columns] = (
            volume_ref[0, s].astype(jnp.float32).astype(jnp.bfloat16)
        )

    def band(shape, offset):
        return lax.broadcasted_iota(jnp.int32, shape, 1) - lax.broadcasted_iota(jnp.int32, shape, 0) + offset

    def signs(plus, minus):
        return (plus.astype(jnp.float32) - minus.astype(jnp.float32)).astype(jnp.bfloat16)

    block = 2 * LANES
    square = (voxel_rows, voxel_rows)
    row = lax.broadcasted_iota(jnp.int32, square, 0) % height
    step = band(square, 0)
    row_matrix = signs((step == 1) & (row < height - 1), (step == -1) & (row > 0))
    step = band((2 * block, block), LANES)
    col_matrix = signs(step == -1, step == 1)

    def differences(q, carry):
        here = pl.ds(pl.multiple_of(q * block, block), block)
        middle = pl.ds(pl.multiple_of(q * block + LANES, LANES), block)
        wide = pl.ds(pl.multiple_of(q * block, block), 2 * block)
        down = jnp.dot(row_matrix, level_ref[:, middle], preferred_element_type=jnp.float32)
        down_ref[:, :, here] = down.reshape(slices, height, block)
        right = jnp.dot(level_ref[:, wide], col_matrix, preferred_element_type=jnp.float32)
        right_ref[:, :, here] = right.reshape(slices, height, block)
        return carry

    lax.fori_loop(0, columns // block, differences, 0)

    def chunk(j, carry):
        here = pl.ds(pl.multiple_of(j * LANES, LANES), LANES)

        for r in range(tiles):
            rows = slice(r * SUBLANES, (r + 1) * SUBLANES)
            values = [volume_ref[0, s, rows, here] for s in range(slices)]
            remaining = jnp.ones(tile, jnp.float32)
            sums = [jnp.zeros(tile, jnp.float32) for _ in range(3)]
            for s in range(slices):
                value = values[s]
                grad_rows = down_ref[s, rows, here]
                grad_cols = right_ref[s, rows, here]
                squares = grad_rows * grad_rows + grad_cols * grad_cols
                facing = LIGHT_ROWS * grad_rows + LIGHT_COLS * grad_cols
                weight = remaining * opacity(volume_ref[1, s, rows, here], tile_alpha)
                remaining = remaining - weight
                if r == 0:
                    held_ref[0, s : s + 1, :] = weight[:1]
                    weight = jnp.where(first_row, 0.0, weight)
                if r == tiles - 1:
                    held_ref[1, s : s + 1, :] = weight[SUBLANES - 1 :]
                    weight = jnp.where(last_row, 0.0, weight)
                emitted = colors(value, tile_colors)
                if 0 < s < slices - 1:
                    grad_depth = (values[s + 1] - values[s - 1]).astype(jnp.float32)
                    weight = weight * shade(grad_depth, facing, squares)
                    for c in range(3):
                        sums[c] = sums[c] + emitted[c] * weight
                else:
                    end = int(s > 0)
                    face_ref[end, rows, here] = facing
                    square_ref[end, rows, here] = squares
                    weight = weight * (1.0 / 255.0)
                    for c in range(3):
                        lit_ref[end, c, rows, here] = emitted[c] * weight
            for c in range(3):
                base_ref[c, rows, here] = sums[c] * (1.0 / 255.0)
            base_ref[3, rows, here] = 1.0 - remaining

        for q, (edge, inner) in enumerate(((0, 1), (height - 1, height - 2))):
            value = volume_ref[0, :, edge, here]
            behind = pltpu.roll(jnp.where(back, 0, value), 1, 0)
            ahead = pltpu.roll(jnp.where(front, 0, value), slices - 1, 0)
            grad_ref[q, 0, :, here] = (ahead - behind).astype(jnp.float32)
            grad_ref[q, 1, :, here] = volume_ref[0, :, inner, here].astype(jnp.float32)
            grad_ref[q, 2, :, here] = right_ref[:, edge, here]
            weight = held_ref[q] * (1.0 / 255.0)
            emitted = colors(value, strip_colors)
            for c in range(3):
                strip_ref[q, c, :, here] = emitted[c] * weight
        return carry

    lax.fori_loop(0, chunks, chunk, 0)


def march_interior(volume, color_map, alpha_map, depth_count):
    _, slices, height, columns = volume.shape
    opacity_scale = OPACITY / (255.0 * slices * depth_count)
    shapes = [
        (4, height, columns),
        (2, height, columns),
        (2, height, columns),
        (2, 3, height, columns),
        (2, 3, slices, columns),
        (2, 3, slices, columns),
    ]
    voxels = slices * height * columns
    return pl.pallas_call(
        functools.partial(interior_kernel, opacity_scale),
        in_specs=[WHOLE] * 3,
        out_specs=[WHOLE] * len(shapes),
        out_shape=[jax.ShapeDtypeStruct(shape, jnp.float32) for shape in shapes],
        scratch_shapes=[
            pltpu.VMEM((2, slices, LANES), jnp.float32),
            pltpu.VMEM((slices * height, columns + 2 * LANES), jnp.bfloat16),
            pltpu.VMEM((slices, height, columns), jnp.float32),
            pltpu.VMEM((slices, height, columns), jnp.float32),
        ],
        compiler_params=pltpu.CompilerParams(vmem_limit_bytes=24 * 1024 * 1024),
        cost_estimate=pl.CostEstimate(flops=voxels * 80, bytes_accessed=voxels * 20, transcendentals=voxels),
    )(volume, color_map, alpha_map.reshape(1, -1))


def edge_kernel(
    share, volume_ref, base_ref, face_ref, square_ref, lit_ref, grad_ref, strip_ref, rows_near_ref, rows_far_ref, far_ref, near_ref, out_ref
):
    _, slices, height, columns = volume_ref.shape
    tiles = height // SUBLANES
    tile = (SUBLANES, LANES)
    row = lax.broadcasted_iota(jnp.int32, tile, 0)
    first_row, last_row = row == 0, row == SUBLANES - 1
    level = lax.broadcasted_iota(jnp.int32, (slices, LANES), 0)
    front, back = level == 0, level == slices - 1
    odd, odd_row = parity("depth") == 1, parity("rows") == 1
    front_end, back_end = ends("depth")
    top_end, bottom_end = ends("rows")

    def chunk(j, carry):
        here = pl.ds(pl.multiple_of(j * LANES, LANES), LANES)
        rows_near = rows_near_ref[:, here].astype(jnp.float32)
        rows_far = rows_far_ref[:, here].astype(jnp.float32)
        above = jnp.where(top_end, 0.0, jnp.where(odd_row, rows_near, rows_far))
        below = jnp.where(bottom_end, 0.0, jnp.where(odd_row, rows_far, rows_near))
        far = far_ref[:, here].astype(jnp.float32)
        near = near_ref[:, here].astype(jnp.float32)
        before = jnp.where(front_end, 0.0, jnp.where(odd, near, far))
        after = jnp.where(back_end, 0.0, jnp.where(odd, far, near))
        extra = []
        for q, edge in enumerate((0, height - 1)):
            inner = grad_ref[q, 1, :, here]
            grad_rows = below - inner if q else inner - above
            grad_cols = grad_ref[q, 2, :, here]
            grad_depth = grad_ref[q, 0, :, here] + jnp.where(
                back, after[edge : edge + 1], jnp.where(front, -before[edge : edge + 1], 0.0)
            )
            shading = shade(
                grad_depth,
                LIGHT_ROWS * grad_rows + LIGHT_COLS * grad_cols,
                grad_rows * grad_rows + grad_cols * grad_cols,
            )
            extra.append([jnp.sum(strip_ref[q, c, :, here] * shading, axis=0, keepdims=True) for c in range(3)])
        for r in range(tiles):
            rows = slice(r * SUBLANES, (r + 1) * SUBLANES)
            planes = [base_ref[c, rows, here] for c in range(4)]
            for end in range(2):
                if end:
                    grad_depth = after[rows] - volume_ref[0, slices - 2, rows, here].astype(jnp.float32)
                else:
                    grad_depth = volume_ref[0, 1, rows, here].astype(jnp.float32) - before[rows]
                shading = shade(grad_depth, face_ref[end, rows, here], square_ref[end, rows, here])
                for c in range(3):
                    planes[c] = planes[c] + lit_ref[end, c, rows, here] * shading
            for c in range(3):
                if r == 0:
                    planes[c] = planes[c] + jnp.where(first_row, extra[0][c], 0.0)
                if r == tiles - 1:
                    planes[c] = planes[c] + jnp.where(last_row, extra[1][c], 0.0)
            for first in range(0, SUBLANES, share):
                block = jnp.concatenate([plane[first : first + share] for plane in planes], axis=0)
                out_ref[(r * SUBLANES + first) // share, :, here] = block.astype(jnp.bfloat16)
        return carry

    lax.fori_loop(0, columns // LANES, chunk, 0)


def add_edges(volume, interior, halos, depth_count):
    _, slices, height, columns = volume.shape
    share = height // depth_count
    return pl.pallas_call(
        functools.partial(edge_kernel, share),
        in_specs=[WHOLE] * 11,
        out_specs=WHOLE,
        out_shape=jax.ShapeDtypeStruct((depth_count, 4 * share, columns), jnp.bfloat16),
        compiler_params=pltpu.CompilerParams(vmem_limit_bytes=24 * 1024 * 1024),
    )(volume, *interior, *halos)


def finish_kernel(parts_ref, out_ref):
    count = parts_ref.shape[0]
    _, share, columns = out_ref.shape
    remaining = jnp.ones((share, columns), jnp.float32)
    sums = [jnp.zeros((share, columns), jnp.float32) for _ in range(3)]
    for k in range(count):
        part = parts_ref[k].astype(jnp.float32)
        for c in range(3):
            sums[c] = sums[c] + remaining * part[c * share : (c + 1) * share]
        remaining = remaining - remaining * part[3 * share :]
    for c in range(3):
        out_ref[c] = sums[c]
    out_ref[3] = 1.0 - remaining


def finish(parts, share):
    columns = parts.shape[2]
    return pl.pallas_call(
        finish_kernel,
        in_specs=[WHOLE],
        out_specs=WHOLE,
        out_shape=jax.ShapeDtypeStruct((4, share, columns), jnp.float32),
        compiler_params=pltpu.CompilerParams(vmem_limit_bytes=4 * 1024 * 1024),
    )(parts)


def swapped(values, axis, start):
    depth_count, row_count = lax.axis_size("depth"), lax.axis_size("rows")
    size = lax.axis_size(axis)
    perm = []
    for d in range(depth_count):
        for r in range(row_count):
            i = d if axis == "depth" else r
            j = i + 1 if i % 2 == start else i - 1
            if 0 <= j < size:
                e, q = (j, r) if axis == "depth" else (d, j)
            elif axis == "depth":
                e, q = (size - 1 - d, r)
            else:
                e, q = (d ^ 1, r)
            perm.append((d * row_count + r, e * row_count + q))
    return lax.ppermute(values, ("depth", "rows"), perm)


def body(volume, color_map, alpha_map):
    depth_count = lax.axis_size("depth")
    share = volume.shape[2] // depth_count
    rows_far, rows_near, far, near = cut_edges(volume)
    rows_far = swapped(rows_far, "rows", 1)
    rows_near = swapped(rows_near, "rows", 0)
    far = swapped(far, "depth", 1)
    near = swapped(near, "depth", 0)
    interior = march_interior(volume, color_map, alpha_map, depth_count)
    parts = add_edges(volume, interior, (rows_near, rows_far, far, near), depth_count)
    parts = lax.all_to_all(parts, "depth", 0, 0, tiled=True)
    return finish(parts, share)


def solution(mesh):
    in_specs = (P(None, "depth", "rows", None), P(), P())
    out_specs = P(None, ("rows", "depth"), None)
    return jax.shard_map(body, mesh=mesh, in_specs=in_specs, out_specs=out_specs, check_vma=False)
```

```python
import functools

import jax
import jax.numpy as jnp
from jax import lax
from jax.experimental import pallas as pl
from jax.experimental.pallas import tpu as pltpu
from jax.sharding import PartitionSpec as P

AMBIENT = 0.3
DIFFUSE = 0.7
LIGHT_DEPTH = 0.48 * DIFFUSE
LIGHT_ROWS = 0.6 * DIFFUSE
LIGHT_COLS = 0.64 * DIFFUSE
OPACITY = 4.0
LANES = 128
SUBLANES = 8
WHOLE = pl.BlockSpec(memory_space=pltpu.VMEM)


def parity(axis):
    return lax.axis_index(axis) % 2


def ends(axis):
    position = lax.axis_index(axis)
    return position == 0, position == lax.axis_size(axis) - 1


def edges_kernel(volume_ref, rows_far_out, rows_near_out, far_out, near_out, strip_ref, plane_ref, sems):
    _, slices, height, _ = volume_ref.shape
    odd, odd_row = parity("depth"), parity("rows")
    last_tile = height // SUBLANES - 1

    def tile(i):
        return pl.ds(pl.multiple_of(i * SUBLANES, SUBLANES), SUBLANES)

    copies = [
        pltpu.make_async_copy(volume_ref.at[0, :, tile((1 - odd_row) * last_tile)], strip_ref.at[0], sems.at[0]),
        pltpu.make_async_copy(volume_ref.at[0, :, tile(odd_row * last_tile)], strip_ref.at[1], sems.at[1]),
        pltpu.make_async_copy(volume_ref.at[0, odd * (slices - 1)], plane_ref.at[0], sems.at[2]),
        pltpu.make_async_copy(volume_ref.at[0, (1 - odd) * (slices - 1)], plane_ref.at[1], sems.at[3]),
    ]
    for copy in copies:
        copy.start()

    def narrow(values):
        return values.astype(jnp.float32).astype(jnp.bfloat16)

    copies[0].wait()
    rows_near_out[...] = narrow(jnp.where(odd_row == 1, strip_ref[0, :, 0, :], strip_ref[0, :, SUBLANES - 1, :]))
    copies[1].wait()
    rows_far_out[...] = narrow(jnp.where(odd_row == 1, strip_ref[1, :, SUBLANES - 1, :], strip_ref[1, :, 0, :]))
    copies[2].wait()
    far_out[...] = narrow(plane_ref[0])
    copies[3].wait()
    near_out[...] = narrow(plane_ref[1])


def cut_edges(volume):
    _, slices, height, columns = volume.shape
    plane = jax.ShapeDtypeStruct((height, columns), jnp.bfloat16)
    strip = jax.ShapeDtypeStruct((slices, columns), jnp.bfloat16)
    return pl.pallas_call(
        edges_kernel,
        in_specs=[pl.BlockSpec(memory_space=pl.ANY)],
        out_specs=[WHOLE] * 4,
        out_shape=[strip, strip, plane, plane],
        scratch_shapes=[
            pltpu.VMEM((2, slices, SUBLANES, columns), jnp.int32),
            pltpu.VMEM((2, height, columns), jnp.int32),
            pltpu.SemaphoreType.DMA((4,)),
        ],
        compiler_params=pltpu.CompilerParams(vmem_limit_bytes=52 * 1024 * 1024),
    )(volume)


def pick(entries, places):
    dims = lax.GatherDimensionNumbers(
        offset_dims=(),
        collapsed_slice_dims=(1,),
        start_index_map=(1,),
        operand_batching_dims=(0,),
        start_indices_batching_dims=(0,),
    )
    return lax.gather(entries, places[..., None], dims, (1, 1), mode=lax.GatherScatterMode.PROMISE_IN_BOUNDS)


def choose(level, tables):
    low, high = tables
    place = level & (LANES - 1)
    return jnp.where(level < LANES, pick(low, place), pick(high, place))


def shade(grad_depth, facing, squares):
    facing = facing + LIGHT_DEPTH * grad_depth
    squares = squares + grad_depth * grad_depth
    return AMBIENT + jnp.abs(facing) * lax.rsqrt(jnp.maximum(squares, 4.0))


def interior_kernel(
    opacity_scale, volume_ref, color_ref, alpha_ref, base_ref, face_ref, square_ref, lit_ref, grad_ref, strip_ref, held_ref
):
    _, slices, height, columns = volume_ref.shape
    tiles = height // SUBLANES
    chunks = columns // LANES
    tile = (SUBLANES, LANES)
    strip = (slices, LANES)

    packed = color_ref[0:1, :] + color_ref[1:2, :] * 256 + color_ref[2:3, :] * 65536
    color_low, color_high = packed[:, :LANES], packed[:, LANES:]
    opacities = alpha_ref[0:1, :].astype(jnp.float32) * opacity_scale

    def colors(value, tables):
        color = choose(value, tables)
        parts = (color & 255, lax.shift_right_logical(color, 8) & 255, lax.shift_right_logical(color, 16))
        return [part.astype(jnp.float32) for part in parts]

    tile_colors = [jnp.broadcast_to(t, tile) for t in (color_low, color_high)]
    tile_opacities = [jnp.broadcast_to(t, tile) for t in (opacities[:, :LANES], opacities[:, LANES:])]
    strip_colors = [jnp.broadcast_to(t, strip) for t in (color_low, color_high)]

    def masks(shape):
        lane = lax.broadcasted_iota(jnp.int32, shape, 1)
        row = lax.broadcasted_iota(jnp.int32, shape, 0)
        return lane == 0, lane == LANES - 1, row == 0, row == shape[0] - 1

    first_lane, last_lane, first_row, last_row = masks(tile)
    strip_first_lane, strip_last_lane, front, back = masks(strip)

    def chunk(j, carry):
        here = pl.ds(pl.multiple_of(j * LANES, LANES), LANES)
        left = pl.ds(pl.multiple_of(jnp.maximum(j - 1, 0) * LANES, LANES), LANES)
        right = pl.ds(pl.multiple_of(jnp.minimum(j + 1, chunks - 1) * LANES, LANES), LANES)

        def across(value, left_value, right_value, first, last):
            west = jnp.where(last & (j > 0), left_value, value)
            west = pltpu.roll(jnp.where(last & (j == 0), 0, west), 1, 1)
            east = jnp.where(first & (j < chunks - 1), right_value, value)
            east = pltpu.roll(jnp.where(first & (j == chunks - 1), 0, east), LANES - 1, 1)
            return (east - west).astype(jnp.float32)

        for r in range(tiles):
            rows = slice(r * SUBLANES, (r + 1) * SUBLANES)
            values = [volume_ref[0, s, rows, here] for s in range(slices)]
            remaining = jnp.ones(tile, jnp.float32)
            sums = [jnp.zeros(tile, jnp.float32) for _ in range(3)]
            for s in range(slices):
                value = values[s]
                up = volume_ref[0, s, (r - 1) * SUBLANES : r * SUBLANES, here] if r > 0 else value
                down = volume_ref[0, s, (r + 1) * SUBLANES : (r + 2) * SUBLANES, here] if r < tiles - 1 else value
                up = pltpu.roll(jnp.where(last_row, up, value), 1, 0)
                down = pltpu.roll(jnp.where(first_row, down, value), SUBLANES - 1, 0)
                grad_rows = (down - up).astype(jnp.float32)
                grad_cols = across(
                    value, volume_ref[0, s, rows, left], volume_ref[0, s, rows, right], first_lane, last_lane
                )
                squares = grad_rows * grad_rows + grad_cols * grad_cols
                facing = LIGHT_ROWS * grad_rows + LIGHT_COLS * grad_cols
                weight = remaining * choose(volume_ref[1, s, rows, here], tile_opacities)
                remaining = remaining - weight
                if r == 0:
                    held_ref[0, s : s + 1, :] = weight[:1]
                    weight = jnp.where(first_row, 0.0, weight)
                if r == tiles - 1:
                    held_ref[1, s : s + 1, :] = weight[SUBLANES - 1 :]
                    weight = jnp.where(last_row, 0.0, weight)
                emitted = colors(value, tile_colors)
                if 0 < s < slices - 1:
                    grad_depth = (values[s + 1] - values[s - 1]).astype(jnp.float32)
                    weight = weight * shade(grad_depth, facing, squares)
                    for c in range(3):
                        sums[c] = sums[c] + emitted[c] * weight
                else:
                    end = int(s > 0)
                    face_ref[end, rows, here] = facing
                    square_ref[end, rows, here] = squares
                    weight = weight * (1.0 / 255.0)
                    for c in range(3):
                        lit_ref[end, c, rows, here] = emitted[c] * weight
            for c in range(3):
                base_ref[c, rows, here] = sums[c] * (1.0 / 255.0)
            base_ref[3, rows, here] = 1.0 - remaining

        for q, (edge, inner) in enumerate(((0, 1), (height - 1, height - 2))):
            value = volume_ref[0, :, edge, here]
            behind = pltpu.roll(jnp.where(back, 0, value), 1, 0)
            ahead = pltpu.roll(jnp.where(front, 0, value), slices - 1, 0)
            grad_ref[q, 0, :, here] = (ahead - behind).astype(jnp.float32)
            grad_ref[q, 1, :, here] = volume_ref[0, :, inner, here].astype(jnp.float32)
            grad_ref[q, 2, :, here] = across(
                value, volume_ref[0, :, edge, left], volume_ref[0, :, edge, right], strip_first_lane, strip_last_lane
            )
            weight = held_ref[q] * (1.0 / 255.0)
            emitted = colors(value, strip_colors)
            for c in range(3):
                strip_ref[q, c, :, here] = emitted[c] * weight
        return carry

    lax.fori_loop(0, chunks, chunk, 0)


def march_interior(volume, color_map, alpha_map, depth_count):
    _, slices, height, columns = volume.shape
    opacity_scale = OPACITY / (255.0 * slices * depth_count)
    shapes = [
        (4, height, columns),
        (2, height, columns),
        (2, height, columns),
        (2, 3, height, columns),
        (2, 3, slices, columns),
        (2, 3, slices, columns),
    ]
    voxels = slices * height * columns
    return pl.pallas_call(
        functools.partial(interior_kernel, opacity_scale),
        in_specs=[WHOLE] * 3,
        out_specs=[WHOLE] * len(shapes),
        out_shape=[jax.ShapeDtypeStruct(shape, jnp.float32) for shape in shapes],
        scratch_shapes=[pltpu.VMEM((2, slices, LANES), jnp.float32)],
        compiler_params=pltpu.CompilerParams(vmem_limit_bytes=24 * 1024 * 1024),
        cost_estimate=pl.CostEstimate(flops=voxels * 80, bytes_accessed=voxels * 20, transcendentals=voxels),
    )(volume, color_map, alpha_map.reshape(1, -1))


def edge_kernel(
    share, volume_ref, base_ref, face_ref, square_ref, lit_ref, grad_ref, strip_ref, rows_near_ref, rows_far_ref, far_ref, near_ref, out_ref
):
    _, slices, height, columns = volume_ref.shape
    tiles = height // SUBLANES
    tile = (SUBLANES, LANES)
    row = lax.broadcasted_iota(jnp.int32, tile, 0)
    first_row, last_row = row == 0, row == SUBLANES - 1
    level = lax.broadcasted_iota(jnp.int32, (slices, LANES), 0)
    front, back = level == 0, level == slices - 1
    odd, odd_row = parity("depth") == 1, parity("rows") == 1
    front_end, back_end = ends("depth")
    top_end, bottom_end = ends("rows")

    def chunk(j, carry):
        here = pl.ds(pl.multiple_of(j * LANES, LANES), LANES)
        rows_near = rows_near_ref[:, here].astype(jnp.float32)
        rows_far = rows_far_ref[:, here].astype(jnp.float32)
        above = jnp.where(top_end, 0.0, jnp.where(odd_row, rows_near, rows_far))
        below = jnp.where(bottom_end, 0.0, jnp.where(odd_row, rows_far, rows_near))
        far = far_ref[:, here].astype(jnp.float32)
        near = near_ref[:, here].astype(jnp.float32)
        before = jnp.where(front_end, 0.0, jnp.where(odd, near, far))
        after = jnp.where(back_end, 0.0, jnp.where(odd, far, near))
        extra = []
        for q, edge in enumerate((0, height - 1)):
            inner = grad_ref[q, 1, :, here]
            grad_rows = below - inner if q else inner - above
            grad_cols = grad_ref[q, 2, :, here]
            grad_depth = grad_ref[q, 0, :, here] + jnp.where(
                back, after[edge : edge + 1], jnp.where(front, -before[edge : edge + 1], 0.0)
            )
            shading = shade(
                grad_depth,
                LIGHT_ROWS * grad_rows + LIGHT_COLS * grad_cols,
                grad_rows * grad_rows + grad_cols * grad_cols,
            )
            extra.append([jnp.sum(strip_ref[q, c, :, here] * shading, axis=0, keepdims=True) for c in range(3)])
        for r in range(tiles):
            rows = slice(r * SUBLANES, (r + 1) * SUBLANES)
            planes = [base_ref[c, rows, here] for c in range(4)]
            for end in range(2):
                if end:
                    grad_depth = after[rows] - volume_ref[0, slices - 2, rows, here].astype(jnp.float32)
                else:
                    grad_depth = volume_ref[0, 1, rows, here].astype(jnp.float32) - before[rows]
                shading = shade(grad_depth, face_ref[end, rows, here], square_ref[end, rows, here])
                for c in range(3):
                    planes[c] = planes[c] + lit_ref[end, c, rows, here] * shading
            for c in range(3):
                if r == 0:
                    planes[c] = planes[c] + jnp.where(first_row, extra[0][c], 0.0)
                if r == tiles - 1:
                    planes[c] = planes[c] + jnp.where(last_row, extra[1][c], 0.0)
            for first in range(0, SUBLANES, share):
                block = jnp.concatenate([plane[first : first + share] for plane in planes], axis=0)
                out_ref[(r * SUBLANES + first) // share, :, here] = block.astype(jnp.bfloat16)
        return carry

    lax.fori_loop(0, columns // LANES, chunk, 0)


def add_edges(volume, interior, halos, depth_count):
    _, slices, height, columns = volume.shape
    share = height // depth_count
    return pl.pallas_call(
        functools.partial(edge_kernel, share),
        in_specs=[WHOLE] * 11,
        out_specs=WHOLE,
        out_shape=jax.ShapeDtypeStruct((depth_count, 4 * share, columns), jnp.bfloat16),
        compiler_params=pltpu.CompilerParams(vmem_limit_bytes=24 * 1024 * 1024),
    )(volume, *interior, *halos)


def finish_kernel(parts_ref, out_ref):
    count = parts_ref.shape[0]
    _, share, columns = out_ref.shape
    remaining = jnp.ones((share, columns), jnp.float32)
    sums = [jnp.zeros((share, columns), jnp.float32) for _ in range(3)]
    for k in range(count):
        part = parts_ref[k].astype(jnp.float32)
        for c in range(3):
            sums[c] = sums[c] + remaining * part[c * share : (c + 1) * share]
        remaining = remaining - remaining * part[3 * share :]
    for c in range(3):
        out_ref[c] = sums[c]
    out_ref[3] = 1.0 - remaining


def finish(parts, share):
    columns = parts.shape[2]
    return pl.pallas_call(
        finish_kernel,
        in_specs=[WHOLE],
        out_specs=WHOLE,
        out_shape=jax.ShapeDtypeStruct((4, share, columns), jnp.float32),
        compiler_params=pltpu.CompilerParams(vmem_limit_bytes=4 * 1024 * 1024),
    )(parts)


def swapped(values, axis, start):
    depth_count, row_count = lax.axis_size("depth"), lax.axis_size("rows")
    size = lax.axis_size(axis)
    perm = []
    for d in range(depth_count):
        for r in range(row_count):
            i = d if axis == "depth" else r
            j = i + 1 if i % 2 == start else i - 1
            if 0 <= j < size:
                e, q = (j, r) if axis == "depth" else (d, j)
            elif axis == "depth":
                e, q = (size - 1 - d, r)
            else:
                e, q = (d ^ 1, r)
            perm.append((d * row_count + r, e * row_count + q))
    return lax.ppermute(values, ("depth", "rows"), perm)


def body(volume, color_map, alpha_map):
    depth_count = lax.axis_size("depth")
    share = volume.shape[2] // depth_count
    rows_far, rows_near, far, near = cut_edges(volume)
    rows_far = swapped(rows_far, "rows", 1)
    rows_near = swapped(rows_near, "rows", 0)
    far = swapped(far, "depth", 1)
    near = swapped(near, "depth", 0)
    interior = march_interior(volume, color_map, alpha_map, depth_count)
    parts = add_edges(volume, interior, (rows_near, rows_far, far, near), depth_count)
    parts = lax.all_to_all(parts, "depth", 0, 0, tiled=True)
    return finish(parts, share)


def solution(mesh):
    in_specs = (P(None, "depth", "rows", None), P(), P())
    out_specs = P(None, ("rows", "depth"), None)
    return jax.shard_map(body, mesh=mesh, in_specs=in_specs, out_specs=out_specs, check_vma=False)
```

```python
import functools

import jax
import jax.numpy as jnp
from jax import lax
from jax.experimental import pallas as pl
from jax.experimental.pallas import tpu as pltpu
from jax.sharding import PartitionSpec as P

AMBIENT = 0.3
DIFFUSE = 0.7
LIGHT_DEPTH = 0.48 * DIFFUSE
LIGHT_ROWS = 0.6 * DIFFUSE
LIGHT_COLS = 0.64 * DIFFUSE
OPACITY = 4.0
LANES = 128
SUBLANES = 8
WHOLE = pl.BlockSpec(memory_space=pltpu.VMEM)


def parity(axis):
    return lax.axis_index(axis) % 2


def ends(axis):
    position = lax.axis_index(axis)
    return position == 0, position == lax.axis_size(axis) - 1


def edges_kernel(volume_ref, rows_far_out, rows_near_out, far_out, near_out, strip_ref, plane_ref, sems):
    _, slices, height, _ = volume_ref.shape
    odd, odd_row = parity("depth"), parity("rows")
    last_tile = height // SUBLANES - 1

    def tile(i):
        return pl.ds(pl.multiple_of(i * SUBLANES, SUBLANES), SUBLANES)

    copies = [
        pltpu.make_async_copy(volume_ref.at[0, :, tile((1 - odd_row) * last_tile)], strip_ref.at[0], sems.at[0]),
        pltpu.make_async_copy(volume_ref.at[0, :, tile(odd_row * last_tile)], strip_ref.at[1], sems.at[1]),
        pltpu.make_async_copy(volume_ref.at[0, odd * (slices - 1)], plane_ref.at[0], sems.at[2]),
        pltpu.make_async_copy(volume_ref.at[0, (1 - odd) * (slices - 1)], plane_ref.at[1], sems.at[3]),
    ]
    for copy in copies:
        copy.start()

    def narrow(values):
        return values.astype(jnp.float32).astype(jnp.bfloat16)

    copies[0].wait()
    rows_near_out[...] = narrow(jnp.where(odd_row == 1, strip_ref[0, :, 0, :], strip_ref[0, :, SUBLANES - 1, :]))
    copies[1].wait()
    rows_far_out[...] = narrow(jnp.where(odd_row == 1, strip_ref[1, :, SUBLANES - 1, :], strip_ref[1, :, 0, :]))
    copies[2].wait()
    far_out[...] = narrow(plane_ref[0])
    copies[3].wait()
    near_out[...] = narrow(plane_ref[1])


def cut_edges(volume):
    _, slices, height, columns = volume.shape
    plane = jax.ShapeDtypeStruct((height, columns), jnp.bfloat16)
    strip = jax.ShapeDtypeStruct((slices, columns), jnp.bfloat16)
    return pl.pallas_call(
        edges_kernel,
        in_specs=[pl.BlockSpec(memory_space=pl.ANY)],
        out_specs=[WHOLE] * 4,
        out_shape=[strip, strip, plane, plane],
        scratch_shapes=[
            pltpu.VMEM((2, slices, SUBLANES, columns), jnp.int32),
            pltpu.VMEM((2, height, columns), jnp.int32),
            pltpu.SemaphoreType.DMA((4,)),
        ],
        compiler_params=pltpu.CompilerParams(vmem_limit_bytes=52 * 1024 * 1024),
    )(volume)


def pick(entries, places):
    dims = lax.GatherDimensionNumbers(
        offset_dims=(),
        collapsed_slice_dims=(1,),
        start_index_map=(1,),
        operand_batching_dims=(0,),
        start_indices_batching_dims=(0,),
    )
    return lax.gather(entries, places[..., None], dims, (1, 1), mode=lax.GatherScatterMode.PROMISE_IN_BOUNDS)


def shade(grad_depth, facing, squares):
    facing = facing + LIGHT_DEPTH * grad_depth
    squares = squares + grad_depth * grad_depth
    return AMBIENT + jnp.abs(facing) * lax.rsqrt(jnp.maximum(squares, 4.0))


def interior_kernel(
    opacity_scale,
    volume_ref,
    color_ref,
    alpha_ref,
    base_ref,
    face_ref,
    square_ref,
    lit_ref,
    grad_ref,
    strip_ref,
    pair_ref,
    held_ref,
):
    _, slices, height, columns = volume_ref.shape
    tiles = height // SUBLANES
    chunks = columns // LANES
    tile = (SUBLANES, LANES)
    strip = (slices, LANES)

    packed = color_ref[0:1, :] + color_ref[1:2, :] * 256 + color_ref[2:3, :] * 65536
    color_low, color_high = packed[:, :LANES], packed[:, LANES:]
    alpha_both = alpha_ref[0:1, :LANES] + alpha_ref[0:1, LANES:] * 256

    def colors(value, tables):
        low, high = tables
        place = value & (LANES - 1)
        color = jnp.where(value < LANES, pick(low, place), pick(high, place))
        parts = (color & 255, lax.shift_right_logical(color, 8) & 255, lax.shift_right_logical(color, 16))
        return [part.astype(jnp.float32) for part in parts]

    def opacity(level, table):
        entry = pick(table, level & (LANES - 1))
        entry = lax.shift_right_logical(entry, lax.shift_right_logical(level & LANES, 4)) & 255
        return entry.astype(jnp.float32) * opacity_scale

    tile_colors = [jnp.broadcast_to(t, tile) for t in (color_low, color_high)]
    tile_alpha = jnp.broadcast_to(alpha_both, tile)
    strip_colors = [jnp.broadcast_to(t, strip) for t in (color_low, color_high)]

    def masks(shape):
        lane = lax.broadcasted_iota(jnp.int32, shape, 1)
        row = lax.broadcasted_iota(jnp.int32, shape, 0)
        return lane == 0, lane == LANES - 1, row == 0, row == shape[0] - 1

    first_lane, last_lane, first_row, last_row = masks(tile)
    strip_first_lane, strip_last_lane, front, back = masks(strip)

    pairs = slices // 2
    top = SUBLANES

    def clear(j, carry):
        pair_ref[j] = jnp.zeros(pair_ref.shape[1:], jnp.int32)
        return carry

    clear(0, 0)
    clear(chunks + 1, 0)
    margin = jnp.zeros((pairs, SUBLANES, LANES), jnp.int32)

    def pack(j, carry):
        here = pl.ds(pl.multiple_of(j * LANES, LANES), LANES)
        pair_ref[j + 1, :, :top] = margin
        pair_ref[j + 1, :, top + height :] = margin
        for p in range(pairs):
            pair_ref[j + 1, p, top : top + height] = volume_ref[0, p, :, here] + lax.shift_left(
                volume_ref[0, p + pairs, :, here], 16
            )
        return carry

    lax.fori_loop(0, chunks, pack, 0)

    def split(difference):
        low = lax.shift_right_arithmetic(lax.shift_left(difference, 16), 16)
        high = lax.shift_right_arithmetic(difference + 32768, 16)
        return low.astype(jnp.float32), high.astype(jnp.float32)

    def across(left_value, value, right_value, first, last):
        west = pltpu.roll(jnp.where(last, left_value, value), 1, 1)
        east = pltpu.roll(jnp.where(first, right_value, value), LANES - 1, 1)
        return split(east - west)

    def chunk(j, carry):
        here = pl.ds(pl.multiple_of(j * LANES, LANES), LANES)

        for r in range(tiles):
            rows = slice(r * SUBLANES, (r + 1) * SUBLANES)
            values = [volume_ref[0, s, rows, here] for s in range(slices)]

            def words(c, p, offset=0):
                return pair_ref[c, p, top + r * SUBLANES + offset : top + (r + 1) * SUBLANES + offset, :]

            down, right = [], []
            for p in range(pairs):
                down.append(split(words(j + 1, p, 1) - words(j + 1, p, -1)))
                right.append(across(words(j, p), words(j + 1, p), words(j + 2, p), first_lane, last_lane))
            remaining = jnp.ones(tile, jnp.float32)
            sums = [jnp.zeros(tile, jnp.float32) for _ in range(3)]
            for s in range(slices):
                value = values[s]
                grad_rows = down[s % pairs][s // pairs]
                grad_cols = right[s % pairs][s // pairs]
                squares = grad_rows * grad_rows + grad_cols * grad_cols
                facing = LIGHT_ROWS * grad_rows + LIGHT_COLS * grad_cols
                weight = remaining * opacity(volume_ref[1, s, rows, here], tile_alpha)
                remaining = remaining - weight
                if r == 0:
                    held_ref[0, s : s + 1, :] = weight[:1]
                    weight = jnp.where(first_row, 0.0, weight)
                if r == tiles - 1:
                    held_ref[1, s : s + 1, :] = weight[SUBLANES - 1 :]
                    weight = jnp.where(last_row, 0.0, weight)
                emitted = colors(value, tile_colors)
                if 0 < s < slices - 1:
                    grad_depth = (values[s + 1] - values[s - 1]).astype(jnp.float32)
                    weight = weight * shade(grad_depth, facing, squares)
                    for c in range(3):
                        sums[c] = sums[c] + emitted[c] * weight
                else:
                    end = int(s > 0)
                    face_ref[end, rows, here] = facing
                    square_ref[end, rows, here] = squares
                    weight = weight * (1.0 / 255.0)
                    for c in range(3):
                        lit_ref[end, c, rows, here] = emitted[c] * weight
            for c in range(3):
                base_ref[c, rows, here] = sums[c] * (1.0 / 255.0)
            base_ref[3, rows, here] = 1.0 - remaining

        for q, (edge, inner) in enumerate(((0, 1), (height - 1, height - 2))):
            value = volume_ref[0, :, edge, here]
            behind = pltpu.roll(jnp.where(back, 0, value), 1, 0)
            ahead = pltpu.roll(jnp.where(front, 0, value), slices - 1, 0)
            grad_ref[q, 0, :, here] = (ahead - behind).astype(jnp.float32)
            grad_ref[q, 1, :, here] = volume_ref[0, :, inner, here].astype(jnp.float32)
            word = pair_ref[j + 1, :, top + edge, :]
            low, high = across(
                pair_ref[j, :, top + edge, :],
                word,
                pair_ref[j + 2, :, top + edge, :],
                strip_first_lane[:pairs],
                strip_last_lane[:pairs],
            )
            grad_ref[q, 2, :pairs, here] = low
            grad_ref[q, 2, pairs:, here] = high
            weight = held_ref[q] * (1.0 / 255.0)
            emitted = colors(value, strip_colors)
            for c in range(3):
                strip_ref[q, c, :, here] = emitted[c] * weight
        return carry

    lax.fori_loop(0, chunks, chunk, 0)


def march_interior(volume, color_map, alpha_map, depth_count):
    _, slices, height, columns = volume.shape
    opacity_scale = OPACITY / (255.0 * slices * depth_count)
    shapes = [
        (4, height, columns),
        (2, height, columns),
        (2, height, columns),
        (2, 3, height, columns),
        (2, 3, slices, columns),
        (2, 3, slices, columns),
    ]
    voxels = slices * height * columns
    return pl.pallas_call(
        functools.partial(interior_kernel, opacity_scale),
        in_specs=[WHOLE] * 3,
        out_specs=[WHOLE] * len(shapes),
        out_shape=[jax.ShapeDtypeStruct(shape, jnp.float32) for shape in shapes],
        scratch_shapes=[
            pltpu.VMEM((columns // LANES + 2, slices // 2, height + 2 * SUBLANES, LANES), jnp.int32),
            pltpu.VMEM((2, slices, LANES), jnp.float32),
        ],
        compiler_params=pltpu.CompilerParams(vmem_limit_bytes=24 * 1024 * 1024),
        cost_estimate=pl.CostEstimate(flops=voxels * 80, bytes_accessed=voxels * 20, transcendentals=voxels),
    )(volume, color_map, alpha_map.reshape(1, -1))


def edge_kernel(
    share, volume_ref, base_ref, face_ref, square_ref, lit_ref, grad_ref, strip_ref, rows_near_ref, rows_far_ref, far_ref, near_ref, out_ref
):
    _, slices, height, columns = volume_ref.shape
    tiles = height // SUBLANES
    tile = (SUBLANES, LANES)
    row = lax.broadcasted_iota(jnp.int32, tile, 0)
    first_row, last_row = row == 0, row == SUBLANES - 1
    level = lax.broadcasted_iota(jnp.int32, (slices, LANES), 0)
    front, back = level == 0, level == slices - 1
    odd, odd_row = parity("depth") == 1, parity("rows") == 1
    front_end, back_end = ends("depth")
    top_end, bottom_end = ends("rows")

    def chunk(j, carry):
        here = pl.ds(pl.multiple_of(j * LANES, LANES), LANES)
        rows_near = rows_near_ref[:, here].astype(jnp.float32)
        rows_far = rows_far_ref[:, here].astype(jnp.float32)
        above = jnp.where(top_end, 0.0, jnp.where(odd_row, rows_near, rows_far))
        below = jnp.where(bottom_end, 0.0, jnp.where(odd_row, rows_far, rows_near))
        far = far_ref[:, here].astype(jnp.float32)
        near = near_ref[:, here].astype(jnp.float32)
        before = jnp.where(front_end, 0.0, jnp.where(odd, near, far))
        after = jnp.where(back_end, 0.0, jnp.where(odd, far, near))
        extra = []
        for q, edge in enumerate((0, height - 1)):
            inner = grad_ref[q, 1, :, here]
            grad_rows = below - inner if q else inner - above
            grad_cols = grad_ref[q, 2, :, here]
            grad_depth = grad_ref[q, 0, :, here] + jnp.where(
                back, after[edge : edge + 1], jnp.where(front, -before[edge : edge + 1], 0.0)
            )
            shading = shade(
                grad_depth,
                LIGHT_ROWS * grad_rows + LIGHT_COLS * grad_cols,
                grad_rows * grad_rows + grad_cols * grad_cols,
            )
            extra.append([jnp.sum(strip_ref[q, c, :, here] * shading, axis=0, keepdims=True) for c in range(3)])
        for r in range(tiles):
            rows = slice(r * SUBLANES, (r + 1) * SUBLANES)
            planes = [base_ref[c, rows, here] for c in range(4)]
            for end in range(2):
                if end:
                    grad_depth = after[rows] - volume_ref[0, slices - 2, rows, here].astype(jnp.float32)
                else:
                    grad_depth = volume_ref[0, 1, rows, here].astype(jnp.float32) - before[rows]
                shading = shade(grad_depth, face_ref[end, rows, here], square_ref[end, rows, here])
                for c in range(3):
                    planes[c] = planes[c] + lit_ref[end, c, rows, here] * shading
            for c in range(3):
                if r == 0:
                    planes[c] = planes[c] + jnp.where(first_row, extra[0][c], 0.0)
                if r == tiles - 1:
                    planes[c] = planes[c] + jnp.where(last_row, extra[1][c], 0.0)
            for first in range(0, SUBLANES, share):
                block = jnp.concatenate([plane[first : first + share] for plane in planes], axis=0)
                out_ref[(r * SUBLANES + first) // share, :, here] = block.astype(jnp.bfloat16)
        return carry

    lax.fori_loop(0, columns // LANES, chunk, 0)


def add_edges(volume, interior, halos, depth_count):
    _, slices, height, columns = volume.shape
    share = height // depth_count
    return pl.pallas_call(
        functools.partial(edge_kernel, share),
        in_specs=[WHOLE] * 11,
        out_specs=WHOLE,
        out_shape=jax.ShapeDtypeStruct((depth_count, 4 * share, columns), jnp.bfloat16),
        compiler_params=pltpu.CompilerParams(vmem_limit_bytes=24 * 1024 * 1024),
    )(volume, *interior, *halos)


def finish_kernel(parts_ref, out_ref):
    count = parts_ref.shape[0]
    _, share, columns = out_ref.shape
    remaining = jnp.ones((share, columns), jnp.float32)
    sums = [jnp.zeros((share, columns), jnp.float32) for _ in range(3)]
    for k in range(count):
        part = parts_ref[k].astype(jnp.float32)
        for c in range(3):
            sums[c] = sums[c] + remaining * part[c * share : (c + 1) * share]
        remaining = remaining - remaining * part[3 * share :]
    for c in range(3):
        out_ref[c] = sums[c]
    out_ref[3] = 1.0 - remaining


def finish(parts, share):
    columns = parts.shape[2]
    return pl.pallas_call(
        finish_kernel,
        in_specs=[WHOLE],
        out_specs=WHOLE,
        out_shape=jax.ShapeDtypeStruct((4, share, columns), jnp.float32),
        compiler_params=pltpu.CompilerParams(vmem_limit_bytes=4 * 1024 * 1024),
    )(parts)


def swapped(values, axis, start):
    depth_count, row_count = lax.axis_size("depth"), lax.axis_size("rows")
    size = lax.axis_size(axis)
    perm = []
    for d in range(depth_count):
        for r in range(row_count):
            i = d if axis == "depth" else r
            j = i + 1 if i % 2 == start else i - 1
            if 0 <= j < size:
                e, q = (j, r) if axis == "depth" else (d, j)
            elif axis == "depth":
                e, q = (size - 1 - d, r)
            else:
                e, q = (d ^ 1, r)
            perm.append((d * row_count + r, e * row_count + q))
    return lax.ppermute(values, ("depth", "rows"), perm)


def body(volume, color_map, alpha_map):
    depth_count = lax.axis_size("depth")
    share = volume.shape[2] // depth_count
    rows_far, rows_near, far, near = cut_edges(volume)
    rows_far = swapped(rows_far, "rows", 1)
    rows_near = swapped(rows_near, "rows", 0)
    far = swapped(far, "depth", 1)
    near = swapped(near, "depth", 0)
    interior = march_interior(volume, color_map, alpha_map, depth_count)
    parts = add_edges(volume, interior, (rows_near, rows_far, far, near), depth_count)
    parts = lax.all_to_all(parts, "depth", 0, 0, tiled=True)
    return finish(parts, share)


def solution(mesh):
    in_specs = (P(None, "depth", "rows", None), P(), P())
    out_specs = P(None, ("rows", "depth"), None)
    return jax.shard_map(body, mesh=mesh, in_specs=in_specs, out_specs=out_specs, check_vma=False)
```

```python
import functools

import jax
import jax.numpy as jnp
from jax import lax
from jax.experimental import pallas as pl
from jax.experimental.pallas import tpu as pltpu
from jax.sharding import PartitionSpec as P

AMBIENT = 0.3
DIFFUSE = 0.7
LIGHT_DEPTH = 0.48 * DIFFUSE
LIGHT_ROWS = 0.6 * DIFFUSE
LIGHT_COLS = 0.64 * DIFFUSE
OPACITY = 4.0
LANES = 128
SUBLANES = 8
WHOLE = pl.BlockSpec(memory_space=pltpu.VMEM)


def parity(axis):
    return lax.axis_index(axis) % 2


def ends(axis):
    position = lax.axis_index(axis)
    return position == 0, position == lax.axis_size(axis) - 1


def edges_kernel(volume_ref, rows_far_out, rows_near_out, far_out, near_out, strip_ref, plane_ref, sems):
    _, slices, height, _ = volume_ref.shape
    odd, odd_row = parity("depth"), parity("rows")
    last_tile = height // SUBLANES - 1

    def tile(i):
        return pl.ds(pl.multiple_of(i * SUBLANES, SUBLANES), SUBLANES)

    copies = [
        pltpu.make_async_copy(volume_ref.at[0, :, tile((1 - odd_row) * last_tile)], strip_ref.at[0], sems.at[0]),
        pltpu.make_async_copy(volume_ref.at[0, :, tile(odd_row * last_tile)], strip_ref.at[1], sems.at[1]),
        pltpu.make_async_copy(volume_ref.at[0, odd * (slices - 1)], plane_ref.at[0], sems.at[2]),
        pltpu.make_async_copy(volume_ref.at[0, (1 - odd) * (slices - 1)], plane_ref.at[1], sems.at[3]),
    ]
    for copy in copies:
        copy.start()

    def narrow(values):
        return values.astype(jnp.float32).astype(jnp.bfloat16)

    copies[0].wait()
    rows_near_out[...] = narrow(jnp.where(odd_row == 1, strip_ref[0, :, 0, :], strip_ref[0, :, SUBLANES - 1, :]))
    copies[1].wait()
    rows_far_out[...] = narrow(jnp.where(odd_row == 1, strip_ref[1, :, SUBLANES - 1, :], strip_ref[1, :, 0, :]))
    copies[2].wait()
    far_out[...] = narrow(plane_ref[0])
    copies[3].wait()
    near_out[...] = narrow(plane_ref[1])


def cut_edges(volume):
    _, slices, height, columns = volume.shape
    plane = jax.ShapeDtypeStruct((height, columns), jnp.bfloat16)
    strip = jax.ShapeDtypeStruct((slices, columns), jnp.bfloat16)
    return pl.pallas_call(
        edges_kernel,
        in_specs=[pl.BlockSpec(memory_space=pl.ANY)],
        out_specs=[WHOLE] * 4,
        out_shape=[strip, strip, plane, plane],
        scratch_shapes=[
            pltpu.VMEM((2, slices, SUBLANES, columns), jnp.int32),
            pltpu.VMEM((2, height, columns), jnp.int32),
            pltpu.SemaphoreType.DMA((4,)),
        ],
        compiler_params=pltpu.CompilerParams(vmem_limit_bytes=52 * 1024 * 1024),
    )(volume)


def pick(entries, places):
    dims = lax.GatherDimensionNumbers(
        offset_dims=(),
        collapsed_slice_dims=(1,),
        start_index_map=(1,),
        operand_batching_dims=(0,),
        start_indices_batching_dims=(0,),
    )
    return lax.gather(entries, places[..., None], dims, (1, 1), mode=lax.GatherScatterMode.PROMISE_IN_BOUNDS)


def shade(grad_depth, facing, squares):
    facing = facing + LIGHT_DEPTH * grad_depth
    squares = squares + grad_depth * grad_depth
    return AMBIENT + jnp.abs(facing) * lax.rsqrt(jnp.maximum(squares, 4.0))


def interior_kernel(
    opacity_scale,
    volume_ref,
    color_ref,
    alpha_ref,
    base_ref,
    face_ref,
    square_ref,
    lit_ref,
    grad_ref,
    strip_ref,
    pair_ref,
    held_ref,
):
    _, slices, height, columns = volume_ref.shape
    tiles = height // SUBLANES
    chunks = columns // LANES
    tile = (SUBLANES, LANES)
    strip = (slices, LANES)

    packed = color_ref[0:1, :] + color_ref[1:2, :] * 256 + color_ref[2:3, :] * 65536
    color_low, color_high = packed[:, :LANES], packed[:, LANES:]
    alpha_both = alpha_ref[0:1, :LANES] + alpha_ref[0:1, LANES:] * 256

    def colors(value, tables):
        low, high = tables
        place = value & (LANES - 1)
        color = jnp.where(value < LANES, pick(low, place), pick(high, place))
        parts = (color & 255, lax.shift_right_logical(color, 8) & 255, lax.shift_right_logical(color, 16))
        return [part.astype(jnp.float32) for part in parts]

    def opacity(level, table):
        entry = pick(table, level & (LANES - 1))
        entry = lax.shift_right_logical(entry, lax.shift_right_logical(level & LANES, 4)) & 255
        return entry.astype(jnp.float32) * opacity_scale

    tile_colors = [jnp.broadcast_to(t, tile) for t in (color_low, color_high)]
    tile_alpha = jnp.broadcast_to(alpha_both, tile)
    strip_colors = [jnp.broadcast_to(t, strip) for t in (color_low, color_high)]

    def masks(shape):
        lane = lax.broadcasted_iota(jnp.int32, shape, 1)
        row = lax.broadcasted_iota(jnp.int32, shape, 0)
        return lane == 0, lane == LANES - 1, row == 0, row == shape[0] - 1

    first_lane, last_lane, first_row, last_row = masks(tile)
    strip_first_lane, strip_last_lane, front, back = masks(strip)

    pairs = slices // 2
    top = SUBLANES

    def clear(j, carry):
        pair_ref[j] = jnp.zeros(pair_ref.shape[1:], jnp.int32)
        return carry

    clear(0, 0)
    clear(chunks + 1, 0)
    margin = jnp.zeros((pairs, SUBLANES, LANES), jnp.int32)

    def pack(j, carry):
        here = pl.ds(pl.multiple_of(j * LANES, LANES), LANES)
        pair_ref[j + 1, :, :top] = margin
        pair_ref[j + 1, :, top + height :] = margin
        for p in range(pairs):
            pair_ref[j + 1, p, top : top + height] = volume_ref[0, p, :, here] + lax.shift_left(
                volume_ref[0, p + pairs, :, here], 16
            )
        return carry

    lax.fori_loop(0, chunks, pack, 0)

    def split(difference):
        low = lax.shift_right_arithmetic(lax.shift_left(difference, 16), 16)
        high = lax.shift_right_arithmetic(difference + 32768, 16)
        return low.astype(jnp.float32), high.astype(jnp.float32)

    def across(left_value, value, right_value, first, last):
        west = pltpu.roll(jnp.where(last, left_value, value), 1, 1)
        east = pltpu.roll(jnp.where(first, right_value, value), LANES - 1, 1)
        return split(east - west)

    def chunk(j, carry):
        here = pl.ds(pl.multiple_of(j * LANES, LANES), LANES)

        for r in range(tiles):
            rows = slice(r * SUBLANES, (r + 1) * SUBLANES)
            values = [volume_ref[0, s, rows, here] for s in range(slices)]

            def words(c, p, offset=0):
                return pair_ref[c, p, top + r * SUBLANES + offset : top + (r + 1) * SUBLANES + offset, :]

            down, right = [], []
            for p in range(pairs):
                down.append(split(words(j + 1, p, 1) - words(j + 1, p, -1)))
                right.append(across(words(j, p), words(j + 1, p), words(j + 2, p), first_lane, last_lane))
            remaining = jnp.ones(tile, jnp.float32)
            sums = [jnp.zeros(tile, jnp.float32) for _ in range(3)]
            for s in range(slices):
                value = values[s]
                grad_rows = down[s % pairs][s // pairs]
                grad_cols = right[s % pairs][s // pairs]
                squares = grad_rows * grad_rows + grad_cols * grad_cols
                facing = LIGHT_ROWS * grad_rows + LIGHT_COLS * grad_cols
                weight = remaining * opacity(volume_ref[1, s, rows, here], tile_alpha)
                remaining = remaining - weight
                if r == 0:
                    held_ref[0, s : s + 1, :] = weight[:1]
                    weight = jnp.where(first_row, 0.0, weight)
                if r == tiles - 1:
                    held_ref[1, s : s + 1, :] = weight[SUBLANES - 1 :]
                    weight = jnp.where(last_row, 0.0, weight)
                emitted = colors(value, tile_colors)
                if 0 < s < slices - 1:
                    grad_depth = (values[s + 1] - values[s - 1]).astype(jnp.float32)
                    weight = weight * shade(grad_depth, facing, squares)
                    for c in range(3):
                        sums[c] = sums[c] + emitted[c] * weight
                else:
                    end = int(s > 0)
                    face_ref[end, rows, here] = facing
                    square_ref[end, rows, here] = squares
                    weight = weight * (1.0 / 255.0)
                    for c in range(3):
                        lit_ref[end, c, rows, here] = emitted[c] * weight
            for c in range(3):
                base_ref[c, rows, here] = sums[c] * (1.0 / 255.0)
            base_ref[3, rows, here] = 1.0 - remaining

        for q, (edge, inner) in enumerate(((0, 1), (height - 1, height - 2))):
            value = volume_ref[0, :, edge, here]
            behind = pltpu.roll(jnp.where(back, 0, value), 1, 0)
            ahead = pltpu.roll(jnp.where(front, 0, value), slices - 1, 0)
            grad_ref[q, 0, :, here] = (ahead - behind).astype(jnp.float32)
            grad_ref[q, 1, :, here] = volume_ref[0, :, inner, here].astype(jnp.float32)
            word = pair_ref[j + 1, :, top + edge, :]
            low, high = across(
                pair_ref[j, :, top + edge, :],
                word,
                pair_ref[j + 2, :, top + edge, :],
                strip_first_lane[:pairs],
                strip_last_lane[:pairs],
            )
            grad_ref[q, 2, :pairs, here] = low
            grad_ref[q, 2, pairs:, here] = high
            weight = held_ref[q] * (1.0 / 255.0)
            emitted = colors(value, strip_colors)
            for c in range(3):
                strip_ref[q, c, :, here] = emitted[c] * weight
        return carry

    lax.fori_loop(0, chunks, chunk, 0)


def march_interior(volume, color_map, alpha_map, depth_count):
    _, slices, height, columns = volume.shape
    opacity_scale = OPACITY / (255.0 * slices * depth_count)
    shapes = [
        (4, height, columns),
        (2, height, columns),
        (2, height, columns),
        (2, 3, height, columns),
        (2, 3, slices, columns),
        (2, 3, slices, columns),
    ]
    voxels = slices * height * columns
    return pl.pallas_call(
        functools.partial(interior_kernel, opacity_scale),
        in_specs=[WHOLE] * 3,
        out_specs=[WHOLE] * len(shapes),
        out_shape=[jax.ShapeDtypeStruct(shape, jnp.float32) for shape in shapes],
        scratch_shapes=[
            pltpu.VMEM((columns // LANES + 2, slices // 2, height + 2 * SUBLANES, LANES), jnp.int32),
            pltpu.VMEM((2, slices, LANES), jnp.float32),
        ],
        compiler_params=pltpu.CompilerParams(vmem_limit_bytes=24 * 1024 * 1024),
        cost_estimate=pl.CostEstimate(flops=voxels * 80, bytes_accessed=voxels * 20, transcendentals=voxels),
    )(volume, color_map, alpha_map.reshape(1, -1))


def edge_kernel(
    share, volume_ref, base_ref, face_ref, square_ref, lit_ref, grad_ref, strip_ref, rows_near_ref, rows_far_ref, far_ref, near_ref, *out_refs
):
    _, slices, height, columns = volume_ref.shape
    tiles = height // SUBLANES
    tile = (SUBLANES, LANES)
    row = lax.broadcasted_iota(jnp.int32, tile, 0)
    first_row, last_row = row == 0, row == SUBLANES - 1
    level = lax.broadcasted_iota(jnp.int32, (slices, LANES), 0)
    front, back = level == 0, level == slices - 1
    odd, odd_row = parity("depth") == 1, parity("rows") == 1
    front_end, back_end = ends("depth")
    top_end, bottom_end = ends("rows")

    def chunk(j, carry):
        here = pl.ds(pl.multiple_of(j * LANES, LANES), LANES)
        rows_near = rows_near_ref[:, here].astype(jnp.float32)
        rows_far = rows_far_ref[:, here].astype(jnp.float32)
        above = jnp.where(top_end, 0.0, jnp.where(odd_row, rows_near, rows_far))
        below = jnp.where(bottom_end, 0.0, jnp.where(odd_row, rows_far, rows_near))
        far = far_ref[:, here].astype(jnp.float32)
        near = near_ref[:, here].astype(jnp.float32)
        before = jnp.where(front_end, 0.0, jnp.where(odd, near, far))
        after = jnp.where(back_end, 0.0, jnp.where(odd, far, near))
        extra = []
        for q, edge in enumerate((0, height - 1)):
            inner = grad_ref[q, 1, :, here]
            grad_rows = below - inner if q else inner - above
            grad_cols = grad_ref[q, 2, :, here]
            grad_depth = grad_ref[q, 0, :, here] + jnp.where(
                back, after[edge : edge + 1], jnp.where(front, -before[edge : edge + 1], 0.0)
            )
            shading = shade(
                grad_depth,
                LIGHT_ROWS * grad_rows + LIGHT_COLS * grad_cols,
                grad_rows * grad_rows + grad_cols * grad_cols,
            )
            extra.append([jnp.sum(strip_ref[q, c, :, here] * shading, axis=0, keepdims=True) for c in range(3)])
        for r in range(tiles):
            rows = slice(r * SUBLANES, (r + 1) * SUBLANES)
            planes = [base_ref[c, rows, here] for c in range(4)]
            for end in range(2):
                if end:
                    grad_depth = after[rows] - volume_ref[0, slices - 2, rows, here].astype(jnp.float32)
                else:
                    grad_depth = volume_ref[0, 1, rows, here].astype(jnp.float32) - before[rows]
                shading = shade(grad_depth, face_ref[end, rows, here], square_ref[end, rows, here])
                for c in range(3):
                    planes[c] = planes[c] + lit_ref[end, c, rows, here] * shading
            for c in range(3):
                if r == 0:
                    planes[c] = planes[c] + jnp.where(first_row, extra[0][c], 0.0)
                if r == tiles - 1:
                    planes[c] = planes[c] + jnp.where(last_row, extra[1][c], 0.0)
            blocks = [
                jnp.concatenate([plane[first : first + share] for plane in planes], axis=0)
                for first in range(0, SUBLANES, share)
            ]
            if len(out_refs) == 1:
                for i, block in enumerate(blocks):
                    out_refs[0][r * len(blocks) + i, :, here] = block.astype(jnp.bfloat16)
            else:
                keep_ref, give_ref = out_refs
                keep_ref[r, :, here] = jnp.where(odd, blocks[1], blocks[0])
                give_ref[r, :, here] = jnp.where(odd, blocks[0], blocks[1]).astype(jnp.bfloat16)
        return carry

    lax.fori_loop(0, columns // LANES, chunk, 0)


def add_edges(volume, interior, halos, depth_count, paired):
    _, slices, height, columns = volume.shape
    share = height // depth_count
    if paired:
        half = (depth_count // 2, 4 * share, columns)
        shapes = [jax.ShapeDtypeStruct(half, jnp.float32), jax.ShapeDtypeStruct(half, jnp.bfloat16)]
    else:
        shapes = [jax.ShapeDtypeStruct((depth_count, 4 * share, columns), jnp.bfloat16)]
    return pl.pallas_call(
        functools.partial(edge_kernel, share),
        in_specs=[WHOLE] * 11,
        out_specs=[WHOLE] * len(shapes),
        out_shape=shapes,
        compiler_params=pltpu.CompilerParams(vmem_limit_bytes=24 * 1024 * 1024),
    )(volume, *interior, *halos)


def over(nearer, farther):
    share = nearer.shape[0] // 4
    clear = 1.0 - nearer[3 * share :]
    return nearer + jnp.concatenate([clear] * 4, axis=0) * farther


def merge_kernel(keep_ref, other_ref, own_ref, *send_refs):
    position = lax.axis_index("depth")
    odd, chip = position % 2 == 1, position // 2
    for k, out_ref in enumerate((own_ref, *send_refs)):
        keep = keep_ref[chip ^ k]
        other = other_ref[chip ^ k].astype(jnp.float32)
        out_ref[...] = over(jnp.where(odd, other, keep), jnp.where(odd, keep, other)).astype(out_ref.dtype)


def merge(keep, other):
    chips, rows, columns = keep.shape
    shapes = [jax.ShapeDtypeStruct((rows, columns), jnp.float32)]
    shapes += [jax.ShapeDtypeStruct((rows, columns), jnp.bfloat16)] * (chips - 1)
    return pl.pallas_call(
        merge_kernel,
        in_specs=[WHOLE] * 2,
        out_specs=[WHOLE] * chips,
        out_shape=shapes,
        compiler_params=pltpu.CompilerParams(vmem_limit_bytes=8 * 1024 * 1024),
    )(keep, other)


def gather_kernel(*refs):
    *part_refs, out_ref = refs
    count = len(part_refs)
    share = out_ref.shape[1]
    chip = lax.axis_index("depth") // 2
    parts = [part_ref[...].astype(jnp.float32) for part_ref in part_refs]
    step = 1
    while step < count:
        swap = (chip & step) != 0
        parts = [
            over(jnp.where(swap, parts[i + 1], parts[i]), jnp.where(swap, parts[i], parts[i + 1]))
            for i in range(0, len(parts), 2)
        ]
        step *= 2
    for c in range(4):
        out_ref[c] = parts[0][c * share : (c + 1) * share]


def gather(parts, share):
    columns = parts[0].shape[1]
    return pl.pallas_call(
        gather_kernel,
        in_specs=[WHOLE] * len(parts),
        out_specs=WHOLE,
        out_shape=jax.ShapeDtypeStruct((4, share, columns), jnp.float32),
        compiler_params=pltpu.CompilerParams(vmem_limit_bytes=4 * 1024 * 1024),
    )(*parts)


def finish_kernel(parts_ref, out_ref):
    count = parts_ref.shape[0]
    _, share, columns = out_ref.shape
    remaining = jnp.ones((share, columns), jnp.float32)
    sums = [jnp.zeros((share, columns), jnp.float32) for _ in range(3)]
    for k in range(count):
        part = parts_ref[k].astype(jnp.float32)
        for c in range(3):
            sums[c] = sums[c] + remaining * part[c * share : (c + 1) * share]
        remaining = remaining - remaining * part[3 * share :]
    for c in range(3):
        out_ref[c] = sums[c]
    out_ref[3] = 1.0 - remaining


def finish(parts, share):
    columns = parts.shape[2]
    return pl.pallas_call(
        finish_kernel,
        in_specs=[WHOLE],
        out_specs=WHOLE,
        out_shape=jax.ShapeDtypeStruct((4, share, columns), jnp.float32),
        compiler_params=pltpu.CompilerParams(vmem_limit_bytes=4 * 1024 * 1024),
    )(parts)


def swapped(values, axis, start):
    depth_count, row_count = lax.axis_size("depth"), lax.axis_size("rows")
    size = lax.axis_size(axis)
    perm = []
    for d in range(depth_count):
        for r in range(row_count):
            i = d if axis == "depth" else r
            j = i + 1 if i % 2 == start else i - 1
            if 0 <= j < size:
                e, q = (j, r) if axis == "depth" else (d, j)
            elif axis == "depth":
                e, q = (size - 1 - d, r)
            else:
                e, q = (d ^ 1, r)
            perm.append((d * row_count + r, e * row_count + q))
    return lax.ppermute(values, ("depth", "rows"), perm)


def exchanged(values, mask):
    return lax.ppermute(values, "depth", [(d, d ^ mask) for d in range(lax.axis_size("depth"))])


def body(volume, color_map, alpha_map):
    depth_count = lax.axis_size("depth")
    share = volume.shape[2] // depth_count
    rows_far, rows_near, far, near = cut_edges(volume)
    rows_far = swapped(rows_far, "rows", 1)
    rows_near = swapped(rows_near, "rows", 0)
    far = swapped(far, "depth", 1)
    near = swapped(near, "depth", 0)
    interior = march_interior(volume, color_map, alpha_map, depth_count)
    halos = (rows_near, rows_far, far, near)
    paired = depth_count == 8 and 2 * share == SUBLANES
    outs = add_edges(volume, interior, halos, depth_count, paired)
    if not paired:
        return finish(lax.all_to_all(outs[0], "depth", 0, 0, tiled=True), share)
    keep, give = outs
    own, *sends = merge(keep, exchanged(give, 1))
    received = [exchanged(send, 2 * k) for k, send in reversed(list(enumerate(sends, 1)))]
    return gather((own, *reversed(received)), share)


def solution(mesh):
    in_specs = (P(None, "depth", "rows", None), P(), P())
    out_specs = P(None, ("rows", "depth"), None)
    return jax.shard_map(body, mesh=mesh, in_specs=in_specs, out_specs=out_specs, check_vma=False)
```

```python
import functools

import jax
import jax.numpy as jnp
from jax import lax
from jax.experimental import pallas as pl
from jax.experimental.pallas import tpu as pltpu
from jax.sharding import PartitionSpec as P

AMBIENT = 0.3
DIFFUSE = 0.7
LIGHT_DEPTH = 0.48 * DIFFUSE
LIGHT_ROWS = 0.6 * DIFFUSE
LIGHT_COLS = 0.64 * DIFFUSE
OPACITY = 4.0
LANES = 128
SUBLANES = 8
WHOLE = pl.BlockSpec(memory_space=pltpu.VMEM)


def parity(axis):
    return lax.axis_index(axis) % 2


def ends(axis):
    position = lax.axis_index(axis)
    return position == 0, position == lax.axis_size(axis) - 1


def edges_kernel(volume_ref, rows_far_out, rows_near_out, far_out, near_out, strip_ref, plane_ref, sems):
    _, slices, height, _ = volume_ref.shape
    odd, odd_row = parity("depth"), parity("rows")
    last_tile = height // SUBLANES - 1

    def tile(i):
        return pl.ds(pl.multiple_of(i * SUBLANES, SUBLANES), SUBLANES)

    copies = [
        pltpu.make_async_copy(volume_ref.at[0, :, tile((1 - odd_row) * last_tile)], strip_ref.at[0], sems.at[0]),
        pltpu.make_async_copy(volume_ref.at[0, :, tile(odd_row * last_tile)], strip_ref.at[1], sems.at[1]),
        pltpu.make_async_copy(volume_ref.at[0, odd * (slices - 1)], plane_ref.at[0], sems.at[2]),
        pltpu.make_async_copy(volume_ref.at[0, (1 - odd) * (slices - 1)], plane_ref.at[1], sems.at[3]),
    ]
    for copy in copies:
        copy.start()

    def narrow(values):
        return values.astype(jnp.float32).astype(jnp.bfloat16)

    copies[0].wait()
    rows_near_out[...] = narrow(jnp.where(odd_row == 1, strip_ref[0, :, 0, :], strip_ref[0, :, SUBLANES - 1, :]))
    copies[1].wait()
    rows_far_out[...] = narrow(jnp.where(odd_row == 1, strip_ref[1, :, SUBLANES - 1, :], strip_ref[1, :, 0, :]))
    copies[2].wait()
    far_out[...] = narrow(plane_ref[0])
    copies[3].wait()
    near_out[...] = narrow(plane_ref[1])


def cut_edges(volume):
    _, slices, height, columns = volume.shape
    plane = jax.ShapeDtypeStruct((height, columns), jnp.bfloat16)
    strip = jax.ShapeDtypeStruct((slices, columns), jnp.bfloat16)
    return pl.pallas_call(
        edges_kernel,
        in_specs=[pl.BlockSpec(memory_space=pl.ANY)],
        out_specs=[WHOLE] * 4,
        out_shape=[strip, strip, plane, plane],
        scratch_shapes=[
            pltpu.VMEM((2, slices, SUBLANES, columns), jnp.int32),
            pltpu.VMEM((2, height, columns), jnp.int32),
            pltpu.SemaphoreType.DMA((4,)),
        ],
        compiler_params=pltpu.CompilerParams(vmem_limit_bytes=52 * 1024 * 1024),
    )(volume)


def pick(entries, places):
    dims = lax.GatherDimensionNumbers(
        offset_dims=(),
        collapsed_slice_dims=(1,),
        start_index_map=(1,),
        operand_batching_dims=(0,),
        start_indices_batching_dims=(0,),
    )
    return lax.gather(entries, places[..., None], dims, (1, 1), mode=lax.GatherScatterMode.PROMISE_IN_BOUNDS)


def shade(grad_depth, facing, squares):
    facing = facing + LIGHT_DEPTH * grad_depth
    squares = squares + grad_depth * grad_depth
    return AMBIENT + jnp.abs(facing) * lax.rsqrt(jnp.maximum(squares, 4.0))


def interior_kernel(
    opacity_scale,
    volume_ref,
    color_ref,
    alpha_ref,
    base_ref,
    face_ref,
    square_ref,
    lit_ref,
    grad_ref,
    strip_ref,
    pair_ref,
    held_ref,
):
    _, slices, height, columns = volume_ref.shape
    tiles = height // SUBLANES
    chunks = columns // LANES
    tile = (SUBLANES, LANES)
    strip = (slices, LANES)

    packed = color_ref[0:1, :] + color_ref[1:2, :] * 256 + color_ref[2:3, :] * 65536
    color_low, color_high = packed[:, :LANES], packed[:, LANES:]
    alpha_both = alpha_ref[0:1, :LANES] + alpha_ref[0:1, LANES:] * 256

    def colors(value, tables):
        low, high = tables
        place = value & (LANES - 1)
        color = jnp.where(value < LANES, pick(low, place), pick(high, place))
        parts = (color & 255, lax.shift_right_logical(color, 8) & 255, lax.shift_right_logical(color, 16))
        return [part.astype(jnp.float32) for part in parts]

    def opacity(level, table):
        entry = pick(table, level & (LANES - 1))
        entry = lax.shift_right_logical(entry, lax.shift_right_logical(level & LANES, 4)) & 255
        return entry.astype(jnp.float32) * opacity_scale

    tile_colors = [jnp.broadcast_to(t, tile) for t in (color_low, color_high)]
    tile_alpha = jnp.broadcast_to(alpha_both, tile)
    strip_colors = [jnp.broadcast_to(t, strip) for t in (color_low, color_high)]

    def masks(shape):
        lane = lax.broadcasted_iota(jnp.int32, shape, 1)
        row = lax.broadcasted_iota(jnp.int32, shape, 0)
        return lane == 0, lane == LANES - 1, row == 0, row == shape[0] - 1

    first_lane, last_lane, first_row, last_row = masks(tile)
    strip_first_lane, strip_last_lane, front, back = masks(strip)

    pairs = slices // 2
    top = SUBLANES

    def clear(j, carry):
        pair_ref[j] = jnp.zeros(pair_ref.shape[1:], jnp.int32)
        return carry

    clear(0, 0)
    clear(chunks + 1, 0)
    margin = jnp.zeros((pairs, SUBLANES, LANES), jnp.int32)

    def pack(j, carry):
        here = pl.ds(pl.multiple_of(j * LANES, LANES), LANES)
        pair_ref[j + 1, :, :top] = margin
        pair_ref[j + 1, :, top + height :] = margin
        for p in range(pairs):
            pair_ref[j + 1, p, top : top + height] = volume_ref[0, p, :, here] + lax.shift_left(
                volume_ref[0, p + pairs, :, here], 16
            )
        return carry

    lax.fori_loop(0, chunks, pack, 0)

    def split(difference):
        low = lax.shift_right_arithmetic(lax.shift_left(difference, 16), 16)
        high = lax.shift_right_arithmetic(difference + 32768, 16)
        return low.astype(jnp.float32), high.astype(jnp.float32)

    def across(left_value, value, right_value, first, last):
        west = pltpu.roll(jnp.where(last, left_value, value), 1, 1)
        east = pltpu.roll(jnp.where(first, right_value, value), LANES - 1, 1)
        return split(east - west)

    def chunk(j, carry):
        here = pl.ds(pl.multiple_of(j * LANES, LANES), LANES)

        for r in range(tiles):
            rows = slice(r * SUBLANES, (r + 1) * SUBLANES)
            values = [volume_ref[0, s, rows, here] for s in range(slices)]

            def words(c, p, offset=0):
                return pair_ref[c, p, top + r * SUBLANES + offset : top + (r + 1) * SUBLANES + offset, :]

            down, right = [], []
            for p in range(pairs):
                down.append(split(words(j + 1, p, 1) - words(j + 1, p, -1)))
                right.append(across(words(j, p), words(j + 1, p), words(j + 2, p), first_lane, last_lane))
            remaining = jnp.ones(tile, jnp.float32)
            sums = [jnp.zeros(tile, jnp.float32) for _ in range(3)]
            for s in range(slices):
                value = values[s]
                grad_rows = down[s % pairs][s // pairs]
                grad_cols = right[s % pairs][s // pairs]
                squares = grad_rows * grad_rows + grad_cols * grad_cols
                facing = LIGHT_ROWS * grad_rows + LIGHT_COLS * grad_cols
                weight = remaining * opacity(volume_ref[1, s, rows, here], tile_alpha)
                remaining = remaining - weight
                if r == 0:
                    held_ref[0, s : s + 1, :] = weight[:1]
                    weight = jnp.where(first_row, 0.0, weight)
                if r == tiles - 1:
                    held_ref[1, s : s + 1, :] = weight[SUBLANES - 1 :]
                    weight = jnp.where(last_row, 0.0, weight)
                emitted = colors(value, tile_colors)
                if 0 < s < slices - 1:
                    grad_depth = (values[s + 1] - values[s - 1]).astype(jnp.float32)
                    weight = weight * shade(grad_depth, facing, squares)
                    for c in range(3):
                        sums[c] = sums[c] + emitted[c] * weight
                else:
                    end = int(s > 0)
                    face_ref[end, rows, here] = facing
                    square_ref[end, rows, here] = squares
                    weight = weight * (1.0 / 255.0)
                    for c in range(3):
                        lit_ref[end, c, rows, here] = emitted[c] * weight
            for c in range(3):
                base_ref[c, rows, here] = sums[c] * (1.0 / 255.0)
            base_ref[3, rows, here] = 1.0 - remaining

        for q, (edge, inner) in enumerate(((0, 1), (height - 1, height - 2))):
            value = volume_ref[0, :, edge, here]
            behind = pltpu.roll(jnp.where(back, 0, value), 1, 0)
            ahead = pltpu.roll(jnp.where(front, 0, value), slices - 1, 0)
            grad_ref[q, 0, :, here] = (ahead - behind).astype(jnp.float32)
            grad_ref[q, 1, :, here] = volume_ref[0, :, inner, here].astype(jnp.float32)
            word = pair_ref[j + 1, :, top + edge, :]
            low, high = across(
                pair_ref[j, :, top + edge, :],
                word,
                pair_ref[j + 2, :, top + edge, :],
                strip_first_lane[:pairs],
                strip_last_lane[:pairs],
            )
            grad_ref[q, 2, :pairs, here] = low
            grad_ref[q, 2, pairs:, here] = high
            weight = held_ref[q] * (1.0 / 255.0)
            emitted = colors(value, strip_colors)
            for c in range(3):
                strip_ref[q, c, :, here] = emitted[c] * weight
        return carry

    lax.fori_loop(0, chunks, chunk, 0)


def march_interior(volume, color_map, alpha_map, depth_count):
    _, slices, height, columns = volume.shape
    opacity_scale = OPACITY / (255.0 * slices * depth_count)
    shapes = [
        (4, height, columns),
        (2, height, columns),
        (2, height, columns),
        (2, 3, height, columns),
        (2, 3, slices, columns),
        (2, 3, slices, columns),
    ]
    voxels = slices * height * columns
    return pl.pallas_call(
        functools.partial(interior_kernel, opacity_scale),
        in_specs=[WHOLE] * 3,
        out_specs=[WHOLE] * len(shapes),
        out_shape=[jax.ShapeDtypeStruct(shape, jnp.float32) for shape in shapes],
        scratch_shapes=[
            pltpu.VMEM((columns // LANES + 2, slices // 2, height + 2 * SUBLANES, LANES), jnp.int32),
            pltpu.VMEM((2, slices, LANES), jnp.float32),
        ],
        compiler_params=pltpu.CompilerParams(vmem_limit_bytes=24 * 1024 * 1024),
        cost_estimate=pl.CostEstimate(flops=voxels * 80, bytes_accessed=voxels * 20, transcendentals=voxels),
    )(volume, color_map, alpha_map.reshape(1, -1))


def edge_kernel(
    share, volume_ref, base_ref, face_ref, square_ref, lit_ref, grad_ref, strip_ref, rows_near_ref, rows_far_ref, far_ref, near_ref, *out_refs
):
    _, slices, height, columns = volume_ref.shape
    tiles = height // SUBLANES
    tile = (SUBLANES, LANES)
    row = lax.broadcasted_iota(jnp.int32, tile, 0)
    first_row, last_row = row == 0, row == SUBLANES - 1
    level = lax.broadcasted_iota(jnp.int32, (slices, LANES), 0)
    front, back = level == 0, level == slices - 1
    odd, odd_row = parity("depth") == 1, parity("rows") == 1
    front_end, back_end = ends("depth")
    top_end, bottom_end = ends("rows")

    def chunk(j, carry):
        here = pl.ds(pl.multiple_of(j * LANES, LANES), LANES)
        rows_near = rows_near_ref[:, here].astype(jnp.float32)
        rows_far = rows_far_ref[:, here].astype(jnp.float32)
        above = jnp.where(top_end, 0.0, jnp.where(odd_row, rows_near, rows_far))
        below = jnp.where(bottom_end, 0.0, jnp.where(odd_row, rows_far, rows_near))
        far = far_ref[:, here].astype(jnp.float32)
        near = near_ref[:, here].astype(jnp.float32)
        before = jnp.where(front_end, 0.0, jnp.where(odd, near, far))
        after = jnp.where(back_end, 0.0, jnp.where(odd, far, near))
        extra = []
        for q, edge in enumerate((0, height - 1)):
            inner = grad_ref[q, 1, :, here]
            grad_rows = below - inner if q else inner - above
            grad_cols = grad_ref[q, 2, :, here]
            grad_depth = grad_ref[q, 0, :, here] + jnp.where(
                back, after[edge : edge + 1], jnp.where(front, -before[edge : edge + 1], 0.0)
            )
            shading = shade(
                grad_depth,
                LIGHT_ROWS * grad_rows + LIGHT_COLS * grad_cols,
                grad_rows * grad_rows + grad_cols * grad_cols,
            )
            extra.append([jnp.sum(strip_ref[q, c, :, here] * shading, axis=0, keepdims=True) for c in range(3)])
        for r in range(tiles):
            rows = slice(r * SUBLANES, (r + 1) * SUBLANES)
            planes = [base_ref[c, rows, here] for c in range(4)]
            for end in range(2):
                if end:
                    grad_depth = after[rows] - volume_ref[0, slices - 2, rows, here].astype(jnp.float32)
                else:
                    grad_depth = volume_ref[0, 1, rows, here].astype(jnp.float32) - before[rows]
                shading = shade(grad_depth, face_ref[end, rows, here], square_ref[end, rows, here])
                for c in range(3):
                    planes[c] = planes[c] + lit_ref[end, c, rows, here] * shading
            for c in range(3):
                if r == 0:
                    planes[c] = planes[c] + jnp.where(first_row, extra[0][c], 0.0)
                if r == tiles - 1:
                    planes[c] = planes[c] + jnp.where(last_row, extra[1][c], 0.0)
            blocks = [
                jnp.concatenate([plane[first : first + share] for plane in planes], axis=0)
                for first in range(0, SUBLANES, share)
            ]
            if len(out_refs) == 1:
                for i, block in enumerate(blocks):
                    out_refs[0][r * len(blocks) + i, :, here] = block.astype(jnp.bfloat16)
            else:
                keep_ref, give_ref = out_refs
                keep_ref[r, :, here] = jnp.where(odd, blocks[1], blocks[0])
                give_ref[r, :, here] = jnp.where(odd, blocks[0], blocks[1]).astype(jnp.bfloat16)
        return carry

    lax.fori_loop(0, columns // LANES, chunk, 0)


def add_edges(volume, interior, halos, depth_count, paired):
    _, slices, height, columns = volume.shape
    share = height // depth_count
    if paired:
        half = (depth_count // 2, 4 * share, columns)
        shapes = [jax.ShapeDtypeStruct(half, jnp.float32), jax.ShapeDtypeStruct(half, jnp.bfloat16)]
    else:
        shapes = [jax.ShapeDtypeStruct((depth_count, 4 * share, columns), jnp.bfloat16)]
    return pl.pallas_call(
        functools.partial(edge_kernel, share),
        in_specs=[WHOLE] * 11,
        out_specs=[WHOLE] * len(shapes),
        out_shape=shapes,
        compiler_params=pltpu.CompilerParams(vmem_limit_bytes=24 * 1024 * 1024),
    )(volume, *interior, *halos)


def over(nearer, farther):
    share = nearer.shape[0] // 4
    clear = 1.0 - nearer[3 * share :]
    return nearer + jnp.concatenate([clear] * 4, axis=0) * farther


def merge_kernel(bit, mask, keep_ref, other_ref, *out_refs):
    position = lax.axis_index("depth")
    farther = (position & mask) != 0

    def merged(i):
        keep = keep_ref[i]
        other = other_ref[i].astype(jnp.float32)
        return over(jnp.where(farther, other, keep), jnp.where(farther, keep, other))

    if len(out_refs) == 1:
        block = merged(0)
        share = block.shape[0] // 4
        for c in range(4):
            out_refs[0][c] = block[c * share : (c + 1) * share]
        return
    keep_out, give_out = out_refs
    side = jnp.where((position & bit) != 0, 1, 0)
    for i in range(keep_out.shape[0]):
        keep_out[i] = merged(2 * i + side)
        give_out[i] = merged(2 * i + 1 - side).astype(give_out.dtype)


def merge(keep, other, mask):
    count, rows, columns = keep.shape
    if count == 1:
        shapes = [jax.ShapeDtypeStruct((4, rows // 4, columns), jnp.float32)]
    else:
        half = (count // 2, rows, columns)
        shapes = [jax.ShapeDtypeStruct(half, jnp.float32), jax.ShapeDtypeStruct(half, jnp.bfloat16)]
    return pl.pallas_call(
        functools.partial(merge_kernel, 2 * mask, mask),
        in_specs=[WHOLE] * 2,
        out_specs=[WHOLE] * len(shapes),
        out_shape=shapes,
        compiler_params=pltpu.CompilerParams(vmem_limit_bytes=4 * 1024 * 1024),
    )(keep, other)


def finish_kernel(parts_ref, out_ref):
    count = parts_ref.shape[0]
    _, share, columns = out_ref.shape
    remaining = jnp.ones((share, columns), jnp.float32)
    sums = [jnp.zeros((share, columns), jnp.float32) for _ in range(3)]
    for k in range(count):
        part = parts_ref[k].astype(jnp.float32)
        for c in range(3):
            sums[c] = sums[c] + remaining * part[c * share : (c + 1) * share]
        remaining = remaining - remaining * part[3 * share :]
    for c in range(3):
        out_ref[c] = sums[c]
    out_ref[3] = 1.0 - remaining


def finish(parts, share):
    columns = parts.shape[2]
    return pl.pallas_call(
        finish_kernel,
        in_specs=[WHOLE],
        out_specs=WHOLE,
        out_shape=jax.ShapeDtypeStruct((4, share, columns), jnp.float32),
        compiler_params=pltpu.CompilerParams(vmem_limit_bytes=4 * 1024 * 1024),
    )(parts)


def swapped(values, axis, start):
    depth_count, row_count = lax.axis_size("depth"), lax.axis_size("rows")
    size = lax.axis_size(axis)
    perm = []
    for d in range(depth_count):
        for r in range(row_count):
            i = d if axis == "depth" else r
            j = i + 1 if i % 2 == start else i - 1
            if 0 <= j < size:
                e, q = (j, r) if axis == "depth" else (d, j)
            elif axis == "depth":
                e, q = (size - 1 - d, r)
            else:
                e, q = (d ^ 1, r)
            perm.append((d * row_count + r, e * row_count + q))
    return lax.ppermute(values, ("depth", "rows"), perm)


def exchanged(values, mask):
    return lax.ppermute(values, "depth", [(d, d ^ mask) for d in range(lax.axis_size("depth"))])


def body(volume, color_map, alpha_map):
    depth_count = lax.axis_size("depth")
    share = volume.shape[2] // depth_count
    rows_far, rows_near, far, near = cut_edges(volume)
    rows_far = swapped(rows_far, "rows", 1)
    rows_near = swapped(rows_near, "rows", 0)
    far = swapped(far, "depth", 1)
    near = swapped(near, "depth", 0)
    interior = march_interior(volume, color_map, alpha_map, depth_count)
    halos = (rows_near, rows_far, far, near)
    paired = 2 * share == SUBLANES and depth_count & (depth_count - 1) == 0
    outs = add_edges(volume, interior, halos, depth_count, paired)
    if not paired:
        return finish(lax.all_to_all(outs[0], "depth", 0, 0, tiled=True), share)
    mask = 1
    while mask < depth_count:
        outs = merge(outs[0], exchanged(outs[1], mask), mask)
        mask *= 2
    return outs[0]


def solution(mesh):
    in_specs = (P(None, "depth", "rows", None), P(), P())
    out_specs = P(None, ("rows", "depth"), None)
    return jax.shard_map(body, mesh=mesh, in_specs=in_specs, out_specs=out_specs, check_vma=False)
```

```python
import functools

import jax
import jax.numpy as jnp
from jax import lax
from jax.experimental import pallas as pl
from jax.experimental.pallas import tpu as pltpu
from jax.sharding import PartitionSpec as P

AMBIENT = 0.3
DIFFUSE = 0.7
LIGHT_DEPTH = 0.48 * DIFFUSE
LIGHT_ROWS = 0.6 * DIFFUSE
LIGHT_COLS = 0.64 * DIFFUSE
OPACITY = 4.0
LANES = 128
SUBLANES = 8
WHOLE = pl.BlockSpec(memory_space=pltpu.VMEM)


def parity(axis):
    return lax.axis_index(axis) % 2


def ends(axis):
    position = lax.axis_index(axis)
    return position == 0, position == lax.axis_size(axis) - 1


def edges_kernel(volume_ref, rows_far_out, rows_near_out, far_out, near_out, strip_ref, plane_ref, sems):
    _, slices, height, _ = volume_ref.shape
    odd, odd_row = parity("depth"), parity("rows")
    last_tile = height // SUBLANES - 1

    def tile(i):
        return pl.ds(pl.multiple_of(i * SUBLANES, SUBLANES), SUBLANES)

    copies = [
        pltpu.make_async_copy(volume_ref.at[0, :, tile((1 - odd_row) * last_tile)], strip_ref.at[0], sems.at[0]),
        pltpu.make_async_copy(volume_ref.at[0, :, tile(odd_row * last_tile)], strip_ref.at[1], sems.at[1]),
        pltpu.make_async_copy(volume_ref.at[0, odd * (slices - 1)], plane_ref.at[0], sems.at[2]),
        pltpu.make_async_copy(volume_ref.at[0, (1 - odd) * (slices - 1)], plane_ref.at[1], sems.at[3]),
    ]
    for copy in copies:
        copy.start()

    def narrow(values):
        return values.astype(jnp.float32).astype(jnp.bfloat16)

    copies[0].wait()
    rows_near_out[...] = narrow(jnp.where(odd_row == 1, strip_ref[0, :, 0, :], strip_ref[0, :, SUBLANES - 1, :]))
    copies[1].wait()
    rows_far_out[...] = narrow(jnp.where(odd_row == 1, strip_ref[1, :, SUBLANES - 1, :], strip_ref[1, :, 0, :]))
    copies[2].wait()
    far_out[...] = narrow(plane_ref[0])
    copies[3].wait()
    near_out[...] = narrow(plane_ref[1])


def cut_edges(volume):
    _, slices, height, columns = volume.shape
    plane = jax.ShapeDtypeStruct((height, columns), jnp.bfloat16)
    strip = jax.ShapeDtypeStruct((slices, columns), jnp.bfloat16)
    return pl.pallas_call(
        edges_kernel,
        in_specs=[pl.BlockSpec(memory_space=pl.ANY)],
        out_specs=[WHOLE] * 4,
        out_shape=[strip, strip, plane, plane],
        scratch_shapes=[
            pltpu.VMEM((2, slices, SUBLANES, columns), jnp.int32),
            pltpu.VMEM((2, height, columns), jnp.int32),
            pltpu.SemaphoreType.DMA((4,)),
        ],
        compiler_params=pltpu.CompilerParams(vmem_limit_bytes=52 * 1024 * 1024),
    )(volume)


def pick(entries, places):
    dims = lax.GatherDimensionNumbers(
        offset_dims=(),
        collapsed_slice_dims=(1,),
        start_index_map=(1,),
        operand_batching_dims=(0,),
        start_indices_batching_dims=(0,),
    )
    return lax.gather(entries, places[..., None], dims, (1, 1), mode=lax.GatherScatterMode.PROMISE_IN_BOUNDS)


def shade(grad_depth, facing, squares):
    facing = facing + LIGHT_DEPTH * grad_depth
    squares = squares + grad_depth * grad_depth
    return AMBIENT + jnp.abs(facing) * lax.rsqrt(jnp.maximum(squares, 4.0))


def interior_kernel(
    opacity_scale,
    volume_ref,
    color_ref,
    alpha_ref,
    base_ref,
    face_ref,
    square_ref,
    lit_ref,
    grad_ref,
    strip_ref,
    pair_ref,
    held_ref,
):
    _, slices, height, columns = volume_ref.shape
    tiles = height // SUBLANES
    chunks = columns // LANES
    tile = (SUBLANES, LANES)
    strip = (slices, LANES)

    packed = color_ref[0:1, :] + color_ref[1:2, :] * 256 + color_ref[2:3, :] * 65536
    color_low, color_high = packed[:, :LANES], packed[:, LANES:]
    alpha_both = alpha_ref[0:1, :LANES] + alpha_ref[0:1, LANES:] * 256

    def colors(value, tables):
        low, high = tables
        place = value & (LANES - 1)
        color = jnp.where(value < LANES, pick(low, place), pick(high, place))
        parts = (color & 255, lax.shift_right_logical(color, 8) & 255, lax.shift_right_logical(color, 16))
        return [part.astype(jnp.float32) for part in parts]

    def opacity(level, table):
        entry = pick(table, level & (LANES - 1))
        entry = lax.shift_right_logical(entry, lax.shift_right_logical(level & LANES, 4)) & 255
        return entry.astype(jnp.float32) * opacity_scale

    tile_colors = [jnp.broadcast_to(t, tile) for t in (color_low, color_high)]
    tile_alpha = jnp.broadcast_to(alpha_both, tile)
    strip_colors = [jnp.broadcast_to(t, strip) for t in (color_low, color_high)]

    def masks(shape):
        lane = lax.broadcasted_iota(jnp.int32, shape, 1)
        row = lax.broadcasted_iota(jnp.int32, shape, 0)
        return lane == 0, lane == LANES - 1, row == 0, row == shape[0] - 1

    first_lane, last_lane, first_row, last_row = masks(tile)
    strip_first_lane, strip_last_lane, front, back = masks(strip)

    pairs = slices // 2
    top = SUBLANES

    def clear(j, carry):
        pair_ref[j] = jnp.zeros(pair_ref.shape[1:], jnp.int32)
        return carry

    clear(0, 0)
    clear(chunks + 1, 0)
    margin = jnp.zeros((pairs, SUBLANES, LANES), jnp.int32)

    def pack(j, carry):
        here = pl.ds(pl.multiple_of(j * LANES, LANES), LANES)
        pair_ref[j + 1, :, :top] = margin
        pair_ref[j + 1, :, top + height :] = margin
        for p in range(pairs):
            pair_ref[j + 1, p, top : top + height] = volume_ref[0, p, :, here] + lax.shift_left(
                volume_ref[0, p + pairs, :, here], 16
            )
        return carry

    lax.fori_loop(0, chunks, pack, 0)

    def split(difference):
        low = lax.shift_right_arithmetic(lax.shift_left(difference, 16), 16)
        high = lax.shift_right_arithmetic(difference + 32768, 16)
        return low.astype(jnp.float32), high.astype(jnp.float32)

    def across(left_value, value, right_value, first, last):
        west = pltpu.roll(jnp.where(last, left_value, value), 1, 1)
        east = pltpu.roll(jnp.where(first, right_value, value), LANES - 1, 1)
        return split(east - west)

    def chunk(j, carry):
        here = pl.ds(pl.multiple_of(j * LANES, LANES), LANES)

        for r in range(tiles):
            rows = slice(r * SUBLANES, (r + 1) * SUBLANES)
            values = [volume_ref[0, s, rows, here] for s in range(slices)]

            def words(c, p, offset=0):
                return pair_ref[c, p, top + r * SUBLANES + offset : top + (r + 1) * SUBLANES + offset, :]

            down, right = [], []
            for p in range(pairs):
                down.append(split(words(j + 1, p, 1) - words(j + 1, p, -1)))
                right.append(across(words(j, p), words(j + 1, p), words(j + 2, p), first_lane, last_lane))
            remaining = jnp.ones(tile, jnp.float32)
            sums = [jnp.zeros(tile, jnp.float32) for _ in range(3)]
            for s in range(slices):
                value = values[s]
                grad_rows = down[s % pairs][s // pairs]
                grad_cols = right[s % pairs][s // pairs]
                squares = grad_rows * grad_rows + grad_cols * grad_cols
                facing = LIGHT_ROWS * grad_rows + LIGHT_COLS * grad_cols
                weight = remaining * opacity(volume_ref[1, s, rows, here], tile_alpha)
                remaining = remaining - weight
                if r == 0:
                    held_ref[0, s : s + 1, :] = weight[:1]
                    weight = jnp.where(first_row, 0.0, weight)
                if r == tiles - 1:
                    held_ref[1, s : s + 1, :] = weight[SUBLANES - 1 :]
                    weight = jnp.where(last_row, 0.0, weight)
                emitted = colors(value, tile_colors)
                if 0 < s < slices - 1:
                    grad_depth = (values[s + 1] - values[s - 1]).astype(jnp.float32)
                    weight = weight * shade(grad_depth, facing, squares)
                    for c in range(3):
                        sums[c] = sums[c] + emitted[c] * weight
                else:
                    end = int(s > 0)
                    face_ref[end, rows, here] = facing
                    square_ref[end, rows, here] = squares
                    weight = weight * (1.0 / 255.0)
                    for c in range(3):
                        lit_ref[end, c, rows, here] = emitted[c] * weight
            for c in range(3):
                base_ref[c, rows, here] = sums[c] * (1.0 / 255.0)
            base_ref[3, rows, here] = 1.0 - remaining

        for q, (edge, inner) in enumerate(((0, 1), (height - 1, height - 2))):
            value = volume_ref[0, :, edge, here]
            behind = pltpu.roll(jnp.where(back, 0, value), 1, 0)
            ahead = pltpu.roll(jnp.where(front, 0, value), slices - 1, 0)
            grad_ref[q, 0, :, here] = (ahead - behind).astype(jnp.float32)
            grad_ref[q, 1, :, here] = volume_ref[0, :, inner, here].astype(jnp.float32)
            word = pair_ref[j + 1, :, top + edge, :]
            low, high = across(
                pair_ref[j, :, top + edge, :],
                word,
                pair_ref[j + 2, :, top + edge, :],
                strip_first_lane[:pairs],
                strip_last_lane[:pairs],
            )
            grad_ref[q, 2, :pairs, here] = low
            grad_ref[q, 2, pairs:, here] = high
            weight = held_ref[q] * (1.0 / 255.0)
            emitted = colors(value, strip_colors)
            for c in range(3):
                strip_ref[q, c, :, here] = emitted[c] * weight
        return carry

    lax.fori_loop(0, chunks, chunk, 0)


def march_interior(volume, color_map, alpha_map, depth_count):
    _, slices, height, columns = volume.shape
    opacity_scale = OPACITY / (255.0 * slices * depth_count)
    shapes = [
        (4, height, columns),
        (2, height, columns),
        (2, height, columns),
        (2, 3, height, columns),
        (2, 3, slices, columns),
        (2, 3, slices, columns),
    ]
    voxels = slices * height * columns
    return pl.pallas_call(
        functools.partial(interior_kernel, opacity_scale),
        in_specs=[WHOLE] * 3,
        out_specs=[WHOLE] * len(shapes),
        out_shape=[jax.ShapeDtypeStruct(shape, jnp.float32) for shape in shapes],
        scratch_shapes=[
            pltpu.VMEM((columns // LANES + 2, slices // 2, height + 2 * SUBLANES, LANES), jnp.int32),
            pltpu.VMEM((2, slices, LANES), jnp.float32),
        ],
        compiler_params=pltpu.CompilerParams(vmem_limit_bytes=24 * 1024 * 1024),
        cost_estimate=pl.CostEstimate(flops=voxels * 80, bytes_accessed=voxels * 20, transcendentals=voxels),
    )(volume, color_map, alpha_map.reshape(1, -1))


def edge_kernel(
    share, volume_ref, base_ref, face_ref, square_ref, lit_ref, grad_ref, strip_ref, rows_near_ref, rows_far_ref, far_ref, near_ref, *out_refs
):
    _, slices, height, columns = volume_ref.shape
    tiles = height // SUBLANES
    tile = (SUBLANES, LANES)
    row = lax.broadcasted_iota(jnp.int32, tile, 0)
    first_row, last_row = row == 0, row == SUBLANES - 1
    level = lax.broadcasted_iota(jnp.int32, (slices, LANES), 0)
    front, back = level == 0, level == slices - 1
    odd, odd_row = parity("depth") == 1, parity("rows") == 1
    front_end, back_end = ends("depth")
    top_end, bottom_end = ends("rows")

    def chunk(j, carry):
        here = pl.ds(pl.multiple_of(j * LANES, LANES), LANES)
        rows_near = rows_near_ref[:, here].astype(jnp.float32)
        rows_far = rows_far_ref[:, here].astype(jnp.float32)
        above = jnp.where(top_end, 0.0, jnp.where(odd_row, rows_near, rows_far))
        below = jnp.where(bottom_end, 0.0, jnp.where(odd_row, rows_far, rows_near))
        far = far_ref[:, here].astype(jnp.float32)
        near = near_ref[:, here].astype(jnp.float32)
        before = jnp.where(front_end, 0.0, jnp.where(odd, near, far))
        after = jnp.where(back_end, 0.0, jnp.where(odd, far, near))
        extra = []
        for q, edge in enumerate((0, height - 1)):
            inner = grad_ref[q, 1, :, here]
            grad_rows = below - inner if q else inner - above
            grad_cols = grad_ref[q, 2, :, here]
            grad_depth = grad_ref[q, 0, :, here] + jnp.where(
                back, after[edge : edge + 1], jnp.where(front, -before[edge : edge + 1], 0.0)
            )
            shading = shade(
                grad_depth,
                LIGHT_ROWS * grad_rows + LIGHT_COLS * grad_cols,
                grad_rows * grad_rows + grad_cols * grad_cols,
            )
            extra.append([jnp.sum(strip_ref[q, c, :, here] * shading, axis=0, keepdims=True) for c in range(3)])
        for r in range(tiles):
            rows = slice(r * SUBLANES, (r + 1) * SUBLANES)
            planes = [base_ref[c, rows, here] for c in range(4)]
            for end in range(2):
                if end:
                    grad_depth = after[rows] - volume_ref[0, slices - 2, rows, here].astype(jnp.float32)
                else:
                    grad_depth = volume_ref[0, 1, rows, here].astype(jnp.float32) - before[rows]
                shading = shade(grad_depth, face_ref[end, rows, here], square_ref[end, rows, here])
                for c in range(3):
                    planes[c] = planes[c] + lit_ref[end, c, rows, here] * shading
            for c in range(3):
                if r == 0:
                    planes[c] = planes[c] + jnp.where(first_row, extra[0][c], 0.0)
                if r == tiles - 1:
                    planes[c] = planes[c] + jnp.where(last_row, extra[1][c], 0.0)
            blocks = [
                jnp.concatenate([plane[first : first + share] for plane in planes], axis=0)
                for first in range(0, SUBLANES, share)
            ]
            if len(out_refs) == 1:
                for i, block in enumerate(blocks):
                    out_refs[0][r * len(blocks) + i, :, here] = block.astype(jnp.bfloat16)
            else:
                keep_ref, give_ref = out_refs
                keep_ref[r, :, here] = jnp.where(odd, blocks[0], blocks[1])
                give_ref[r, :, here] = jnp.where(odd, blocks[1], blocks[0]).astype(jnp.bfloat16)
        return carry

    lax.fori_loop(0, columns // LANES, chunk, 0)


def add_edges(volume, interior, halos, depth_count, paired):
    _, slices, height, columns = volume.shape
    share = height // depth_count
    if paired:
        half = (depth_count // 2, 4 * share, columns)
        shapes = [jax.ShapeDtypeStruct(half, jnp.float32), jax.ShapeDtypeStruct(half, jnp.bfloat16)]
    else:
        shapes = [jax.ShapeDtypeStruct((depth_count, 4 * share, columns), jnp.bfloat16)]
    return pl.pallas_call(
        functools.partial(edge_kernel, share),
        in_specs=[WHOLE] * 11,
        out_specs=[WHOLE] * len(shapes),
        out_shape=shapes,
        compiler_params=pltpu.CompilerParams(vmem_limit_bytes=24 * 1024 * 1024),
    )(volume, *interior, *halos)


def over(nearer, farther):
    share = nearer.shape[0] // 4
    clear = 1.0 - nearer[3 * share :]
    return nearer + jnp.concatenate([clear] * 4, axis=0) * farther


def merge_kernel(keep_ref, other_ref, *send_refs):
    position = lax.axis_index("depth")
    odd, chip = position % 2 == 1, position // 2
    for k, out_ref in enumerate(send_refs):
        keep = keep_ref[chip ^ k]
        other = other_ref[chip ^ k].astype(jnp.float32)
        out_ref[...] = over(jnp.where(odd, other, keep), jnp.where(odd, keep, other)).astype(out_ref.dtype)


def merge(keep, other):
    chips, rows, columns = keep.shape
    return pl.pallas_call(
        merge_kernel,
        in_specs=[WHOLE] * 2,
        out_specs=[WHOLE] * chips,
        out_shape=[jax.ShapeDtypeStruct((rows, columns), jnp.bfloat16)] * chips,
        compiler_params=pltpu.CompilerParams(vmem_limit_bytes=8 * 1024 * 1024),
    )(keep, other)


def gather_kernel(*refs):
    *part_refs, out_ref = refs
    part_refs.reverse()
    count = len(part_refs)
    share = out_ref.shape[1]
    chip = lax.axis_index("depth") // 2
    parts = [part_ref[...].astype(jnp.float32) for part_ref in part_refs]
    step = 1
    while step < count:
        swap = (chip & step) != 0
        parts = [
            over(jnp.where(swap, parts[i + 1], parts[i]), jnp.where(swap, parts[i], parts[i + 1]))
            for i in range(0, len(parts), 2)
        ]
        step *= 2
    for c in range(4):
        out_ref[c] = parts[0][c * share : (c + 1) * share]


def gather(parts, share):
    columns = parts[0].shape[1]
    return pl.pallas_call(
        gather_kernel,
        in_specs=[WHOLE] * len(parts),
        out_specs=WHOLE,
        out_shape=jax.ShapeDtypeStruct((4, share, columns), jnp.float32),
        compiler_params=pltpu.CompilerParams(vmem_limit_bytes=4 * 1024 * 1024),
    )(*parts)


def finish_kernel(parts_ref, out_ref):
    count = parts_ref.shape[0]
    _, share, columns = out_ref.shape
    remaining = jnp.ones((share, columns), jnp.float32)
    sums = [jnp.zeros((share, columns), jnp.float32) for _ in range(3)]
    for k in range(count):
        part = parts_ref[k].astype(jnp.float32)
        for c in range(3):
            sums[c] = sums[c] + remaining * part[c * share : (c + 1) * share]
        remaining = remaining - remaining * part[3 * share :]
    for c in range(3):
        out_ref[c] = sums[c]
    out_ref[3] = 1.0 - remaining


def finish(parts, share):
    columns = parts.shape[2]
    return pl.pallas_call(
        finish_kernel,
        in_specs=[WHOLE],
        out_specs=WHOLE,
        out_shape=jax.ShapeDtypeStruct((4, share, columns), jnp.float32),
        compiler_params=pltpu.CompilerParams(vmem_limit_bytes=4 * 1024 * 1024),
    )(parts)


def swapped(values, axis, start):
    depth_count, row_count = lax.axis_size("depth"), lax.axis_size("rows")
    size = lax.axis_size(axis)
    perm = []
    for d in range(depth_count):
        for r in range(row_count):
            i = d if axis == "depth" else r
            j = i + 1 if i % 2 == start else i - 1
            if 0 <= j < size:
                e, q = (j, r) if axis == "depth" else (d, j)
            elif axis == "depth":
                e, q = (size - 1 - d, r)
            else:
                e, q = (d ^ 1, r)
            perm.append((d * row_count + r, e * row_count + q))
    return lax.ppermute(values, ("depth", "rows"), perm)


def exchanged(values, mask):
    return lax.ppermute(values, "depth", [(d, d ^ mask) for d in range(lax.axis_size("depth"))])


def body(volume, color_map, alpha_map):
    depth_count = lax.axis_size("depth")
    share = volume.shape[2] // depth_count
    rows_far, rows_near, far, near = cut_edges(volume)
    rows_far = swapped(rows_far, "rows", 1)
    rows_near = swapped(rows_near, "rows", 0)
    far = swapped(far, "depth", 1)
    near = swapped(near, "depth", 0)
    interior = march_interior(volume, color_map, alpha_map, depth_count)
    halos = (rows_near, rows_far, far, near)
    paired = depth_count == 8 and 2 * share == SUBLANES
    outs = add_edges(volume, interior, halos, depth_count, paired)
    if not paired:
        return finish(lax.all_to_all(outs[0], "depth", 0, 0, tiled=True), share)
    keep, give = outs
    sends = merge(keep, exchanged(give, 1))
    return gather([exchanged(send, 2 * k + 1) for k, send in reversed(list(enumerate(sends)))], share)


def solution(mesh):
    in_specs = (P(None, "depth", "rows", None), P(), P())
    out_specs = P(None, ("rows", "depth"), None)
    return jax.shard_map(body, mesh=mesh, in_specs=in_specs, out_specs=out_specs, check_vma=False)
```

```python
import functools

import jax
import jax.numpy as jnp
from jax import lax
from jax.experimental import pallas as pl
from jax.experimental.pallas import tpu as pltpu
from jax.sharding import PartitionSpec as P

AMBIENT = 0.3
DIFFUSE = 0.7
LIGHT_DEPTH = 0.48 * DIFFUSE
LIGHT_ROWS = 0.6 * DIFFUSE
LIGHT_COLS = 0.64 * DIFFUSE
OPACITY = 4.0
LANES = 128
SUBLANES = 8
WHOLE = pl.BlockSpec(memory_space=pltpu.VMEM)


def parity(axis):
    return lax.axis_index(axis) % 2


def ends(axis):
    position = lax.axis_index(axis)
    return position == 0, position == lax.axis_size(axis) - 1


def edges_kernel(volume_ref, rows_far_out, rows_near_out, far_out, near_out, strip_ref, plane_ref, sems):
    _, slices, height, _ = volume_ref.shape
    odd, odd_row = parity("depth"), parity("rows")
    last_tile = height // SUBLANES - 1

    def tile(i):
        return pl.ds(pl.multiple_of(i * SUBLANES, SUBLANES), SUBLANES)

    copies = [
        pltpu.make_async_copy(volume_ref.at[0, :, tile((1 - odd_row) * last_tile)], strip_ref.at[0], sems.at[0]),
        pltpu.make_async_copy(volume_ref.at[0, :, tile(odd_row * last_tile)], strip_ref.at[1], sems.at[1]),
        pltpu.make_async_copy(volume_ref.at[0, odd * (slices - 1)], plane_ref.at[0], sems.at[2]),
        pltpu.make_async_copy(volume_ref.at[0, (1 - odd) * (slices - 1)], plane_ref.at[1], sems.at[3]),
    ]
    for copy in copies:
        copy.start()

    def narrow(values):
        return values.astype(jnp.float32).astype(jnp.bfloat16)

    copies[0].wait()
    rows_near_out[...] = narrow(jnp.where(odd_row == 1, strip_ref[0, :, 0, :], strip_ref[0, :, SUBLANES - 1, :]))
    copies[1].wait()
    rows_far_out[...] = narrow(jnp.where(odd_row == 1, strip_ref[1, :, SUBLANES - 1, :], strip_ref[1, :, 0, :]))
    copies[2].wait()
    far_out[...] = narrow(plane_ref[0])
    copies[3].wait()
    near_out[...] = narrow(plane_ref[1])


def cut_edges(volume):
    _, slices, height, columns = volume.shape
    plane = jax.ShapeDtypeStruct((height, columns), jnp.bfloat16)
    strip = jax.ShapeDtypeStruct((slices, columns), jnp.bfloat16)
    return pl.pallas_call(
        edges_kernel,
        in_specs=[pl.BlockSpec(memory_space=pl.ANY)],
        out_specs=[WHOLE] * 4,
        out_shape=[strip, strip, plane, plane],
        scratch_shapes=[
            pltpu.VMEM((2, slices, SUBLANES, columns), jnp.int32),
            pltpu.VMEM((2, height, columns), jnp.int32),
            pltpu.SemaphoreType.DMA((4,)),
        ],
        compiler_params=pltpu.CompilerParams(vmem_limit_bytes=52 * 1024 * 1024),
    )(volume)


def pick(entries, places):
    dims = lax.GatherDimensionNumbers(
        offset_dims=(),
        collapsed_slice_dims=(1,),
        start_index_map=(1,),
        operand_batching_dims=(0,),
        start_indices_batching_dims=(0,),
    )
    return lax.gather(entries, places[..., None], dims, (1, 1), mode=lax.GatherScatterMode.PROMISE_IN_BOUNDS)


def shade(grad_depth, facing, squares):
    facing = facing + LIGHT_DEPTH * grad_depth
    squares = squares + grad_depth * grad_depth
    return AMBIENT + jnp.abs(facing) * lax.rsqrt(jnp.maximum(squares, 4.0))


def interior_kernel(
    opacity_scale,
    volume_ref,
    color_ref,
    alpha_ref,
    base_ref,
    face_ref,
    square_ref,
    lit_ref,
    grad_ref,
    strip_ref,
    pair_ref,
    held_ref,
):
    _, slices, height, columns = volume_ref.shape
    tiles = height // SUBLANES
    chunks = columns // LANES
    tile = (SUBLANES, LANES)
    strip = (slices, LANES)

    packed = color_ref[0:1, :] + color_ref[1:2, :] * 256 + color_ref[2:3, :] * 65536
    color_low, color_high = packed[:, :LANES], packed[:, LANES:]
    alpha_both = alpha_ref[0:1, :LANES] + alpha_ref[0:1, LANES:] * 256

    def colors(value, tables):
        low, high = tables
        place = value & (LANES - 1)
        color = jnp.where(value < LANES, pick(low, place), pick(high, place))
        parts = (color & 255, lax.shift_right_logical(color, 8) & 255, lax.shift_right_logical(color, 16))
        return [part.astype(jnp.float32) for part in parts]

    def opacity(level, table):
        entry = pick(table, level & (LANES - 1))
        entry = lax.shift_right_logical(entry, lax.shift_right_logical(level & LANES, 4)) & 255
        return entry.astype(jnp.float32) * opacity_scale

    tile_colors = [jnp.broadcast_to(t, tile) for t in (color_low, color_high)]
    tile_alpha = jnp.broadcast_to(alpha_both, tile)
    strip_colors = [jnp.broadcast_to(t, strip) for t in (color_low, color_high)]

    def masks(shape):
        lane = lax.broadcasted_iota(jnp.int32, shape, 1)
        row = lax.broadcasted_iota(jnp.int32, shape, 0)
        return lane == 0, lane == LANES - 1, row == 0, row == shape[0] - 1

    first_lane, last_lane, first_row, last_row = masks(tile)
    strip_first_lane, strip_last_lane, front, back = masks(strip)

    pairs = slices // 2
    top = SUBLANES

    def clear(j, carry):
        pair_ref[j] = jnp.zeros(pair_ref.shape[1:], jnp.int32)
        return carry

    clear(0, 0)
    clear(chunks + 1, 0)
    margin = jnp.zeros((pairs, SUBLANES, LANES), jnp.int32)

    def pack(j, carry):
        here = pl.ds(pl.multiple_of(j * LANES, LANES), LANES)
        pair_ref[j + 1, :, :top] = margin
        pair_ref[j + 1, :, top + height :] = margin
        for p in range(pairs):
            pair_ref[j + 1, p, top : top + height] = volume_ref[0, p, :, here] + lax.shift_left(
                volume_ref[0, p + pairs, :, here], 16
            )
        return carry

    lax.fori_loop(0, chunks, pack, 0)

    def split(difference):
        low = lax.shift_right_arithmetic(lax.shift_left(difference, 16), 16)
        high = lax.shift_right_arithmetic(difference + 32768, 16)
        return low.astype(jnp.float32), high.astype(jnp.float32)

    def across(left_value, value, right_value, first, last):
        west = pltpu.roll(jnp.where(last, left_value, value), 1, 1)
        east = pltpu.roll(jnp.where(first, right_value, value), LANES - 1, 1)
        return split(east - west)

    def chunk(j, carry):
        here = pl.ds(pl.multiple_of(j * LANES, LANES), LANES)

        for r in range(tiles):
            rows = slice(r * SUBLANES, (r + 1) * SUBLANES)
            values = [volume_ref[0, s, rows, here] for s in range(slices)]

            def words(c, p, offset=0):
                return pair_ref[c, p, top + r * SUBLANES + offset : top + (r + 1) * SUBLANES + offset, :]

            down, right = [], []
            for p in range(pairs):
                down.append(split(words(j + 1, p, 1) - words(j + 1, p, -1)))
                right.append(across(words(j, p), words(j + 1, p), words(j + 2, p), first_lane, last_lane))
            remaining = jnp.ones(tile, jnp.float32)
            sums = [jnp.zeros(tile, jnp.float32) for _ in range(3)]
            for s in range(slices):
                value = values[s]
                grad_rows = down[s % pairs][s // pairs]
                grad_cols = right[s % pairs][s // pairs]
                squares = grad_rows * grad_rows + grad_cols * grad_cols
                facing = LIGHT_ROWS * grad_rows + LIGHT_COLS * grad_cols
                weight = remaining * opacity(volume_ref[1, s, rows, here], tile_alpha)
                remaining = remaining - weight
                if r == 0:
                    held_ref[0, s : s + 1, :] = weight[:1]
                    weight = jnp.where(first_row, 0.0, weight)
                if r == tiles - 1:
                    held_ref[1, s : s + 1, :] = weight[SUBLANES - 1 :]
                    weight = jnp.where(last_row, 0.0, weight)
                emitted = colors(value, tile_colors)
                if 0 < s < slices - 1:
                    grad_depth = (values[s + 1] - values[s - 1]).astype(jnp.float32)
                    weight = weight * shade(grad_depth, facing, squares)
                    for c in range(3):
                        sums[c] = sums[c] + emitted[c] * weight
                else:
                    end = int(s > 0)
                    face_ref[end, rows, here] = facing
                    square_ref[end, rows, here] = squares
                    weight = weight * (1.0 / 255.0)
                    for c in range(3):
                        lit_ref[end, c, rows, here] = emitted[c] * weight
            for c in range(3):
                base_ref[c, rows, here] = sums[c] * (1.0 / 255.0)
            base_ref[3, rows, here] = 1.0 - remaining

        for q, (edge, inner) in enumerate(((0, 1), (height - 1, height - 2))):
            value = volume_ref[0, :, edge, here]
            behind = pltpu.roll(jnp.where(back, 0, value), 1, 0)
            ahead = pltpu.roll(jnp.where(front, 0, value), slices - 1, 0)
            grad_ref[q, 0, :, here] = (ahead - behind).astype(jnp.float32)
            grad_ref[q, 1, :, here] = volume_ref[0, :, inner, here].astype(jnp.float32)
            word = pair_ref[j + 1, :, top + edge, :]
            low, high = across(
                pair_ref[j, :, top + edge, :],
                word,
                pair_ref[j + 2, :, top + edge, :],
                strip_first_lane[:pairs],
                strip_last_lane[:pairs],
            )
            grad_ref[q, 2, :pairs, here] = low
            grad_ref[q, 2, pairs:, here] = high
            weight = held_ref[q] * (1.0 / 255.0)
            emitted = colors(value, strip_colors)
            for c in range(3):
                strip_ref[q, c, :, here] = emitted[c] * weight
        return carry

    lax.fori_loop(0, chunks, chunk, 0)


def march_interior(volume, color_map, alpha_map, depth_count):
    _, slices, height, columns = volume.shape
    opacity_scale = OPACITY / (255.0 * slices * depth_count)
    shapes = [
        (4, height, columns),
        (2, height, columns),
        (2, height, columns),
        (2, 3, height, columns),
        (2, 3, slices, columns),
        (2, 3, slices, columns),
    ]
    voxels = slices * height * columns
    return pl.pallas_call(
        functools.partial(interior_kernel, opacity_scale),
        in_specs=[WHOLE] * 3,
        out_specs=[WHOLE] * len(shapes),
        out_shape=[jax.ShapeDtypeStruct(shape, jnp.float32) for shape in shapes],
        scratch_shapes=[
            pltpu.VMEM((columns // LANES + 2, slices // 2, height + 2 * SUBLANES, LANES), jnp.int32),
            pltpu.VMEM((2, slices, LANES), jnp.float32),
        ],
        compiler_params=pltpu.CompilerParams(vmem_limit_bytes=24 * 1024 * 1024),
        cost_estimate=pl.CostEstimate(flops=voxels * 80, bytes_accessed=voxels * 20, transcendentals=voxels),
    )(volume, color_map, alpha_map.reshape(1, -1))


def edge_kernel(
    share, volume_ref, base_ref, face_ref, square_ref, lit_ref, grad_ref, strip_ref, rows_near_ref, rows_far_ref, far_ref, near_ref, *out_refs
):
    _, slices, height, columns = volume_ref.shape
    tiles = height // SUBLANES
    tile = (SUBLANES, LANES)
    row = lax.broadcasted_iota(jnp.int32, tile, 0)
    first_row, last_row = row == 0, row == SUBLANES - 1
    level = lax.broadcasted_iota(jnp.int32, (slices, LANES), 0)
    front, back = level == 0, level == slices - 1
    if len(out_refs) > 1:
        keep_ref, give_ref, same_ref, cross_ref, theirs_ref, mine_ref = out_refs
    odd, odd_row = parity("depth") == 1, parity("rows") == 1
    front_end, back_end = ends("depth")
    top_end, bottom_end = ends("rows")

    def chunk(j, carry):
        here = pl.ds(pl.multiple_of(j * LANES, LANES), LANES)
        rows_near = rows_near_ref[:, here].astype(jnp.float32)
        rows_far = rows_far_ref[:, here].astype(jnp.float32)
        above = jnp.where(top_end, 0.0, jnp.where(odd_row, rows_near, rows_far))
        below = jnp.where(bottom_end, 0.0, jnp.where(odd_row, rows_far, rows_near))
        far = far_ref[:, here].astype(jnp.float32)
        near = near_ref[:, here].astype(jnp.float32)
        before = jnp.where(front_end, 0.0, jnp.where(odd, near, far))
        after = jnp.where(back_end, 0.0, jnp.where(odd, far, near))
        extra = []
        for q, edge in enumerate((0, height - 1)):
            inner = grad_ref[q, 1, :, here]
            grad_rows = below - inner if q else inner - above
            grad_cols = grad_ref[q, 2, :, here]
            grad_depth = grad_ref[q, 0, :, here] + jnp.where(
                back, after[edge : edge + 1], jnp.where(front, -before[edge : edge + 1], 0.0)
            )
            shading = shade(
                grad_depth,
                LIGHT_ROWS * grad_rows + LIGHT_COLS * grad_cols,
                grad_rows * grad_rows + grad_cols * grad_cols,
            )
            extra.append([jnp.sum(strip_ref[q, c, :, here] * shading, axis=0, keepdims=True) for c in range(3)])
        for r in range(tiles):
            rows = slice(r * SUBLANES, (r + 1) * SUBLANES)
            planes = [base_ref[c, rows, here] for c in range(4)]
            for end in range(2):
                if end:
                    grad_depth = after[rows] - volume_ref[0, slices - 2, rows, here].astype(jnp.float32)
                else:
                    grad_depth = volume_ref[0, 1, rows, here].astype(jnp.float32) - before[rows]
                shading = shade(grad_depth, face_ref[end, rows, here], square_ref[end, rows, here])
                for c in range(3):
                    planes[c] = planes[c] + lit_ref[end, c, rows, here] * shading
            for c in range(3):
                if r == 0:
                    planes[c] = planes[c] + jnp.where(first_row, extra[0][c], 0.0)
                if r == tiles - 1:
                    planes[c] = planes[c] + jnp.where(last_row, extra[1][c], 0.0)
            blocks = [
                jnp.concatenate([plane[first : first + share] for plane in planes], axis=0)
                for first in range(0, SUBLANES, share)
            ]
            if len(out_refs) == 1:
                for i, block in enumerate(blocks):
                    out_refs[0][r * len(blocks) + i, :, here] = block.astype(jnp.bfloat16)
            else:
                theirs_ref[r, :, here] = jnp.where(odd, blocks[0], blocks[1])
                mine_ref[r, :, here] = jnp.where(odd, blocks[1], blocks[0]).astype(jnp.bfloat16)
        return carry

    lax.fori_loop(0, columns // LANES, chunk, 0)
    if len(out_refs) > 1:
        chip = lax.axis_index("depth") // 2
        last = theirs_ref.shape[0] - 1
        for k in range(last):
            keep_ref[k] = theirs_ref[chip ^ k]
            give_ref[k] = mine_ref[chip ^ k]
        same_ref[...] = mine_ref[chip ^ last]
        cross_ref[...] = theirs_ref[chip ^ last].astype(jnp.bfloat16)


def add_edges(volume, interior, halos, depth_count, paired):
    _, slices, height, columns = volume.shape
    share = height // depth_count
    scratch = []
    if paired:
        chips = depth_count // 2
        block = (4 * share, columns)
        shapes = [
            jax.ShapeDtypeStruct((chips - 1, *block), jnp.float32),
            jax.ShapeDtypeStruct((chips - 1, *block), jnp.bfloat16),
            jax.ShapeDtypeStruct(block, jnp.bfloat16),
            jax.ShapeDtypeStruct(block, jnp.bfloat16),
        ]
        scratch = [pltpu.VMEM((chips, *block), jnp.float32), pltpu.VMEM((chips, *block), jnp.bfloat16)]
    else:
        shapes = [jax.ShapeDtypeStruct((depth_count, 4 * share, columns), jnp.bfloat16)]
    return pl.pallas_call(
        functools.partial(edge_kernel, share),
        in_specs=[WHOLE] * 11,
        out_specs=[WHOLE] * len(shapes),
        out_shape=shapes,
        scratch_shapes=scratch,
        compiler_params=pltpu.CompilerParams(vmem_limit_bytes=24 * 1024 * 1024),
    )(volume, *interior, *halos)


def over(nearer, farther):
    share = nearer.shape[0] // 4
    clear = 1.0 - nearer[3 * share :]
    return nearer + jnp.concatenate([clear] * 4, axis=0) * farther


def merge_kernel(keep_ref, other_ref, *send_refs):
    odd = parity("depth") == 1
    for k, out_ref in enumerate(send_refs):
        keep = keep_ref[k]
        other = other_ref[k].astype(jnp.float32)
        out_ref[...] = over(jnp.where(odd, other, keep), jnp.where(odd, keep, other)).astype(out_ref.dtype)


def merge(keep, other):
    count, rows, columns = keep.shape
    return pl.pallas_call(
        merge_kernel,
        in_specs=[WHOLE] * 2,
        out_specs=[WHOLE] * count,
        out_shape=[jax.ShapeDtypeStruct((rows, columns), jnp.bfloat16)] * count,
        compiler_params=pltpu.CompilerParams(vmem_limit_bytes=4 * 1024 * 1024),
    )(keep, other)


def gather_kernel(same_ref, cross_ref, *refs):
    *part_refs, out_ref = refs
    share = out_ref.shape[1]
    position = lax.axis_index("depth")
    odd, chip = position % 2 == 1, position // 2
    parts = [part_ref[...].astype(jnp.float32) for part_ref in reversed(part_refs)]
    same, cross = same_ref[...].astype(jnp.float32), cross_ref[...].astype(jnp.float32)
    parts.append(over(jnp.where(odd, cross, same), jnp.where(odd, same, cross)))
    step = 1
    while len(parts) > 1:
        swap = (chip & step) != 0
        parts = [
            over(jnp.where(swap, parts[i + 1], parts[i]), jnp.where(swap, parts[i], parts[i + 1]))
            for i in range(0, len(parts), 2)
        ]
        step *= 2
    for c in range(4):
        out_ref[c] = parts[0][c * share : (c + 1) * share]


def gather(parts, share):
    columns = parts[0].shape[1]
    return pl.pallas_call(
        gather_kernel,
        in_specs=[WHOLE] * len(parts),
        out_specs=WHOLE,
        out_shape=jax.ShapeDtypeStruct((4, share, columns), jnp.float32),
        compiler_params=pltpu.CompilerParams(vmem_limit_bytes=4 * 1024 * 1024),
    )(*parts)


def finish_kernel(parts_ref, out_ref):
    count = parts_ref.shape[0]
    _, share, columns = out_ref.shape
    remaining = jnp.ones((share, columns), jnp.float32)
    sums = [jnp.zeros((share, columns), jnp.float32) for _ in range(3)]
    for k in range(count):
        part = parts_ref[k].astype(jnp.float32)
        for c in range(3):
            sums[c] = sums[c] + remaining * part[c * share : (c + 1) * share]
        remaining = remaining - remaining * part[3 * share :]
    for c in range(3):
        out_ref[c] = sums[c]
    out_ref[3] = 1.0 - remaining


def finish(parts, share):
    columns = parts.shape[2]
    return pl.pallas_call(
        finish_kernel,
        in_specs=[WHOLE],
        out_specs=WHOLE,
        out_shape=jax.ShapeDtypeStruct((4, share, columns), jnp.float32),
        compiler_params=pltpu.CompilerParams(vmem_limit_bytes=4 * 1024 * 1024),
    )(parts)


def swapped(values, axis, start):
    depth_count, row_count = lax.axis_size("depth"), lax.axis_size("rows")
    size = lax.axis_size(axis)
    perm = []
    for d in range(depth_count):
        for r in range(row_count):
            i = d if axis == "depth" else r
            j = i + 1 if i % 2 == start else i - 1
            if 0 <= j < size:
                e, q = (j, r) if axis == "depth" else (d, j)
            elif axis == "depth":
                e, q = (size - 1 - d, r)
            else:
                e, q = (d ^ 1, r)
            perm.append((d * row_count + r, e * row_count + q))
    return lax.ppermute(values, ("depth", "rows"), perm)


def exchanged(values, mask):
    return lax.ppermute(values, "depth", [(d, d ^ mask) for d in range(lax.axis_size("depth"))])


def body(volume, color_map, alpha_map):
    depth_count = lax.axis_size("depth")
    share = volume.shape[2] // depth_count
    rows_far, rows_near, far, near = cut_edges(volume)
    rows_far = swapped(rows_far, "rows", 1)
    rows_near = swapped(rows_near, "rows", 0)
    far = swapped(far, "depth", 1)
    near = swapped(near, "depth", 0)
    interior = march_interior(volume, color_map, alpha_map, depth_count)
    halos = (rows_near, rows_far, far, near)
    paired = depth_count == 8 and 2 * share == SUBLANES
    outs = add_edges(volume, interior, halos, depth_count, paired)
    if not paired:
        return finish(lax.all_to_all(outs[0], "depth", 0, 0, tiled=True), share)
    keep, give, same, cross = outs
    other = exchanged(give, 1)
    same, cross = exchanged(same, depth_count - 2), exchanged(cross, depth_count - 1)
    sends = merge(keep, other)
    received = [exchanged(send, 2 * k + 1) for k, send in reversed(list(enumerate(sends)))]
    return gather((same, cross, *received), share)


def solution(mesh):
    in_specs = (P(None, "depth", "rows", None), P(), P())
    out_specs = P(None, ("rows", "depth"), None)
    return jax.shard_map(body, mesh=mesh, in_specs=in_specs, out_specs=out_specs, check_vma=False)
```

```python
import functools

import jax
import jax.numpy as jnp
from jax import lax
from jax.experimental import pallas as pl
from jax.experimental.pallas import tpu as pltpu
from jax.sharding import PartitionSpec as P

AMBIENT = 0.3
DIFFUSE = 0.7
LIGHT_DEPTH = 0.48 * DIFFUSE
LIGHT_ROWS = 0.6 * DIFFUSE
LIGHT_COLS = 0.64 * DIFFUSE
OPACITY = 4.0
LANES = 128
SUBLANES = 8
WHOLE = pl.BlockSpec(memory_space=pltpu.VMEM)


def parity(axis):
    return lax.axis_index(axis) % 2


def ends(axis):
    position = lax.axis_index(axis)
    return position == 0, position == lax.axis_size(axis) - 1


def edges_kernel(volume_ref, rows_far_out, rows_near_out, far_out, near_out, strip_ref, plane_ref, sems):
    _, slices, height, _ = volume_ref.shape
    odd, odd_row = parity("depth"), parity("rows")

    copies = [
        pltpu.make_async_copy(volume_ref.at[0, :, (1 - odd_row) * (height - 1)], strip_ref.at[0], sems.at[0]),
        pltpu.make_async_copy(volume_ref.at[0, :, odd_row * (height - 1)], strip_ref.at[1], sems.at[1]),
        pltpu.make_async_copy(volume_ref.at[0, odd * (slices - 1)], plane_ref.at[0], sems.at[2]),
        pltpu.make_async_copy(volume_ref.at[0, (1 - odd) * (slices - 1)], plane_ref.at[1], sems.at[3]),
    ]
    for copy in copies:
        copy.start()

    def narrow(values):
        return values.astype(jnp.float32).astype(jnp.bfloat16)

    copies[0].wait()
    rows_near_out[...] = narrow(strip_ref[0])
    copies[1].wait()
    rows_far_out[...] = narrow(strip_ref[1])
    copies[2].wait()
    far_out[...] = narrow(plane_ref[0])
    copies[3].wait()
    near_out[...] = narrow(plane_ref[1])


def cut_edges(volume):
    _, slices, height, columns = volume.shape
    plane = jax.ShapeDtypeStruct((height, columns), jnp.bfloat16)
    strip = jax.ShapeDtypeStruct((slices, columns), jnp.bfloat16)
    return pl.pallas_call(
        edges_kernel,
        in_specs=[pl.BlockSpec(memory_space=pl.ANY)],
        out_specs=[WHOLE] * 4,
        out_shape=[strip, strip, plane, plane],
        scratch_shapes=[
            pltpu.VMEM((2, slices, columns), jnp.int32),
            pltpu.VMEM((2, height, columns), jnp.int32),
            pltpu.SemaphoreType.DMA((4,)),
        ],
        compiler_params=pltpu.CompilerParams(vmem_limit_bytes=52 * 1024 * 1024),
    )(volume)


def pick(entries, places):
    dims = lax.GatherDimensionNumbers(
        offset_dims=(),
        collapsed_slice_dims=(1,),
        start_index_map=(1,),
        operand_batching_dims=(0,),
        start_indices_batching_dims=(0,),
    )
    return lax.gather(entries, places[..., None], dims, (1, 1), mode=lax.GatherScatterMode.PROMISE_IN_BOUNDS)


def shade(grad_depth, facing, squares):
    facing = facing + LIGHT_DEPTH * grad_depth
    squares = squares + grad_depth * grad_depth
    return AMBIENT + jnp.abs(facing) * lax.rsqrt(jnp.maximum(squares, 4.0))


def interior_kernel(
    opacity_scale,
    volume_ref,
    color_ref,
    alpha_ref,
    base_ref,
    face_ref,
    square_ref,
    lit_ref,
    grad_ref,
    strip_ref,
    pair_ref,
    held_ref,
):
    _, slices, height, columns = volume_ref.shape
    tiles = height // SUBLANES
    chunks = columns // LANES
    tile = (SUBLANES, LANES)
    strip = (slices, LANES)

    packed = color_ref[0:1, :] + color_ref[1:2, :] * 256 + color_ref[2:3, :] * 65536
    color_low, color_high = packed[:, :LANES], packed[:, LANES:]
    alpha_both = alpha_ref[0:1, :LANES] + alpha_ref[0:1, LANES:] * 256

    def colors(value, tables):
        low, high = tables
        place = value & (LANES - 1)
        color = jnp.where(value < LANES, pick(low, place), pick(high, place))
        parts = (color & 255, lax.shift_right_logical(color, 8) & 255, lax.shift_right_logical(color, 16))
        return [part.astype(jnp.float32) for part in parts]

    def opacity(level, table):
        entry = pick(table, level & (LANES - 1))
        entry = lax.shift_right_logical(entry, lax.shift_right_logical(level & LANES, 4)) & 255
        return entry.astype(jnp.float32) * opacity_scale

    tile_colors = [jnp.broadcast_to(t, tile) for t in (color_low, color_high)]
    tile_alpha = jnp.broadcast_to(alpha_both, tile)
    strip_colors = [jnp.broadcast_to(t, strip) for t in (color_low, color_high)]

    def masks(shape):
        lane = lax.broadcasted_iota(jnp.int32, shape, 1)
        row = lax.broadcasted_iota(jnp.int32, shape, 0)
        return lane == 0, lane == LANES - 1, row == 0, row == shape[0] - 1

    first_lane, last_lane, first_row, last_row = masks(tile)
    strip_first_lane, strip_last_lane, front, back = masks(strip)

    pairs = slices // 2
    top = SUBLANES

    def clear(j, carry):
        pair_ref[j] = jnp.zeros(pair_ref.shape[1:], jnp.int32)
        return carry

    clear(0, 0)
    clear(chunks + 1, 0)
    margin = jnp.zeros((pairs, SUBLANES, LANES), jnp.int32)

    def pack(j, carry):
        here = pl.ds(pl.multiple_of(j * LANES, LANES), LANES)
        pair_ref[j + 1, :, :top] = margin
        pair_ref[j + 1, :, top + height :] = margin
        for p in range(pairs):
            pair_ref[j + 1, p, top : top + height] = volume_ref[0, p, :, here] + lax.shift_left(
                volume_ref[0, p + pairs, :, here], 16
            )
        return carry

    lax.fori_loop(0, chunks, pack, 0)

    def split(difference):
        low = lax.shift_right_arithmetic(lax.shift_left(difference, 16), 16)
        high = lax.shift_right_arithmetic(difference + 32768, 16)
        return low.astype(jnp.float32), high.astype(jnp.float32)

    def across(left_value, value, right_value, first, last):
        west = pltpu.roll(jnp.where(last, left_value, value), 1, 1)
        east = pltpu.roll(jnp.where(first, right_value, value), LANES - 1, 1)
        return split(east - west)

    def chunk(j, carry):
        here = pl.ds(pl.multiple_of(j * LANES, LANES), LANES)

        for r in range(tiles):
            rows = slice(r * SUBLANES, (r + 1) * SUBLANES)
            values = [volume_ref[0, s, rows, here] for s in range(slices)]

            def words(c, p, offset=0):
                return pair_ref[c, p, top + r * SUBLANES + offset : top + (r + 1) * SUBLANES + offset, :]

            down, right = [], []
            for p in range(pairs):
                down.append(split(words(j + 1, p, 1) - words(j + 1, p, -1)))
                right.append(across(words(j, p), words(j + 1, p), words(j + 2, p), first_lane, last_lane))
            remaining = jnp.ones(tile, jnp.float32)
            sums = [jnp.zeros(tile, jnp.float32) for _ in range(3)]
            for s in range(slices):
                value = values[s]
                grad_rows = down[s % pairs][s // pairs]
                grad_cols = right[s % pairs][s // pairs]
                squares = grad_rows * grad_rows + grad_cols * grad_cols
                facing = LIGHT_ROWS * grad_rows + LIGHT_COLS * grad_cols
                weight = remaining * opacity(volume_ref[1, s, rows, here], tile_alpha)
                remaining = remaining - weight
                if r == 0:
                    held_ref[0, s : s + 1, :] = weight[:1]
                    weight = jnp.where(first_row, 0.0, weight)
                if r == tiles - 1:
                    held_ref[1, s : s + 1, :] = weight[SUBLANES - 1 :]
                    weight = jnp.where(last_row, 0.0, weight)
                emitted = colors(value, tile_colors)
                if 0 < s < slices - 1:
                    grad_depth = (values[s + 1] - values[s - 1]).astype(jnp.float32)
                    weight = weight * shade(grad_depth, facing, squares)
                    for c in range(3):
                        sums[c] = sums[c] + emitted[c] * weight
                else:
                    end = int(s > 0)
                    face_ref[end, rows, here] = facing
                    square_ref[end, rows, here] = squares
                    weight = weight * (1.0 / 255.0)
                    for c in range(3):
                        lit_ref[end, c, rows, here] = emitted[c] * weight
            for c in range(3):
                base_ref[c, rows, here] = sums[c] * (1.0 / 255.0)
            base_ref[3, rows, here] = 1.0 - remaining

        for q, (edge, inner) in enumerate(((0, 1), (height - 1, height - 2))):
            value = volume_ref[0, :, edge, here]
            behind = pltpu.roll(jnp.where(back, 0, value), 1, 0)
            ahead = pltpu.roll(jnp.where(front, 0, value), slices - 1, 0)
            grad_ref[q, 0, :, here] = (ahead - behind).astype(jnp.float32)
            grad_ref[q, 1, :, here] = volume_ref[0, :, inner, here].astype(jnp.float32)
            word = pair_ref[j + 1, :, top + edge, :]
            low, high = across(
                pair_ref[j, :, top + edge, :],
                word,
                pair_ref[j + 2, :, top + edge, :],
                strip_first_lane[:pairs],
                strip_last_lane[:pairs],
            )
            grad_ref[q, 2, :pairs, here] = low
            grad_ref[q, 2, pairs:, here] = high
            weight = held_ref[q] * (1.0 / 255.0)
            emitted = colors(value, strip_colors)
            for c in range(3):
                strip_ref[q, c, :, here] = emitted[c] * weight
        return carry

    lax.fori_loop(0, chunks, chunk, 0)


def march_interior(volume, color_map, alpha_map, depth_count):
    _, slices, height, columns = volume.shape
    opacity_scale = OPACITY / (255.0 * slices * depth_count)
    shapes = [
        (4, height, columns),
        (2, height, columns),
        (2, height, columns),
        (2, 3, height, columns),
        (2, 3, slices, columns),
        (2, 3, slices, columns),
    ]
    voxels = slices * height * columns
    return pl.pallas_call(
        functools.partial(interior_kernel, opacity_scale),
        in_specs=[WHOLE] * 3,
        out_specs=[WHOLE] * len(shapes),
        out_shape=[jax.ShapeDtypeStruct(shape, jnp.float32) for shape in shapes],
        scratch_shapes=[
            pltpu.VMEM((columns // LANES + 2, slices // 2, height + 2 * SUBLANES, LANES), jnp.int32),
            pltpu.VMEM((2, slices, LANES), jnp.float32),
        ],
        compiler_params=pltpu.CompilerParams(vmem_limit_bytes=24 * 1024 * 1024),
        cost_estimate=pl.CostEstimate(flops=voxels * 80, bytes_accessed=voxels * 20, transcendentals=voxels),
    )(volume, color_map, alpha_map.reshape(1, -1))


def row_sums(first, second):
    count = first.shape[0]
    if count != SUBLANES:
        return jnp.sum(first, axis=0, keepdims=True), jnp.sum(second, axis=0, keepdims=True)
    upper = lax.broadcasted_iota(jnp.int32, first.shape, 0) < 4
    both = jnp.where(upper, first, second) + pltpu.roll(jnp.where(upper, second, first), 4, 0)
    both = both + pltpu.roll(both, 6, 0)
    both = both + pltpu.roll(both, 7, 0)
    return both, pltpu.roll(both, 3, 0)


def edge_kernel(
    share, volume_ref, base_ref, face_ref, square_ref, lit_ref, grad_ref, strip_ref, rows_near_ref, rows_far_ref, far_ref, near_ref, *out_refs
):
    _, slices, height, columns = volume_ref.shape
    tiles = height // SUBLANES
    tile = (SUBLANES, LANES)
    row = lax.broadcasted_iota(jnp.int32, tile, 0)
    first_row, last_row, upper = row == 0, row == SUBLANES - 1, row < SUBLANES // 2
    level = lax.broadcasted_iota(jnp.int32, (slices, LANES), 0)
    front, back = level == 0, level == slices - 1
    odd, odd_row = parity("depth") == 1, parity("rows") == 1
    front_end, back_end = ends("depth")
    top_end, bottom_end = ends("rows")

    def chunk(j, carry):
        here = pl.ds(pl.multiple_of(j * LANES, LANES), LANES)
        rows_near = rows_near_ref[:, here].astype(jnp.float32)
        rows_far = rows_far_ref[:, here].astype(jnp.float32)
        above = jnp.where(top_end, 0.0, jnp.where(odd_row, rows_near, rows_far))
        below = jnp.where(bottom_end, 0.0, jnp.where(odd_row, rows_far, rows_near))
        far = far_ref[:, here].astype(jnp.float32)
        near = near_ref[:, here].astype(jnp.float32)
        before = jnp.where(front_end, 0.0, jnp.where(odd, near, far))
        after = jnp.where(back_end, 0.0, jnp.where(odd, far, near))
        extra = []
        for q, edge in enumerate((0, height - 1)):
            inner = grad_ref[q, 1, :, here]
            grad_rows = below - inner if q else inner - above
            grad_cols = grad_ref[q, 2, :, here]
            grad_depth = grad_ref[q, 0, :, here] + jnp.where(
                back, after[edge : edge + 1], jnp.where(front, -before[edge : edge + 1], 0.0)
            )
            shading = shade(
                grad_depth,
                LIGHT_ROWS * grad_rows + LIGHT_COLS * grad_cols,
                grad_rows * grad_rows + grad_cols * grad_cols,
            )
            extra.append([strip_ref[q, c, :, here] * shading for c in range(3)])
        extra = [row_sums(extra[0][c], extra[1][c]) for c in range(3)]
        for r in range(tiles):
            rows = slice(r * SUBLANES, (r + 1) * SUBLANES)
            planes = [base_ref[c, rows, here] for c in range(4)]
            for end in range(2):
                if end:
                    grad_depth = after[rows] - volume_ref[0, slices - 2, rows, here].astype(jnp.float32)
                else:
                    grad_depth = volume_ref[0, 1, rows, here].astype(jnp.float32) - before[rows]
                shading = shade(grad_depth, face_ref[end, rows, here], square_ref[end, rows, here])
                for c in range(3):
                    planes[c] = planes[c] + lit_ref[end, c, rows, here] * shading
            for c in range(3):
                if r == 0:
                    planes[c] = planes[c] + jnp.where(first_row, extra[c][0], 0.0)
                if r == tiles - 1:
                    planes[c] = planes[c] + jnp.where(last_row, extra[c][1], 0.0)
            if len(out_refs) == 1:
                for i, first in enumerate(range(0, SUBLANES, share)):
                    block = jnp.concatenate([plane[first : first + share] for plane in planes], axis=0)
                    out_refs[0][r * (SUBLANES // share) + i, :, here] = block.astype(jnp.bfloat16)
            else:
                keep_ref, give_ref = out_refs
                halves = [(planes[c], pltpu.roll(planes[c + 1], SUBLANES // 2, 0)) for c in (0, 2)]
                even = jnp.concatenate([jnp.where(upper, own, turned) for own, turned in halves], axis=0)
                uneven = jnp.concatenate([jnp.where(upper, turned, own) for own, turned in halves], axis=0)
                keep_ref[r, :, here] = jnp.where(odd, even, uneven)
                give_ref[r, :, here] = jnp.where(odd, uneven, even).astype(jnp.bfloat16)
        return carry

    lax.fori_loop(0, columns // LANES, chunk, 0)


def add_edges(volume, interior, halos, depth_count, paired):
    _, slices, height, columns = volume.shape
    share = height // depth_count
    if paired:
        half = (depth_count // 2, 4 * share, columns)
        shapes = [jax.ShapeDtypeStruct(half, jnp.float32), jax.ShapeDtypeStruct(half, jnp.bfloat16)]
    else:
        shapes = [jax.ShapeDtypeStruct((depth_count, 4 * share, columns), jnp.bfloat16)]
    return pl.pallas_call(
        functools.partial(edge_kernel, share),
        in_specs=[WHOLE] * 11,
        out_specs=[WHOLE] * len(shapes),
        out_shape=shapes,
        compiler_params=pltpu.CompilerParams(vmem_limit_bytes=24 * 1024 * 1024),
    )(volume, *interior, *halos)


def over(nearer, farther, uneven):
    share = nearer.shape[0] // 4
    clear = 1.0 - jnp.where(uneven, nearer[2 * share : 3 * share], nearer[3 * share :])
    return nearer + jnp.concatenate([clear] * 4, axis=0) * farther


def merge_kernel(keep_ref, other_ref, *send_refs):
    position = lax.axis_index("depth")
    odd, chip = position % 2 == 1, position // 2
    for k, out_ref in enumerate(send_refs):
        keep = keep_ref[chip ^ k]
        other = other_ref[chip ^ k].astype(jnp.float32)
        block = over(jnp.where(odd, other, keep), jnp.where(odd, keep, other), jnp.logical_not(odd))
        out_ref[...] = block.astype(out_ref.dtype)


def merge(keep, other):
    chips, rows, columns = keep.shape
    return pl.pallas_call(
        merge_kernel,
        in_specs=[WHOLE] * 2,
        out_specs=[WHOLE] * chips,
        out_shape=[jax.ShapeDtypeStruct((rows, columns), jnp.bfloat16)] * chips,
        compiler_params=pltpu.CompilerParams(vmem_limit_bytes=8 * 1024 * 1024),
    )(keep, other)


def gather_kernel(*refs):
    *part_refs, out_ref = refs
    part_refs.reverse()
    count = len(part_refs)
    share = out_ref.shape[1]
    position = lax.axis_index("depth")
    odd, chip = position % 2 == 1, position // 2
    parts = [part_ref[...].astype(jnp.float32) for part_ref in part_refs]
    step = 1
    while step < count:
        swap = (chip & step) != 0
        parts = [
            over(jnp.where(swap, parts[i + 1], parts[i]), jnp.where(swap, parts[i], parts[i + 1]), odd)
            for i in range(0, len(parts), 2)
        ]
        step *= 2
    planes = [parts[0][c * share : (c + 1) * share] for c in range(4)]
    for c in range(4):
        out_ref[c] = jnp.where(odd, planes[c ^ 1], planes[c])


def gather(parts, share):
    columns = parts[0].shape[1]
    return pl.pallas_call(
        gather_kernel,
        in_specs=[WHOLE] * len(parts),
        out_specs=WHOLE,
        out_shape=jax.ShapeDtypeStruct((4, share, columns), jnp.float32),
        compiler_params=pltpu.CompilerParams(vmem_limit_bytes=4 * 1024 * 1024),
    )(*parts)


def finish_kernel(parts_ref, out_ref):
    count = parts_ref.shape[0]
    _, share, columns = out_ref.shape
    remaining = jnp.ones((share, columns), jnp.float32)
    sums = [jnp.zeros((share, columns), jnp.float32) for _ in range(3)]
    for k in range(count):
        part = parts_ref[k].astype(jnp.float32)
        for c in range(3):
            sums[c] = sums[c] + remaining * part[c * share : (c + 1) * share]
        remaining = remaining - remaining * part[3 * share :]
    for c in range(3):
        out_ref[c] = sums[c]
    out_ref[3] = 1.0 - remaining


def finish(parts, share):
    columns = parts.shape[2]
    return pl.pallas_call(
        finish_kernel,
        in_specs=[WHOLE],
        out_specs=WHOLE,
        out_shape=jax.ShapeDtypeStruct((4, share, columns), jnp.float32),
        compiler_params=pltpu.CompilerParams(vmem_limit_bytes=4 * 1024 * 1024),
    )(parts)


def swapped(values, axis, start):
    depth_count, row_count = lax.axis_size("depth"), lax.axis_size("rows")
    size = lax.axis_size(axis)
    perm = []
    for d in range(depth_count):
        for r in range(row_count):
            i = d if axis == "depth" else r
            j = i + 1 if i % 2 == start else i - 1
            if 0 <= j < size:
                e, q = (j, r) if axis == "depth" else (d, j)
            elif axis == "depth":
                e, q = (size - 1 - d, r)
            else:
                e, q = (d ^ 1, r)
            perm.append((d * row_count + r, e * row_count + q))
    return lax.ppermute(values, ("depth", "rows"), perm)


def exchanged(values, mask):
    return lax.ppermute(values, "depth", [(d, d ^ mask) for d in range(lax.axis_size("depth"))])


def body(volume, color_map, alpha_map):
    depth_count = lax.axis_size("depth")
    share = volume.shape[2] // depth_count
    rows_far, rows_near, far, near = cut_edges(volume)
    rows_far = swapped(rows_far, "rows", 1)
    rows_near = swapped(rows_near, "rows", 0)
    far = swapped(far, "depth", 1)
    near = swapped(near, "depth", 0)
    interior = march_interior(volume, color_map, alpha_map, depth_count)
    halos = (rows_near, rows_far, far, near)
    paired = depth_count == 8 and 2 * share == SUBLANES
    outs = add_edges(volume, interior, halos, depth_count, paired)
    if not paired:
        return finish(lax.all_to_all(outs[0], "depth", 0, 0, tiled=True), share)
    keep, give = outs
    sends = merge(keep, exchanged(give, 1))
    return gather([exchanged(send, 2 * k + 1) for k, send in reversed(list(enumerate(sends)))], share)


def solution(mesh):
    in_specs = (P(None, "depth", "rows", None), P(), P())
    out_specs = P(None, ("rows", "depth"), None)
    return jax.shard_map(body, mesh=mesh, in_specs=in_specs, out_specs=out_specs, check_vma=False)
```

```python
import functools

import jax
import jax.numpy as jnp
from jax import lax
from jax.experimental import pallas as pl
from jax.experimental.pallas import tpu as pltpu
from jax.sharding import PartitionSpec as P

AMBIENT = 0.3
DIFFUSE = 0.7
LIGHT_DEPTH = 0.48 * DIFFUSE
LIGHT_ROWS = 0.6 * DIFFUSE
LIGHT_COLS = 0.64 * DIFFUSE
OPACITY = 4.0
LANES = 128
SUBLANES = 8
WHOLE = pl.BlockSpec(memory_space=pltpu.VMEM)


def parity(axis):
    return lax.axis_index(axis) % 2


def ends(axis):
    position = lax.axis_index(axis)
    return position == 0, position == lax.axis_size(axis) - 1


def edges_kernel(volume_ref, first_out, rows_near_out, second_out, rows_far_out, strip_ref, plane_ref, sems):
    _, slices, height, columns = volume_ref.shape
    odd, odd_row = parity("depth"), parity("rows")
    far_first = 1 - odd_row
    last_first = odd ^ far_first ^ 1
    copies = [
        pltpu.make_async_copy(volume_ref.at[0, last_first * (slices - 1)], plane_ref.at[0], sems.at[0]),
        pltpu.make_async_copy(volume_ref.at[0, :, (1 - odd_row) * (height - 1)], strip_ref.at[0], sems.at[1]),
        pltpu.make_async_copy(volume_ref.at[0, (1 - last_first) * (slices - 1)], plane_ref.at[1], sems.at[2]),
        pltpu.make_async_copy(volume_ref.at[0, :, odd_row * (height - 1)], strip_ref.at[1], sems.at[3]),
    ]
    for copy in copies:
        copy.start()

    def narrow(values):
        return values.astype(jnp.float32).astype(jnp.bfloat16)

    def padded(strip):
        return narrow(jnp.concatenate([strip, jnp.zeros((height - slices, columns), jnp.int32)], axis=0))

    copies[0].wait()
    first_out[...] = narrow(plane_ref[0])
    copies[1].wait()
    rows_near_out[...] = padded(strip_ref[0])
    copies[2].wait()
    second_out[...] = narrow(plane_ref[1])
    copies[3].wait()
    rows_far_out[...] = padded(strip_ref[1])


def cut_edges(volume):
    _, slices, height, columns = volume.shape
    plane = jax.ShapeDtypeStruct((height, columns), jnp.bfloat16)
    return pl.pallas_call(
        edges_kernel,
        in_specs=[pl.BlockSpec(memory_space=pl.ANY)],
        out_specs=[WHOLE] * 4,
        out_shape=[plane] * 4,
        scratch_shapes=[
            pltpu.VMEM((2, slices, columns), jnp.int32),
            pltpu.VMEM((2, height, columns), jnp.int32),
            pltpu.SemaphoreType.DMA((4,)),
        ],
        compiler_params=pltpu.CompilerParams(vmem_limit_bytes=52 * 1024 * 1024),
    )(volume)


def pick(entries, places):
    dims = lax.GatherDimensionNumbers(
        offset_dims=(),
        collapsed_slice_dims=(1,),
        start_index_map=(1,),
        operand_batching_dims=(0,),
        start_indices_batching_dims=(0,),
    )
    return lax.gather(entries, places[..., None], dims, (1, 1), mode=lax.GatherScatterMode.PROMISE_IN_BOUNDS)


def shade(grad_depth, facing, squares):
    facing = facing + LIGHT_DEPTH * grad_depth
    squares = squares + grad_depth * grad_depth
    return AMBIENT + jnp.abs(facing) * lax.rsqrt(jnp.maximum(squares, 4.0))


def interior_kernel(
    opacity_scale,
    volume_ref,
    color_ref,
    alpha_ref,
    base_ref,
    face_ref,
    square_ref,
    lit_ref,
    grad_ref,
    strip_ref,
    pair_ref,
    held_ref,
):
    _, slices, height, columns = volume_ref.shape
    tiles = height // SUBLANES
    chunks = columns // LANES
    tile = (SUBLANES, LANES)
    strip = (slices, LANES)

    packed = color_ref[0:1, :] + color_ref[1:2, :] * 256 + color_ref[2:3, :] * 65536
    color_low, color_high = packed[:, :LANES], packed[:, LANES:]
    alpha_both = alpha_ref[0:1, :LANES] + alpha_ref[0:1, LANES:] * 256

    def colors(value, tables):
        low, high = tables
        place = value & (LANES - 1)
        color = jnp.where(value < LANES, pick(low, place), pick(high, place))
        parts = (color & 255, lax.shift_right_logical(color, 8) & 255, lax.shift_right_logical(color, 16))
        return [part.astype(jnp.float32) for part in parts]

    def opacity(level, table):
        entry = pick(table, level & (LANES - 1))
        entry = lax.shift_right_logical(entry, lax.shift_right_logical(level & LANES, 4)) & 255
        return entry.astype(jnp.float32) * opacity_scale

    tile_colors = [jnp.broadcast_to(t, tile) for t in (color_low, color_high)]
    tile_alpha = jnp.broadcast_to(alpha_both, tile)
    strip_colors = [jnp.broadcast_to(t, strip) for t in (color_low, color_high)]

    def masks(shape):
        lane = lax.broadcasted_iota(jnp.int32, shape, 1)
        row = lax.broadcasted_iota(jnp.int32, shape, 0)
        return lane == 0, lane == LANES - 1, row == 0, row == shape[0] - 1

    first_lane, last_lane, first_row, last_row = masks(tile)
    strip_first_lane, strip_last_lane, front, back = masks(strip)

    pairs = slices // 2
    top = SUBLANES

    def clear(j, carry):
        pair_ref[j] = jnp.zeros(pair_ref.shape[1:], jnp.int32)
        return carry

    clear(0, 0)
    clear(chunks + 1, 0)
    margin = jnp.zeros((pairs, SUBLANES, LANES), jnp.int32)

    def pack(j, carry):
        here = pl.ds(pl.multiple_of(j * LANES, LANES), LANES)
        pair_ref[j + 1, :, :top] = margin
        pair_ref[j + 1, :, top + height :] = margin
        for p in range(pairs):
            pair_ref[j + 1, p, top : top + height] = volume_ref[0, p, :, here] + lax.shift_left(
                volume_ref[0, p + pairs, :, here], 16
            )
        return carry

    lax.fori_loop(0, chunks, pack, 0)

    def split(difference):
        low = lax.shift_right_arithmetic(lax.shift_left(difference, 16), 16)
        high = lax.shift_right_arithmetic(difference + 32768, 16)
        return low.astype(jnp.float32), high.astype(jnp.float32)

    def across(left_value, value, right_value, first, last):
        west = pltpu.roll(jnp.where(last, left_value, value), 1, 1)
        east = pltpu.roll(jnp.where(first, right_value, value), LANES - 1, 1)
        return split(east - west)

    def chunk(j, carry):
        here = pl.ds(pl.multiple_of(j * LANES, LANES), LANES)

        for r in range(tiles):
            rows = slice(r * SUBLANES, (r + 1) * SUBLANES)
            values = [volume_ref[0, s, rows, here] for s in range(slices)]

            def words(c, p, offset=0):
                return pair_ref[c, p, top + r * SUBLANES + offset : top + (r + 1) * SUBLANES + offset, :]

            down, right = [], []
            for p in range(pairs):
                down.append(split(words(j + 1, p, 1) - words(j + 1, p, -1)))
                right.append(across(words(j, p), words(j + 1, p), words(j + 2, p), first_lane, last_lane))
            remaining = jnp.ones(tile, jnp.float32)
            sums = [jnp.zeros(tile, jnp.float32) for _ in range(3)]
            for s in range(slices):
                value = values[s]
                grad_rows = down[s % pairs][s // pairs]
                grad_cols = right[s % pairs][s // pairs]
                squares = grad_rows * grad_rows + grad_cols * grad_cols
                facing = LIGHT_ROWS * grad_rows + LIGHT_COLS * grad_cols
                weight = remaining * opacity(volume_ref[1, s, rows, here], tile_alpha)
                remaining = remaining - weight
                if r == 0:
                    held_ref[0, s : s + 1, :] = weight[:1]
                    weight = jnp.where(first_row, 0.0, weight)
                if r == tiles - 1:
                    held_ref[1, s : s + 1, :] = weight[SUBLANES - 1 :]
                    weight = jnp.where(last_row, 0.0, weight)
                emitted = colors(value, tile_colors)
                if 0 < s < slices - 1:
                    grad_depth = (values[s + 1] - values[s - 1]).astype(jnp.float32)
                    weight = weight * shade(grad_depth, facing, squares)
                    for c in range(3):
                        sums[c] = sums[c] + emitted[c] * weight
                else:
                    end = int(s > 0)
                    face_ref[end, rows, here] = facing
                    square_ref[end, rows, here] = squares
                    weight = weight * (1.0 / 255.0)
                    for c in range(3):
                        lit_ref[end, c, rows, here] = emitted[c] * weight
            for c in range(3):
                base_ref[c, rows, here] = sums[c] * (1.0 / 255.0)
            base_ref[3, rows, here] = 1.0 - remaining

        for q, (edge, inner) in enumerate(((0, 1), (height - 1, height - 2))):
            value = volume_ref[0, :, edge, here]
            behind = pltpu.roll(jnp.where(back, 0, value), 1, 0)
            ahead = pltpu.roll(jnp.where(front, 0, value), slices - 1, 0)
            grad_ref[q, 0, :, here] = (ahead - behind).astype(jnp.float32)
            grad_ref[q, 1, :, here] = volume_ref[0, :, inner, here].astype(jnp.float32)
            word = pair_ref[j + 1, :, top + edge, :]
            low, high = across(
                pair_ref[j, :, top + edge, :],
                word,
                pair_ref[j + 2, :, top + edge, :],
                strip_first_lane[:pairs],
                strip_last_lane[:pairs],
            )
            grad_ref[q, 2, :pairs, here] = low
            grad_ref[q, 2, pairs:, here] = high
            weight = held_ref[q] * (1.0 / 255.0)
            emitted = colors(value, strip_colors)
            for c in range(3):
                strip_ref[q, c, :, here] = emitted[c] * weight
        return carry

    lax.fori_loop(0, chunks, chunk, 0)


def march_interior(volume, color_map, alpha_map, depth_count):
    _, slices, height, columns = volume.shape
    opacity_scale = OPACITY / (255.0 * slices * depth_count)
    shapes = [
        (4, height, columns),
        (2, height, columns),
        (2, height, columns),
        (2, 3, height, columns),
        (2, 3, slices, columns),
        (2, 3, slices, columns),
    ]
    voxels = slices * height * columns
    return pl.pallas_call(
        functools.partial(interior_kernel, opacity_scale),
        in_specs=[WHOLE] * 3,
        out_specs=[WHOLE] * len(shapes),
        out_shape=[jax.ShapeDtypeStruct(shape, jnp.float32) for shape in shapes],
        scratch_shapes=[
            pltpu.VMEM((columns // LANES + 2, slices // 2, height + 2 * SUBLANES, LANES), jnp.int32),
            pltpu.VMEM((2, slices, LANES), jnp.float32),
        ],
        compiler_params=pltpu.CompilerParams(vmem_limit_bytes=24 * 1024 * 1024),
        cost_estimate=pl.CostEstimate(flops=voxels * 80, bytes_accessed=voxels * 20, transcendentals=voxels),
    )(volume, color_map, alpha_map.reshape(1, -1))


def row_sums(first, second):
    count = first.shape[0]
    if count != SUBLANES:
        return jnp.sum(first, axis=0, keepdims=True), jnp.sum(second, axis=0, keepdims=True)
    upper = lax.broadcasted_iota(jnp.int32, first.shape, 0) < 4
    both = jnp.where(upper, first, second) + pltpu.roll(jnp.where(upper, second, first), 4, 0)
    both = both + pltpu.roll(both, 6, 0)
    both = both + pltpu.roll(both, 7, 0)
    return both, pltpu.roll(both, 3, 0)


def edge_kernel(
    share, volume_ref, base_ref, face_ref, square_ref, lit_ref, grad_ref, strip_ref, first_ref, rows_near_ref, second_ref, rows_far_ref, *out_refs
):
    _, slices, height, columns = volume_ref.shape
    tiles = height // SUBLANES
    tile = (SUBLANES, LANES)
    row = lax.broadcasted_iota(jnp.int32, tile, 0)
    first_row, last_row, upper = row == 0, row == SUBLANES - 1, row < SUBLANES // 2
    level = lax.broadcasted_iota(jnp.int32, (slices, LANES), 0)
    front, back = level == 0, level == slices - 1
    odd, odd_row = parity("depth") == 1, parity("rows") == 1
    front_came_first = odd == odd_row
    front_end, back_end = ends("depth")
    top_end, bottom_end = ends("rows")

    def chunk(j, carry):
        here = pl.ds(pl.multiple_of(j * LANES, LANES), LANES)
        rows_near = rows_near_ref[:, here].astype(jnp.float32)[:slices]
        rows_far = rows_far_ref[:, here].astype(jnp.float32)[:slices]
        above = jnp.where(top_end, 0.0, jnp.where(odd_row, rows_near, rows_far))
        below = jnp.where(bottom_end, 0.0, jnp.where(odd_row, rows_far, rows_near))
        first = first_ref[:, here].astype(jnp.float32)
        second = second_ref[:, here].astype(jnp.float32)
        before = jnp.where(front_end, 0.0, jnp.where(front_came_first, first, second))
        after = jnp.where(back_end, 0.0, jnp.where(front_came_first, second, first))
        extra = []
        for q, edge in enumerate((0, height - 1)):
            inner = grad_ref[q, 1, :, here]
            grad_rows = below - inner if q else inner - above
            grad_cols = grad_ref[q, 2, :, here]
            grad_depth = grad_ref[q, 0, :, here] + jnp.where(
                back, after[edge : edge + 1], jnp.where(front, -before[edge : edge + 1], 0.0)
            )
            shading = shade(
                grad_depth,
                LIGHT_ROWS * grad_rows + LIGHT_COLS * grad_cols,
                grad_rows * grad_rows + grad_cols * grad_cols,
            )
            extra.append([strip_ref[q, c, :, here] * shading for c in range(3)])
        extra = [row_sums(extra[0][c], extra[1][c]) for c in range(3)]
        for r in range(tiles):
            rows = slice(r * SUBLANES, (r + 1) * SUBLANES)
            planes = [base_ref[c, rows, here] for c in range(4)]
            for end in range(2):
                if end:
                    grad_depth = after[rows] - volume_ref[0, slices - 2, rows, here].astype(jnp.float32)
                else:
                    grad_depth = volume_ref[0, 1, rows, here].astype(jnp.float32) - before[rows]
                shading = shade(grad_depth, face_ref[end, rows, here], square_ref[end, rows, here])
                for c in range(3):
                    planes[c] = planes[c] + lit_ref[end, c, rows, here] * shading
            for c in range(3):
                if r == 0:
                    planes[c] = planes[c] + jnp.where(first_row, extra[c][0], 0.0)
                if r == tiles - 1:
                    planes[c] = planes[c] + jnp.where(last_row, extra[c][1], 0.0)
            if len(out_refs) == 1:
                for i, first in enumerate(range(0, SUBLANES, share)):
                    block = jnp.concatenate([plane[first : first + share] for plane in planes], axis=0)
                    out_refs[0][r * (SUBLANES // share) + i, :, here] = block.astype(jnp.bfloat16)
            else:
                keep_ref, give_ref = out_refs
                halves = [(planes[c], pltpu.roll(planes[c + 1], SUBLANES // 2, 0)) for c in (0, 2)]
                even = jnp.concatenate([jnp.where(upper, own, turned) for own, turned in halves], axis=0)
                uneven = jnp.concatenate([jnp.where(upper, turned, own) for own, turned in halves], axis=0)
                keep_ref[r, :, here] = jnp.where(odd, even, uneven)
                give_ref[r, :, here] = jnp.where(odd, uneven, even).astype(jnp.bfloat16)
        return carry

    lax.fori_loop(0, columns // LANES, chunk, 0)


def add_edges(volume, interior, halos, depth_count, paired):
    _, slices, height, columns = volume.shape
    share = height // depth_count
    if paired:
        half = (depth_count // 2, 4 * share, columns)
        shapes = [jax.ShapeDtypeStruct(half, jnp.float32), jax.ShapeDtypeStruct(half, jnp.bfloat16)]
    else:
        shapes = [jax.ShapeDtypeStruct((depth_count, 4 * share, columns), jnp.bfloat16)]
    return pl.pallas_call(
        functools.partial(edge_kernel, share),
        in_specs=[WHOLE] * 11,
        out_specs=[WHOLE] * len(shapes),
        out_shape=shapes,
        compiler_params=pltpu.CompilerParams(vmem_limit_bytes=24 * 1024 * 1024),
    )(volume, *interior, *halos)


def over(nearer, farther, uneven):
    share = nearer.shape[0] // 4
    clear = 1.0 - jnp.where(uneven, nearer[2 * share : 3 * share], nearer[3 * share :])
    return nearer + jnp.concatenate([clear] * 4, axis=0) * farther


def merge_kernel(keep_ref, other_ref, *send_refs):
    position = lax.axis_index("depth")
    odd, chip = position % 2 == 1, position // 2
    for k, out_ref in enumerate(send_refs):
        keep = keep_ref[chip ^ k]
        other = other_ref[chip ^ k].astype(jnp.float32)
        block = over(jnp.where(odd, other, keep), jnp.where(odd, keep, other), jnp.logical_not(odd))
        out_ref[...] = block.astype(out_ref.dtype)


def merge(keep, other):
    chips, rows, columns = keep.shape
    return pl.pallas_call(
        merge_kernel,
        in_specs=[WHOLE] * 2,
        out_specs=[WHOLE] * chips,
        out_shape=[jax.ShapeDtypeStruct((rows, columns), jnp.bfloat16)] * chips,
        compiler_params=pltpu.CompilerParams(vmem_limit_bytes=8 * 1024 * 1024),
    )(keep, other)


def gather_kernel(*refs):
    *part_refs, out_ref = refs
    part_refs.reverse()
    count = len(part_refs)
    share = out_ref.shape[1]
    position = lax.axis_index("depth")
    odd, chip = position % 2 == 1, position // 2
    parts = [part_ref[...].astype(jnp.float32) for part_ref in part_refs]
    step = 1
    while step < count:
        swap = (chip & step) != 0
        parts = [
            over(jnp.where(swap, parts[i + 1], parts[i]), jnp.where(swap, parts[i], parts[i + 1]), odd)
            for i in range(0, len(parts), 2)
        ]
        step *= 2
    planes = [parts[0][c * share : (c + 1) * share] for c in range(4)]
    for c in range(4):
        out_ref[c] = jnp.where(odd, planes[c ^ 1], planes[c])


def gather(parts, share):
    columns = parts[0].shape[1]
    return pl.pallas_call(
        gather_kernel,
        in_specs=[WHOLE] * len(parts),
        out_specs=WHOLE,
        out_shape=jax.ShapeDtypeStruct((4, share, columns), jnp.float32),
        compiler_params=pltpu.CompilerParams(vmem_limit_bytes=4 * 1024 * 1024),
    )(*parts)


def finish_kernel(parts_ref, out_ref):
    count = parts_ref.shape[0]
    _, share, columns = out_ref.shape
    remaining = jnp.ones((share, columns), jnp.float32)
    sums = [jnp.zeros((share, columns), jnp.float32) for _ in range(3)]
    for k in range(count):
        part = parts_ref[k].astype(jnp.float32)
        for c in range(3):
            sums[c] = sums[c] + remaining * part[c * share : (c + 1) * share]
        remaining = remaining - remaining * part[3 * share :]
    for c in range(3):
        out_ref[c] = sums[c]
    out_ref[3] = 1.0 - remaining


def finish(parts, share):
    columns = parts.shape[2]
    return pl.pallas_call(
        finish_kernel,
        in_specs=[WHOLE],
        out_specs=WHOLE,
        out_shape=jax.ShapeDtypeStruct((4, share, columns), jnp.float32),
        compiler_params=pltpu.CompilerParams(vmem_limit_bytes=4 * 1024 * 1024),
    )(parts)


def swapped(values, kinds):
    depth_count, row_count = lax.axis_size("depth"), lax.axis_size("rows")
    perm = []
    for d in range(depth_count):
        for r in range(row_count):
            kind = kinds[r % 2]
            e, q = d, r
            if kind == "near slab":
                e = d ^ 1
            elif kind == "far slab":
                e = d + 1 if d % 2 else d - 1
                e = depth_count - 1 - d if not 0 <= e < depth_count else e
            else:
                q = r ^ 1 if kind == "near row" else (r + 1 if r % 2 else r - 1)
                if not 0 <= q < row_count:
                    e, q = d ^ 1, r
            perm.append((d * row_count + r, e * row_count + q))
    return lax.ppermute(values, ("depth", "rows"), perm)


def exchanged(values, mask):
    return lax.ppermute(values, "depth", [(d, d ^ mask) for d in range(lax.axis_size("depth"))])


def body(volume, color_map, alpha_map):
    depth_count = lax.axis_size("depth")
    share = volume.shape[2] // depth_count
    first, rows_near, second, rows_far = cut_edges(volume)
    first = swapped(first, ("far slab", "near slab"))
    rows_near = swapped(rows_near, ("near row", "near row"))
    second = swapped(second, ("near slab", "far slab"))
    rows_far = swapped(rows_far, ("far row", "far row"))
    interior = march_interior(volume, color_map, alpha_map, depth_count)
    halos = (first, rows_near, second, rows_far)
    paired = depth_count == 8 and 2 * share == SUBLANES
    outs = add_edges(volume, interior, halos, depth_count, paired)
    if not paired:
        return finish(lax.all_to_all(outs[0], "depth", 0, 0, tiled=True), share)
    keep, give = outs
    sends = merge(keep, exchanged(give, 1))
    return gather([exchanged(send, 2 * k + 1) for k, send in reversed(list(enumerate(sends)))], share)


def solution(mesh):
    in_specs = (P(None, "depth", "rows", None), P(), P())
    out_specs = P(None, ("rows", "depth"), None)
    return jax.shard_map(body, mesh=mesh, in_specs=in_specs, out_specs=out_specs, check_vma=False)
```

```python
import functools

import jax
import jax.numpy as jnp
from jax import lax
from jax.experimental import pallas as pl
from jax.experimental.pallas import tpu as pltpu
from jax.sharding import PartitionSpec as P

AMBIENT = 0.3
DIFFUSE = 0.7
LIGHT_DEPTH = 0.48 * DIFFUSE
LIGHT_ROWS = 0.6 * DIFFUSE
LIGHT_COLS = 0.64 * DIFFUSE
OPACITY = 4.0
LANES = 128
SUBLANES = 8
WHOLE = pl.BlockSpec(memory_space=pltpu.VMEM)


def parity(axis):
    return lax.axis_index(axis) % 2


def ends(axis):
    position = lax.axis_index(axis)
    return position == 0, position == lax.axis_size(axis) - 1


def edges_kernel(volume_ref, first_out, rows_near_out, second_out, rows_far_out, strip_ref, plane_ref, sems):
    _, slices, height, columns = volume_ref.shape
    odd, odd_row = parity("depth"), parity("rows")
    far_first = 1 - odd_row
    last_first = odd ^ far_first ^ 1
    copies = [
        pltpu.make_async_copy(volume_ref.at[0, last_first * (slices - 1)], plane_ref.at[0], sems.at[0]),
        pltpu.make_async_copy(volume_ref.at[0, :, (1 - odd_row) * (height - 1)], strip_ref.at[0], sems.at[1]),
        pltpu.make_async_copy(volume_ref.at[0, (1 - last_first) * (slices - 1)], plane_ref.at[1], sems.at[2]),
        pltpu.make_async_copy(volume_ref.at[0, :, odd_row * (height - 1)], strip_ref.at[1], sems.at[3]),
    ]
    for copy in copies:
        copy.start()

    def narrow(values):
        return values.astype(jnp.float32).astype(jnp.bfloat16)

    def padded(strip):
        return narrow(jnp.concatenate([strip, jnp.zeros((height - slices, columns), jnp.int32)], axis=0))

    copies[0].wait()
    first_out[...] = narrow(plane_ref[0])
    copies[1].wait()
    rows_near_out[...] = padded(strip_ref[0])
    copies[2].wait()
    second_out[...] = narrow(plane_ref[1])
    copies[3].wait()
    rows_far_out[...] = padded(strip_ref[1])


def cut_edges(volume):
    _, slices, height, columns = volume.shape
    plane = jax.ShapeDtypeStruct((height, columns), jnp.bfloat16)
    return pl.pallas_call(
        edges_kernel,
        in_specs=[pl.BlockSpec(memory_space=pl.ANY)],
        out_specs=[WHOLE] * 4,
        out_shape=[plane] * 4,
        scratch_shapes=[
            pltpu.VMEM((2, slices, columns), jnp.int32),
            pltpu.VMEM((2, height, columns), jnp.int32),
            pltpu.SemaphoreType.DMA((4,)),
        ],
        compiler_params=pltpu.CompilerParams(vmem_limit_bytes=52 * 1024 * 1024),
    )(volume)


def pick(entries, places):
    dims = lax.GatherDimensionNumbers(
        offset_dims=(),
        collapsed_slice_dims=(1,),
        start_index_map=(1,),
        operand_batching_dims=(0,),
        start_indices_batching_dims=(0,),
    )
    return lax.gather(entries, places[..., None], dims, (1, 1), mode=lax.GatherScatterMode.PROMISE_IN_BOUNDS)


def shade(grad_depth, facing, squares):
    facing = facing + LIGHT_DEPTH * grad_depth
    squares = squares + grad_depth * grad_depth
    return AMBIENT + jnp.abs(facing) * lax.rsqrt(jnp.maximum(squares, 4.0))


def interior_kernel(
    opacity_scale,
    volume_ref,
    color_ref,
    alpha_ref,
    base_ref,
    face_ref,
    square_ref,
    lit_ref,
    grad_ref,
    strip_ref,
    pair_ref,
    held_ref,
):
    _, slices, height, columns = volume_ref.shape
    tiles = height // SUBLANES
    chunks = columns // LANES
    tile = (SUBLANES, LANES)
    strip = (slices, LANES)

    packed = color_ref[0:1, :] + color_ref[1:2, :] * 256 + color_ref[2:3, :] * 65536
    color_low, color_high = packed[:, :LANES], packed[:, LANES:]
    alpha_both = alpha_ref[0:1, :LANES] + alpha_ref[0:1, LANES:] * 256

    def colors(value, tables):
        low, high = tables
        place = value & (LANES - 1)
        color = jnp.where(value < LANES, pick(low, place), pick(high, place))
        parts = (color & 255, lax.shift_right_logical(color, 8) & 255, lax.shift_right_logical(color, 16))
        return [part.astype(jnp.float32) for part in parts]

    def opacity(level, table):
        entry = pick(table, level & (LANES - 1))
        entry = lax.shift_right_logical(entry, lax.shift_right_logical(level & LANES, 4)) & 255
        return entry.astype(jnp.float32) * opacity_scale

    tile_colors = [jnp.broadcast_to(t, tile) for t in (color_low, color_high)]
    tile_alpha = jnp.broadcast_to(alpha_both, tile)
    strip_colors = [jnp.broadcast_to(t, strip) for t in (color_low, color_high)]

    def masks(shape):
        lane = lax.broadcasted_iota(jnp.int32, shape, 1)
        row = lax.broadcasted_iota(jnp.int32, shape, 0)
        return lane == 0, lane == LANES - 1, row == 0, row == shape[0] - 1

    first_lane, last_lane, first_row, last_row = masks(tile)
    strip_first_lane, strip_last_lane, front, back = masks(strip)

    pairs = slices // 2
    top = SUBLANES

    def clear(j, carry):
        pair_ref[j] = jnp.zeros(pair_ref.shape[1:], jnp.int32)
        return carry

    clear(0, 0)
    clear(chunks + 1, 0)
    margin = jnp.zeros((pairs, SUBLANES, LANES), jnp.int32)

    def pack(j, carry):
        here = pl.ds(pl.multiple_of(j * LANES, LANES), LANES)
        pair_ref[j + 1, :, :top] = margin
        pair_ref[j + 1, :, top + height :] = margin
        for p in range(pairs):
            pair_ref[j + 1, p, top : top + height] = volume_ref[0, p, :, here] + lax.shift_left(
                volume_ref[0, p + pairs, :, here], 16
            )
        return carry

    lax.fori_loop(0, chunks, pack, 0)

    def split(difference):
        low = lax.shift_right_arithmetic(lax.shift_left(difference, 16), 16)
        high = lax.shift_right_arithmetic(difference + 32768, 16)
        return low.astype(jnp.float32), high.astype(jnp.float32)

    def across(left_value, value, right_value, first, last):
        west = pltpu.roll(jnp.where(last, left_value, value), 1, 1)
        east = pltpu.roll(jnp.where(first, right_value, value), LANES - 1, 1)
        return split(east - west)

    def chunk(j, carry):
        here = pl.ds(pl.multiple_of(j * LANES, LANES), LANES)

        for r in range(tiles):
            rows = slice(r * SUBLANES, (r + 1) * SUBLANES)
            values = [volume_ref[0, s, rows, here] for s in range(slices)]

            def words(c, p, offset=0):
                return pair_ref[c, p, top + r * SUBLANES + offset : top + (r + 1) * SUBLANES + offset, :]

            down, right = [], []
            for p in range(pairs):
                down.append(split(words(j + 1, p, 1) - words(j + 1, p, -1)))
                right.append(across(words(j, p), words(j + 1, p), words(j + 2, p), first_lane, last_lane))
            remaining = jnp.ones(tile, jnp.float32)
            sums = [jnp.zeros(tile, jnp.float32) for _ in range(3)]
            for s in range(slices):
                value = values[s]
                grad_rows = down[s % pairs][s // pairs]
                grad_cols = right[s % pairs][s // pairs]
                squares = grad_rows * grad_rows + grad_cols * grad_cols
                facing = LIGHT_ROWS * grad_rows + LIGHT_COLS * grad_cols
                weight = remaining * opacity(volume_ref[1, s, rows, here], tile_alpha)
                remaining = remaining - weight
                if r == 0:
                    held_ref[0, s : s + 1, :] = weight[:1]
                    weight = jnp.where(first_row, 0.0, weight)
                if r == tiles - 1:
                    held_ref[1, s : s + 1, :] = weight[SUBLANES - 1 :]
                    weight = jnp.where(last_row, 0.0, weight)
                emitted = colors(value, tile_colors)
                if 0 < s < slices - 1:
                    grad_depth = (values[s + 1] - values[s - 1]).astype(jnp.float32)
                    weight = weight * shade(grad_depth, facing, squares)
                    for c in range(3):
                        sums[c] = sums[c] + emitted[c] * weight
                else:
                    end = int(s > 0)
                    face_ref[end, rows, here] = facing
                    square_ref[end, rows, here] = squares
                    weight = weight * (1.0 / 255.0)
                    for c in range(3):
                        lit_ref[end, c, rows, here] = emitted[c] * weight
            for c in range(3):
                base_ref[c, rows, here] = sums[c] * (1.0 / 255.0)
            base_ref[3, rows, here] = 1.0 - remaining

        for q, (edge, inner) in enumerate(((0, 1), (height - 1, height - 2))):
            value = volume_ref[0, :, edge, here]
            behind = pltpu.roll(jnp.where(back, 0, value), 1, 0)
            ahead = pltpu.roll(jnp.where(front, 0, value), slices - 1, 0)
            grad_ref[q, 0, :, here] = (ahead - behind).astype(jnp.float32)
            grad_ref[q, 1, :, here] = volume_ref[0, :, inner, here].astype(jnp.float32)
            word = pair_ref[j + 1, :, top + edge, :]
            low, high = across(
                pair_ref[j, :, top + edge, :],
                word,
                pair_ref[j + 2, :, top + edge, :],
                strip_first_lane[:pairs],
                strip_last_lane[:pairs],
            )
            grad_ref[q, 2, :pairs, here] = low
            grad_ref[q, 2, pairs:, here] = high
            weight = held_ref[q] * (1.0 / 255.0)
            emitted = colors(value, strip_colors)
            for c in range(3):
                strip_ref[q, c, :, here] = emitted[c] * weight
        return carry

    lax.fori_loop(0, chunks, chunk, 0)


def march_interior(volume, color_map, alpha_map, depth_count):
    _, slices, height, columns = volume.shape
    opacity_scale = OPACITY / (255.0 * slices * depth_count)
    shapes = [
        (4, height, columns),
        (2, height, columns),
        (2, height, columns),
        (2, 3, height, columns),
        (2, 3, slices, columns),
        (2, 3, slices, columns),
    ]
    voxels = slices * height * columns
    return pl.pallas_call(
        functools.partial(interior_kernel, opacity_scale),
        in_specs=[WHOLE] * 3,
        out_specs=[WHOLE] * len(shapes),
        out_shape=[jax.ShapeDtypeStruct(shape, jnp.float32) for shape in shapes],
        scratch_shapes=[
            pltpu.VMEM((columns // LANES + 2, slices // 2, height + 2 * SUBLANES, LANES), jnp.int32),
            pltpu.VMEM((2, slices, LANES), jnp.float32),
        ],
        compiler_params=pltpu.CompilerParams(vmem_limit_bytes=24 * 1024 * 1024),
        cost_estimate=pl.CostEstimate(flops=voxels * 80, bytes_accessed=voxels * 20, transcendentals=voxels),
    )(volume, color_map, alpha_map.reshape(1, -1))


def row_sums(first, second):
    count = first.shape[0]
    if count != SUBLANES:
        return jnp.sum(first, axis=0, keepdims=True), jnp.sum(second, axis=0, keepdims=True)
    upper = lax.broadcasted_iota(jnp.int32, first.shape, 0) < 4
    both = jnp.where(upper, first, second) + pltpu.roll(jnp.where(upper, second, first), 4, 0)
    both = both + pltpu.roll(both, 6, 0)
    both = both + pltpu.roll(both, 7, 0)
    return both, pltpu.roll(both, 3, 0)


def edge_kernel(
    share, volume_ref, base_ref, face_ref, square_ref, lit_ref, grad_ref, strip_ref, first_ref, rows_near_ref, second_ref, rows_far_ref, *out_refs
):
    _, slices, height, columns = volume_ref.shape
    tiles = height // SUBLANES
    tile = (SUBLANES, LANES)
    row = lax.broadcasted_iota(jnp.int32, tile, 0)
    first_row, last_row, upper = row == 0, row == SUBLANES - 1, row < SUBLANES // 2
    level = lax.broadcasted_iota(jnp.int32, (slices, LANES), 0)
    front, back = level == 0, level == slices - 1
    odd, odd_row = parity("depth") == 1, parity("rows") == 1
    chip = lax.axis_index("depth") // 2
    front_came_first = odd == odd_row
    front_end, back_end = ends("depth")
    top_end, bottom_end = ends("rows")

    def chunk(j, carry):
        here = pl.ds(pl.multiple_of(j * LANES, LANES), LANES)
        rows_near = rows_near_ref[:, here].astype(jnp.float32)[:slices]
        rows_far = rows_far_ref[:, here].astype(jnp.float32)[:slices]
        above = jnp.where(top_end, 0.0, jnp.where(odd_row, rows_near, rows_far))
        below = jnp.where(bottom_end, 0.0, jnp.where(odd_row, rows_far, rows_near))
        first = first_ref[:, here].astype(jnp.float32)
        second = second_ref[:, here].astype(jnp.float32)
        before = jnp.where(front_end, 0.0, jnp.where(front_came_first, first, second))
        after = jnp.where(back_end, 0.0, jnp.where(front_came_first, second, first))
        extra = []
        for q, edge in enumerate((0, height - 1)):
            inner = grad_ref[q, 1, :, here]
            grad_rows = below - inner if q else inner - above
            grad_cols = grad_ref[q, 2, :, here]
            grad_depth = grad_ref[q, 0, :, here] + jnp.where(
                back, after[edge : edge + 1], jnp.where(front, -before[edge : edge + 1], 0.0)
            )
            shading = shade(
                grad_depth,
                LIGHT_ROWS * grad_rows + LIGHT_COLS * grad_cols,
                grad_rows * grad_rows + grad_cols * grad_cols,
            )
            extra.append([strip_ref[q, c, :, here] * shading for c in range(3)])
        extra = [row_sums(extra[0][c], extra[1][c]) for c in range(3)]
        for r in range(tiles):
            rows = slice(r * SUBLANES, (r + 1) * SUBLANES)
            planes = [base_ref[c, rows, here] for c in range(4)]
            for end in range(2):
                if end:
                    grad_depth = after[rows] - volume_ref[0, slices - 2, rows, here].astype(jnp.float32)
                else:
                    grad_depth = volume_ref[0, 1, rows, here].astype(jnp.float32) - before[rows]
                shading = shade(grad_depth, face_ref[end, rows, here], square_ref[end, rows, here])
                for c in range(3):
                    planes[c] = planes[c] + lit_ref[end, c, rows, here] * shading
            for c in range(3):
                if r == 0:
                    planes[c] = planes[c] + jnp.where(first_row, extra[c][0], 0.0)
                if r == tiles - 1:
                    planes[c] = planes[c] + jnp.where(last_row, extra[c][1], 0.0)
            if len(out_refs) == 1:
                for i, first in enumerate(range(0, SUBLANES, share)):
                    block = jnp.concatenate([plane[first : first + share] for plane in planes], axis=0)
                    out_refs[0][r * (SUBLANES // share) + i, :, here] = block.astype(jnp.bfloat16)
            else:
                keep_ref, give_ref = out_refs
                halves = [(planes[c], pltpu.roll(planes[c + 1], SUBLANES // 2, 0)) for c in (0, 2)]
                even = jnp.concatenate([jnp.where(upper, own, turned) for own, turned in halves], axis=0)
                uneven = jnp.concatenate([jnp.where(upper, turned, own) for own, turned in halves], axis=0)
                keep_even = odd != (chip == r)
                keep_ref[r, :, here] = jnp.where(keep_even, even, uneven)
                give_ref[r, :, here] = jnp.where(keep_even, uneven, even).astype(jnp.bfloat16)
        return carry

    lax.fori_loop(0, columns // LANES, chunk, 0)


def add_edges(volume, interior, halos, depth_count, paired):
    _, slices, height, columns = volume.shape
    share = height // depth_count
    if paired:
        half = (depth_count // 2, 4 * share, columns)
        shapes = [jax.ShapeDtypeStruct(half, jnp.float32), jax.ShapeDtypeStruct(half, jnp.bfloat16)]
    else:
        shapes = [jax.ShapeDtypeStruct((depth_count, 4 * share, columns), jnp.bfloat16)]
    return pl.pallas_call(
        functools.partial(edge_kernel, share),
        in_specs=[WHOLE] * 11,
        out_specs=[WHOLE] * len(shapes),
        out_shape=shapes,
        compiler_params=pltpu.CompilerParams(vmem_limit_bytes=24 * 1024 * 1024),
    )(volume, *interior, *halos)


def over(nearer, farther, uneven):
    share = nearer.shape[0] // 4
    clear = 1.0 - jnp.where(uneven, nearer[2 * share : 3 * share], nearer[3 * share :])
    return nearer + jnp.concatenate([clear] * 4, axis=0) * farther


def merge_kernel(keep_ref, other_ref, *out_refs):
    position = lax.axis_index("depth")
    odd, chip = position % 2 == 1, position // 2
    for k, out_ref in enumerate(out_refs):
        keep = keep_ref[chip ^ k]
        other = other_ref[chip ^ k].astype(jnp.float32)
        uneven = jnp.logical_not(odd) if k else odd
        block = over(jnp.where(odd, other, keep), jnp.where(odd, keep, other), uneven)
        out_ref[...] = block.astype(out_ref.dtype)


def merge(keep, other):
    chips, rows, columns = keep.shape
    shapes = [jax.ShapeDtypeStruct((rows, columns), jnp.bfloat16 if k else jnp.float32) for k in range(chips)]
    return pl.pallas_call(
        merge_kernel,
        in_specs=[WHOLE] * 2,
        out_specs=[WHOLE] * chips,
        out_shape=shapes,
        compiler_params=pltpu.CompilerParams(vmem_limit_bytes=8 * 1024 * 1024),
    )(keep, other)


def gather_kernel(*refs):
    *part_refs, out_ref = refs
    part_refs.reverse()
    count = len(part_refs)
    share = out_ref.shape[1]
    position = lax.axis_index("depth")
    odd, chip = position % 2 == 1, position // 2
    parts = [part_ref[...].astype(jnp.float32) for part_ref in part_refs]
    step = 1
    while step < count:
        swap = (chip & step) != 0
        parts = [
            over(jnp.where(swap, parts[i + 1], parts[i]), jnp.where(swap, parts[i], parts[i + 1]), odd)
            for i in range(0, len(parts), 2)
        ]
        step *= 2
    planes = [parts[0][c * share : (c + 1) * share] for c in range(4)]
    for c in range(4):
        out_ref[c] = jnp.where(odd, planes[c ^ 1], planes[c])


def gather(parts, share):
    columns = parts[0].shape[1]
    return pl.pallas_call(
        gather_kernel,
        in_specs=[WHOLE] * len(parts),
        out_specs=WHOLE,
        out_shape=jax.ShapeDtypeStruct((4, share, columns), jnp.float32),
        compiler_params=pltpu.CompilerParams(vmem_limit_bytes=4 * 1024 * 1024),
    )(*parts)


def finish_kernel(parts_ref, out_ref):
    count = parts_ref.shape[0]
    _, share, columns = out_ref.shape
    remaining = jnp.ones((share, columns), jnp.float32)
    sums = [jnp.zeros((share, columns), jnp.float32) for _ in range(3)]
    for k in range(count):
        part = parts_ref[k].astype(jnp.float32)
        for c in range(3):
            sums[c] = sums[c] + remaining * part[c * share : (c + 1) * share]
        remaining = remaining - remaining * part[3 * share :]
    for c in range(3):
        out_ref[c] = sums[c]
    out_ref[3] = 1.0 - remaining


def finish(parts, share):
    columns = parts.shape[2]
    return pl.pallas_call(
        finish_kernel,
        in_specs=[WHOLE],
        out_specs=WHOLE,
        out_shape=jax.ShapeDtypeStruct((4, share, columns), jnp.float32),
        compiler_params=pltpu.CompilerParams(vmem_limit_bytes=4 * 1024 * 1024),
    )(parts)


def swapped(values, kinds):
    depth_count, row_count = lax.axis_size("depth"), lax.axis_size("rows")
    perm = []
    for d in range(depth_count):
        for r in range(row_count):
            kind = kinds[r % 2]
            e, q = d, r
            if kind == "near slab":
                e = d ^ 1
            elif kind == "far slab":
                e = d + 1 if d % 2 else d - 1
                e = depth_count - 1 - d if not 0 <= e < depth_count else e
            else:
                q = r ^ 1 if kind == "near row" else (r + 1 if r % 2 else r - 1)
                if not 0 <= q < row_count:
                    e, q = d ^ 1, r
            perm.append((d * row_count + r, e * row_count + q))
    return lax.ppermute(values, ("depth", "rows"), perm)


def exchanged(values, mask):
    return lax.ppermute(values, "depth", [(d, d ^ mask) for d in range(lax.axis_size("depth"))])


def body(volume, color_map, alpha_map):
    depth_count = lax.axis_size("depth")
    share = volume.shape[2] // depth_count
    first, rows_near, second, rows_far = cut_edges(volume)
    first = swapped(first, ("far slab", "near slab"))
    rows_near = swapped(rows_near, ("near row", "near row"))
    second = swapped(second, ("near slab", "far slab"))
    rows_far = swapped(rows_far, ("far row", "far row"))
    interior = march_interior(volume, color_map, alpha_map, depth_count)
    halos = (first, rows_near, second, rows_far)
    paired = depth_count == 8 and 2 * share == SUBLANES
    outs = add_edges(volume, interior, halos, depth_count, paired)
    if not paired:
        return finish(lax.all_to_all(outs[0], "depth", 0, 0, tiled=True), share)
    keep, give = outs
    own, *sends = merge(keep, exchanged(give, 1))
    received = [exchanged(send, 2 * k + 1) for k, send in reversed(list(enumerate(sends, 1)))]
    return gather((*received, own), share)


def solution(mesh):
    in_specs = (P(None, "depth", "rows", None), P(), P())
    out_specs = P(None, ("rows", "depth"), None)
    return jax.shard_map(body, mesh=mesh, in_specs=in_specs, out_specs=out_specs, check_vma=False)
```

```python
import functools

import jax
import jax.numpy as jnp
from jax import lax
from jax.experimental import pallas as pl
from jax.experimental.pallas import tpu as pltpu
from jax.sharding import PartitionSpec as P

AMBIENT = 0.3
DIFFUSE = 0.7
LIGHT_DEPTH = 0.48 * DIFFUSE
LIGHT_ROWS = 0.6 * DIFFUSE
LIGHT_COLS = 0.64 * DIFFUSE
OPACITY = 4.0
LANES = 128
SUBLANES = 8
WHOLE = pl.BlockSpec(memory_space=pltpu.VMEM)


def parity(axis):
    return lax.axis_index(axis) % 2


def ends(axis):
    position = lax.axis_index(axis)
    return position == 0, position == lax.axis_size(axis) - 1


def edges_kernel(volume_ref, first_out, rows_near_out, second_out, rows_far_out, strip_ref, plane_ref, sems):
    _, slices, height, columns = volume_ref.shape
    odd, odd_row = parity("depth"), parity("rows")
    far_first = 1 - odd_row
    last_first = odd ^ far_first ^ 1
    copies = [
        pltpu.make_async_copy(volume_ref.at[0, last_first * (slices - 1)], plane_ref.at[0], sems.at[0]),
        pltpu.make_async_copy(volume_ref.at[0, :, (1 - odd_row) * (height - 1)], strip_ref.at[0], sems.at[1]),
        pltpu.make_async_copy(volume_ref.at[0, (1 - last_first) * (slices - 1)], plane_ref.at[1], sems.at[2]),
        pltpu.make_async_copy(volume_ref.at[0, :, odd_row * (height - 1)], strip_ref.at[1], sems.at[3]),
    ]
    for copy in copies:
        copy.start()

    def narrow(values):
        return values.astype(jnp.float32).astype(jnp.bfloat16)

    def padded(strip):
        return narrow(jnp.concatenate([strip, jnp.zeros((height - slices, columns), jnp.int32)], axis=0))

    copies[0].wait()
    first_out[...] = narrow(plane_ref[0])
    copies[1].wait()
    rows_near_out[...] = padded(strip_ref[0])
    copies[2].wait()
    second_out[...] = narrow(plane_ref[1])
    copies[3].wait()
    rows_far_out[...] = padded(strip_ref[1])


def cut_edges(volume):
    _, slices, height, columns = volume.shape
    plane = jax.ShapeDtypeStruct((height, columns), jnp.bfloat16)
    return pl.pallas_call(
        edges_kernel,
        in_specs=[pl.BlockSpec(memory_space=pl.ANY)],
        out_specs=[WHOLE] * 4,
        out_shape=[plane] * 4,
        scratch_shapes=[
            pltpu.VMEM((2, slices, columns), jnp.int32),
            pltpu.VMEM((2, height, columns), jnp.int32),
            pltpu.SemaphoreType.DMA((4,)),
        ],
        compiler_params=pltpu.CompilerParams(vmem_limit_bytes=52 * 1024 * 1024),
    )(volume)


def pick(entries, places):
    dims = lax.GatherDimensionNumbers(
        offset_dims=(),
        collapsed_slice_dims=(1,),
        start_index_map=(1,),
        operand_batching_dims=(0,),
        start_indices_batching_dims=(0,),
    )
    return lax.gather(entries, places[..., None], dims, (1, 1), mode=lax.GatherScatterMode.PROMISE_IN_BOUNDS)


def shade(grad_depth, facing, squares):
    facing = facing + LIGHT_DEPTH * grad_depth
    squares = squares + grad_depth * grad_depth
    return AMBIENT + jnp.abs(facing) * lax.rsqrt(jnp.maximum(squares, 4.0))


def interior_kernel(
    opacity_scale,
    volume_ref,
    color_ref,
    alpha_ref,
    base_ref,
    face_ref,
    square_ref,
    lit_ref,
    grad_ref,
    strip_ref,
    pair_ref,
    held_ref,
):
    _, slices, height, columns = volume_ref.shape
    tiles = height // SUBLANES
    chunks = columns // LANES
    tile = (SUBLANES, LANES)
    strip = (slices, LANES)

    packed = color_ref[0:1, :] + color_ref[1:2, :] * 256 + color_ref[2:3, :] * 65536
    color_low, color_high = packed[:, :LANES], packed[:, LANES:]
    alpha_both = alpha_ref[0:1, :LANES] + alpha_ref[0:1, LANES:] * 256

    def colors(value, tables):
        low, high = tables
        place = value & (LANES - 1)
        color = jnp.where(value < LANES, pick(low, place), pick(high, place))
        parts = (color & 255, lax.shift_right_logical(color, 8) & 255, lax.shift_right_logical(color, 16))
        return [part.astype(jnp.float32) for part in parts]

    def opacity(level, table):
        entry = pick(table, level & (LANES - 1))
        entry = lax.shift_right_logical(entry, lax.shift_right_logical(level & LANES, 4)) & 255
        return entry.astype(jnp.float32) * opacity_scale

    tile_colors = [jnp.broadcast_to(t, tile) for t in (color_low, color_high)]
    tile_alpha = jnp.broadcast_to(alpha_both, tile)
    strip_colors = [jnp.broadcast_to(t, strip) for t in (color_low, color_high)]

    def masks(shape):
        lane = lax.broadcasted_iota(jnp.int32, shape, 1)
        row = lax.broadcasted_iota(jnp.int32, shape, 0)
        return lane == 0, lane == LANES - 1, row == 0, row == shape[0] - 1

    first_lane, last_lane, first_row, last_row = masks(tile)
    strip_first_lane, strip_last_lane, front, back = masks(strip)

    pairs = slices // 2
    top = SUBLANES

    def clear(j, carry):
        pair_ref[j] = jnp.zeros(pair_ref.shape[1:], jnp.int32)
        return carry

    clear(0, 0)
    clear(chunks + 1, 0)
    margin = jnp.zeros((pairs, SUBLANES, LANES), jnp.int32)

    def pack(j, carry):
        here = pl.ds(pl.multiple_of(j * LANES, LANES), LANES)
        pair_ref[j + 1, :, :top] = margin
        pair_ref[j + 1, :, top + height :] = margin
        for p in range(pairs):
            pair_ref[j + 1, p, top : top + height] = volume_ref[0, p, :, here] + lax.shift_left(
                volume_ref[0, p + pairs, :, here], 16
            )
        return carry

    lax.fori_loop(0, chunks, pack, 0)

    def split(difference):
        low = lax.shift_right_arithmetic(lax.shift_left(difference, 16), 16)
        high = lax.shift_right_arithmetic(difference + 32768, 16)
        return low.astype(jnp.float32), high.astype(jnp.float32)

    def across(left_value, value, right_value, first, last):
        west = pltpu.roll(jnp.where(last, left_value, value), 1, 1)
        east = pltpu.roll(jnp.where(first, right_value, value), LANES - 1, 1)
        return split(east - west)

    def chunk(j, carry):
        here = pl.ds(pl.multiple_of(j * LANES, LANES), LANES)

        for r in range(tiles):
            rows = slice(r * SUBLANES, (r + 1) * SUBLANES)
            values = [volume_ref[0, s, rows, here] for s in range(slices)]

            def words(c, p, offset=0):
                return pair_ref[c, p, top + r * SUBLANES + offset : top + (r + 1) * SUBLANES + offset, :]

            down, right = [], []
            for p in range(pairs):
                down.append(split(words(j + 1, p, 1) - words(j + 1, p, -1)))
                right.append(across(words(j, p), words(j + 1, p), words(j + 2, p), first_lane, last_lane))
            remaining = jnp.ones(tile, jnp.float32)
            sums = [jnp.zeros(tile, jnp.float32) for _ in range(3)]
            for s in range(slices):
                value = values[s]
                grad_rows = down[s % pairs][s // pairs]
                grad_cols = right[s % pairs][s // pairs]
                squares = grad_rows * grad_rows + grad_cols * grad_cols
                facing = LIGHT_ROWS * grad_rows + LIGHT_COLS * grad_cols
                weight = remaining * opacity(volume_ref[1, s, rows, here], tile_alpha)
                remaining = remaining - weight
                if r == 0:
                    held_ref[0, s : s + 1, :] = weight[:1]
                    weight = jnp.where(first_row, 0.0, weight)
                if r == tiles - 1:
                    held_ref[1, s : s + 1, :] = weight[SUBLANES - 1 :]
                    weight = jnp.where(last_row, 0.0, weight)
                emitted = colors(value, tile_colors)
                if 0 < s < slices - 1:
                    grad_depth = (values[s + 1] - values[s - 1]).astype(jnp.float32)
                    weight = weight * shade(grad_depth, facing, squares)
                    for c in range(3):
                        sums[c] = sums[c] + emitted[c] * weight
                else:
                    end = int(s > 0)
                    face_ref[end, rows, here] = facing
                    square_ref[end, rows, here] = squares
                    weight = weight * (1.0 / 255.0)
                    for c in range(3):
                        lit_ref[end, c, rows, here] = emitted[c] * weight
            for c in range(3):
                base_ref[c, rows, here] = sums[c] * (1.0 / 255.0)
            base_ref[3, rows, here] = 1.0 - remaining

        for q, (edge, inner) in enumerate(((0, 1), (height - 1, height - 2))):
            value = volume_ref[0, :, edge, here]
            behind = pltpu.roll(jnp.where(back, 0, value), 1, 0)
            ahead = pltpu.roll(jnp.where(front, 0, value), slices - 1, 0)
            grad_ref[q, 0, :, here] = (ahead - behind).astype(jnp.float32)
            grad_ref[q, 1, :, here] = volume_ref[0, :, inner, here].astype(jnp.float32)
            word = pair_ref[j + 1, :, top + edge, :]
            low, high = across(
                pair_ref[j, :, top + edge, :],
                word,
                pair_ref[j + 2, :, top + edge, :],
                strip_first_lane[:pairs],
                strip_last_lane[:pairs],
            )
            grad_ref[q, 2, :pairs, here] = low
            grad_ref[q, 2, pairs:, here] = high
            weight = held_ref[q] * (1.0 / 255.0)
            emitted = colors(value, strip_colors)
            for c in range(3):
                strip_ref[q, c, :, here] = emitted[c] * weight
        return carry

    lax.fori_loop(0, chunks, chunk, 0)


def march_interior(volume, color_map, alpha_map, depth_count):
    _, slices, height, columns = volume.shape
    opacity_scale = OPACITY / (255.0 * slices * depth_count)
    shapes = [
        (4, height, columns),
        (2, height, columns),
        (2, height, columns),
        (2, 3, height, columns),
        (2, 3, slices, columns),
        (2, 3, slices, columns),
    ]
    voxels = slices * height * columns
    return pl.pallas_call(
        functools.partial(interior_kernel, opacity_scale),
        in_specs=[WHOLE] * 3,
        out_specs=[WHOLE] * len(shapes),
        out_shape=[jax.ShapeDtypeStruct(shape, jnp.float32) for shape in shapes],
        scratch_shapes=[
            pltpu.VMEM((columns // LANES + 2, slices // 2, height + 2 * SUBLANES, LANES), jnp.int32),
            pltpu.VMEM((2, slices, LANES), jnp.float32),
        ],
        compiler_params=pltpu.CompilerParams(vmem_limit_bytes=24 * 1024 * 1024),
        cost_estimate=pl.CostEstimate(flops=voxels * 80, bytes_accessed=voxels * 20, transcendentals=voxels),
    )(volume, color_map, alpha_map.reshape(1, -1))


def row_sums(first, second):
    count = first.shape[0]
    if count != SUBLANES:
        return jnp.sum(first, axis=0, keepdims=True), jnp.sum(second, axis=0, keepdims=True)
    upper = lax.broadcasted_iota(jnp.int32, first.shape, 0) < 4
    both = jnp.where(upper, first, second) + pltpu.roll(jnp.where(upper, second, first), 4, 0)
    both = both + pltpu.roll(both, 6, 0)
    both = both + pltpu.roll(both, 7, 0)
    return both, pltpu.roll(both, 3, 0)


def edge_kernel(
    share, volume_ref, base_ref, face_ref, square_ref, lit_ref, grad_ref, strip_ref, first_ref, rows_near_ref, second_ref, rows_far_ref, *out_refs
):
    _, slices, height, columns = volume_ref.shape
    tiles = height // SUBLANES
    tile = (SUBLANES, LANES)
    row = lax.broadcasted_iota(jnp.int32, tile, 0)
    first_row, last_row, upper = row == 0, row == SUBLANES - 1, row < SUBLANES // 2
    level = lax.broadcasted_iota(jnp.int32, (slices, LANES), 0)
    front, back = level == 0, level == slices - 1
    odd, odd_row = parity("depth") == 1, parity("rows") == 1
    front_came_first = odd == odd_row
    front_end, back_end = ends("depth")
    top_end, bottom_end = ends("rows")

    def chunk(j, carry):
        here = pl.ds(pl.multiple_of(j * LANES, LANES), LANES)
        rows_near = rows_near_ref[:, here].astype(jnp.float32)[:slices]
        rows_far = rows_far_ref[:, here].astype(jnp.float32)[:slices]
        above = jnp.where(top_end, 0.0, jnp.where(odd_row, rows_near, rows_far))
        below = jnp.where(bottom_end, 0.0, jnp.where(odd_row, rows_far, rows_near))
        first = first_ref[:, here].astype(jnp.float32)
        second = second_ref[:, here].astype(jnp.float32)
        before = jnp.where(front_end, 0.0, jnp.where(front_came_first, first, second))
        after = jnp.where(back_end, 0.0, jnp.where(front_came_first, second, first))
        extra = []
        for q, edge in enumerate((0, height - 1)):
            inner = grad_ref[q, 1, :, here]
            grad_rows = below - inner if q else inner - above
            grad_cols = grad_ref[q, 2, :, here]
            grad_depth = grad_ref[q, 0, :, here] + jnp.where(
                back, after[edge : edge + 1], jnp.where(front, -before[edge : edge + 1], 0.0)
            )
            shading = shade(
                grad_depth,
                LIGHT_ROWS * grad_rows + LIGHT_COLS * grad_cols,
                grad_rows * grad_rows + grad_cols * grad_cols,
            )
            extra.append([strip_ref[q, c, :, here] * shading for c in range(3)])
        extra = [row_sums(extra[0][c], extra[1][c]) for c in range(3)]
        for r in range(tiles):
            rows = slice(r * SUBLANES, (r + 1) * SUBLANES)
            planes = [base_ref[c, rows, here] for c in range(4)]
            for end in range(2):
                if end:
                    grad_depth = after[rows] - volume_ref[0, slices - 2, rows, here].astype(jnp.float32)
                else:
                    grad_depth = volume_ref[0, 1, rows, here].astype(jnp.float32) - before[rows]
                shading = shade(grad_depth, face_ref[end, rows, here], square_ref[end, rows, here])
                for c in range(3):
                    planes[c] = planes[c] + lit_ref[end, c, rows, here] * shading
            for c in range(3):
                if r == 0:
                    planes[c] = planes[c] + jnp.where(first_row, extra[c][0], 0.0)
                if r == tiles - 1:
                    planes[c] = planes[c] + jnp.where(last_row, extra[c][1], 0.0)
            if len(out_refs) == 1:
                for i, first in enumerate(range(0, SUBLANES, share)):
                    block = jnp.concatenate([plane[first : first + share] for plane in planes], axis=0)
                    out_refs[0][r * (SUBLANES // share) + i, :, here] = block.astype(jnp.bfloat16)
            else:
                halves = [(planes[c], pltpu.roll(planes[c + 1], SUBLANES // 2, 0)) for c in (0, 2)]
                even = jnp.concatenate([jnp.where(upper, own, turned) for own, turned in halves], axis=0)
                uneven = jnp.concatenate([jnp.where(upper, turned, own) for own, turned in halves], axis=0)
                blocks_ref, _ = out_refs
                blocks_ref[r, 0, :, here] = even
                blocks_ref[r, 1, :, here] = uneven
        return carry

    lax.fori_loop(0, columns // LANES, chunk, 0)
    if len(out_refs) > 1:
        blocks_ref, give_ref = out_refs
        chip, core, mask = route()
        given = (blocks_ref[chip, 1 - core], blocks_ref[chip ^ 3, core], blocks_ref[chip ^ mask ^ 3, 0], blocks_ref[chip ^ mask ^ 3, 1])
        for i, block in enumerate(given):
            give_ref[i] = block.astype(jnp.bfloat16)


def add_edges(volume, interior, halos, depth_count, paired):
    _, slices, height, columns = volume.shape
    share = height // depth_count
    if paired:
        block = (4 * share, columns)
        shapes = [
            jax.ShapeDtypeStruct((depth_count // 2, 2, *block), jnp.float32),
            jax.ShapeDtypeStruct((4, *block), jnp.bfloat16),
        ]
    else:
        shapes = [jax.ShapeDtypeStruct((depth_count, 4 * share, columns), jnp.bfloat16)]
    return pl.pallas_call(
        functools.partial(edge_kernel, share),
        in_specs=[WHOLE] * 11,
        out_specs=[WHOLE] * len(shapes),
        out_shape=shapes,
        compiler_params=pltpu.CompilerParams(vmem_limit_bytes=24 * 1024 * 1024),
    )(volume, *interior, *halos)


def served(depth):
    chip, core = depth // 2, depth % 2
    return 1 + (core ^ (chip & 1) ^ (chip >> 1))


def route():
    position = lax.axis_index("depth")
    return position // 2, position % 2, served(position)


def over(nearer, farther, uneven):
    share = nearer.shape[0] // 4
    clear = 1.0 - jnp.where(uneven, nearer[2 * share : 3 * share], nearer[3 * share :])
    return nearer + jnp.concatenate([clear] * 4, axis=0) * farther


def merge_kernel(blocks_ref, other_ref, own_ref, cross_ref, side_ref):
    chip, core, mask = route()
    odd = core == 1

    def merged(keep, i, uneven):
        other = other_ref[i].astype(jnp.float32)
        return over(jnp.where(odd, other, keep), jnp.where(odd, keep, other), uneven)

    own_ref[...] = merged(blocks_ref[chip, core], 0, odd)
    for i, p in enumerate((1 - core, core)):
        side_ref[i] = merged(blocks_ref[chip ^ mask, p], 2 + p, p == 1).astype(jnp.bfloat16)
    cross_ref[...] = merged(blocks_ref[chip ^ 3, 1 - core], 1, jnp.logical_not(odd)).astype(jnp.bfloat16)


def merge(blocks, other):
    rows, columns = other.shape[1:]
    return pl.pallas_call(
        merge_kernel,
        in_specs=[WHOLE] * 2,
        out_specs=[WHOLE] * 3,
        out_shape=[
            jax.ShapeDtypeStruct((rows, columns), jnp.float32),
            jax.ShapeDtypeStruct((rows, columns), jnp.bfloat16),
            jax.ShapeDtypeStruct((2, rows, columns), jnp.bfloat16),
        ],
        compiler_params=pltpu.CompilerParams(vmem_limit_bytes=8 * 1024 * 1024),
    )(blocks, other)


def pass_kernel(side_ref, out_ref):
    out_ref[...] = side_ref[1]


def pass_on(side):
    return pl.pallas_call(
        pass_kernel,
        in_specs=[WHOLE],
        out_specs=WHOLE,
        out_shape=jax.ShapeDtypeStruct(side.shape[1:], side.dtype),
        compiler_params=pltpu.CompilerParams(vmem_limit_bytes=4 * 1024 * 1024),
    )(side)


def gather_kernel(side_ref, cross_ref, passed_ref, own_ref, out_ref):
    share = out_ref.shape[1]
    chip, core, mask = route()
    odd, serves_x = core == 1, mask == 1
    side, passed = side_ref[0].astype(jnp.float32), passed_ref[...].astype(jnp.float32)
    parts = [
        own_ref[...],
        jnp.where(serves_x, side, passed),
        jnp.where(serves_x, passed, side),
        cross_ref[...].astype(jnp.float32),
    ]
    step = 1
    while len(parts) > 1:
        swap = (chip & step) != 0
        parts = [
            over(jnp.where(swap, parts[i + 1], parts[i]), jnp.where(swap, parts[i], parts[i + 1]), odd)
            for i in range(0, len(parts), 2)
        ]
        step *= 2
    planes = [parts[0][c * share : (c + 1) * share] for c in range(4)]
    for c in range(4):
        out_ref[c] = jnp.where(odd, planes[c ^ 1], planes[c])


def gather(parts, share):
    columns = parts[-1].shape[1]
    return pl.pallas_call(
        gather_kernel,
        in_specs=[WHOLE] * len(parts),
        out_specs=WHOLE,
        out_shape=jax.ShapeDtypeStruct((4, share, columns), jnp.float32),
        compiler_params=pltpu.CompilerParams(vmem_limit_bytes=4 * 1024 * 1024),
    )(*parts)


def finish_kernel(parts_ref, out_ref):
    count = parts_ref.shape[0]
    _, share, columns = out_ref.shape
    remaining = jnp.ones((share, columns), jnp.float32)
    sums = [jnp.zeros((share, columns), jnp.float32) for _ in range(3)]
    for k in range(count):
        part = parts_ref[k].astype(jnp.float32)
        for c in range(3):
            sums[c] = sums[c] + remaining * part[c * share : (c + 1) * share]
        remaining = remaining - remaining * part[3 * share :]
    for c in range(3):
        out_ref[c] = sums[c]
    out_ref[3] = 1.0 - remaining


def finish(parts, share):
    columns = parts.shape[2]
    return pl.pallas_call(
        finish_kernel,
        in_specs=[WHOLE],
        out_specs=WHOLE,
        out_shape=jax.ShapeDtypeStruct((4, share, columns), jnp.float32),
        compiler_params=pltpu.CompilerParams(vmem_limit_bytes=4 * 1024 * 1024),
    )(parts)


def swapped(values, kinds):
    depth_count, row_count = lax.axis_size("depth"), lax.axis_size("rows")
    perm = []
    for d in range(depth_count):
        for r in range(row_count):
            kind = kinds[r % 2]
            e, q = d, r
            if kind == "near slab":
                e = d ^ 1
            elif kind == "far slab":
                e = d + 1 if d % 2 else d - 1
                e = depth_count - 1 - d if not 0 <= e < depth_count else e
            else:
                q = r ^ 1 if kind == "near row" else (r + 1 if r % 2 else r - 1)
                if not 0 <= q < row_count:
                    e, q = d ^ 1, r
            perm.append((d * row_count + r, e * row_count + q))
    return lax.ppermute(values, ("depth", "rows"), perm)


def exchanged(values, mask):
    masks = [mask(d) if callable(mask) else mask for d in range(lax.axis_size("depth"))]
    return lax.ppermute(values, "depth", [(d, d ^ m) for d, m in enumerate(masks)])


def body(volume, color_map, alpha_map):
    depth_count = lax.axis_size("depth")
    share = volume.shape[2] // depth_count
    first, rows_near, second, rows_far = cut_edges(volume)
    first = swapped(first, ("far slab", "near slab"))
    rows_near = swapped(rows_near, ("near row", "near row"))
    second = swapped(second, ("near slab", "far slab"))
    rows_far = swapped(rows_far, ("far row", "far row"))
    interior = march_interior(volume, color_map, alpha_map, depth_count)
    halos = (first, rows_near, second, rows_far)
    paired = depth_count == 8 and 2 * share == SUBLANES
    outs = add_edges(volume, interior, halos, depth_count, paired)
    if not paired:
        return finish(lax.all_to_all(outs[0], "depth", 0, 0, tiled=True), share)
    blocks, give = outs
    own, cross, side = merge(blocks, exchanged(give, 1))
    side = exchanged(side, lambda d: 2 * served(d) + 1)
    cross = exchanged(cross, 7)
    return gather((side, cross, exchanged(pass_on(side), 1), own), share)


def solution(mesh):
    in_specs = (P(None, "depth", "rows", None), P(), P())
    out_specs = P(None, ("rows", "depth"), None)
    return jax.shard_map(body, mesh=mesh, in_specs=in_specs, out_specs=out_specs, check_vma=False)
```

```python
import functools

import jax
import jax.numpy as jnp
from jax import lax
from jax.experimental import pallas as pl
from jax.experimental.pallas import tpu as pltpu
from jax.sharding import PartitionSpec as P

AMBIENT = 0.3
DIFFUSE = 0.7
LIGHT_DEPTH = 0.48 * DIFFUSE
LIGHT_ROWS = 0.6 * DIFFUSE
LIGHT_COLS = 0.64 * DIFFUSE
OPACITY = 4.0
LANES = 128
SUBLANES = 8
WHOLE = pl.BlockSpec(memory_space=pltpu.VMEM)


def parity(axis):
    return lax.axis_index(axis) % 2


def ends(axis):
    position = lax.axis_index(axis)
    return position == 0, position == lax.axis_size(axis) - 1


def edges_kernel(volume_ref, first_out, rows_near_out, second_out, rows_far_out, strip_ref, plane_ref, sems):
    _, slices, height, columns = volume_ref.shape
    odd, odd_row = parity("depth"), parity("rows")
    far_first = 1 - odd_row
    last_first = odd ^ far_first ^ 1
    copies = [
        pltpu.make_async_copy(volume_ref.at[0, last_first * (slices - 1)], plane_ref.at[0], sems.at[0]),
        pltpu.make_async_copy(volume_ref.at[0, :, (1 - odd_row) * (height - 1)], strip_ref.at[0], sems.at[1]),
        pltpu.make_async_copy(volume_ref.at[0, (1 - last_first) * (slices - 1)], plane_ref.at[1], sems.at[2]),
        pltpu.make_async_copy(volume_ref.at[0, :, odd_row * (height - 1)], strip_ref.at[1], sems.at[3]),
    ]
    for copy in copies:
        copy.start()

    def narrow(values):
        return values.astype(jnp.float32).astype(jnp.bfloat16)

    def padded(strip):
        return narrow(jnp.concatenate([strip, jnp.zeros((height - slices, columns), jnp.int32)], axis=0))

    copies[0].wait()
    first_out[...] = narrow(plane_ref[0])
    copies[1].wait()
    rows_near_out[...] = padded(strip_ref[0])
    copies[2].wait()
    second_out[...] = narrow(plane_ref[1])
    copies[3].wait()
    rows_far_out[...] = narrow(strip_ref[1])


def cut_edges(volume):
    _, slices, height, columns = volume.shape
    plane = jax.ShapeDtypeStruct((height, columns), jnp.bfloat16)
    strip = jax.ShapeDtypeStruct((slices, columns), jnp.bfloat16)
    return pl.pallas_call(
        edges_kernel,
        in_specs=[pl.BlockSpec(memory_space=pl.ANY)],
        out_specs=[WHOLE] * 4,
        out_shape=[plane, plane, plane, strip],
        scratch_shapes=[
            pltpu.VMEM((2, slices, columns), jnp.int32),
            pltpu.VMEM((2, height, columns), jnp.int32),
            pltpu.SemaphoreType.DMA((4,)),
        ],
        compiler_params=pltpu.CompilerParams(vmem_limit_bytes=52 * 1024 * 1024),
    )(volume)


def pick(entries, places):
    dims = lax.GatherDimensionNumbers(
        offset_dims=(),
        collapsed_slice_dims=(1,),
        start_index_map=(1,),
        operand_batching_dims=(0,),
        start_indices_batching_dims=(0,),
    )
    return lax.gather(entries, places[..., None], dims, (1, 1), mode=lax.GatherScatterMode.PROMISE_IN_BOUNDS)


def shade(grad_depth, facing, squares):
    facing = facing + LIGHT_DEPTH * grad_depth
    squares = squares + grad_depth * grad_depth
    return AMBIENT + jnp.abs(facing) * lax.rsqrt(jnp.maximum(squares, 4.0))


def interior_kernel(
    opacity_scale,
    volume_ref,
    color_ref,
    alpha_ref,
    base_ref,
    face_ref,
    square_ref,
    lit_ref,
    grad_ref,
    strip_ref,
    pair_ref,
    held_ref,
):
    _, slices, height, columns = volume_ref.shape
    tiles = height // SUBLANES
    chunks = columns // LANES
    tile = (SUBLANES, LANES)
    strip = (slices, LANES)

    packed = color_ref[0:1, :] + color_ref[1:2, :] * 256 + color_ref[2:3, :] * 65536
    color_low, color_high = packed[:, :LANES], packed[:, LANES:]
    alpha_both = alpha_ref[0:1, :LANES] + alpha_ref[0:1, LANES:] * 256

    def colors(value, tables):
        low, high = tables
        place = value & (LANES - 1)
        color = jnp.where(value < LANES, pick(low, place), pick(high, place))
        parts = (color & 255, lax.shift_right_logical(color, 8) & 255, lax.shift_right_logical(color, 16))
        return [part.astype(jnp.float32) for part in parts]

    def opacity(level, table):
        entry = pick(table, level & (LANES - 1))
        entry = lax.shift_right_logical(entry, lax.shift_right_logical(level & LANES, 4)) & 255
        return entry.astype(jnp.float32) * opacity_scale

    tile_colors = [jnp.broadcast_to(t, tile) for t in (color_low, color_high)]
    tile_alpha = jnp.broadcast_to(alpha_both, tile)
    strip_colors = [jnp.broadcast_to(t, strip) for t in (color_low, color_high)]

    def masks(shape):
        lane = lax.broadcasted_iota(jnp.int32, shape, 1)
        row = lax.broadcasted_iota(jnp.int32, shape, 0)
        return lane == 0, lane == LANES - 1, row == 0, row == shape[0] - 1

    first_lane, last_lane, first_row, last_row = masks(tile)
    strip_first_lane, strip_last_lane, front, back = masks(strip)

    pairs = slices // 2
    top = SUBLANES

    def clear(j, carry):
        pair_ref[j] = jnp.zeros(pair_ref.shape[1:], jnp.int32)
        return carry

    clear(0, 0)
    clear(chunks + 1, 0)
    margin = jnp.zeros((pairs, SUBLANES, LANES), jnp.int32)

    def pack(j, carry):
        here = pl.ds(pl.multiple_of(j * LANES, LANES), LANES)
        pair_ref[j + 1, :, :top] = margin
        pair_ref[j + 1, :, top + height :] = margin
        for p in range(pairs):
            pair_ref[j + 1, p, top : top + height] = volume_ref[0, p, :, here] + lax.shift_left(
                volume_ref[0, p + pairs, :, here], 16
            )
        return carry

    lax.fori_loop(0, chunks, pack, 0)

    def split(difference):
        low = lax.shift_right_arithmetic(lax.shift_left(difference, 16), 16)
        high = lax.shift_right_arithmetic(difference + 32768, 16)
        return low.astype(jnp.float32), high.astype(jnp.float32)

    def across(left_value, value, right_value, first, last):
        west = pltpu.roll(jnp.where(last, left_value, value), 1, 1)
        east = pltpu.roll(jnp.where(first, right_value, value), LANES - 1, 1)
        return split(east - west)

    def chunk(j, carry):
        here = pl.ds(pl.multiple_of(j * LANES, LANES), LANES)

        for r in range(tiles):
            rows = slice(r * SUBLANES, (r + 1) * SUBLANES)
            values = [volume_ref[0, s, rows, here] for s in range(slices)]

            def words(c, p, offset=0):
                return pair_ref[c, p, top + r * SUBLANES + offset : top + (r + 1) * SUBLANES + offset, :]

            down, right = [], []
            for p in range(pairs):
                down.append(split(words(j + 1, p, 1) - words(j + 1, p, -1)))
                right.append(across(words(j, p), words(j + 1, p), words(j + 2, p), first_lane, last_lane))
            remaining = jnp.ones(tile, jnp.float32)
            sums = [jnp.zeros(tile, jnp.float32) for _ in range(3)]
            for s in range(slices):
                value = values[s]
                grad_rows = down[s % pairs][s // pairs]
                grad_cols = right[s % pairs][s // pairs]
                squares = grad_rows * grad_rows + grad_cols * grad_cols
                facing = LIGHT_ROWS * grad_rows + LIGHT_COLS * grad_cols
                weight = remaining * opacity(volume_ref[1, s, rows, here], tile_alpha)
                remaining = remaining - weight
                if r == 0:
                    held_ref[0, s : s + 1, :] = weight[:1]
                    weight = jnp.where(first_row, 0.0, weight)
                if r == tiles - 1:
                    held_ref[1, s : s + 1, :] = weight[SUBLANES - 1 :]
                    weight = jnp.where(last_row, 0.0, weight)
                emitted = colors(value, tile_colors)
                if 0 < s < slices - 1:
                    grad_depth = (values[s + 1] - values[s - 1]).astype(jnp.float32)
                    weight = weight * shade(grad_depth, facing, squares)
                    for c in range(3):
                        sums[c] = sums[c] + emitted[c] * weight
                else:
                    end = int(s > 0)
                    face_ref[end, rows, here] = facing
                    square_ref[end, rows, here] = squares
                    weight = weight * (1.0 / 255.0)
                    for c in range(3):
                        lit_ref[end, c, rows, here] = emitted[c] * weight
            for c in range(3):
                base_ref[c, rows, here] = sums[c] * (1.0 / 255.0)
            base_ref[3, rows, here] = 1.0 - remaining

        for q, (edge, inner) in enumerate(((0, 1), (height - 1, height - 2))):
            value = volume_ref[0, :, edge, here]
            behind = pltpu.roll(jnp.where(back, 0, value), 1, 0)
            ahead = pltpu.roll(jnp.where(front, 0, value), slices - 1, 0)
            grad_ref[q, 0, :, here] = (ahead - behind).astype(jnp.float32)
            grad_ref[q, 1, :, here] = volume_ref[0, :, inner, here].astype(jnp.float32)
            word = pair_ref[j + 1, :, top + edge, :]
            low, high = across(
                pair_ref[j, :, top + edge, :],
                word,
                pair_ref[j + 2, :, top + edge, :],
                strip_first_lane[:pairs],
                strip_last_lane[:pairs],
            )
            grad_ref[q, 2, :pairs, here] = low
            grad_ref[q, 2, pairs:, here] = high
            weight = held_ref[q] * (1.0 / 255.0)
            emitted = colors(value, strip_colors)
            for c in range(3):
                strip_ref[q, c, :, here] = emitted[c] * weight
        return carry

    lax.fori_loop(0, chunks, chunk, 0)


def march_interior(volume, color_map, alpha_map, depth_count):
    _, slices, height, columns = volume.shape
    opacity_scale = OPACITY / (255.0 * slices * depth_count)
    shapes = [
        (4, height, columns),
        (2, height, columns),
        (2, height, columns),
        (2, 3, height, columns),
        (2, 3, slices, columns),
        (2, 3, slices, columns),
    ]
    voxels = slices * height * columns
    return pl.pallas_call(
        functools.partial(interior_kernel, opacity_scale),
        in_specs=[WHOLE] * 3,
        out_specs=[WHOLE] * len(shapes),
        out_shape=[jax.ShapeDtypeStruct(shape, jnp.float32) for shape in shapes],
        scratch_shapes=[
            pltpu.VMEM((columns // LANES + 2, slices // 2, height + 2 * SUBLANES, LANES), jnp.int32),
            pltpu.VMEM((2, slices, LANES), jnp.float32),
        ],
        compiler_params=pltpu.CompilerParams(vmem_limit_bytes=24 * 1024 * 1024),
        cost_estimate=pl.CostEstimate(flops=voxels * 80, bytes_accessed=voxels * 20, transcendentals=voxels),
    )(volume, color_map, alpha_map.reshape(1, -1))


def row_sums(first, second):
    count = first.shape[0]
    if count != SUBLANES:
        return jnp.sum(first, axis=0, keepdims=True), jnp.sum(second, axis=0, keepdims=True)
    upper = lax.broadcasted_iota(jnp.int32, first.shape, 0) < 4
    both = jnp.where(upper, first, second) + pltpu.roll(jnp.where(upper, second, first), 4, 0)
    both = both + pltpu.roll(both, 6, 0)
    both = both + pltpu.roll(both, 7, 0)
    return both, pltpu.roll(both, 3, 0)


def edge_kernel(
    share, volume_ref, base_ref, face_ref, square_ref, lit_ref, grad_ref, strip_ref, first_ref, rows_near_ref, second_ref, rows_far_ref, *out_refs
):
    _, slices, height, columns = volume_ref.shape
    tiles = height // SUBLANES
    tile = (SUBLANES, LANES)
    row = lax.broadcasted_iota(jnp.int32, tile, 0)
    first_row, last_row, upper = row == 0, row == SUBLANES - 1, row < SUBLANES // 2
    level = lax.broadcasted_iota(jnp.int32, (slices, LANES), 0)
    front, back = level == 0, level == slices - 1
    odd, odd_row = parity("depth") == 1, parity("rows") == 1
    front_came_first = odd == odd_row
    front_end, back_end = ends("depth")
    top_end, bottom_end = ends("rows")

    def chunk(j, carry):
        here = pl.ds(pl.multiple_of(j * LANES, LANES), LANES)
        rows_near = rows_near_ref[:, here].astype(jnp.float32)[:slices]
        rows_far = rows_far_ref[:, here].astype(jnp.float32)
        above = jnp.where(top_end, 0.0, jnp.where(odd_row, rows_near, rows_far))
        below = jnp.where(bottom_end, 0.0, jnp.where(odd_row, rows_far, rows_near))
        first = first_ref[:, here].astype(jnp.float32)
        second = second_ref[:, here].astype(jnp.float32)
        before = jnp.where(front_end, 0.0, jnp.where(front_came_first, first, second))
        after = jnp.where(back_end, 0.0, jnp.where(front_came_first, second, first))
        extra = []
        for q, edge in enumerate((0, height - 1)):
            inner = grad_ref[q, 1, :, here]
            grad_rows = below - inner if q else inner - above
            grad_cols = grad_ref[q, 2, :, here]
            grad_depth = grad_ref[q, 0, :, here] + jnp.where(
                back, after[edge : edge + 1], jnp.where(front, -before[edge : edge + 1], 0.0)
            )
            shading = shade(
                grad_depth,
                LIGHT_ROWS * grad_rows + LIGHT_COLS * grad_cols,
                grad_rows * grad_rows + grad_cols * grad_cols,
            )
            extra.append([strip_ref[q, c, :, here] * shading for c in range(3)])
        extra = [row_sums(extra[0][c], extra[1][c]) for c in range(3)]
        for r in range(tiles):
            rows = slice(r * SUBLANES, (r + 1) * SUBLANES)
            planes = [base_ref[c, rows, here] for c in range(4)]
            for end in range(2):
                if end:
                    grad_depth = after[rows] - volume_ref[0, slices - 2, rows, here].astype(jnp.float32)
                else:
                    grad_depth = volume_ref[0, 1, rows, here].astype(jnp.float32) - before[rows]
                shading = shade(grad_depth, face_ref[end, rows, here], square_ref[end, rows, here])
                for c in range(3):
                    planes[c] = planes[c] + lit_ref[end, c, rows, here] * shading
            for c in range(3):
                if r == 0:
                    planes[c] = planes[c] + jnp.where(first_row, extra[c][0], 0.0)
                if r == tiles - 1:
                    planes[c] = planes[c] + jnp.where(last_row, extra[c][1], 0.0)
            if len(out_refs) == 1:
                for i, first in enumerate(range(0, SUBLANES, share)):
                    block = jnp.concatenate([plane[first : first + share] for plane in planes], axis=0)
                    out_refs[0][r * (SUBLANES // share) + i, :, here] = block.astype(jnp.bfloat16)
            else:
                halves = [(planes[c], pltpu.roll(planes[c + 1], SUBLANES // 2, 0)) for c in (0, 2)]
                even = jnp.concatenate([jnp.where(upper, own, turned) for own, turned in halves], axis=0)
                uneven = jnp.concatenate([jnp.where(upper, turned, own) for own, turned in halves], axis=0)
                blocks_ref, _ = out_refs
                blocks_ref[r, 0, :, here] = even
                blocks_ref[r, 1, :, here] = uneven
        return carry

    lax.fori_loop(0, columns // LANES, chunk, 0)
    if len(out_refs) > 1:
        blocks_ref, give_ref = out_refs
        chip, core, mask = route()
        given = (blocks_ref[chip, 1 - core], blocks_ref[chip ^ 3, core], blocks_ref[chip ^ mask ^ 3, 0], blocks_ref[chip ^ mask ^ 3, 1])
        for i, block in enumerate(given):
            give_ref[i] = block.astype(jnp.bfloat16)


def add_edges(volume, interior, halos, depth_count, paired):
    _, slices, height, columns = volume.shape
    share = height // depth_count
    if paired:
        block = (4 * share, columns)
        shapes = [
            jax.ShapeDtypeStruct((depth_count // 2, 2, *block), jnp.float32),
            jax.ShapeDtypeStruct((4, *block), jnp.bfloat16),
        ]
    else:
        shapes = [jax.ShapeDtypeStruct((depth_count, 4 * share, columns), jnp.bfloat16)]
    return pl.pallas_call(
        functools.partial(edge_kernel, share),
        in_specs=[WHOLE] * 11,
        out_specs=[WHOLE] * len(shapes),
        out_shape=shapes,
        compiler_params=pltpu.CompilerParams(vmem_limit_bytes=24 * 1024 * 1024),
    )(volume, *interior, *halos)


def served(depth):
    chip, core = depth // 2, depth % 2
    return 1 + (core ^ (chip & 1) ^ (chip >> 1))


def route():
    position = lax.axis_index("depth")
    return position // 2, position % 2, served(position)


def over(nearer, farther, uneven):
    share = nearer.shape[0] // 4
    clear = 1.0 - jnp.where(uneven, nearer[2 * share : 3 * share], nearer[3 * share :])
    return nearer + jnp.concatenate([clear] * 4, axis=0) * farther


def merge_kernel(blocks_ref, other_ref, own_ref, cross_ref, side_ref):
    chip, core, mask = route()
    odd = core == 1

    def merged(keep, i, uneven):
        other = other_ref[i].astype(jnp.float32)
        return over(jnp.where(odd, other, keep), jnp.where(odd, keep, other), uneven)

    own_ref[...] = merged(blocks_ref[chip, core], 0, odd)
    for i, p in enumerate((1 - core, core)):
        side_ref[i] = merged(blocks_ref[chip ^ mask, p], 2 + p, p == 1).astype(jnp.bfloat16)
    cross_ref[...] = merged(blocks_ref[chip ^ 3, 1 - core], 1, jnp.logical_not(odd)).astype(jnp.bfloat16)


def merge(blocks, other):
    rows, columns = other.shape[1:]
    return pl.pallas_call(
        merge_kernel,
        in_specs=[WHOLE] * 2,
        out_specs=[WHOLE] * 3,
        out_shape=[
            jax.ShapeDtypeStruct((rows, columns), jnp.float32),
            jax.ShapeDtypeStruct((rows, columns), jnp.bfloat16),
            jax.ShapeDtypeStruct((2, rows, columns), jnp.bfloat16),
        ],
        compiler_params=pltpu.CompilerParams(vmem_limit_bytes=8 * 1024 * 1024),
    )(blocks, other)


def pass_kernel(side_ref, out_ref):
    out_ref[...] = side_ref[1]


def pass_on(side):
    return pl.pallas_call(
        pass_kernel,
        in_specs=[WHOLE],
        out_specs=WHOLE,
        out_shape=jax.ShapeDtypeStruct(side.shape[1:], side.dtype),
        compiler_params=pltpu.CompilerParams(vmem_limit_bytes=4 * 1024 * 1024),
    )(side)


def gather_kernel(side_ref, cross_ref, passed_ref, own_ref, out_ref):
    share = out_ref.shape[1]
    chip, core, mask = route()
    odd, serves_x = core == 1, mask == 1
    side, passed = side_ref[0].astype(jnp.float32), passed_ref[...].astype(jnp.float32)
    parts = [
        own_ref[...],
        jnp.where(serves_x, side, passed),
        jnp.where(serves_x, passed, side),
        cross_ref[...].astype(jnp.float32),
    ]
    step = 1
    while len(parts) > 1:
        swap = (chip & step) != 0
        parts = [
            over(jnp.where(swap, parts[i + 1], parts[i]), jnp.where(swap, parts[i], parts[i + 1]), odd)
            for i in range(0, len(parts), 2)
        ]
        step *= 2
    planes = [parts[0][c * share : (c + 1) * share] for c in range(4)]
    for c in range(4):
        out_ref[c] = jnp.where(odd, planes[c ^ 1], planes[c])


def gather(parts, share):
    columns = parts[-1].shape[1]
    return pl.pallas_call(
        gather_kernel,
        in_specs=[WHOLE] * len(parts),
        out_specs=WHOLE,
        out_shape=jax.ShapeDtypeStruct((4, share, columns), jnp.float32),
        compiler_params=pltpu.CompilerParams(vmem_limit_bytes=4 * 1024 * 1024),
    )(*parts)


def finish_kernel(parts_ref, out_ref):
    count = parts_ref.shape[0]
    _, share, columns = out_ref.shape
    remaining = jnp.ones((share, columns), jnp.float32)
    sums = [jnp.zeros((share, columns), jnp.float32) for _ in range(3)]
    for k in range(count):
        part = parts_ref[k].astype(jnp.float32)
        for c in range(3):
            sums[c] = sums[c] + remaining * part[c * share : (c + 1) * share]
        remaining = remaining - remaining * part[3 * share :]
    for c in range(3):
        out_ref[c] = sums[c]
    out_ref[3] = 1.0 - remaining


def finish(parts, share):
    columns = parts.shape[2]
    return pl.pallas_call(
        finish_kernel,
        in_specs=[WHOLE],
        out_specs=WHOLE,
        out_shape=jax.ShapeDtypeStruct((4, share, columns), jnp.float32),
        compiler_params=pltpu.CompilerParams(vmem_limit_bytes=4 * 1024 * 1024),
    )(parts)


def swapped(values, kinds):
    depth_count, row_count = lax.axis_size("depth"), lax.axis_size("rows")
    perm = []
    for d in range(depth_count):
        for r in range(row_count):
            kind = kinds[r % 2]
            e, q = d, r
            if kind == "near slab":
                e = d ^ 1
            elif kind == "far slab":
                e = d + 1 if d % 2 else d - 1
                e = depth_count - 1 - d if not 0 <= e < depth_count else e
            else:
                q = r ^ 1 if kind == "near row" else (r + 1 if r % 2 else r - 1)
                if not 0 <= q < row_count:
                    e, q = d ^ 1, r
            perm.append((d * row_count + r, e * row_count + q))
    return lax.ppermute(values, ("depth", "rows"), perm)


def exchanged(values, mask):
    masks = [mask(d) if callable(mask) else mask for d in range(lax.axis_size("depth"))]
    return lax.ppermute(values, "depth", [(d, d ^ m) for d, m in enumerate(masks)])


def body(volume, color_map, alpha_map):
    depth_count = lax.axis_size("depth")
    share = volume.shape[2] // depth_count
    first, rows_near, second, rows_far = cut_edges(volume)
    first = swapped(first, ("far slab", "near slab"))
    rows_near = swapped(rows_near, ("near row", "near row"))
    second = swapped(second, ("near slab", "far slab"))
    rows_far = swapped(rows_far, ("far row", "far row"))
    interior = march_interior(volume, color_map, alpha_map, depth_count)
    halos = (first, rows_near, second, rows_far)
    paired = depth_count == 8 and 2 * share == SUBLANES
    outs = add_edges(volume, interior, halos, depth_count, paired)
    if not paired:
        return finish(lax.all_to_all(outs[0], "depth", 0, 0, tiled=True), share)
    blocks, give = outs
    own, cross, side = merge(blocks, exchanged(give, 1))
    side = exchanged(side, lambda d: 2 * served(d) + 1)
    cross = exchanged(cross, 7)
    return gather((side, cross, exchanged(pass_on(side), 1), own), share)


def solution(mesh):
    in_specs = (P(None, "depth", "rows", None), P(), P())
    out_specs = P(None, ("rows", "depth"), None)
    return jax.shard_map(body, mesh=mesh, in_specs=in_specs, out_specs=out_specs, check_vma=False)
```

```python
import functools

import jax
import jax.numpy as jnp
from jax import lax
from jax.experimental import pallas as pl
from jax.experimental.pallas import tpu as pltpu
from jax.sharding import PartitionSpec as P

AMBIENT = 0.3
DIFFUSE = 0.7
LIGHT_DEPTH = 0.48 * DIFFUSE
LIGHT_ROWS = 0.6 * DIFFUSE
LIGHT_COLS = 0.64 * DIFFUSE
OPACITY = 4.0
LANES = 128
SUBLANES = 8
WHOLE = pl.BlockSpec(memory_space=pltpu.VMEM)


def parity(axis):
    return lax.axis_index(axis) % 2


def ends(axis):
    position = lax.axis_index(axis)
    return position == 0, position == lax.axis_size(axis) - 1


def edges_kernel(volume_ref, first_out, rows_near_out, second_out, rows_far_out, strip_ref, plane_ref, sems):
    _, slices, height, columns = volume_ref.shape
    odd, odd_row = parity("depth"), parity("rows")
    far_first = 1 - odd_row
    last_first = odd ^ far_first ^ 1
    copies = [
        pltpu.make_async_copy(volume_ref.at[0, last_first * (slices - 1)], plane_ref.at[0], sems.at[0]),
        pltpu.make_async_copy(volume_ref.at[0, :, (1 - odd_row) * (height - 1)], strip_ref.at[0], sems.at[1]),
        pltpu.make_async_copy(volume_ref.at[0, (1 - last_first) * (slices - 1)], plane_ref.at[1], sems.at[2]),
        pltpu.make_async_copy(volume_ref.at[0, :, odd_row * (height - 1)], strip_ref.at[1], sems.at[3]),
    ]
    for copy in copies:
        copy.start()

    def narrow(values):
        return values.astype(jnp.float32).astype(jnp.bfloat16)

    def padded(strip):
        return narrow(jnp.concatenate([strip, jnp.zeros((height - slices, columns), jnp.int32)], axis=0))

    copies[0].wait()
    first_out[...] = narrow(plane_ref[0])
    copies[1].wait()
    rows_near_out[...] = padded(strip_ref[0])
    copies[2].wait()
    second_out[...] = narrow(plane_ref[1])
    copies[3].wait()
    rows_far_out[...] = narrow(strip_ref[1])


def cut_edges(volume):
    _, slices, height, columns = volume.shape
    plane = jax.ShapeDtypeStruct((height, columns), jnp.bfloat16)
    strip = jax.ShapeDtypeStruct((slices, columns), jnp.bfloat16)
    return pl.pallas_call(
        edges_kernel,
        in_specs=[pl.BlockSpec(memory_space=pl.ANY)],
        out_specs=[WHOLE] * 4,
        out_shape=[plane, plane, plane, strip],
        scratch_shapes=[
            pltpu.VMEM((2, slices, columns), jnp.int32),
            pltpu.VMEM((2, height, columns), jnp.int32),
            pltpu.SemaphoreType.DMA((4,)),
        ],
        compiler_params=pltpu.CompilerParams(vmem_limit_bytes=52 * 1024 * 1024),
    )(volume)


def pick(entries, places):
    dims = lax.GatherDimensionNumbers(
        offset_dims=(),
        collapsed_slice_dims=(1,),
        start_index_map=(1,),
        operand_batching_dims=(0,),
        start_indices_batching_dims=(0,),
    )
    return lax.gather(entries, places[..., None], dims, (1, 1), mode=lax.GatherScatterMode.PROMISE_IN_BOUNDS)


def shade(grad_depth, facing, squares):
    facing = facing + LIGHT_DEPTH * grad_depth
    squares = squares + grad_depth * grad_depth
    return AMBIENT + jnp.abs(facing) * lax.rsqrt(jnp.maximum(squares, 4.0))


def interior_kernel(
    opacity_scale,
    volume_ref,
    color_ref,
    alpha_ref,
    base_ref,
    face_ref,
    square_ref,
    lit_ref,
    grad_ref,
    strip_ref,
    pair_ref,
    held_ref,
):
    _, slices, height, columns = volume_ref.shape
    tiles = height // SUBLANES
    chunks = columns // LANES
    tile = (SUBLANES, LANES)
    strip = (slices, LANES)

    packed = color_ref[0:1, :] + color_ref[1:2, :] * 256 + color_ref[2:3, :] * 65536
    color_low, color_high = packed[:, :LANES], packed[:, LANES:]
    alpha_both = alpha_ref[0:1, :LANES] + alpha_ref[0:1, LANES:] * 256

    def colors(value, tables):
        low, high = tables
        place = value & (LANES - 1)
        color = jnp.where(value < LANES, pick(low, place), pick(high, place))
        parts = (color & 255, lax.shift_right_logical(color, 8) & 255, lax.shift_right_logical(color, 16))
        return [part.astype(jnp.float32) for part in parts]

    def opacity(level, table):
        entry = pick(table, level & (LANES - 1))
        entry = lax.shift_right_logical(entry, lax.shift_right_logical(level & LANES, 4)) & 255
        return entry.astype(jnp.float32) * opacity_scale

    tile_colors = [jnp.broadcast_to(t, tile) for t in (color_low, color_high)]
    tile_alpha = jnp.broadcast_to(alpha_both, tile)
    strip_colors = [jnp.broadcast_to(t, strip) for t in (color_low, color_high)]

    def masks(shape):
        lane = lax.broadcasted_iota(jnp.int32, shape, 1)
        row = lax.broadcasted_iota(jnp.int32, shape, 0)
        return lane == 0, lane == LANES - 1, row == 0, row == shape[0] - 1

    first_lane, last_lane, first_row, last_row = masks(tile)
    strip_first_lane, strip_last_lane, front, back = masks(strip)

    pairs = slices // 2
    top = SUBLANES

    def clear(j, carry):
        pair_ref[j] = jnp.zeros(pair_ref.shape[1:], jnp.int32)
        return carry

    clear(0, 0)
    clear(chunks + 1, 0)
    margin = jnp.zeros((pairs, SUBLANES, LANES), jnp.int32)

    def pack(j, carry):
        here = pl.ds(pl.multiple_of(j * LANES, LANES), LANES)
        pair_ref[j + 1, :, :top] = margin
        pair_ref[j + 1, :, top + height :] = margin
        for p in range(pairs):
            pair_ref[j + 1, p, top : top + height] = volume_ref[0, p, :, here] + lax.shift_left(
                volume_ref[0, p + pairs, :, here], 16
            )
        return carry

    lax.fori_loop(0, chunks, pack, 0)

    def split(difference):
        low = lax.shift_right_arithmetic(lax.shift_left(difference, 16), 16)
        high = lax.shift_right_arithmetic(difference + 32768, 16)
        return low.astype(jnp.float32), high.astype(jnp.float32)

    def across(left_value, value, right_value, first, last):
        west = pltpu.roll(jnp.where(last, left_value, value), 1, 1)
        east = pltpu.roll(jnp.where(first, right_value, value), LANES - 1, 1)
        return split(east - west)

    def chunk(j, carry):
        here = pl.ds(pl.multiple_of(j * LANES, LANES), LANES)

        for r in range(tiles):
            rows = slice(r * SUBLANES, (r + 1) * SUBLANES)
            values = [volume_ref[0, s, rows, here] for s in range(slices)]

            def words(c, p, offset=0):
                return pair_ref[c, p, top + r * SUBLANES + offset : top + (r + 1) * SUBLANES + offset, :]

            down, right = [], []
            for p in range(pairs):
                down.append(split(words(j + 1, p, 1) - words(j + 1, p, -1)))
                right.append(across(words(j, p), words(j + 1, p), words(j + 2, p), first_lane, last_lane))
            remaining = jnp.ones(tile, jnp.float32)
            sums = [jnp.zeros(tile, jnp.float32) for _ in range(3)]
            for s in range(slices):
                value = values[s]
                grad_rows = down[s % pairs][s // pairs]
                grad_cols = right[s % pairs][s // pairs]
                squares = grad_rows * grad_rows + grad_cols * grad_cols
                facing = LIGHT_ROWS * grad_rows + LIGHT_COLS * grad_cols
                weight = remaining * opacity(volume_ref[1, s, rows, here], tile_alpha)
                remaining = remaining - weight
                if r == 0:
                    held_ref[0, s : s + 1, :] = weight[:1]
                    weight = jnp.where(first_row, 0.0, weight)
                if r == tiles - 1:
                    held_ref[1, s : s + 1, :] = weight[SUBLANES - 1 :]
                    weight = jnp.where(last_row, 0.0, weight)
                emitted = colors(value, tile_colors)
                if 0 < s < slices - 1:
                    grad_depth = (values[s + 1] - values[s - 1]).astype(jnp.float32)
                    weight = weight * shade(grad_depth, facing, squares)
                    for c in range(3):
                        sums[c] = sums[c] + emitted[c] * weight
                else:
                    end = int(s > 0)
                    face_ref[end, rows, here] = facing
                    square_ref[end, rows, here] = squares
                    weight = weight * (1.0 / 255.0)
                    for c in range(3):
                        lit_ref[end, c, rows, here] = emitted[c] * weight
            for c in range(3):
                base_ref[c, rows, here] = sums[c] * (1.0 / 255.0)
            base_ref[3, rows, here] = 1.0 - remaining

        for q, (edge, inner) in enumerate(((0, 1), (height - 1, height - 2))):
            value = volume_ref[0, :, edge, here]
            behind = pltpu.roll(jnp.where(back, 0, value), 1, 0)
            ahead = pltpu.roll(jnp.where(front, 0, value), slices - 1, 0)
            grad_ref[q, 0, :, here] = (ahead - behind).astype(jnp.float32)
            grad_ref[q, 1, :, here] = volume_ref[0, :, inner, here].astype(jnp.float32)
            word = pair_ref[j + 1, :, top + edge, :]
            low, high = across(
                pair_ref[j, :, top + edge, :],
                word,
                pair_ref[j + 2, :, top + edge, :],
                strip_first_lane[:pairs],
                strip_last_lane[:pairs],
            )
            grad_ref[q, 2, :pairs, here] = low
            grad_ref[q, 2, pairs:, here] = high
            weight = held_ref[q] * (1.0 / 255.0)
            emitted = colors(value, strip_colors)
            for c in range(3):
                strip_ref[q, c, :, here] = emitted[c] * weight
        return carry

    lax.fori_loop(0, chunks, chunk, 0, unroll=2)


def march_interior(volume, color_map, alpha_map, depth_count):
    _, slices, height, columns = volume.shape
    opacity_scale = OPACITY / (255.0 * slices * depth_count)
    shapes = [
        (4, height, columns),
        (2, height, columns),
        (2, height, columns),
        (2, 3, height, columns),
        (2, 3, slices, columns),
        (2, 3, slices, columns),
    ]
    voxels = slices * height * columns
    return pl.pallas_call(
        functools.partial(interior_kernel, opacity_scale),
        in_specs=[WHOLE] * 3,
        out_specs=[WHOLE] * len(shapes),
        out_shape=[jax.ShapeDtypeStruct(shape, jnp.float32) for shape in shapes],
        scratch_shapes=[
            pltpu.VMEM((columns // LANES + 2, slices // 2, height + 2 * SUBLANES, LANES), jnp.int32),
            pltpu.VMEM((2, slices, LANES), jnp.float32),
        ],
        compiler_params=pltpu.CompilerParams(vmem_limit_bytes=24 * 1024 * 1024),
        cost_estimate=pl.CostEstimate(flops=voxels * 80, bytes_accessed=voxels * 20, transcendentals=voxels),
    )(volume, color_map, alpha_map.reshape(1, -1))


def row_sums(first, second):
    count = first.shape[0]
    if count != SUBLANES:
        return jnp.sum(first, axis=0, keepdims=True), jnp.sum(second, axis=0, keepdims=True)
    upper = lax.broadcasted_iota(jnp.int32, first.shape, 0) < 4
    both = jnp.where(upper, first, second) + pltpu.roll(jnp.where(upper, second, first), 4, 0)
    both = both + pltpu.roll(both, 6, 0)
    both = both + pltpu.roll(both, 7, 0)
    return both, pltpu.roll(both, 3, 0)


def edge_kernel(
    share, volume_ref, base_ref, face_ref, square_ref, lit_ref, grad_ref, strip_ref, first_ref, rows_near_ref, second_ref, rows_far_ref, *out_refs
):
    _, slices, height, columns = volume_ref.shape
    tiles = height // SUBLANES
    tile = (SUBLANES, LANES)
    row = lax.broadcasted_iota(jnp.int32, tile, 0)
    first_row, last_row, upper = row == 0, row == SUBLANES - 1, row < SUBLANES // 2
    level = lax.broadcasted_iota(jnp.int32, (slices, LANES), 0)
    front, back = level == 0, level == slices - 1
    odd, odd_row = parity("depth") == 1, parity("rows") == 1
    front_came_first = odd == odd_row
    front_end, back_end = ends("depth")
    top_end, bottom_end = ends("rows")

    def chunk(j, carry):
        here = pl.ds(pl.multiple_of(j * LANES, LANES), LANES)
        rows_near = rows_near_ref[:, here].astype(jnp.float32)[:slices]
        rows_far = rows_far_ref[:, here].astype(jnp.float32)
        above = jnp.where(top_end, 0.0, jnp.where(odd_row, rows_near, rows_far))
        below = jnp.where(bottom_end, 0.0, jnp.where(odd_row, rows_far, rows_near))
        first = first_ref[:, here].astype(jnp.float32)
        second = second_ref[:, here].astype(jnp.float32)
        before = jnp.where(front_end, 0.0, jnp.where(front_came_first, first, second))
        after = jnp.where(back_end, 0.0, jnp.where(front_came_first, second, first))
        extra = []
        for q, edge in enumerate((0, height - 1)):
            inner = grad_ref[q, 1, :, here]
            grad_rows = below - inner if q else inner - above
            grad_cols = grad_ref[q, 2, :, here]
            grad_depth = grad_ref[q, 0, :, here] + jnp.where(
                back, after[edge : edge + 1], jnp.where(front, -before[edge : edge + 1], 0.0)
            )
            shading = shade(
                grad_depth,
                LIGHT_ROWS * grad_rows + LIGHT_COLS * grad_cols,
                grad_rows * grad_rows + grad_cols * grad_cols,
            )
            extra.append([strip_ref[q, c, :, here] * shading for c in range(3)])
        extra = [row_sums(extra[0][c], extra[1][c]) for c in range(3)]
        for r in range(tiles):
            rows = slice(r * SUBLANES, (r + 1) * SUBLANES)
            planes = [base_ref[c, rows, here] for c in range(4)]
            for end in range(2):
                if end:
                    grad_depth = after[rows] - volume_ref[0, slices - 2, rows, here].astype(jnp.float32)
                else:
                    grad_depth = volume_ref[0, 1, rows, here].astype(jnp.float32) - before[rows]
                shading = shade(grad_depth, face_ref[end, rows, here], square_ref[end, rows, here])
                for c in range(3):
                    planes[c] = planes[c] + lit_ref[end, c, rows, here] * shading
            for c in range(3):
                if r == 0:
                    planes[c] = planes[c] + jnp.where(first_row, extra[c][0], 0.0)
                if r == tiles - 1:
                    planes[c] = planes[c] + jnp.where(last_row, extra[c][1], 0.0)
            if len(out_refs) == 1:
                for i, first in enumerate(range(0, SUBLANES, share)):
                    block = jnp.concatenate([plane[first : first + share] for plane in planes], axis=0)
                    out_refs[0][r * (SUBLANES // share) + i, :, here] = block.astype(jnp.bfloat16)
            else:
                halves = [(planes[c], pltpu.roll(planes[c + 1], SUBLANES // 2, 0)) for c in (0, 2)]
                even = jnp.concatenate([jnp.where(upper, own, turned) for own, turned in halves], axis=0)
                uneven = jnp.concatenate([jnp.where(upper, turned, own) for own, turned in halves], axis=0)
                blocks_ref, _ = out_refs
                blocks_ref[r, 0, :, here] = even
                blocks_ref[r, 1, :, here] = uneven
        return carry

    lax.fori_loop(0, columns // LANES, chunk, 0, unroll=4)
    if len(out_refs) > 1:
        blocks_ref, give_ref = out_refs
        chip, core, mask = route()
        given = (blocks_ref[chip, 1 - core], blocks_ref[chip ^ 3, core], blocks_ref[chip ^ mask ^ 3, 0], blocks_ref[chip ^ mask ^ 3, 1])
        for i, block in enumerate(given):
            give_ref[i] = block.astype(jnp.bfloat16)


def add_edges(volume, interior, halos, depth_count, paired):
    _, slices, height, columns = volume.shape
    share = height // depth_count
    if paired:
        block = (4 * share, columns)
        shapes = [
            jax.ShapeDtypeStruct((depth_count // 2, 2, *block), jnp.float32),
            jax.ShapeDtypeStruct((4, *block), jnp.bfloat16),
        ]
    else:
        shapes = [jax.ShapeDtypeStruct((depth_count, 4 * share, columns), jnp.bfloat16)]
    return pl.pallas_call(
        functools.partial(edge_kernel, share),
        in_specs=[WHOLE] * 11,
        out_specs=[WHOLE] * len(shapes),
        out_shape=shapes,
        compiler_params=pltpu.CompilerParams(vmem_limit_bytes=24 * 1024 * 1024),
    )(volume, *interior, *halos)


def served(depth):
    chip, core = depth // 2, depth % 2
    return 1 + (core ^ (chip & 1) ^ (chip >> 1))


def route():
    position = lax.axis_index("depth")
    return position // 2, position % 2, served(position)


def over(nearer, farther, uneven):
    share = nearer.shape[0] // 4
    clear = 1.0 - jnp.where(uneven, nearer[2 * share : 3 * share], nearer[3 * share :])
    return nearer + jnp.concatenate([clear] * 4, axis=0) * farther


def merge_kernel(blocks_ref, other_ref, own_ref, cross_ref, side_ref):
    chip, core, mask = route()
    odd = core == 1

    def merged(keep, i, uneven):
        other = other_ref[i].astype(jnp.float32)
        return over(jnp.where(odd, other, keep), jnp.where(odd, keep, other), uneven)

    own_ref[...] = merged(blocks_ref[chip, core], 0, odd)
    for i, p in enumerate((1 - core, core)):
        side_ref[i] = merged(blocks_ref[chip ^ mask, p], 2 + p, p == 1).astype(jnp.bfloat16)
    cross_ref[...] = merged(blocks_ref[chip ^ 3, 1 - core], 1, jnp.logical_not(odd)).astype(jnp.bfloat16)


def merge(blocks, other):
    rows, columns = other.shape[1:]
    return pl.pallas_call(
        merge_kernel,
        in_specs=[WHOLE] * 2,
        out_specs=[WHOLE] * 3,
        out_shape=[
            jax.ShapeDtypeStruct((rows, columns), jnp.float32),
            jax.ShapeDtypeStruct((rows, columns), jnp.bfloat16),
            jax.ShapeDtypeStruct((2, rows, columns), jnp.bfloat16),
        ],
        compiler_params=pltpu.CompilerParams(vmem_limit_bytes=8 * 1024 * 1024),
    )(blocks, other)


def pass_kernel(side_ref, out_ref):
    out_ref[...] = side_ref[1]


def pass_on(side):
    return pl.pallas_call(
        pass_kernel,
        in_specs=[WHOLE],
        out_specs=WHOLE,
        out_shape=jax.ShapeDtypeStruct(side.shape[1:], side.dtype),
        compiler_params=pltpu.CompilerParams(vmem_limit_bytes=4 * 1024 * 1024),
    )(side)


def gather_kernel(side_ref, cross_ref, passed_ref, own_ref, out_ref):
    share = out_ref.shape[1]
    chip, core, mask = route()
    odd, serves_x = core == 1, mask == 1
    side, passed = side_ref[0].astype(jnp.float32), passed_ref[...].astype(jnp.float32)
    parts = [
        own_ref[...],
        jnp.where(serves_x, side, passed),
        jnp.where(serves_x, passed, side),
        cross_ref[...].astype(jnp.float32),
    ]
    step = 1
    while len(parts) > 1:
        swap = (chip & step) != 0
        parts = [
            over(jnp.where(swap, parts[i + 1], parts[i]), jnp.where(swap, parts[i], parts[i + 1]), odd)
            for i in range(0, len(parts), 2)
        ]
        step *= 2
    planes = [parts[0][c * share : (c + 1) * share] for c in range(4)]
    for c in range(4):
        out_ref[c] = jnp.where(odd, planes[c ^ 1], planes[c])


def gather(parts, share):
    columns = parts[-1].shape[1]
    return pl.pallas_call(
        gather_kernel,
        in_specs=[WHOLE] * len(parts),
        out_specs=WHOLE,
        out_shape=jax.ShapeDtypeStruct((4, share, columns), jnp.float32),
        compiler_params=pltpu.CompilerParams(vmem_limit_bytes=4 * 1024 * 1024),
    )(*parts)


def finish_kernel(parts_ref, out_ref):
    count = parts_ref.shape[0]
    _, share, columns = out_ref.shape
    remaining = jnp.ones((share, columns), jnp.float32)
    sums = [jnp.zeros((share, columns), jnp.float32) for _ in range(3)]
    for k in range(count):
        part = parts_ref[k].astype(jnp.float32)
        for c in range(3):
            sums[c] = sums[c] + remaining * part[c * share : (c + 1) * share]
        remaining = remaining - remaining * part[3 * share :]
    for c in range(3):
        out_ref[c] = sums[c]
    out_ref[3] = 1.0 - remaining


def finish(parts, share):
    columns = parts.shape[2]
    return pl.pallas_call(
        finish_kernel,
        in_specs=[WHOLE],
        out_specs=WHOLE,
        out_shape=jax.ShapeDtypeStruct((4, share, columns), jnp.float32),
        compiler_params=pltpu.CompilerParams(vmem_limit_bytes=4 * 1024 * 1024),
    )(parts)


def swapped(values, kinds):
    depth_count, row_count = lax.axis_size("depth"), lax.axis_size("rows")
    perm = []
    for d in range(depth_count):
        for r in range(row_count):
            kind = kinds[r % 2]
            e, q = d, r
            if kind == "near slab":
                e = d ^ 1
            elif kind == "far slab":
                e = d + 1 if d % 2 else d - 1
                e = depth_count - 1 - d if not 0 <= e < depth_count else e
            else:
                q = r ^ 1 if kind == "near row" else (r + 1 if r % 2 else r - 1)
                if not 0 <= q < row_count:
                    e, q = d ^ 1, r
            perm.append((d * row_count + r, e * row_count + q))
    return lax.ppermute(values, ("depth", "rows"), perm)


def exchanged(values, mask):
    masks = [mask(d) if callable(mask) else mask for d in range(lax.axis_size("depth"))]
    return lax.ppermute(values, "depth", [(d, d ^ m) for d, m in enumerate(masks)])


def body(volume, color_map, alpha_map):
    depth_count = lax.axis_size("depth")
    share = volume.shape[2] // depth_count
    first, rows_near, second, rows_far = cut_edges(volume)
    first = swapped(first, ("far slab", "near slab"))
    rows_near = swapped(rows_near, ("near row", "near row"))
    second = swapped(second, ("near slab", "far slab"))
    rows_far = swapped(rows_far, ("far row", "far row"))
    interior = march_interior(volume, color_map, alpha_map, depth_count)
    halos = (first, rows_near, second, rows_far)
    paired = depth_count == 8 and 2 * share == SUBLANES
    outs = add_edges(volume, interior, halos, depth_count, paired)
    if not paired:
        return finish(lax.all_to_all(outs[0], "depth", 0, 0, tiled=True), share)
    blocks, give = outs
    own, cross, side = merge(blocks, exchanged(give, 1))
    side = exchanged(side, lambda d: 2 * served(d) + 1)
    cross = exchanged(cross, 7)
    return gather((side, cross, exchanged(pass_on(side), 1), own), share)


def solution(mesh):
    in_specs = (P(None, "depth", "rows", None), P(), P())
    out_specs = P(None, ("rows", "depth"), None)
    return jax.shard_map(body, mesh=mesh, in_specs=in_specs, out_specs=out_specs, check_vma=False)
```

```python
import functools

import jax
import jax.numpy as jnp
from jax import lax
from jax.experimental import pallas as pl
from jax.experimental.pallas import tpu as pltpu
from jax.sharding import PartitionSpec as P

AMBIENT = 0.3
DIFFUSE = 0.7
LIGHT_DEPTH = 0.48 * DIFFUSE
LIGHT_ROWS = 0.6 * DIFFUSE
LIGHT_COLS = 0.64 * DIFFUSE
OPACITY = 4.0
LANES = 128
SUBLANES = 8
WHOLE = pl.BlockSpec(memory_space=pltpu.VMEM)


def parity(axis):
    return lax.axis_index(axis) % 2


def ends(axis):
    position = lax.axis_index(axis)
    return position == 0, position == lax.axis_size(axis) - 1


def edges_kernel(volume_ref, first_out, rows_near_out, second_out, rows_far_out, strip_ref, plane_ref, sems):
    _, slices, height, columns = volume_ref.shape
    odd, odd_row = parity("depth"), parity("rows")
    far_first = 1 - odd_row
    last_first = odd ^ far_first ^ 1
    tiles = height // SUBLANES

    def plane_copies(i, s):
        for t in range(tiles):
            rows = pl.ds(t * SUBLANES, SUBLANES)
            yield pltpu.make_async_copy(volume_ref.at[0, s, rows], plane_ref.at[i, rows], sems.at[i, t])

    def strip_copy(i, row):
        return pltpu.make_async_copy(volume_ref.at[0, :, row], strip_ref.at[i], sems.at[2, i])

    copies = [
        list(plane_copies(0, last_first * (slices - 1))),
        [strip_copy(0, (1 - odd_row) * (height - 1))],
        list(plane_copies(1, (1 - last_first) * (slices - 1))),
        [strip_copy(1, odd_row * (height - 1))],
    ]
    for group in copies:
        for copy in group:
            copy.start()

    def arrive(group):
        for copy in group:
            copy.wait()

    def narrow(values):
        return values.astype(jnp.float32).astype(jnp.bfloat16)

    def padded(strip):
        return narrow(jnp.concatenate([strip, jnp.zeros((height - slices, columns), jnp.int32)], axis=0))

    arrive(copies[0])
    first_out[...] = narrow(plane_ref[0])
    arrive(copies[1])
    rows_near_out[...] = padded(strip_ref[0])
    arrive(copies[2])
    second_out[...] = narrow(plane_ref[1])
    arrive(copies[3])
    rows_far_out[...] = narrow(strip_ref[1])


def cut_edges(volume):
    _, slices, height, columns = volume.shape
    plane = jax.ShapeDtypeStruct((height, columns), jnp.bfloat16)
    strip = jax.ShapeDtypeStruct((slices, columns), jnp.bfloat16)
    return pl.pallas_call(
        edges_kernel,
        in_specs=[pl.BlockSpec(memory_space=pl.ANY)],
        out_specs=[WHOLE] * 4,
        out_shape=[plane, plane, plane, strip],
        scratch_shapes=[
            pltpu.VMEM((2, slices, columns), jnp.int32),
            pltpu.VMEM((2, height, columns), jnp.int32),
            pltpu.SemaphoreType.DMA((3, max(2, height // SUBLANES))),
        ],
        compiler_params=pltpu.CompilerParams(vmem_limit_bytes=52 * 1024 * 1024),
    )(volume)


def pick(entries, places):
    dims = lax.GatherDimensionNumbers(
        offset_dims=(),
        collapsed_slice_dims=(1,),
        start_index_map=(1,),
        operand_batching_dims=(0,),
        start_indices_batching_dims=(0,),
    )
    return lax.gather(entries, places[..., None], dims, (1, 1), mode=lax.GatherScatterMode.PROMISE_IN_BOUNDS)


def shade(grad_depth, facing, squares):
    facing = facing + LIGHT_DEPTH * grad_depth
    squares = squares + grad_depth * grad_depth
    return AMBIENT + jnp.abs(facing) * lax.rsqrt(jnp.maximum(squares, 4.0))


def interior_kernel(
    opacity_scale,
    volume_ref,
    color_ref,
    alpha_ref,
    base_ref,
    face_ref,
    square_ref,
    lit_ref,
    grad_ref,
    strip_ref,
    pair_ref,
    held_ref,
):
    _, slices, height, columns = volume_ref.shape
    tiles = height // SUBLANES
    chunks = columns // LANES
    tile = (SUBLANES, LANES)
    strip = (slices, LANES)

    packed = color_ref[0:1, :] + color_ref[1:2, :] * 256 + color_ref[2:3, :] * 65536
    color_low, color_high = packed[:, :LANES], packed[:, LANES:]
    alpha_both = alpha_ref[0:1, :LANES] + alpha_ref[0:1, LANES:] * 256

    def colors(value, tables):
        low, high = tables
        place = value & (LANES - 1)
        color = jnp.where(value < LANES, pick(low, place), pick(high, place))
        parts = (color & 255, lax.shift_right_logical(color, 8) & 255, lax.shift_right_logical(color, 16))
        return [part.astype(jnp.float32) for part in parts]

    def opacity(level, table):
        entry = pick(table, level & (LANES - 1))
        entry = lax.shift_right_logical(entry, lax.shift_right_logical(level & LANES, 4)) & 255
        return entry.astype(jnp.float32) * opacity_scale

    tile_colors = [jnp.broadcast_to(t, tile) for t in (color_low, color_high)]
    tile_alpha = jnp.broadcast_to(alpha_both, tile)
    strip_colors = [jnp.broadcast_to(t, strip) for t in (color_low, color_high)]

    def masks(shape):
        lane = lax.broadcasted_iota(jnp.int32, shape, 1)
        row = lax.broadcasted_iota(jnp.int32, shape, 0)
        return lane == 0, lane == LANES - 1, row == 0, row == shape[0] - 1

    first_lane, last_lane, first_row, last_row = masks(tile)
    strip_first_lane, strip_last_lane, front, back = masks(strip)

    pairs = slices // 2
    top = SUBLANES

    def clear(j, carry):
        pair_ref[j] = jnp.zeros(pair_ref.shape[1:], jnp.int32)
        return carry

    clear(0, 0)
    clear(chunks + 1, 0)
    margin = jnp.zeros((pairs, SUBLANES, LANES), jnp.int32)

    def pack(j, carry):
        here = pl.ds(pl.multiple_of(j * LANES, LANES), LANES)
        pair_ref[j + 1, :, :top] = margin
        pair_ref[j + 1, :, top + height :] = margin
        for p in range(pairs):
            pair_ref[j + 1, p, top : top + height] = volume_ref[0, p, :, here] + lax.shift_left(
                volume_ref[0, p + pairs, :, here], 16
            )
        return carry

    lax.fori_loop(0, chunks, pack, 0)

    def split(difference):
        low = lax.shift_right_arithmetic(lax.shift_left(difference, 16), 16)
        high = lax.shift_right_arithmetic(difference + 32768, 16)
        return low.astype(jnp.float32), high.astype(jnp.float32)

    def across(left_value, value, right_value, first, last):
        west = pltpu.roll(jnp.where(last, left_value, value), 1, 1)
        east = pltpu.roll(jnp.where(first, right_value, value), LANES - 1, 1)
        return split(east - west)

    def chunk(j, carry):
        here = pl.ds(pl.multiple_of(j * LANES, LANES), LANES)

        for r in range(tiles):
            rows = slice(r * SUBLANES, (r + 1) * SUBLANES)
            values = [volume_ref[0, s, rows, here] for s in range(slices)]

            def words(c, p, offset=0):
                return pair_ref[c, p, top + r * SUBLANES + offset : top + (r + 1) * SUBLANES + offset, :]

            down, right = [], []
            for p in range(pairs):
                down.append(split(words(j + 1, p, 1) - words(j + 1, p, -1)))
                right.append(across(words(j, p), words(j + 1, p), words(j + 2, p), first_lane, last_lane))
            remaining = jnp.ones(tile, jnp.float32)
            sums = [jnp.zeros(tile, jnp.float32) for _ in range(3)]
            for s in range(slices):
                value = values[s]
                grad_rows = down[s % pairs][s // pairs]
                grad_cols = right[s % pairs][s // pairs]
                squares = grad_rows * grad_rows + grad_cols * grad_cols
                facing = LIGHT_ROWS * grad_rows + LIGHT_COLS * grad_cols
                weight = remaining * opacity(volume_ref[1, s, rows, here], tile_alpha)
                remaining = remaining - weight
                if r == 0:
                    held_ref[0, s : s + 1, :] = weight[:1]
                    weight = jnp.where(first_row, 0.0, weight)
                if r == tiles - 1:
                    held_ref[1, s : s + 1, :] = weight[SUBLANES - 1 :]
                    weight = jnp.where(last_row, 0.0, weight)
                emitted = colors(value, tile_colors)
                if 0 < s < slices - 1:
                    grad_depth = (values[s + 1] - values[s - 1]).astype(jnp.float32)
                    weight = weight * shade(grad_depth, facing, squares)
                    for c in range(3):
                        sums[c] = sums[c] + emitted[c] * weight
                else:
                    end = int(s > 0)
                    face_ref[end, rows, here] = facing
                    square_ref[end, rows, here] = squares
                    weight = weight * (1.0 / 255.0)
                    for c in range(3):
                        lit_ref[end, c, rows, here] = emitted[c] * weight
            for c in range(3):
                base_ref[c, rows, here] = sums[c] * (1.0 / 255.0)
            base_ref[3, rows, here] = 1.0 - remaining

        for q, (edge, inner) in enumerate(((0, 1), (height - 1, height - 2))):
            value = volume_ref[0, :, edge, here]
            behind = pltpu.roll(jnp.where(back, 0, value), 1, 0)
            ahead = pltpu.roll(jnp.where(front, 0, value), slices - 1, 0)
            grad_ref[q, 0, :, here] = (ahead - behind).astype(jnp.float32)
            grad_ref[q, 1, :, here] = volume_ref[0, :, inner, here].astype(jnp.float32)
            word = pair_ref[j + 1, :, top + edge, :]
            low, high = across(
                pair_ref[j, :, top + edge, :],
                word,
                pair_ref[j + 2, :, top + edge, :],
                strip_first_lane[:pairs],
                strip_last_lane[:pairs],
            )
            grad_ref[q, 2, :pairs, here] = low
            grad_ref[q, 2, pairs:, here] = high
            weight = held_ref[q] * (1.0 / 255.0)
            emitted = colors(value, strip_colors)
            for c in range(3):
                strip_ref[q, c, :, here] = emitted[c] * weight
        return carry

    lax.fori_loop(0, chunks, chunk, 0, unroll=2)


def march_interior(volume, color_map, alpha_map, depth_count):
    _, slices, height, columns = volume.shape
    opacity_scale = OPACITY / (255.0 * slices * depth_count)
    shapes = [
        (4, height, columns),
        (2, height, columns),
        (2, height, columns),
        (2, 3, height, columns),
        (2, 3, slices, columns),
        (2, 3, slices, columns),
    ]
    voxels = slices * height * columns
    return pl.pallas_call(
        functools.partial(interior_kernel, opacity_scale),
        in_specs=[WHOLE] * 3,
        out_specs=[WHOLE] * len(shapes),
        out_shape=[jax.ShapeDtypeStruct(shape, jnp.float32) for shape in shapes],
        scratch_shapes=[
            pltpu.VMEM((columns // LANES + 2, slices // 2, height + 2 * SUBLANES, LANES), jnp.int32),
            pltpu.VMEM((2, slices, LANES), jnp.float32),
        ],
        compiler_params=pltpu.CompilerParams(vmem_limit_bytes=24 * 1024 * 1024),
        cost_estimate=pl.CostEstimate(flops=voxels * 80, bytes_accessed=voxels * 20, transcendentals=voxels),
    )(volume, color_map, alpha_map.reshape(1, -1))


def row_sums(first, second):
    count = first.shape[0]
    if count != SUBLANES:
        return jnp.sum(first, axis=0, keepdims=True), jnp.sum(second, axis=0, keepdims=True)
    upper = lax.broadcasted_iota(jnp.int32, first.shape, 0) < 4
    both = jnp.where(upper, first, second) + pltpu.roll(jnp.where(upper, second, first), 4, 0)
    both = both + pltpu.roll(both, 6, 0)
    both = both + pltpu.roll(both, 7, 0)
    return both, pltpu.roll(both, 3, 0)


def edge_kernel(
    share, volume_ref, base_ref, face_ref, square_ref, lit_ref, grad_ref, strip_ref, first_ref, rows_near_ref, second_ref, rows_far_ref, *out_refs
):
    _, slices, height, columns = volume_ref.shape
    tiles = height // SUBLANES
    tile = (SUBLANES, LANES)
    row = lax.broadcasted_iota(jnp.int32, tile, 0)
    first_row, last_row, upper = row == 0, row == SUBLANES - 1, row < SUBLANES // 2
    level = lax.broadcasted_iota(jnp.int32, (slices, LANES), 0)
    front, back = level == 0, level == slices - 1
    odd, odd_row = parity("depth") == 1, parity("rows") == 1
    front_came_first = odd == odd_row
    front_end, back_end = ends("depth")
    top_end, bottom_end = ends("rows")

    def chunk(j, carry):
        here = pl.ds(pl.multiple_of(j * LANES, LANES), LANES)
        rows_near = rows_near_ref[:, here].astype(jnp.float32)[:slices]
        rows_far = rows_far_ref[:, here].astype(jnp.float32)
        above = jnp.where(top_end, 0.0, jnp.where(odd_row, rows_near, rows_far))
        below = jnp.where(bottom_end, 0.0, jnp.where(odd_row, rows_far, rows_near))
        first = first_ref[:, here].astype(jnp.float32)
        second = second_ref[:, here].astype(jnp.float32)
        before = jnp.where(front_end, 0.0, jnp.where(front_came_first, first, second))
        after = jnp.where(back_end, 0.0, jnp.where(front_came_first, second, first))
        extra = []
        for q, edge in enumerate((0, height - 1)):
            inner = grad_ref[q, 1, :, here]
            grad_rows = below - inner if q else inner - above
            grad_cols = grad_ref[q, 2, :, here]
            grad_depth = grad_ref[q, 0, :, here] + jnp.where(
                back, after[edge : edge + 1], jnp.where(front, -before[edge : edge + 1], 0.0)
            )
            shading = shade(
                grad_depth,
                LIGHT_ROWS * grad_rows + LIGHT_COLS * grad_cols,
                grad_rows * grad_rows + grad_cols * grad_cols,
            )
            extra.append([strip_ref[q, c, :, here] * shading for c in range(3)])
        extra = [row_sums(extra[0][c], extra[1][c]) for c in range(3)]
        for r in range(tiles):
            rows = slice(r * SUBLANES, (r + 1) * SUBLANES)
            planes = [base_ref[c, rows, here] for c in range(4)]
            for end in range(2):
                if end:
                    grad_depth = after[rows] - volume_ref[0, slices - 2, rows, here].astype(jnp.float32)
                else:
                    grad_depth = volume_ref[0, 1, rows, here].astype(jnp.float32) - before[rows]
                shading = shade(grad_depth, face_ref[end, rows, here], square_ref[end, rows, here])
                for c in range(3):
                    planes[c] = planes[c] + lit_ref[end, c, rows, here] * shading
            for c in range(3):
                if r == 0:
                    planes[c] = planes[c] + jnp.where(first_row, extra[c][0], 0.0)
                if r == tiles - 1:
                    planes[c] = planes[c] + jnp.where(last_row, extra[c][1], 0.0)
            if len(out_refs) == 1:
                for i, first in enumerate(range(0, SUBLANES, share)):
                    block = jnp.concatenate([plane[first : first + share] for plane in planes], axis=0)
                    out_refs[0][r * (SUBLANES // share) + i, :, here] = block.astype(jnp.bfloat16)
            else:
                halves = [(planes[c], pltpu.roll(planes[c + 1], SUBLANES // 2, 0)) for c in (0, 2)]
                even = jnp.concatenate([jnp.where(upper, own, turned) for own, turned in halves], axis=0)
                uneven = jnp.concatenate([jnp.where(upper, turned, own) for own, turned in halves], axis=0)
                blocks_ref, _ = out_refs
                blocks_ref[r, 0, :, here] = even
                blocks_ref[r, 1, :, here] = uneven
        return carry

    lax.fori_loop(0, columns // LANES, chunk, 0, unroll=4)
    if len(out_refs) > 1:
        blocks_ref, give_ref = out_refs
        chip, core, mask = route()
        given = (blocks_ref[chip, 1 - core], blocks_ref[chip ^ 3, core], blocks_ref[chip ^ mask ^ 3, 0], blocks_ref[chip ^ mask ^ 3, 1])
        for i, block in enumerate(given):
            give_ref[i] = block.astype(jnp.bfloat16)


def add_edges(volume, interior, halos, depth_count, paired):
    _, slices, height, columns = volume.shape
    share = height // depth_count
    if paired:
        block = (4 * share, columns)
        shapes = [
            jax.ShapeDtypeStruct((depth_count // 2, 2, *block), jnp.float32),
            jax.ShapeDtypeStruct((4, *block), jnp.bfloat16),
        ]
    else:
        shapes = [jax.ShapeDtypeStruct((depth_count, 4 * share, columns), jnp.bfloat16)]
    return pl.pallas_call(
        functools.partial(edge_kernel, share),
        in_specs=[WHOLE] * 11,
        out_specs=[WHOLE] * len(shapes),
        out_shape=shapes,
        compiler_params=pltpu.CompilerParams(vmem_limit_bytes=24 * 1024 * 1024),
    )(volume, *interior, *halos)


def served(depth):
    chip, core = depth // 2, depth % 2
    return 1 + (core ^ (chip & 1) ^ (chip >> 1))


def route():
    position = lax.axis_index("depth")
    return position // 2, position % 2, served(position)


def over(nearer, farther, uneven):
    share = nearer.shape[0] // 4
    clear = 1.0 - jnp.where(uneven, nearer[2 * share : 3 * share], nearer[3 * share :])
    return nearer + jnp.concatenate([clear] * 4, axis=0) * farther


def merge_kernel(blocks_ref, other_ref, own_ref, cross_ref, side_ref):
    chip, core, mask = route()
    odd = core == 1

    def merged(keep, i, uneven):
        other = other_ref[i].astype(jnp.float32)
        return over(jnp.where(odd, other, keep), jnp.where(odd, keep, other), uneven)

    own_ref[...] = merged(blocks_ref[chip, core], 0, odd)
    for i, p in enumerate((1 - core, core)):
        side_ref[i] = merged(blocks_ref[chip ^ mask, p], 2 + p, p == 1).astype(jnp.bfloat16)
    cross_ref[...] = merged(blocks_ref[chip ^ 3, 1 - core], 1, jnp.logical_not(odd)).astype(jnp.bfloat16)


def merge(blocks, other):
    rows, columns = other.shape[1:]
    return pl.pallas_call(
        merge_kernel,
        in_specs=[WHOLE] * 2,
        out_specs=[WHOLE] * 3,
        out_shape=[
            jax.ShapeDtypeStruct((rows, columns), jnp.float32),
            jax.ShapeDtypeStruct((rows, columns), jnp.bfloat16),
            jax.ShapeDtypeStruct((2, rows, columns), jnp.bfloat16),
        ],
        compiler_params=pltpu.CompilerParams(vmem_limit_bytes=8 * 1024 * 1024),
    )(blocks, other)


def pass_kernel(side_ref, out_ref):
    out_ref[...] = side_ref[1]


def pass_on(side):
    return pl.pallas_call(
        pass_kernel,
        in_specs=[WHOLE],
        out_specs=WHOLE,
        out_shape=jax.ShapeDtypeStruct(side.shape[1:], side.dtype),
        compiler_params=pltpu.CompilerParams(vmem_limit_bytes=4 * 1024 * 1024),
    )(side)


def gather_kernel(side_ref, cross_ref, passed_ref, own_ref, out_ref, plane_ref, sems):
    share = out_ref.shape[1]
    chip, core, mask = route()
    odd, serves_x = core == 1, mask == 1
    side, passed = side_ref[0].astype(jnp.float32), passed_ref[...].astype(jnp.float32)
    parts = [
        own_ref[...],
        jnp.where(serves_x, side, passed),
        jnp.where(serves_x, passed, side),
        cross_ref[...].astype(jnp.float32),
    ]
    step = 1
    while len(parts) > 1:
        swap = (chip & step) != 0
        parts = [
            over(jnp.where(swap, parts[i + 1], parts[i]), jnp.where(swap, parts[i], parts[i + 1]), odd)
            for i in range(0, len(parts), 2)
        ]
        step *= 2
    planes = [parts[0][c * share : (c + 1) * share] for c in range(4)]
    copies = [pltpu.make_async_copy(plane_ref.at[c], out_ref.at[c], sems.at[c]) for c in range(4)]
    for c, copy in enumerate(copies):
        plane_ref[c] = jnp.where(odd, planes[c ^ 1], planes[c])
        copy.start()
    for copy in copies:
        copy.wait()


def gather(parts, share):
    columns = parts[-1].shape[1]
    return pl.pallas_call(
        gather_kernel,
        in_specs=[WHOLE] * len(parts),
        out_specs=pl.BlockSpec(memory_space=pl.ANY),
        out_shape=jax.ShapeDtypeStruct((4, share, columns), jnp.float32),
        scratch_shapes=[pltpu.VMEM((4, share, columns), jnp.float32), pltpu.SemaphoreType.DMA((4,))],
        compiler_params=pltpu.CompilerParams(vmem_limit_bytes=4 * 1024 * 1024),
    )(*parts)


def finish_kernel(parts_ref, out_ref):
    count = parts_ref.shape[0]
    _, share, columns = out_ref.shape
    remaining = jnp.ones((share, columns), jnp.float32)
    sums = [jnp.zeros((share, columns), jnp.float32) for _ in range(3)]
    for k in range(count):
        part = parts_ref[k].astype(jnp.float32)
        for c in range(3):
            sums[c] = sums[c] + remaining * part[c * share : (c + 1) * share]
        remaining = remaining - remaining * part[3 * share :]
    for c in range(3):
        out_ref[c] = sums[c]
    out_ref[3] = 1.0 - remaining


def finish(parts, share):
    columns = parts.shape[2]
    return pl.pallas_call(
        finish_kernel,
        in_specs=[WHOLE],
        out_specs=WHOLE,
        out_shape=jax.ShapeDtypeStruct((4, share, columns), jnp.float32),
        compiler_params=pltpu.CompilerParams(vmem_limit_bytes=4 * 1024 * 1024),
    )(parts)


def swapped(values, kinds):
    depth_count, row_count = lax.axis_size("depth"), lax.axis_size("rows")
    perm = []
    for d in range(depth_count):
        for r in range(row_count):
            kind = kinds[r % 2]
            e, q = d, r
            if kind == "near slab":
                e = d ^ 1
            elif kind == "far slab":
                e = d + 1 if d % 2 else d - 1
                e = depth_count - 1 - d if not 0 <= e < depth_count else e
            else:
                q = r ^ 1 if kind == "near row" else (r + 1 if r % 2 else r - 1)
                if not 0 <= q < row_count:
                    e, q = d ^ 1, r
            perm.append((d * row_count + r, e * row_count + q))
    return lax.ppermute(values, ("depth", "rows"), perm)


def exchanged(values, mask):
    masks = [mask(d) if callable(mask) else mask for d in range(lax.axis_size("depth"))]
    return lax.ppermute(values, "depth", [(d, d ^ m) for d, m in enumerate(masks)])


def body(volume, color_map, alpha_map):
    depth_count = lax.axis_size("depth")
    share = volume.shape[2] // depth_count
    first, rows_near, second, rows_far = cut_edges(volume)
    first = swapped(first, ("far slab", "near slab"))
    rows_near = swapped(rows_near, ("near row", "near row"))
    second = swapped(second, ("near slab", "far slab"))
    rows_far = swapped(rows_far, ("far row", "far row"))
    interior = march_interior(volume, color_map, alpha_map, depth_count)
    halos = (first, rows_near, second, rows_far)
    paired = depth_count == 8 and 2 * share == SUBLANES
    outs = add_edges(volume, interior, halos, depth_count, paired)
    if not paired:
        return finish(lax.all_to_all(outs[0], "depth", 0, 0, tiled=True), share)
    blocks, give = outs
    own, cross, side = merge(blocks, exchanged(give, 1))
    side = exchanged(side, lambda d: 2 * served(d) + 1)
    cross = exchanged(cross, 7)
    return gather((side, cross, exchanged(pass_on(side), 1), own), share)


def solution(mesh):
    in_specs = (P(None, "depth", "rows", None), P(), P())
    out_specs = P(None, ("rows", "depth"), None)
    return jax.shard_map(body, mesh=mesh, in_specs=in_specs, out_specs=out_specs, check_vma=False)
```

```python
import functools

import jax
import jax.numpy as jnp
from jax import lax
from jax.experimental import pallas as pl
from jax.experimental.pallas import tpu as pltpu
from jax.sharding import PartitionSpec as P

AMBIENT = 0.3
DIFFUSE = 0.7
LIGHT_DEPTH = 0.48 * DIFFUSE
LIGHT_ROWS = 0.6 * DIFFUSE
LIGHT_COLS = 0.64 * DIFFUSE
OPACITY = 4.0
LANES = 128
SUBLANES = 8
WHOLE = pl.BlockSpec(memory_space=pltpu.VMEM)


def parity(axis):
    return lax.axis_index(axis) % 2


def ends(axis):
    position = lax.axis_index(axis)
    return position == 0, position == lax.axis_size(axis) - 1


def edges_kernel(volume_ref, first_out, rows_near_out, second_out, rows_far_out, strip_ref, plane_ref, sems):
    _, slices, height, columns = volume_ref.shape
    odd, odd_row = parity("depth"), parity("rows")
    far_first = 1 - odd_row
    last_first = odd ^ far_first ^ 1
    tiles = height // SUBLANES

    def plane_copies(i, s):
        for t in range(tiles):
            rows = pl.ds(t * SUBLANES, SUBLANES)
            yield pltpu.make_async_copy(volume_ref.at[0, s, rows], plane_ref.at[i, rows], sems.at[i, t])

    def strip_copy(i, row):
        return pltpu.make_async_copy(volume_ref.at[0, :, row], strip_ref.at[i], sems.at[2, i])

    copies = [
        list(plane_copies(0, last_first * (slices - 1))),
        [strip_copy(0, (1 - odd_row) * (height - 1))],
        list(plane_copies(1, (1 - last_first) * (slices - 1))),
        [strip_copy(1, odd_row * (height - 1))],
    ]
    for group in copies:
        for copy in group:
            copy.start()

    def arrive(group):
        for copy in group:
            copy.wait()

    def narrow(values):
        return values.astype(jnp.float32).astype(jnp.bfloat16)

    def padded(strip):
        return narrow(jnp.concatenate([strip, jnp.zeros((height - slices, columns), jnp.int32)], axis=0))

    arrive(copies[0])
    first_out[...] = narrow(plane_ref[0])
    arrive(copies[1])
    rows_near_out[...] = padded(strip_ref[0])
    arrive(copies[2])
    second_out[...] = narrow(plane_ref[1])
    arrive(copies[3])
    rows_far_out[...] = narrow(strip_ref[1])


def cut_edges(volume):
    _, slices, height, columns = volume.shape
    plane = jax.ShapeDtypeStruct((height, columns), jnp.bfloat16)
    strip = jax.ShapeDtypeStruct((slices, columns), jnp.bfloat16)
    return pl.pallas_call(
        edges_kernel,
        in_specs=[pl.BlockSpec(memory_space=pl.ANY)],
        out_specs=[WHOLE] * 4,
        out_shape=[plane, plane, plane, strip],
        scratch_shapes=[
            pltpu.VMEM((2, slices, columns), jnp.int32),
            pltpu.VMEM((2, height, columns), jnp.int32),
            pltpu.SemaphoreType.DMA((3, max(2, height // SUBLANES))),
        ],
        compiler_params=pltpu.CompilerParams(vmem_limit_bytes=52 * 1024 * 1024),
    )(volume)


def pick(entries, places):
    dims = lax.GatherDimensionNumbers(
        offset_dims=(),
        collapsed_slice_dims=(1,),
        start_index_map=(1,),
        operand_batching_dims=(0,),
        start_indices_batching_dims=(0,),
    )
    return lax.gather(entries, places[..., None], dims, (1, 1), mode=lax.GatherScatterMode.PROMISE_IN_BOUNDS)


def shade(grad_depth, facing, squares):
    facing = facing + LIGHT_DEPTH * grad_depth
    squares = squares + grad_depth * grad_depth
    return AMBIENT + jnp.abs(facing) * lax.rsqrt(jnp.maximum(squares, 4.0))


def interior_kernel(
    opacity_scale,
    volume_ref,
    color_ref,
    alpha_ref,
    base_ref,
    face_ref,
    square_ref,
    lit_ref,
    grad_ref,
    strip_ref,
    pair_ref,
    held_ref,
):
    _, slices, height, columns = volume_ref.shape
    tiles = height // SUBLANES
    chunks = columns // LANES
    tile = (SUBLANES, LANES)
    strip = (slices, LANES)

    packed = color_ref[0:1, :] + color_ref[1:2, :] * 256 + color_ref[2:3, :] * 65536
    color_low, color_high = packed[:, :LANES], packed[:, LANES:]
    alpha_both = alpha_ref[0:1, :LANES] + alpha_ref[0:1, LANES:] * 256

    def colors(value, tables):
        low, high = tables
        place = value & (LANES - 1)
        color = jnp.where(value < LANES, pick(low, place), pick(high, place))
        parts = (color & 255, lax.shift_right_logical(color, 8) & 255, lax.shift_right_logical(color, 16))
        return [part.astype(jnp.float32) for part in parts]

    def opacity(level, table):
        entry = pick(table, level & (LANES - 1))
        entry = lax.shift_right_logical(entry, lax.shift_right_logical(level & LANES, 4)) & 255
        return entry.astype(jnp.float32) * opacity_scale

    tile_colors = [jnp.broadcast_to(t, tile) for t in (color_low, color_high)]
    tile_alpha = jnp.broadcast_to(alpha_both, tile)
    strip_colors = [jnp.broadcast_to(t, strip) for t in (color_low, color_high)]

    def masks(shape):
        lane = lax.broadcasted_iota(jnp.int32, shape, 1)
        row = lax.broadcasted_iota(jnp.int32, shape, 0)
        return lane == 0, lane == LANES - 1, row == 0, row == shape[0] - 1

    first_lane, last_lane, first_row, last_row = masks(tile)
    strip_first_lane, strip_last_lane, front, back = masks(strip)

    pairs = slices // 2
    top = SUBLANES

    def clear(j, carry):
        pair_ref[j] = jnp.zeros(pair_ref.shape[1:], jnp.int32)
        return carry

    clear(0, 0)
    clear(chunks + 1, 0)
    margin = jnp.zeros((pairs, SUBLANES, LANES), jnp.int32)

    def pack(j, carry):
        here = pl.ds(pl.multiple_of(j * LANES, LANES), LANES)
        pair_ref[j + 1, :, :top] = margin
        pair_ref[j + 1, :, top + height :] = margin
        for p in range(pairs):
            pair_ref[j + 1, p, top : top + height] = volume_ref[0, p, :, here] + lax.shift_left(
                volume_ref[0, p + pairs, :, here], 16
            )
        return carry

    lax.fori_loop(0, chunks, pack, 0)

    def split(difference):
        low = lax.shift_right_arithmetic(lax.shift_left(difference, 16), 16)
        high = lax.shift_right_arithmetic(difference + 32768, 16)
        return low.astype(jnp.float32), high.astype(jnp.float32)

    def across(left_value, value, right_value, first, last):
        west = pltpu.roll(jnp.where(last, left_value, value), 1, 1)
        east = pltpu.roll(jnp.where(first, right_value, value), LANES - 1, 1)
        return split(east - west)

    def chunk(j, carry):
        here = pl.ds(pl.multiple_of(j * LANES, LANES), LANES)

        for r in range(tiles):
            rows = slice(r * SUBLANES, (r + 1) * SUBLANES)
            values = [volume_ref[0, s, rows, here] for s in range(slices)]

            def words(c, p, offset=0):
                return pair_ref[c, p, top + r * SUBLANES + offset : top + (r + 1) * SUBLANES + offset, :]

            down, right = [], []
            for p in range(pairs):
                down.append(split(words(j + 1, p, 1) - words(j + 1, p, -1)))
                right.append(across(words(j, p), words(j + 1, p), words(j + 2, p), first_lane, last_lane))
            remaining = jnp.ones(tile, jnp.float32)
            sums = [jnp.zeros(tile, jnp.float32) for _ in range(3)]
            for s in range(slices):
                value = values[s]
                grad_rows = down[s % pairs][s // pairs]
                grad_cols = right[s % pairs][s // pairs]
                squares = grad_rows * grad_rows + grad_cols * grad_cols
                facing = LIGHT_ROWS * grad_rows + LIGHT_COLS * grad_cols
                weight = remaining * opacity(volume_ref[1, s, rows, here], tile_alpha)
                remaining = remaining - weight
                if r == 0:
                    held_ref[0, s : s + 1, :] = weight[:1]
                    weight = jnp.where(first_row, 0.0, weight)
                if r == tiles - 1:
                    held_ref[1, s : s + 1, :] = weight[SUBLANES - 1 :]
                    weight = jnp.where(last_row, 0.0, weight)
                emitted = colors(value, tile_colors)
                if 0 < s < slices - 1:
                    grad_depth = (values[s + 1] - values[s - 1]).astype(jnp.float32)
                    weight = weight * shade(grad_depth, facing, squares)
                    for c in range(3):
                        sums[c] = sums[c] + emitted[c] * weight
                else:
                    end = int(s > 0)
                    face_ref[end, rows, here] = facing
                    square_ref[end, rows, here] = squares
                    weight = weight * (1.0 / 255.0)
                    for c in range(3):
                        lit_ref[end, c, rows, here] = emitted[c] * weight
            for c in range(3):
                base_ref[c, rows, here] = sums[c] * (1.0 / 255.0)
            base_ref[3, rows, here] = 1.0 - remaining

        for q, (edge, inner) in enumerate(((0, 1), (height - 1, height - 2))):
            value = volume_ref[0, :, edge, here]
            behind = pltpu.roll(jnp.where(back, 0, value), 1, 0)
            ahead = pltpu.roll(jnp.where(front, 0, value), slices - 1, 0)
            grad_ref[q, 0, :, here] = (ahead - behind).astype(jnp.float32)
            grad_ref[q, 1, :, here] = volume_ref[0, :, inner, here].astype(jnp.float32)
            word = pair_ref[j + 1, :, top + edge, :]
            low, high = across(
                pair_ref[j, :, top + edge, :],
                word,
                pair_ref[j + 2, :, top + edge, :],
                strip_first_lane[:pairs],
                strip_last_lane[:pairs],
            )
            grad_ref[q, 2, :pairs, here] = low
            grad_ref[q, 2, pairs:, here] = high
            weight = held_ref[q] * (1.0 / 255.0)
            emitted = colors(value, strip_colors)
            for c in range(3):
                strip_ref[q, c, :, here] = emitted[c] * weight
        return carry

    lax.fori_loop(0, chunks, chunk, 0, unroll=2)


def march_interior(volume, color_map, alpha_map, depth_count):
    _, slices, height, columns = volume.shape
    opacity_scale = OPACITY / (255.0 * slices * depth_count)
    shapes = [
        (4, height, columns),
        (2, height, columns),
        (2, height, columns),
        (2, 3, height, columns),
        (2, 3, slices, columns),
        (2, 3, slices, columns),
    ]
    voxels = slices * height * columns
    return pl.pallas_call(
        functools.partial(interior_kernel, opacity_scale),
        in_specs=[WHOLE] * 3,
        out_specs=[WHOLE] * len(shapes),
        out_shape=[jax.ShapeDtypeStruct(shape, jnp.float32) for shape in shapes],
        scratch_shapes=[
            pltpu.VMEM((columns // LANES + 2, slices // 2, height + 2 * SUBLANES, LANES), jnp.int32),
            pltpu.VMEM((2, slices, LANES), jnp.float32),
        ],
        compiler_params=pltpu.CompilerParams(vmem_limit_bytes=24 * 1024 * 1024),
        cost_estimate=pl.CostEstimate(flops=voxels * 80, bytes_accessed=voxels * 20, transcendentals=voxels),
    )(volume, color_map, alpha_map.reshape(1, -1))


def row_sums(first, second):
    count = first.shape[0]
    if count != SUBLANES:
        return jnp.sum(first, axis=0, keepdims=True), jnp.sum(second, axis=0, keepdims=True)
    upper = lax.broadcasted_iota(jnp.int32, first.shape, 0) < 4
    both = jnp.where(upper, first, second) + pltpu.roll(jnp.where(upper, second, first), 4, 0)
    both = both + pltpu.roll(both, 6, 0)
    both = both + pltpu.roll(both, 7, 0)
    return both, pltpu.roll(both, 3, 0)


def plane_terms(volume_ref, face_ref, square_ref, lit_ref, halo, end, rows, here):
    slices = volume_ref.shape[1]
    inner = volume_ref[0, jnp.where(end == 1, slices - 2, 1), rows, here].astype(jnp.float32)
    grad_depth = jnp.where(end == 1, halo - inner, inner - halo)
    shading = shade(grad_depth, face_ref[end, rows, here], square_ref[end, rows, here])
    return [lit_ref[end, c, rows, here] * shading for c in range(3)]


def first_end():
    front_end, back_end = ends("depth")
    end = jnp.where(parity("depth") == parity("rows"), 0, 1)
    return end, jnp.where(end == 1, back_end, front_end), jnp.where(end == 1, front_end, back_end)


def first_plane_kernel(volume_ref, base_ref, face_ref, square_ref, lit_ref, first_ref, sums_ref):
    _, height, columns = base_ref.shape
    end, outside, _ = first_end()

    def chunk(j, carry):
        here = pl.ds(pl.multiple_of(j * LANES, LANES), LANES)
        first = jnp.where(outside, 0.0, first_ref[:, here].astype(jnp.float32))
        for r in range(height // SUBLANES):
            rows = slice(r * SUBLANES, (r + 1) * SUBLANES)
            terms = plane_terms(volume_ref, face_ref, square_ref, lit_ref, first[rows], end, rows, here)
            for c in range(3):
                sums_ref[c, rows, here] = base_ref[c, rows, here] + terms[c]
        return carry

    lax.fori_loop(0, columns // LANES, chunk, 0, unroll=4)


def add_first_plane(volume, base, face, square, lit, first):
    return pl.pallas_call(
        first_plane_kernel,
        in_specs=[WHOLE] * 6,
        out_specs=WHOLE,
        out_shape=jax.ShapeDtypeStruct((3, *base.shape[1:]), jnp.float32),
        compiler_params=pltpu.CompilerParams(vmem_limit_bytes=8 * 1024 * 1024),
        cost_estimate=pl.CostEstimate(flops=base.size * 20, bytes_accessed=base.size * 12, transcendentals=base.size // 4),
    )(volume, base, face, square, lit, first)


def edge_kernel(
    share, volume_ref, sums_ref, base_ref, face_ref, square_ref, lit_ref, grad_ref, strip_ref, first_ref, rows_near_ref, second_ref, rows_far_ref, *out_refs
):
    _, slices, height, columns = volume_ref.shape
    tiles = height // SUBLANES
    tile = (SUBLANES, LANES)
    row = lax.broadcasted_iota(jnp.int32, tile, 0)
    first_row, last_row, upper = row == 0, row == SUBLANES - 1, row < SUBLANES // 2
    level = lax.broadcasted_iota(jnp.int32, (slices, LANES), 0)
    front, back = level == 0, level == slices - 1
    odd, odd_row = parity("depth") == 1, parity("rows") == 1
    front_came_first = odd == odd_row
    front_end, back_end = ends("depth")
    top_end, bottom_end = ends("rows")
    end, _, outside = first_end()

    def chunk(j, carry):
        here = pl.ds(pl.multiple_of(j * LANES, LANES), LANES)
        rows_near = rows_near_ref[:, here].astype(jnp.float32)[:slices]
        rows_far = rows_far_ref[:, here].astype(jnp.float32)
        above = jnp.where(top_end, 0.0, jnp.where(odd_row, rows_near, rows_far))
        below = jnp.where(bottom_end, 0.0, jnp.where(odd_row, rows_far, rows_near))
        first = first_ref[:, here].astype(jnp.float32)
        second = second_ref[:, here].astype(jnp.float32)
        before = jnp.where(front_end, 0.0, jnp.where(front_came_first, first, second))
        after = jnp.where(back_end, 0.0, jnp.where(front_came_first, second, first))
        last = jnp.where(outside, 0.0, second)
        extra = []
        for q, edge in enumerate((0, height - 1)):
            inner = grad_ref[q, 1, :, here]
            grad_rows = below - inner if q else inner - above
            grad_cols = grad_ref[q, 2, :, here]
            grad_depth = grad_ref[q, 0, :, here] + jnp.where(
                back, after[edge : edge + 1], jnp.where(front, -before[edge : edge + 1], 0.0)
            )
            shading = shade(
                grad_depth,
                LIGHT_ROWS * grad_rows + LIGHT_COLS * grad_cols,
                grad_rows * grad_rows + grad_cols * grad_cols,
            )
            extra.append([strip_ref[q, c, :, here] * shading for c in range(3)])
        extra = [row_sums(extra[0][c], extra[1][c]) for c in range(3)]
        for r in range(tiles):
            rows = slice(r * SUBLANES, (r + 1) * SUBLANES)
            terms = plane_terms(volume_ref, face_ref, square_ref, lit_ref, last[rows], 1 - end, rows, here)
            planes = [sums_ref[c, rows, here] + terms[c] for c in range(3)] + [base_ref[3, rows, here]]
            for c in range(3):
                if r == 0:
                    planes[c] = planes[c] + jnp.where(first_row, extra[c][0], 0.0)
                if r == tiles - 1:
                    planes[c] = planes[c] + jnp.where(last_row, extra[c][1], 0.0)
            if len(out_refs) == 1:
                for i, first in enumerate(range(0, SUBLANES, share)):
                    block = jnp.concatenate([plane[first : first + share] for plane in planes], axis=0)
                    out_refs[0][r * (SUBLANES // share) + i, :, here] = block.astype(jnp.bfloat16)
            else:
                halves = [(planes[c], pltpu.roll(planes[c + 1], SUBLANES // 2, 0)) for c in (0, 2)]
                even = jnp.concatenate([jnp.where(upper, own, turned) for own, turned in halves], axis=0)
                uneven = jnp.concatenate([jnp.where(upper, turned, own) for own, turned in halves], axis=0)
                blocks_ref, _ = out_refs
                blocks_ref[r, 0, :, here] = even
                blocks_ref[r, 1, :, here] = uneven
        return carry

    lax.fori_loop(0, columns // LANES, chunk, 0, unroll=4)
    if len(out_refs) > 1:
        blocks_ref, give_ref = out_refs
        chip, core, mask = route()
        given = (blocks_ref[chip, 1 - core], blocks_ref[chip ^ 3, core], blocks_ref[chip ^ mask ^ 3, 0], blocks_ref[chip ^ mask ^ 3, 1])
        for i, block in enumerate(given):
            give_ref[i] = block.astype(jnp.bfloat16)


def add_edges(volume, sums, interior, halos, depth_count, paired):
    _, slices, height, columns = volume.shape
    share = height // depth_count
    if paired:
        block = (4 * share, columns)
        shapes = [
            jax.ShapeDtypeStruct((depth_count // 2, 2, *block), jnp.float32),
            jax.ShapeDtypeStruct((4, *block), jnp.bfloat16),
        ]
    else:
        shapes = [jax.ShapeDtypeStruct((depth_count, 4 * share, columns), jnp.bfloat16)]
    return pl.pallas_call(
        functools.partial(edge_kernel, share),
        in_specs=[WHOLE] * 12,
        out_specs=[WHOLE] * len(shapes),
        out_shape=shapes,
        compiler_params=pltpu.CompilerParams(vmem_limit_bytes=24 * 1024 * 1024),
    )(volume, sums, *interior, *halos)


def served(depth):
    chip, core = depth // 2, depth % 2
    return 1 + (core ^ (chip & 1) ^ (chip >> 1))


def route():
    position = lax.axis_index("depth")
    return position // 2, position % 2, served(position)


def over(nearer, farther, uneven):
    share = nearer.shape[0] // 4
    clear = 1.0 - jnp.where(uneven, nearer[2 * share : 3 * share], nearer[3 * share :])
    return nearer + jnp.concatenate([clear] * 4, axis=0) * farther


def merge_kernel(blocks_ref, other_ref, own_ref, cross_ref, side_ref):
    chip, core, mask = route()
    odd = core == 1

    def merged(keep, i, uneven):
        other = other_ref[i].astype(jnp.float32)
        return over(jnp.where(odd, other, keep), jnp.where(odd, keep, other), uneven)

    own_ref[...] = merged(blocks_ref[chip, core], 0, odd)
    for i, p in enumerate((1 - core, core)):
        side_ref[i] = merged(blocks_ref[chip ^ mask, p], 2 + p, p == 1).astype(jnp.bfloat16)
    cross_ref[...] = merged(blocks_ref[chip ^ 3, 1 - core], 1, jnp.logical_not(odd)).astype(jnp.bfloat16)


def merge(blocks, other):
    rows, columns = other.shape[1:]
    return pl.pallas_call(
        merge_kernel,
        in_specs=[WHOLE] * 2,
        out_specs=[WHOLE] * 3,
        out_shape=[
            jax.ShapeDtypeStruct((rows, columns), jnp.float32),
            jax.ShapeDtypeStruct((rows, columns), jnp.bfloat16),
            jax.ShapeDtypeStruct((2, rows, columns), jnp.bfloat16),
        ],
        compiler_params=pltpu.CompilerParams(vmem_limit_bytes=8 * 1024 * 1024),
    )(blocks, other)


def pass_kernel(side_ref, out_ref):
    out_ref[...] = side_ref[1]


def pass_on(side):
    return pl.pallas_call(
        pass_kernel,
        in_specs=[WHOLE],
        out_specs=WHOLE,
        out_shape=jax.ShapeDtypeStruct(side.shape[1:], side.dtype),
        compiler_params=pltpu.CompilerParams(vmem_limit_bytes=4 * 1024 * 1024),
    )(side)


def gather_kernel(side_ref, cross_ref, passed_ref, own_ref, out_ref, plane_ref, sems):
    share = out_ref.shape[1]
    chip, core, mask = route()
    odd, serves_x = core == 1, mask == 1
    side, passed = side_ref[0].astype(jnp.float32), passed_ref[...].astype(jnp.float32)
    parts = [
        own_ref[...],
        jnp.where(serves_x, side, passed),
        jnp.where(serves_x, passed, side),
        cross_ref[...].astype(jnp.float32),
    ]
    step = 1
    while len(parts) > 1:
        swap = (chip & step) != 0
        parts = [
            over(jnp.where(swap, parts[i + 1], parts[i]), jnp.where(swap, parts[i], parts[i + 1]), odd)
            for i in range(0, len(parts), 2)
        ]
        step *= 2
    planes = [parts[0][c * share : (c + 1) * share] for c in range(4)]
    copies = [pltpu.make_async_copy(plane_ref.at[c], out_ref.at[c], sems.at[c]) for c in range(4)]
    for c, copy in enumerate(copies):
        plane_ref[c] = jnp.where(odd, planes[c ^ 1], planes[c])
        copy.start()
    for copy in copies:
        copy.wait()


def gather(parts, share):
    columns = parts[-1].shape[1]
    return pl.pallas_call(
        gather_kernel,
        in_specs=[WHOLE] * len(parts),
        out_specs=pl.BlockSpec(memory_space=pl.ANY),
        out_shape=jax.ShapeDtypeStruct((4, share, columns), jnp.float32),
        scratch_shapes=[pltpu.VMEM((4, share, columns), jnp.float32), pltpu.SemaphoreType.DMA((4,))],
        compiler_params=pltpu.CompilerParams(vmem_limit_bytes=4 * 1024 * 1024),
    )(*parts)


def finish_kernel(parts_ref, out_ref):
    count = parts_ref.shape[0]
    _, share, columns = out_ref.shape
    remaining = jnp.ones((share, columns), jnp.float32)
    sums = [jnp.zeros((share, columns), jnp.float32) for _ in range(3)]
    for k in range(count):
        part = parts_ref[k].astype(jnp.float32)
        for c in range(3):
            sums[c] = sums[c] + remaining * part[c * share : (c + 1) * share]
        remaining = remaining - remaining * part[3 * share :]
    for c in range(3):
        out_ref[c] = sums[c]
    out_ref[3] = 1.0 - remaining


def finish(parts, share):
    columns = parts.shape[2]
    return pl.pallas_call(
        finish_kernel,
        in_specs=[WHOLE],
        out_specs=WHOLE,
        out_shape=jax.ShapeDtypeStruct((4, share, columns), jnp.float32),
        compiler_params=pltpu.CompilerParams(vmem_limit_bytes=4 * 1024 * 1024),
    )(parts)


def swapped(values, kinds):
    depth_count, row_count = lax.axis_size("depth"), lax.axis_size("rows")
    perm = []
    for d in range(depth_count):
        for r in range(row_count):
            kind = kinds[r % 2]
            e, q = d, r
            if kind == "near slab":
                e = d ^ 1
            elif kind == "far slab":
                e = d + 1 if d % 2 else d - 1
                e = depth_count - 1 - d if not 0 <= e < depth_count else e
            else:
                q = r ^ 1 if kind == "near row" else (r + 1 if r % 2 else r - 1)
                if not 0 <= q < row_count:
                    e, q = d ^ 1, r
            perm.append((d * row_count + r, e * row_count + q))
    return lax.ppermute(values, ("depth", "rows"), perm)


def exchanged(values, mask):
    masks = [mask(d) if callable(mask) else mask for d in range(lax.axis_size("depth"))]
    return lax.ppermute(values, "depth", [(d, d ^ m) for d, m in enumerate(masks)])


def body(volume, color_map, alpha_map):
    depth_count = lax.axis_size("depth")
    share = volume.shape[2] // depth_count
    first, rows_near, second, rows_far = cut_edges(volume)
    first = swapped(first, ("far slab", "near slab"))
    rows_near = swapped(rows_near, ("near row", "near row"))
    second = swapped(second, ("near slab", "far slab"))
    rows_far = swapped(rows_far, ("far row", "far row"))
    interior = march_interior(volume, color_map, alpha_map, depth_count)
    halos = (first, rows_near, second, rows_far)
    paired = depth_count == 8 and 2 * share == SUBLANES
    sums = add_first_plane(volume, *interior[:4], first)
    outs = add_edges(volume, sums, interior, halos, depth_count, paired)
    if not paired:
        return finish(lax.all_to_all(outs[0], "depth", 0, 0, tiled=True), share)
    blocks, give = outs
    own, cross, side = merge(blocks, exchanged(give, 1))
    side = exchanged(side, lambda d: 2 * served(d) + 1)
    cross = exchanged(cross, 7)
    return gather((side, cross, exchanged(pass_on(side), 1), own), share)


def solution(mesh):
    in_specs = (P(None, "depth", "rows", None), P(), P())
    out_specs = P(None, ("rows", "depth"), None)
    return jax.shard_map(body, mesh=mesh, in_specs=in_specs, out_specs=out_specs, check_vma=False)
```

```python
import functools

import jax
import jax.numpy as jnp
from jax import lax
from jax.experimental import pallas as pl
from jax.experimental.pallas import tpu as pltpu
from jax.sharding import PartitionSpec as P

AMBIENT = 0.3
DIFFUSE = 0.7
LIGHT_DEPTH = 0.48 * DIFFUSE
LIGHT_ROWS = 0.6 * DIFFUSE
LIGHT_COLS = 0.64 * DIFFUSE
OPACITY = 4.0
LANES = 128
SUBLANES = 8
WHOLE = pl.BlockSpec(memory_space=pltpu.VMEM)


def parity(axis):
    return lax.axis_index(axis) % 2


def ends(axis):
    position = lax.axis_index(axis)
    return position == 0, position == lax.axis_size(axis) - 1


def edges_kernel(volume_ref, first_out, rows_near_out, second_out, rows_far_out, strip_ref, plane_ref, sems):
    _, slices, height, columns = volume_ref.shape
    odd, odd_row = parity("depth"), parity("rows")
    far_first = 1 - odd_row
    last_first = odd ^ far_first ^ 1
    tiles = height // SUBLANES

    def plane_copies(i, s):
        for t in range(tiles):
            rows = pl.ds(t * SUBLANES, SUBLANES)
            yield pltpu.make_async_copy(volume_ref.at[0, s, rows], plane_ref.at[i, rows], sems.at[i, t])

    def strip_copy(i, row):
        return pltpu.make_async_copy(volume_ref.at[0, :, row], strip_ref.at[i], sems.at[2, i])

    copies = [
        list(plane_copies(0, last_first * (slices - 1))),
        [strip_copy(0, (1 - odd_row) * (height - 1))],
        list(plane_copies(1, (1 - last_first) * (slices - 1))),
        [strip_copy(1, odd_row * (height - 1))],
    ]
    for group in copies:
        for copy in group:
            copy.start()

    def arrive(group):
        for copy in group:
            copy.wait()

    def narrow(values):
        return values.astype(jnp.float32).astype(jnp.bfloat16)

    def padded(strip):
        return narrow(jnp.concatenate([strip, jnp.zeros((height - slices, columns), jnp.int32)], axis=0))

    arrive(copies[0])
    first_out[...] = narrow(plane_ref[0])
    arrive(copies[1])
    rows_near_out[...] = padded(strip_ref[0])
    arrive(copies[2])
    second_out[...] = narrow(plane_ref[1])
    arrive(copies[3])
    rows_far_out[...] = narrow(strip_ref[1])


def cut_edges(volume):
    _, slices, height, columns = volume.shape
    plane = jax.ShapeDtypeStruct((height, columns), jnp.bfloat16)
    strip = jax.ShapeDtypeStruct((slices, columns), jnp.bfloat16)
    return pl.pallas_call(
        edges_kernel,
        in_specs=[pl.BlockSpec(memory_space=pl.ANY)],
        out_specs=[WHOLE] * 4,
        out_shape=[plane, plane, plane, strip],
        scratch_shapes=[
            pltpu.VMEM((2, slices, columns), jnp.int32),
            pltpu.VMEM((2, height, columns), jnp.int32),
            pltpu.SemaphoreType.DMA((3, max(2, height // SUBLANES))),
        ],
        compiler_params=pltpu.CompilerParams(vmem_limit_bytes=52 * 1024 * 1024),
    )(volume)


def pick(entries, places):
    dims = lax.GatherDimensionNumbers(
        offset_dims=(),
        collapsed_slice_dims=(1,),
        start_index_map=(1,),
        operand_batching_dims=(0,),
        start_indices_batching_dims=(0,),
    )
    return lax.gather(entries, places[..., None], dims, (1, 1), mode=lax.GatherScatterMode.PROMISE_IN_BOUNDS)


def shade(grad_depth, facing, squares):
    facing = facing + LIGHT_DEPTH * grad_depth
    squares = squares + grad_depth * grad_depth
    return AMBIENT + jnp.abs(facing) * lax.rsqrt(jnp.maximum(squares, 4.0))


def interior_kernel(
    opacity_scale,
    volume_ref,
    color_ref,
    alpha_ref,
    base_ref,
    face_ref,
    square_ref,
    lit_ref,
    grad_ref,
    strip_ref,
    pair_ref,
    held_ref,
):
    _, slices, height, columns = volume_ref.shape
    tiles = height // SUBLANES
    chunks = columns // LANES
    tile = (SUBLANES, LANES)
    strip = (slices, LANES)

    packed = color_ref[0:1, :] + color_ref[1:2, :] * 256 + color_ref[2:3, :] * 65536
    color_low, color_high = packed[:, :LANES], packed[:, LANES:]
    alpha_both = alpha_ref[0:1, :LANES] + alpha_ref[0:1, LANES:] * 256

    def colors(value, tables):
        low, high = tables
        place = value & (LANES - 1)
        color = jnp.where(value < LANES, pick(low, place), pick(high, place))
        parts = (color & 255, lax.shift_right_logical(color, 8) & 255, lax.shift_right_logical(color, 16))
        return [part.astype(jnp.float32) for part in parts]

    def opacity(level, table):
        entry = pick(table, level & (LANES - 1))
        entry = lax.shift_right_logical(entry, lax.shift_right_logical(level & LANES, 4)) & 255
        return entry.astype(jnp.float32) * opacity_scale

    tile_colors = [jnp.broadcast_to(t, tile) for t in (color_low, color_high)]
    tile_alpha = jnp.broadcast_to(alpha_both, tile)
    strip_colors = [jnp.broadcast_to(t, strip) for t in (color_low, color_high)]

    def masks(shape):
        lane = lax.broadcasted_iota(jnp.int32, shape, 1)
        row = lax.broadcasted_iota(jnp.int32, shape, 0)
        return lane == 0, lane == LANES - 1, row == 0, row == shape[0] - 1

    first_lane, last_lane, first_row, last_row = masks(tile)
    strip_first_lane, strip_last_lane, front, back = masks(strip)

    pairs = slices // 2
    top = SUBLANES

    def clear(j, carry):
        pair_ref[j] = jnp.zeros(pair_ref.shape[1:], jnp.int32)
        return carry

    clear(0, 0)
    clear(chunks + 1, 0)
    margin = jnp.zeros((pairs, SUBLANES, LANES), jnp.int32)

    def pack(j, carry):
        here = pl.ds(pl.multiple_of(j * LANES, LANES), LANES)
        pair_ref[j + 1, :, :top] = margin
        pair_ref[j + 1, :, top + height :] = margin
        for p in range(pairs):
            pair_ref[j + 1, p, top : top + height] = volume_ref[0, p, :, here] + lax.shift_left(
                volume_ref[0, p + pairs, :, here], 16
            )
        return carry

    lax.fori_loop(0, chunks, pack, 0)

    def split(difference):
        low = lax.shift_right_arithmetic(lax.shift_left(difference, 16), 16)
        high = lax.shift_right_arithmetic(difference + 32768, 16)
        return low.astype(jnp.float32), high.astype(jnp.float32)

    def across(left_value, value, right_value, first, last):
        west = pltpu.roll(jnp.where(last, left_value, value), 1, 1)
        east = pltpu.roll(jnp.where(first, right_value, value), LANES - 1, 1)
        return split(east - west)

    def chunk(j, carry):
        here = pl.ds(pl.multiple_of(j * LANES, LANES), LANES)

        for r in range(tiles):
            rows = slice(r * SUBLANES, (r + 1) * SUBLANES)
            values = [volume_ref[0, s, rows, here] for s in range(slices)]

            def words(c, p, offset=0):
                return pair_ref[c, p, top + r * SUBLANES + offset : top + (r + 1) * SUBLANES + offset, :]

            down, right = [], []
            for p in range(pairs):
                down.append(split(words(j + 1, p, 1) - words(j + 1, p, -1)))
                right.append(across(words(j, p), words(j + 1, p), words(j + 2, p), first_lane, last_lane))
            remaining = jnp.ones(tile, jnp.float32)
            sums = [jnp.zeros(tile, jnp.float32) for _ in range(3)]
            for s in range(slices):
                value = values[s]
                grad_rows = down[s % pairs][s // pairs]
                grad_cols = right[s % pairs][s // pairs]
                squares = grad_rows * grad_rows + grad_cols * grad_cols
                facing = LIGHT_ROWS * grad_rows + LIGHT_COLS * grad_cols
                weight = remaining * opacity(volume_ref[1, s, rows, here], tile_alpha)
                remaining = remaining - weight
                if r == 0:
                    held_ref[0, s : s + 1, :] = weight[:1]
                    weight = jnp.where(first_row, 0.0, weight)
                if r == tiles - 1:
                    held_ref[1, s : s + 1, :] = weight[SUBLANES - 1 :]
                    weight = jnp.where(last_row, 0.0, weight)
                emitted = colors(value, tile_colors)
                if 0 < s < slices - 1:
                    grad_depth = (values[s + 1] - values[s - 1]).astype(jnp.float32)
                    weight = weight * shade(grad_depth, facing, squares)
                    for c in range(3):
                        sums[c] = sums[c] + emitted[c] * weight
                else:
                    end = int(s > 0)
                    face_ref[end, rows, here] = facing
                    square_ref[end, rows, here] = squares
                    weight = weight * (1.0 / 255.0)
                    for c in range(3):
                        lit_ref[end, c, rows, here] = emitted[c] * weight
            for c in range(3):
                base_ref[c, rows, here] = sums[c] * (1.0 / 255.0)
            base_ref[3, rows, here] = 1.0 - remaining

        for q, (edge, inner) in enumerate(((0, 1), (height - 1, height - 2))):
            value = volume_ref[0, :, edge, here]
            behind = pltpu.roll(jnp.where(back, 0, value), 1, 0)
            ahead = pltpu.roll(jnp.where(front, 0, value), slices - 1, 0)
            grad_ref[q, 0, :, here] = (ahead - behind).astype(jnp.float32)
            grad_ref[q, 1, :, here] = volume_ref[0, :, inner, here].astype(jnp.float32)
            word = pair_ref[j + 1, :, top + edge, :]
            low, high = across(
                pair_ref[j, :, top + edge, :],
                word,
                pair_ref[j + 2, :, top + edge, :],
                strip_first_lane[:pairs],
                strip_last_lane[:pairs],
            )
            grad_ref[q, 2, :pairs, here] = low
            grad_ref[q, 2, pairs:, here] = high
            weight = held_ref[q] * (1.0 / 255.0)
            emitted = colors(value, strip_colors)
            for c in range(3):
                strip_ref[q, c, :, here] = emitted[c] * weight
        return carry

    lax.fori_loop(0, chunks, chunk, 0, unroll=4)


def march_interior(volume, color_map, alpha_map, depth_count):
    _, slices, height, columns = volume.shape
    opacity_scale = OPACITY / (255.0 * slices * depth_count)
    shapes = [
        (4, height, columns),
        (2, height, columns),
        (2, height, columns),
        (2, 3, height, columns),
        (2, 3, slices, columns),
        (2, 3, slices, columns),
    ]
    voxels = slices * height * columns
    return pl.pallas_call(
        functools.partial(interior_kernel, opacity_scale),
        in_specs=[WHOLE] * 3,
        out_specs=[WHOLE] * len(shapes),
        out_shape=[jax.ShapeDtypeStruct(shape, jnp.float32) for shape in shapes],
        scratch_shapes=[
            pltpu.VMEM((columns // LANES + 2, slices // 2, height + 2 * SUBLANES, LANES), jnp.int32),
            pltpu.VMEM((2, slices, LANES), jnp.float32),
        ],
        compiler_params=pltpu.CompilerParams(vmem_limit_bytes=24 * 1024 * 1024),
        cost_estimate=pl.CostEstimate(flops=voxels * 80, bytes_accessed=voxels * 20, transcendentals=voxels),
    )(volume, color_map, alpha_map.reshape(1, -1))


def row_sums(first, second):
    count = first.shape[0]
    if count != SUBLANES:
        return jnp.sum(first, axis=0, keepdims=True), jnp.sum(second, axis=0, keepdims=True)
    upper = lax.broadcasted_iota(jnp.int32, first.shape, 0) < 4
    both = jnp.where(upper, first, second) + pltpu.roll(jnp.where(upper, second, first), 4, 0)
    both = both + pltpu.roll(both, 6, 0)
    both = both + pltpu.roll(both, 7, 0)
    return both, pltpu.roll(both, 3, 0)


def plane_terms(volume_ref, face_ref, square_ref, lit_ref, halo, end, rows, here):
    slices = volume_ref.shape[1]
    inner = volume_ref[0, jnp.where(end == 1, slices - 2, 1), rows, here].astype(jnp.float32)
    grad_depth = jnp.where(end == 1, halo - inner, inner - halo)
    shading = shade(grad_depth, face_ref[end, rows, here], square_ref[end, rows, here])
    return [lit_ref[end, c, rows, here] * shading for c in range(3)]


def first_end():
    front_end, back_end = ends("depth")
    end = jnp.where(parity("depth") == parity("rows"), 0, 1)
    return end, jnp.where(end == 1, back_end, front_end), jnp.where(end == 1, front_end, back_end)


def first_plane_kernel(volume_ref, base_ref, face_ref, square_ref, lit_ref, first_ref, sums_ref):
    _, height, columns = base_ref.shape
    end, outside, _ = first_end()

    def chunk(j, carry):
        here = pl.ds(pl.multiple_of(j * LANES, LANES), LANES)
        first = jnp.where(outside, 0.0, first_ref[:, here].astype(jnp.float32))
        for r in range(height // SUBLANES):
            rows = slice(r * SUBLANES, (r + 1) * SUBLANES)
            terms = plane_terms(volume_ref, face_ref, square_ref, lit_ref, first[rows], end, rows, here)
            for c in range(3):
                sums_ref[c, rows, here] = base_ref[c, rows, here] + terms[c]
        return carry

    lax.fori_loop(0, columns // LANES, chunk, 0, unroll=4)


def add_first_plane(volume, base, face, square, lit, first):
    return pl.pallas_call(
        first_plane_kernel,
        in_specs=[WHOLE] * 6,
        out_specs=WHOLE,
        out_shape=jax.ShapeDtypeStruct((3, *base.shape[1:]), jnp.float32),
        compiler_params=pltpu.CompilerParams(vmem_limit_bytes=8 * 1024 * 1024),
        cost_estimate=pl.CostEstimate(flops=base.size * 20, bytes_accessed=base.size * 12, transcendentals=base.size // 4),
    )(volume, base, face, square, lit, first)


def edge_kernel(
    share, volume_ref, sums_ref, base_ref, face_ref, square_ref, lit_ref, grad_ref, strip_ref, first_ref, rows_near_ref, second_ref, rows_far_ref, *out_refs
):
    _, slices, height, columns = volume_ref.shape
    tiles = height // SUBLANES
    tile = (SUBLANES, LANES)
    row = lax.broadcasted_iota(jnp.int32, tile, 0)
    first_row, last_row, upper = row == 0, row == SUBLANES - 1, row < SUBLANES // 2
    level = lax.broadcasted_iota(jnp.int32, (slices, LANES), 0)
    front, back = level == 0, level == slices - 1
    odd, odd_row = parity("depth") == 1, parity("rows") == 1
    front_came_first = odd == odd_row
    front_end, back_end = ends("depth")
    top_end, bottom_end = ends("rows")
    end, _, outside = first_end()

    def chunk(j, carry):
        here = pl.ds(pl.multiple_of(j * LANES, LANES), LANES)
        rows_near = rows_near_ref[:, here].astype(jnp.float32)[:slices]
        rows_far = rows_far_ref[:, here].astype(jnp.float32)
        above = jnp.where(top_end, 0.0, jnp.where(odd_row, rows_near, rows_far))
        below = jnp.where(bottom_end, 0.0, jnp.where(odd_row, rows_far, rows_near))
        first = first_ref[:, here].astype(jnp.float32)
        second = second_ref[:, here].astype(jnp.float32)
        before = jnp.where(front_end, 0.0, jnp.where(front_came_first, first, second))
        after = jnp.where(back_end, 0.0, jnp.where(front_came_first, second, first))
        last = jnp.where(outside, 0.0, second)
        extra = []
        for q, edge in enumerate((0, height - 1)):
            inner = grad_ref[q, 1, :, here]
            grad_rows = below - inner if q else inner - above
            grad_cols = grad_ref[q, 2, :, here]
            grad_depth = grad_ref[q, 0, :, here] + jnp.where(
                back, after[edge : edge + 1], jnp.where(front, -before[edge : edge + 1], 0.0)
            )
            shading = shade(
                grad_depth,
                LIGHT_ROWS * grad_rows + LIGHT_COLS * grad_cols,
                grad_rows * grad_rows + grad_cols * grad_cols,
            )
            extra.append([strip_ref[q, c, :, here] * shading for c in range(3)])
        extra = [row_sums(extra[0][c], extra[1][c]) for c in range(3)]
        for r in range(tiles):
            rows = slice(r * SUBLANES, (r + 1) * SUBLANES)
            terms = plane_terms(volume_ref, face_ref, square_ref, lit_ref, last[rows], 1 - end, rows, here)
            planes = [sums_ref[c, rows, here] + terms[c] for c in range(3)] + [base_ref[3, rows, here]]
            for c in range(3):
                if r == 0:
                    planes[c] = planes[c] + jnp.where(first_row, extra[c][0], 0.0)
                if r == tiles - 1:
                    planes[c] = planes[c] + jnp.where(last_row, extra[c][1], 0.0)
            if len(out_refs) == 1:
                for i, first in enumerate(range(0, SUBLANES, share)):
                    block = jnp.concatenate([plane[first : first + share] for plane in planes], axis=0)
                    out_refs[0][r * (SUBLANES // share) + i, :, here] = block.astype(jnp.bfloat16)
            else:
                halves = [(planes[c], pltpu.roll(planes[c + 1], SUBLANES // 2, 0)) for c in (0, 2)]
                even = jnp.concatenate([jnp.where(upper, own, turned) for own, turned in halves], axis=0)
                uneven = jnp.concatenate([jnp.where(upper, turned, own) for own, turned in halves], axis=0)
                blocks_ref, _ = out_refs
                blocks_ref[r, 0, :, here] = even
                blocks_ref[r, 1, :, here] = uneven
        return carry

    lax.fori_loop(0, columns // LANES, chunk, 0, unroll=8)
    if len(out_refs) > 1:
        blocks_ref, give_ref = out_refs
        chip, core, mask = route()
        given = (blocks_ref[chip, 1 - core], blocks_ref[chip ^ 3, core], blocks_ref[chip ^ mask ^ 3, 0], blocks_ref[chip ^ mask ^ 3, 1])
        for i, block in enumerate(given):
            give_ref[i] = block.astype(jnp.bfloat16)


def add_edges(volume, sums, interior, halos, depth_count, paired):
    _, slices, height, columns = volume.shape
    share = height // depth_count
    if paired:
        block = (4 * share, columns)
        shapes = [
            jax.ShapeDtypeStruct((depth_count // 2, 2, *block), jnp.float32),
            jax.ShapeDtypeStruct((4, *block), jnp.bfloat16),
        ]
    else:
        shapes = [jax.ShapeDtypeStruct((depth_count, 4 * share, columns), jnp.bfloat16)]
    return pl.pallas_call(
        functools.partial(edge_kernel, share),
        in_specs=[WHOLE] * 12,
        out_specs=[WHOLE] * len(shapes),
        out_shape=shapes,
        compiler_params=pltpu.CompilerParams(vmem_limit_bytes=24 * 1024 * 1024),
    )(volume, sums, *interior, *halos)


def served(depth):
    chip, core = depth // 2, depth % 2
    return 1 + (core ^ (chip & 1) ^ (chip >> 1))


def route():
    position = lax.axis_index("depth")
    return position // 2, position % 2, served(position)


def over(nearer, farther, uneven):
    share = nearer.shape[0] // 4
    clear = 1.0 - jnp.where(uneven, nearer[2 * share : 3 * share], nearer[3 * share :])
    return nearer + jnp.concatenate([clear] * 4, axis=0) * farther


def merge_kernel(blocks_ref, other_ref, own_ref, cross_ref, side_ref):
    chip, core, mask = route()
    odd = core == 1

    def merged(keep, i, uneven):
        other = other_ref[i].astype(jnp.float32)
        return over(jnp.where(odd, other, keep), jnp.where(odd, keep, other), uneven)

    own_ref[...] = merged(blocks_ref[chip, core], 0, odd)
    for i, p in enumerate((1 - core, core)):
        side_ref[i] = merged(blocks_ref[chip ^ mask, p], 2 + p, p == 1).astype(jnp.bfloat16)
    cross_ref[...] = merged(blocks_ref[chip ^ 3, 1 - core], 1, jnp.logical_not(odd)).astype(jnp.bfloat16)


def merge(blocks, other):
    rows, columns = other.shape[1:]
    return pl.pallas_call(
        merge_kernel,
        in_specs=[WHOLE] * 2,
        out_specs=[WHOLE] * 3,
        out_shape=[
            jax.ShapeDtypeStruct((rows, columns), jnp.float32),
            jax.ShapeDtypeStruct((rows, columns), jnp.bfloat16),
            jax.ShapeDtypeStruct((2, rows, columns), jnp.bfloat16),
        ],
        compiler_params=pltpu.CompilerParams(vmem_limit_bytes=8 * 1024 * 1024),
    )(blocks, other)


def pass_kernel(side_ref, out_ref):
    out_ref[...] = side_ref[1]


def pass_on(side):
    return pl.pallas_call(
        pass_kernel,
        in_specs=[WHOLE],
        out_specs=WHOLE,
        out_shape=jax.ShapeDtypeStruct(side.shape[1:], side.dtype),
        compiler_params=pltpu.CompilerParams(vmem_limit_bytes=4 * 1024 * 1024),
    )(side)


def gather_kernel(side_ref, cross_ref, passed_ref, own_ref, out_ref):
    share = out_ref.shape[1]
    chip, core, mask = route()
    odd, serves_x = core == 1, mask == 1
    side, passed = side_ref[0].astype(jnp.float32), passed_ref[...].astype(jnp.float32)
    parts = [
        own_ref[...],
        jnp.where(serves_x, side, passed),
        jnp.where(serves_x, passed, side),
        cross_ref[...].astype(jnp.float32),
    ]
    step = 1
    while len(parts) > 1:
        swap = (chip & step) != 0
        parts = [
            over(jnp.where(swap, parts[i + 1], parts[i]), jnp.where(swap, parts[i], parts[i + 1]), odd)
            for i in range(0, len(parts), 2)
        ]
        step *= 2
    planes = [parts[0][c * share : (c + 1) * share] for c in range(4)]
    for c in range(4):
        out_ref[c] = jnp.where(odd, planes[c ^ 1], planes[c])


def gather(parts, share):
    columns = parts[-1].shape[1]
    return pl.pallas_call(
        gather_kernel,
        in_specs=[WHOLE] * len(parts),
        out_specs=WHOLE,
        out_shape=jax.ShapeDtypeStruct((4, share, columns), jnp.float32),
        compiler_params=pltpu.CompilerParams(vmem_limit_bytes=4 * 1024 * 1024),
    )(*parts)


def finish_kernel(parts_ref, out_ref):
    count = parts_ref.shape[0]
    _, share, columns = out_ref.shape
    remaining = jnp.ones((share, columns), jnp.float32)
    sums = [jnp.zeros((share, columns), jnp.float32) for _ in range(3)]
    for k in range(count):
        part = parts_ref[k].astype(jnp.float32)
        for c in range(3):
            sums[c] = sums[c] + remaining * part[c * share : (c + 1) * share]
        remaining = remaining - remaining * part[3 * share :]
    for c in range(3):
        out_ref[c] = sums[c]
    out_ref[3] = 1.0 - remaining


def finish(parts, share):
    columns = parts.shape[2]
    return pl.pallas_call(
        finish_kernel,
        in_specs=[WHOLE],
        out_specs=WHOLE,
        out_shape=jax.ShapeDtypeStruct((4, share, columns), jnp.float32),
        compiler_params=pltpu.CompilerParams(vmem_limit_bytes=4 * 1024 * 1024),
    )(parts)


def swapped(values, kinds):
    depth_count, row_count = lax.axis_size("depth"), lax.axis_size("rows")
    perm = []
    for d in range(depth_count):
        for r in range(row_count):
            kind = kinds[r % 2]
            e, q = d, r
            if kind == "near slab":
                e = d ^ 1
            elif kind == "far slab":
                e = d + 1 if d % 2 else d - 1
                e = depth_count - 1 - d if not 0 <= e < depth_count else e
            else:
                q = r ^ 1 if kind == "near row" else (r + 1 if r % 2 else r - 1)
                if not 0 <= q < row_count:
                    e, q = d ^ 1, r
            perm.append((d * row_count + r, e * row_count + q))
    return lax.ppermute(values, ("depth", "rows"), perm)


def exchanged(values, mask):
    masks = [mask(d) if callable(mask) else mask for d in range(lax.axis_size("depth"))]
    return lax.ppermute(values, "depth", [(d, d ^ m) for d, m in enumerate(masks)])


def body(volume, color_map, alpha_map):
    depth_count = lax.axis_size("depth")
    share = volume.shape[2] // depth_count
    first, rows_near, second, rows_far = cut_edges(volume)
    first = swapped(first, ("far slab", "near slab"))
    rows_near = swapped(rows_near, ("near row", "near row"))
    second = swapped(second, ("near slab", "far slab"))
    rows_far = swapped(rows_far, ("far row", "far row"))
    interior = march_interior(volume, color_map, alpha_map, depth_count)
    halos = (first, rows_near, second, rows_far)
    paired = depth_count == 8 and 2 * share == SUBLANES
    sums = add_first_plane(volume, *interior[:4], first)
    outs = add_edges(volume, sums, interior, halos, depth_count, paired)
    if not paired:
        return finish(lax.all_to_all(outs[0], "depth", 0, 0, tiled=True), share)
    blocks, give = outs
    own, cross, side = merge(blocks, exchanged(give, 1))
    side = exchanged(side, lambda d: 2 * served(d) + 1)
    cross = exchanged(cross, 7)
    return gather((side, cross, exchanged(pass_on(side), 1), own), share)


def solution(mesh):
    in_specs = (P(None, "depth", "rows", None), P(), P())
    out_specs = P(None, ("rows", "depth"), None)
    return jax.shard_map(body, mesh=mesh, in_specs=in_specs, out_specs=out_specs, check_vma=False)
```

```python
import functools

import jax
import jax.numpy as jnp
from jax import lax
from jax.experimental import pallas as pl
from jax.experimental.pallas import tpu as pltpu
from jax.sharding import PartitionSpec as P

AMBIENT = 0.3
DIFFUSE = 0.7
LIGHT_DEPTH = 0.48 * DIFFUSE
LIGHT_ROWS = 0.6 * DIFFUSE
LIGHT_COLS = 0.64 * DIFFUSE
OPACITY = 4.0
LANES = 128
SUBLANES = 8
WHOLE = pl.BlockSpec(memory_space=pltpu.VMEM)


def parity(axis):
    return lax.axis_index(axis) % 2


def ends(axis):
    position = lax.axis_index(axis)
    return position == 0, position == lax.axis_size(axis) - 1


def edges_kernel(volume_ref, first_out, rows_near_out, second_out, rows_far_out, strip_ref, plane_ref, sems):
    _, slices, height, columns = volume_ref.shape
    odd, odd_row = parity("depth"), parity("rows")
    far_first = 1 - odd_row
    last_first = odd ^ far_first ^ 1
    tiles = height // SUBLANES

    def plane_copies(i, s):
        for t in range(tiles):
            rows = pl.ds(t * SUBLANES, SUBLANES)
            yield pltpu.make_async_copy(volume_ref.at[0, s, rows], plane_ref.at[i, rows], sems.at[i, t])

    def strip_copy(i, row):
        return pltpu.make_async_copy(volume_ref.at[0, :, row], strip_ref.at[i], sems.at[2, i])

    copies = [
        list(plane_copies(0, last_first * (slices - 1))),
        [strip_copy(0, (1 - odd_row) * (height - 1))],
        list(plane_copies(1, (1 - last_first) * (slices - 1))),
        [strip_copy(1, odd_row * (height - 1))],
    ]
    for group in copies:
        for copy in group:
            copy.start()

    def arrive(group):
        for copy in group:
            copy.wait()

    def narrow(values):
        return values.astype(jnp.float32).astype(jnp.bfloat16)

    def padded(strip):
        return narrow(jnp.concatenate([strip, jnp.zeros((height - slices, columns), jnp.int32)], axis=0))

    arrive(copies[0])
    first_out[...] = narrow(plane_ref[0])
    arrive(copies[1])
    rows_near_out[...] = padded(strip_ref[0])
    arrive(copies[2])
    second_out[...] = narrow(plane_ref[1])
    arrive(copies[3])
    rows_far_out[...] = narrow(strip_ref[1])


def cut_edges(volume):
    _, slices, height, columns = volume.shape
    plane = jax.ShapeDtypeStruct((height, columns), jnp.bfloat16)
    strip = jax.ShapeDtypeStruct((slices, columns), jnp.bfloat16)
    return pl.pallas_call(
        edges_kernel,
        in_specs=[pl.BlockSpec(memory_space=pl.ANY)],
        out_specs=[WHOLE] * 4,
        out_shape=[plane, plane, plane, strip],
        scratch_shapes=[
            pltpu.VMEM((2, slices, columns), jnp.int32),
            pltpu.VMEM((2, height, columns), jnp.int32),
            pltpu.SemaphoreType.DMA((3, max(2, height // SUBLANES))),
        ],
        compiler_params=pltpu.CompilerParams(vmem_limit_bytes=52 * 1024 * 1024),
    )(volume)


def pick(entries, places):
    dims = lax.GatherDimensionNumbers(
        offset_dims=(),
        collapsed_slice_dims=(1,),
        start_index_map=(1,),
        operand_batching_dims=(0,),
        start_indices_batching_dims=(0,),
    )
    return lax.gather(entries, places[..., None], dims, (1, 1), mode=lax.GatherScatterMode.PROMISE_IN_BOUNDS)


def shade(grad_depth, facing, squares):
    facing = facing + LIGHT_DEPTH * grad_depth
    squares = squares + grad_depth * grad_depth
    return AMBIENT + jnp.abs(facing) * lax.rsqrt(jnp.maximum(squares, 4.0))


def interior_kernel(
    opacity_scale,
    volume_ref,
    color_ref,
    alpha_ref,
    base_ref,
    face_ref,
    square_ref,
    lit_ref,
    grad_ref,
    strip_ref,
    pair_ref,
    held_ref,
):
    _, slices, height, columns = volume_ref.shape
    tiles = height // SUBLANES
    chunks = columns // LANES
    tile = (SUBLANES, LANES)
    strip = (slices, LANES)

    packed = color_ref[0:1, :] + color_ref[1:2, :] * 256 + color_ref[2:3, :] * 65536
    color_low, color_high = packed[:, :LANES], packed[:, LANES:]
    alpha_both = alpha_ref[0:1, :LANES] + alpha_ref[0:1, LANES:] * 256

    def colors(value, tables):
        low, high = tables
        place = value & (LANES - 1)
        color = jnp.where(value < LANES, pick(low, place), pick(high, place))
        parts = (color & 255, lax.shift_right_logical(color, 8) & 255, lax.shift_right_logical(color, 16))
        return [part.astype(jnp.float32) for part in parts]

    def opacity(level, table):
        entry = pick(table, level & (LANES - 1))
        entry = lax.shift_right_logical(entry, lax.shift_right_logical(level & LANES, 4)) & 255
        return entry.astype(jnp.float32) * opacity_scale

    tile_colors = [jnp.broadcast_to(t, tile) for t in (color_low, color_high)]
    tile_alpha = jnp.broadcast_to(alpha_both, tile)
    strip_colors = [jnp.broadcast_to(t, strip) for t in (color_low, color_high)]

    def masks(shape):
        lane = lax.broadcasted_iota(jnp.int32, shape, 1)
        row = lax.broadcasted_iota(jnp.int32, shape, 0)
        return lane == 0, lane == LANES - 1, row == 0, row == shape[0] - 1

    first_lane, last_lane, first_row, last_row = masks(tile)
    strip_first_lane, strip_last_lane, front, back = masks(strip)

    pairs = slices // 2
    top = SUBLANES

    def clear(j, carry):
        pair_ref[j] = jnp.zeros(pair_ref.shape[1:], jnp.int32)
        return carry

    clear(0, 0)
    clear(chunks + 1, 0)
    margin = jnp.zeros((pairs, SUBLANES, LANES), jnp.int32)

    def pack(j, carry):
        here = pl.ds(pl.multiple_of(j * LANES, LANES), LANES)
        pair_ref[j + 1, :, :top] = margin
        pair_ref[j + 1, :, top + height :] = margin
        for p in range(pairs):
            pair_ref[j + 1, p, top : top + height] = volume_ref[0, p, :, here] + lax.shift_left(
                volume_ref[0, p + pairs, :, here], 16
            )
        return carry

    lax.fori_loop(0, chunks, pack, 0)

    def split(difference):
        low = lax.shift_right_arithmetic(lax.shift_left(difference, 16), 16)
        high = lax.shift_right_arithmetic(difference + 32768, 16)
        return low.astype(jnp.float32), high.astype(jnp.float32)

    def across(left_value, value, right_value, first, last):
        west = pltpu.roll(jnp.where(last, left_value, value), 1, 1)
        east = pltpu.roll(jnp.where(first, right_value, value), LANES - 1, 1)
        return split(east - west)

    def chunk(j, carry):
        here = pl.ds(pl.multiple_of(j * LANES, LANES), LANES)

        for r in range(tiles):
            rows = slice(r * SUBLANES, (r + 1) * SUBLANES)
            values = [volume_ref[0, s, rows, here] for s in range(slices)]

            def words(c, p, offset=0):
                return pair_ref[c, p, top + r * SUBLANES + offset : top + (r + 1) * SUBLANES + offset, :]

            down, right = [], []
            for p in range(pairs):
                down.append(split(words(j + 1, p, 1) - words(j + 1, p, -1)))
                right.append(across(words(j, p), words(j + 1, p), words(j + 2, p), first_lane, last_lane))
            remaining = jnp.ones(tile, jnp.float32)
            sums = [jnp.zeros(tile, jnp.float32) for _ in range(3)]
            for s in range(slices):
                value = values[s]
                grad_rows = down[s % pairs][s // pairs]
                grad_cols = right[s % pairs][s // pairs]
                squares = grad_rows * grad_rows + grad_cols * grad_cols
                facing = LIGHT_ROWS * grad_rows + LIGHT_COLS * grad_cols
                weight = remaining * opacity(volume_ref[1, s, rows, here], tile_alpha)
                remaining = remaining - weight
                if r == 0:
                    held_ref[0, s : s + 1, :] = weight[:1]
                    weight = jnp.where(first_row, 0.0, weight)
                if r == tiles - 1:
                    held_ref[1, s : s + 1, :] = weight[SUBLANES - 1 :]
                    weight = jnp.where(last_row, 0.0, weight)
                emitted = colors(value, tile_colors)
                if 0 < s < slices - 1:
                    grad_depth = (values[s + 1] - values[s - 1]).astype(jnp.float32)
                    weight = weight * shade(grad_depth, facing, squares)
                    for c in range(3):
                        sums[c] = sums[c] + emitted[c] * weight
                else:
                    end = int(s > 0)
                    face_ref[end, rows, here] = facing
                    square_ref[end, rows, here] = squares
                    weight = weight * (1.0 / 255.0)
                    for c in range(3):
                        lit_ref[end, c, rows, here] = emitted[c] * weight
            for c in range(3):
                base_ref[c, rows, here] = sums[c] * (1.0 / 255.0)
            base_ref[3, rows, here] = 1.0 - remaining

        for q, (edge, inner) in enumerate(((0, 1), (height - 1, height - 2))):
            value = volume_ref[0, :, edge, here]
            behind = pltpu.roll(jnp.where(back, 0, value), 1, 0)
            ahead = pltpu.roll(jnp.where(front, 0, value), slices - 1, 0)
            grad_ref[q, 0, :, here] = (ahead - behind).astype(jnp.float32)
            grad_ref[q, 1, :, here] = volume_ref[0, :, inner, here].astype(jnp.float32)
            word = pair_ref[j + 1, :, top + edge, :]
            low, high = across(
                pair_ref[j, :, top + edge, :],
                word,
                pair_ref[j + 2, :, top + edge, :],
                strip_first_lane[:pairs],
                strip_last_lane[:pairs],
            )
            grad_ref[q, 2, :pairs, here] = low
            grad_ref[q, 2, pairs:, here] = high
            weight = held_ref[q] * (1.0 / 255.0)
            emitted = colors(value, strip_colors)
            for c in range(3):
                strip_ref[q, c, :, here] = emitted[c] * weight
        return carry

    lax.fori_loop(0, chunks, chunk, 0, unroll=4)


def march_interior(volume, color_map, alpha_map, depth_count):
    _, slices, height, columns = volume.shape
    opacity_scale = OPACITY / (255.0 * slices * depth_count)
    shapes = [
        (4, height, columns),
        (2, height, columns),
        (2, height, columns),
        (2, 3, height, columns),
        (2, 3, slices, columns),
        (2, 3, slices, columns),
    ]
    voxels = slices * height * columns
    return pl.pallas_call(
        functools.partial(interior_kernel, opacity_scale),
        in_specs=[WHOLE] * 3,
        out_specs=[WHOLE] * len(shapes),
        out_shape=[jax.ShapeDtypeStruct(shape, jnp.float32) for shape in shapes],
        scratch_shapes=[
            pltpu.VMEM((columns // LANES + 2, slices // 2, height + 2 * SUBLANES, LANES), jnp.int32),
            pltpu.VMEM((2, slices, LANES), jnp.float32),
        ],
        compiler_params=pltpu.CompilerParams(vmem_limit_bytes=24 * 1024 * 1024),
        cost_estimate=pl.CostEstimate(flops=voxels * 80, bytes_accessed=voxels * 20, transcendentals=voxels),
    )(volume, color_map, alpha_map.reshape(1, -1))


def row_sums(first, second):
    count = first.shape[0]
    if count != SUBLANES:
        return jnp.sum(first, axis=0, keepdims=True), jnp.sum(second, axis=0, keepdims=True)
    upper = lax.broadcasted_iota(jnp.int32, first.shape, 0) < 4
    both = jnp.where(upper, first, second) + pltpu.roll(jnp.where(upper, second, first), 4, 0)
    both = both + pltpu.roll(both, 6, 0)
    both = both + pltpu.roll(both, 7, 0)
    return both, pltpu.roll(both, 3, 0)


def plane_terms(volume_ref, face_ref, square_ref, lit_ref, halo, end, rows, here):
    slices = volume_ref.shape[1]
    inner = volume_ref[0, jnp.where(end == 1, slices - 2, 1), rows, here].astype(jnp.float32)
    grad_depth = jnp.where(end == 1, halo - inner, inner - halo)
    shading = shade(grad_depth, face_ref[end, rows, here], square_ref[end, rows, here])
    return [lit_ref[end, c, rows, here] * shading for c in range(3)]


def first_end():
    front_end, back_end = ends("depth")
    end = jnp.where(parity("depth") == parity("rows"), 0, 1)
    return end, jnp.where(end == 1, back_end, front_end), jnp.where(end == 1, front_end, back_end)


def first_plane_kernel(volume_ref, base_ref, face_ref, square_ref, lit_ref, first_ref, sums_ref):
    _, height, columns = base_ref.shape
    end, outside, _ = first_end()

    def chunk(j, carry):
        here = pl.ds(pl.multiple_of(j * LANES, LANES), LANES)
        first = jnp.where(outside, 0.0, first_ref[:, here].astype(jnp.float32))
        for r in range(height // SUBLANES):
            rows = slice(r * SUBLANES, (r + 1) * SUBLANES)
            terms = plane_terms(volume_ref, face_ref, square_ref, lit_ref, first[rows], end, rows, here)
            for c in range(3):
                sums_ref[c, rows, here] = base_ref[c, rows, here] + terms[c]
        return carry

    lax.fori_loop(0, columns // LANES, chunk, 0, unroll=4)


def add_first_plane(volume, base, face, square, lit, first):
    return pl.pallas_call(
        first_plane_kernel,
        in_specs=[WHOLE] * 6,
        out_specs=WHOLE,
        out_shape=jax.ShapeDtypeStruct((3, *base.shape[1:]), jnp.float32),
        compiler_params=pltpu.CompilerParams(vmem_limit_bytes=8 * 1024 * 1024),
        cost_estimate=pl.CostEstimate(flops=base.size * 20, bytes_accessed=base.size * 12, transcendentals=base.size // 4),
    )(volume, base, face, square, lit, first)


def edge_kernel(
    share, volume_ref, sums_ref, base_ref, face_ref, square_ref, lit_ref, grad_ref, strip_ref, first_ref, rows_near_ref, second_ref, rows_far_ref, *out_refs
):
    _, slices, height, columns = volume_ref.shape
    tiles = height // SUBLANES
    tile = (SUBLANES, LANES)
    row = lax.broadcasted_iota(jnp.int32, tile, 0)
    first_row, last_row, upper = row == 0, row == SUBLANES - 1, row < SUBLANES // 2
    level = lax.broadcasted_iota(jnp.int32, (slices, LANES), 0)
    front, back = level == 0, level == slices - 1
    odd, odd_row = parity("depth") == 1, parity("rows") == 1
    chip = lax.axis_index("depth") // 2
    front_came_first = odd == odd_row
    front_end, back_end = ends("depth")
    top_end, bottom_end = ends("rows")
    end, _, outside = first_end()

    def chunk(j, carry):
        here = pl.ds(pl.multiple_of(j * LANES, LANES), LANES)
        rows_near = rows_near_ref[:, here].astype(jnp.float32)[:slices]
        rows_far = rows_far_ref[:, here].astype(jnp.float32)
        above = jnp.where(top_end, 0.0, jnp.where(odd_row, rows_near, rows_far))
        below = jnp.where(bottom_end, 0.0, jnp.where(odd_row, rows_far, rows_near))
        first = first_ref[:, here].astype(jnp.float32)
        second = second_ref[:, here].astype(jnp.float32)
        before = jnp.where(front_end, 0.0, jnp.where(front_came_first, first, second))
        after = jnp.where(back_end, 0.0, jnp.where(front_came_first, second, first))
        last = jnp.where(outside, 0.0, second)
        extra = []
        for q, edge in enumerate((0, height - 1)):
            inner = grad_ref[q, 1, :, here]
            grad_rows = below - inner if q else inner - above
            grad_cols = grad_ref[q, 2, :, here]
            grad_depth = grad_ref[q, 0, :, here] + jnp.where(
                back, after[edge : edge + 1], jnp.where(front, -before[edge : edge + 1], 0.0)
            )
            shading = shade(
                grad_depth,
                LIGHT_ROWS * grad_rows + LIGHT_COLS * grad_cols,
                grad_rows * grad_rows + grad_cols * grad_cols,
            )
            extra.append([strip_ref[q, c, :, here] * shading for c in range(3)])
        extra = [row_sums(extra[0][c], extra[1][c]) for c in range(3)]
        for r in range(tiles):
            rows = slice(r * SUBLANES, (r + 1) * SUBLANES)
            terms = plane_terms(volume_ref, face_ref, square_ref, lit_ref, last[rows], 1 - end, rows, here)
            planes = [sums_ref[c, rows, here] + terms[c] for c in range(3)] + [base_ref[3, rows, here]]
            for c in range(3):
                if r == 0:
                    planes[c] = planes[c] + jnp.where(first_row, extra[c][0], 0.0)
                if r == tiles - 1:
                    planes[c] = planes[c] + jnp.where(last_row, extra[c][1], 0.0)
            if len(out_refs) == 1:
                for i, first in enumerate(range(0, SUBLANES, share)):
                    block = jnp.concatenate([plane[first : first + share] for plane in planes], axis=0)
                    out_refs[0][r * (SUBLANES // share) + i, :, here] = block.astype(jnp.bfloat16)
            else:
                halves = [(planes[c], pltpu.roll(planes[c + 1], SUBLANES // 2, 0)) for c in (0, 2)]
                even = jnp.concatenate([jnp.where(upper, own, turned) for own, turned in halves], axis=0)
                uneven = jnp.concatenate([jnp.where(upper, turned, own) for own, turned in halves], axis=0)
                keep_ref, give_ref = out_refs
                keep_even = odd != (chip == r)
                keep_ref[r, :, here] = jnp.where(keep_even, even, uneven)
                give_ref[r, :, here] = jnp.where(keep_even, uneven, even).astype(jnp.bfloat16)
        return carry

    lax.fori_loop(0, columns // LANES, chunk, 0, unroll=8)


def add_edges(volume, sums, interior, halos, depth_count, paired):
    _, slices, height, columns = volume.shape
    share = height // depth_count
    if paired:
        half = (depth_count // 2, 4 * share, columns)
        shapes = [jax.ShapeDtypeStruct(half, jnp.float32), jax.ShapeDtypeStruct(half, jnp.bfloat16)]
    else:
        shapes = [jax.ShapeDtypeStruct((depth_count, 4 * share, columns), jnp.bfloat16)]
    return pl.pallas_call(
        functools.partial(edge_kernel, share),
        in_specs=[WHOLE] * 12,
        out_specs=[WHOLE] * len(shapes),
        out_shape=shapes,
        compiler_params=pltpu.CompilerParams(vmem_limit_bytes=24 * 1024 * 1024),
    )(volume, sums, *interior, *halos)


def over(nearer, farther, uneven):
    share = nearer.shape[0] // 4
    clear = 1.0 - jnp.where(uneven, nearer[2 * share : 3 * share], nearer[3 * share :])
    return nearer + jnp.concatenate([clear] * 4, axis=0) * farther


def merge_kernel(keep_ref, other_ref, *out_refs):
    position = lax.axis_index("depth")
    odd, chip = position % 2 == 1, position // 2
    for k, out_ref in enumerate(out_refs):
        keep = keep_ref[chip ^ k]
        other = other_ref[chip ^ k].astype(jnp.float32)
        uneven = jnp.logical_not(odd) if k else odd
        block = over(jnp.where(odd, other, keep), jnp.where(odd, keep, other), uneven)
        out_ref[...] = block.astype(out_ref.dtype)


def merge(keep, other):
    chips, rows, columns = keep.shape
    shapes = [jax.ShapeDtypeStruct((rows, columns), jnp.bfloat16 if k else jnp.float32) for k in range(chips)]
    return pl.pallas_call(
        merge_kernel,
        in_specs=[WHOLE] * 2,
        out_specs=[WHOLE] * chips,
        out_shape=shapes,
        compiler_params=pltpu.CompilerParams(vmem_limit_bytes=8 * 1024 * 1024),
    )(keep, other)


def gather_kernel(*refs):
    *part_refs, out_ref = refs
    part_refs.reverse()
    count = len(part_refs)
    share = out_ref.shape[1]
    position = lax.axis_index("depth")
    odd, chip = position % 2 == 1, position // 2
    parts = [part_ref[...].astype(jnp.float32) for part_ref in part_refs]
    step = 1
    while step < count:
        swap = (chip & step) != 0
        parts = [
            over(jnp.where(swap, parts[i + 1], parts[i]), jnp.where(swap, parts[i], parts[i + 1]), odd)
            for i in range(0, len(parts), 2)
        ]
        step *= 2
    planes = [parts[0][c * share : (c + 1) * share] for c in range(4)]
    for c in range(4):
        out_ref[c] = jnp.where(odd, planes[c ^ 1], planes[c])


def gather(parts, share):
    columns = parts[0].shape[1]
    return pl.pallas_call(
        gather_kernel,
        in_specs=[WHOLE] * len(parts),
        out_specs=WHOLE,
        out_shape=jax.ShapeDtypeStruct((4, share, columns), jnp.float32),
        compiler_params=pltpu.CompilerParams(vmem_limit_bytes=4 * 1024 * 1024),
    )(*parts)


def finish_kernel(parts_ref, out_ref):
    count = parts_ref.shape[0]
    _, share, columns = out_ref.shape
    remaining = jnp.ones((share, columns), jnp.float32)
    sums = [jnp.zeros((share, columns), jnp.float32) for _ in range(3)]
    for k in range(count):
        part = parts_ref[k].astype(jnp.float32)
        for c in range(3):
            sums[c] = sums[c] + remaining * part[c * share : (c + 1) * share]
        remaining = remaining - remaining * part[3 * share :]
    for c in range(3):
        out_ref[c] = sums[c]
    out_ref[3] = 1.0 - remaining


def finish(parts, share):
    columns = parts.shape[2]
    return pl.pallas_call(
        finish_kernel,
        in_specs=[WHOLE],
        out_specs=WHOLE,
        out_shape=jax.ShapeDtypeStruct((4, share, columns), jnp.float32),
        compiler_params=pltpu.CompilerParams(vmem_limit_bytes=4 * 1024 * 1024),
    )(parts)


def swapped(values, kinds):
    depth_count, row_count = lax.axis_size("depth"), lax.axis_size("rows")
    perm = []
    for d in range(depth_count):
        for r in range(row_count):
            kind = kinds[r % 2]
            e, q = d, r
            if kind == "near slab":
                e = d ^ 1
            elif kind == "far slab":
                e = d + 1 if d % 2 else d - 1
                e = depth_count - 1 - d if not 0 <= e < depth_count else e
            else:
                q = r ^ 1 if kind == "near row" else (r + 1 if r % 2 else r - 1)
                if not 0 <= q < row_count:
                    e, q = d ^ 1, r
            perm.append((d * row_count + r, e * row_count + q))
    return lax.ppermute(values, ("depth", "rows"), perm)


def exchanged(values, mask):
    return lax.ppermute(values, "depth", [(d, d ^ mask) for d in range(lax.axis_size("depth"))])


def body(volume, color_map, alpha_map):
    depth_count = lax.axis_size("depth")
    share = volume.shape[2] // depth_count
    first, rows_near, second, rows_far = cut_edges(volume)
    first = swapped(first, ("far slab", "near slab"))
    rows_near = swapped(rows_near, ("near row", "near row"))
    second = swapped(second, ("near slab", "far slab"))
    rows_far = swapped(rows_far, ("far row", "far row"))
    interior = march_interior(volume, color_map, alpha_map, depth_count)
    halos = (first, rows_near, second, rows_far)
    paired = depth_count == 8 and 2 * share == SUBLANES
    sums = add_first_plane(volume, *interior[:4], first)
    outs = add_edges(volume, sums, interior, halos, depth_count, paired)
    if not paired:
        return finish(lax.all_to_all(outs[0], "depth", 0, 0, tiled=True), share)
    keep, give = outs
    own, *sends = merge(keep, exchanged(give, 1))
    received = [exchanged(send, 2 * k + 1) for k, send in reversed(list(enumerate(sends, 1)))]
    return gather((*received, own), share)


def solution(mesh):
    in_specs = (P(None, "depth", "rows", None), P(), P())
    out_specs = P(None, ("rows", "depth"), None)
    return jax.shard_map(body, mesh=mesh, in_specs=in_specs, out_specs=out_specs, check_vma=False)
```

```python
import functools

import jax
import jax.numpy as jnp
from jax import lax
from jax.experimental import pallas as pl
from jax.experimental.pallas import tpu as pltpu
from jax.sharding import PartitionSpec as P

AMBIENT = 0.3
DIFFUSE = 0.7
LIGHT_DEPTH = 0.48 * DIFFUSE
LIGHT_ROWS = 0.6 * DIFFUSE
LIGHT_COLS = 0.64 * DIFFUSE
OPACITY = 4.0
LANES = 128
SUBLANES = 8
WHOLE = pl.BlockSpec(memory_space=pltpu.VMEM)


def parity(axis):
    return lax.axis_index(axis) % 2


def ends(axis):
    position = lax.axis_index(axis)
    return position == 0, position == lax.axis_size(axis) - 1


def edges_kernel(volume_ref, first_out, rows_near_out, second_out, rows_far_out, strip_ref, plane_ref, sems):
    _, slices, height, columns = volume_ref.shape
    odd, odd_row = parity("depth"), parity("rows")
    far_first = 1 - odd_row
    last_first = odd ^ far_first ^ 1
    tiles = height // SUBLANES

    def plane_copies(i, s):
        for t in range(tiles):
            rows = pl.ds(t * SUBLANES, SUBLANES)
            yield pltpu.make_async_copy(volume_ref.at[0, s, rows], plane_ref.at[i, rows], sems.at[i, t])

    def strip_copy(i, row):
        return pltpu.make_async_copy(volume_ref.at[0, :, row], strip_ref.at[i], sems.at[2, i])

    copies = [
        list(plane_copies(0, last_first * (slices - 1))),
        [strip_copy(0, (1 - odd_row) * (height - 1))],
        list(plane_copies(1, (1 - last_first) * (slices - 1))),
        [strip_copy(1, odd_row * (height - 1))],
    ]
    for group in (copies[1], copies[3], copies[0], copies[2]):
        for copy in group:
            copy.start()

    def arrive(group):
        for copy in group:
            copy.wait()

    def narrow(values):
        return values.astype(jnp.float32).astype(jnp.bfloat16)

    def padded(strip):
        return narrow(jnp.concatenate([strip, jnp.zeros((height - slices, columns), jnp.int32)], axis=0))

    arrive(copies[0])
    first_out[...] = narrow(plane_ref[0])
    arrive(copies[2])
    second_out[...] = narrow(plane_ref[1])
    arrive(copies[1])
    rows_near_out[...] = padded(strip_ref[0])
    arrive(copies[3])
    rows_far_out[...] = narrow(strip_ref[1])


def cut_edges(volume):
    _, slices, height, columns = volume.shape
    plane = jax.ShapeDtypeStruct((height, columns), jnp.bfloat16)
    strip = jax.ShapeDtypeStruct((slices, columns), jnp.bfloat16)
    return pl.pallas_call(
        edges_kernel,
        in_specs=[pl.BlockSpec(memory_space=pl.ANY)],
        out_specs=[WHOLE] * 4,
        out_shape=[plane, plane, plane, strip],
        scratch_shapes=[
            pltpu.VMEM((2, slices, columns), jnp.int32),
            pltpu.VMEM((2, height, columns), jnp.int32),
            pltpu.SemaphoreType.DMA((3, max(2, height // SUBLANES))),
        ],
        compiler_params=pltpu.CompilerParams(vmem_limit_bytes=52 * 1024 * 1024),
    )(volume)


def pick(entries, places):
    dims = lax.GatherDimensionNumbers(
        offset_dims=(),
        collapsed_slice_dims=(1,),
        start_index_map=(1,),
        operand_batching_dims=(0,),
        start_indices_batching_dims=(0,),
    )
    return lax.gather(entries, places[..., None], dims, (1, 1), mode=lax.GatherScatterMode.PROMISE_IN_BOUNDS)


def shade(grad_depth, facing, squares):
    facing = facing + LIGHT_DEPTH * grad_depth
    squares = squares + grad_depth * grad_depth
    return AMBIENT + jnp.abs(facing) * lax.rsqrt(jnp.maximum(squares, 4.0))


def interior_kernel(
    opacity_scale,
    volume_ref,
    color_ref,
    alpha_ref,
    base_ref,
    face_ref,
    square_ref,
    lit_ref,
    grad_ref,
    strip_ref,
    pair_ref,
    held_ref,
):
    _, slices, height, columns = volume_ref.shape
    tiles = height // SUBLANES
    chunks = columns // LANES
    tile = (SUBLANES, LANES)
    strip = (slices, LANES)

    packed = color_ref[0:1, :] + color_ref[1:2, :] * 256 + color_ref[2:3, :] * 65536
    color_low, color_high = packed[:, :LANES], packed[:, LANES:]
    alpha_both = alpha_ref[0:1, :LANES] + alpha_ref[0:1, LANES:] * 256

    def colors(value, tables):
        low, high = tables
        place = value & (LANES - 1)
        color = jnp.where(value < LANES, pick(low, place), pick(high, place))
        parts = (color & 255, lax.shift_right_logical(color, 8) & 255, lax.shift_right_logical(color, 16))
        return [part.astype(jnp.float32) for part in parts]

    def opacity(level, table):
        entry = pick(table, level & (LANES - 1))
        entry = lax.shift_right_logical(entry, lax.shift_right_logical(level & LANES, 4)) & 255
        return entry.astype(jnp.float32) * opacity_scale

    tile_colors = [jnp.broadcast_to(t, tile) for t in (color_low, color_high)]
    tile_alpha = jnp.broadcast_to(alpha_both, tile)
    strip_colors = [jnp.broadcast_to(t, strip) for t in (color_low, color_high)]

    def masks(shape):
        lane = lax.broadcasted_iota(jnp.int32, shape, 1)
        row = lax.broadcasted_iota(jnp.int32, shape, 0)
        return lane == 0, lane == LANES - 1, row == 0, row == shape[0] - 1

    first_lane, last_lane, first_row, last_row = masks(tile)
    strip_first_lane, strip_last_lane, front, back = masks(strip)

    pairs = slices // 2
    top = SUBLANES

    def clear(j, carry):
        pair_ref[j] = jnp.zeros(pair_ref.shape[1:], jnp.int32)
        return carry

    clear(0, 0)
    clear(chunks + 1, 0)
    margin = jnp.zeros((pairs, SUBLANES, LANES), jnp.int32)

    def pack(j, carry):
        here = pl.ds(pl.multiple_of(j * LANES, LANES), LANES)
        pair_ref[j + 1, :, :top] = margin
        pair_ref[j + 1, :, top + height :] = margin
        for p in range(pairs):
            pair_ref[j + 1, p, top : top + height] = volume_ref[0, p, :, here] + lax.shift_left(
                volume_ref[0, p + pairs, :, here], 16
            )
        return carry

    lax.fori_loop(0, chunks, pack, 0)

    def split(difference):
        low = lax.shift_right_arithmetic(lax.shift_left(difference, 16), 16)
        high = lax.shift_right_arithmetic(difference + 32768, 16)
        return low.astype(jnp.float32), high.astype(jnp.float32)

    def across(left_value, value, right_value, first, last):
        west = pltpu.roll(jnp.where(last, left_value, value), 1, 1)
        east = pltpu.roll(jnp.where(first, right_value, value), LANES - 1, 1)
        return split(east - west)

    def chunk(j, carry):
        here = pl.ds(pl.multiple_of(j * LANES, LANES), LANES)

        for r in range(tiles):
            rows = slice(r * SUBLANES, (r + 1) * SUBLANES)
            values = [volume_ref[0, s, rows, here] for s in range(slices)]

            def words(c, p, offset=0):
                return pair_ref[c, p, top + r * SUBLANES + offset : top + (r + 1) * SUBLANES + offset, :]

            down, right = [], []
            for p in range(pairs):
                down.append(split(words(j + 1, p, 1) - words(j + 1, p, -1)))
                right.append(across(words(j, p), words(j + 1, p), words(j + 2, p), first_lane, last_lane))
            remaining = jnp.ones(tile, jnp.float32)
            sums = [jnp.zeros(tile, jnp.float32) for _ in range(3)]
            for s in range(slices):
                value = values[s]
                grad_rows = down[s % pairs][s // pairs]
                grad_cols = right[s % pairs][s // pairs]
                squares = grad_rows * grad_rows + grad_cols * grad_cols
                facing = LIGHT_ROWS * grad_rows + LIGHT_COLS * grad_cols
                weight = remaining * opacity(volume_ref[1, s, rows, here], tile_alpha)
                remaining = remaining - weight
                if r == 0:
                    held_ref[0, s : s + 1, :] = weight[:1]
                    weight = jnp.where(first_row, 0.0, weight)
                if r == tiles - 1:
                    held_ref[1, s : s + 1, :] = weight[SUBLANES - 1 :]
                    weight = jnp.where(last_row, 0.0, weight)
                emitted = colors(value, tile_colors)
                if 0 < s < slices - 1:
                    grad_depth = (values[s + 1] - values[s - 1]).astype(jnp.float32)
                    weight = weight * shade(grad_depth, facing, squares)
                    for c in range(3):
                        sums[c] = sums[c] + emitted[c] * weight
                else:
                    end = int(s > 0)
                    face_ref[end, rows, here] = facing
                    square_ref[end, rows, here] = squares
                    weight = weight * (1.0 / 255.0)
                    for c in range(3):
                        lit_ref[end, c, rows, here] = emitted[c] * weight
            for c in range(3):
                base_ref[c, rows, here] = sums[c] * (1.0 / 255.0)
            base_ref[3, rows, here] = 1.0 - remaining

        for q, (edge, inner) in enumerate(((0, 1), (height - 1, height - 2))):
            value = volume_ref[0, :, edge, here]
            behind = pltpu.roll(jnp.where(back, 0, value), 1, 0)
            ahead = pltpu.roll(jnp.where(front, 0, value), slices - 1, 0)
            grad_ref[q, 0, :, here] = (ahead - behind).astype(jnp.float32)
            grad_ref[q, 1, :, here] = volume_ref[0, :, inner, here].astype(jnp.float32)
            word = pair_ref[j + 1, :, top + edge, :]
            low, high = across(
                pair_ref[j, :, top + edge, :],
                word,
                pair_ref[j + 2, :, top + edge, :],
                strip_first_lane[:pairs],
                strip_last_lane[:pairs],
            )
            grad_ref[q, 2, :pairs, here] = low
            grad_ref[q, 2, pairs:, here] = high
            weight = held_ref[q] * (1.0 / 255.0)
            emitted = colors(value, strip_colors)
            for c in range(3):
                strip_ref[q, c, :, here] = emitted[c] * weight
        return carry

    lax.fori_loop(0, chunks, chunk, 0, unroll=4)


def march_interior(volume, color_map, alpha_map, depth_count):
    _, slices, height, columns = volume.shape
    opacity_scale = OPACITY / (255.0 * slices * depth_count)
    shapes = [
        (4, height, columns),
        (2, height, columns),
        (2, height, columns),
        (2, 3, height, columns),
        (2, 3, slices, columns),
        (2, 3, slices, columns),
    ]
    voxels = slices * height * columns
    return pl.pallas_call(
        functools.partial(interior_kernel, opacity_scale),
        in_specs=[WHOLE] * 3,
        out_specs=[WHOLE] * len(shapes),
        out_shape=[jax.ShapeDtypeStruct(shape, jnp.float32) for shape in shapes],
        scratch_shapes=[
            pltpu.VMEM((columns // LANES + 2, slices // 2, height + 2 * SUBLANES, LANES), jnp.int32),
            pltpu.VMEM((2, slices, LANES), jnp.float32),
        ],
        compiler_params=pltpu.CompilerParams(vmem_limit_bytes=24 * 1024 * 1024),
        cost_estimate=pl.CostEstimate(flops=voxels * 80, bytes_accessed=voxels * 20, transcendentals=voxels),
    )(volume, color_map, alpha_map.reshape(1, -1))


def row_sums(first, second):
    count = first.shape[0]
    if count != SUBLANES:
        return jnp.sum(first, axis=0, keepdims=True), jnp.sum(second, axis=0, keepdims=True)
    upper = lax.broadcasted_iota(jnp.int32, first.shape, 0) < 4
    both = jnp.where(upper, first, second) + pltpu.roll(jnp.where(upper, second, first), 4, 0)
    both = both + pltpu.roll(both, 6, 0)
    both = both + pltpu.roll(both, 7, 0)
    return both, pltpu.roll(both, 3, 0)


def plane_terms(volume_ref, face_ref, square_ref, lit_ref, halo, end, rows, here):
    slices = volume_ref.shape[1]
    inner = volume_ref[0, jnp.where(end == 1, slices - 2, 1), rows, here].astype(jnp.float32)
    grad_depth = jnp.where(end == 1, halo - inner, inner - halo)
    shading = shade(grad_depth, face_ref[end, rows, here], square_ref[end, rows, here])
    return [lit_ref[end, c, rows, here] * shading for c in range(3)]


def first_end():
    front_end, back_end = ends("depth")
    end = jnp.where(parity("depth") == parity("rows"), 0, 1)
    return end, jnp.where(end == 1, back_end, front_end), jnp.where(end == 1, front_end, back_end)


def first_plane_kernel(volume_ref, base_ref, face_ref, square_ref, lit_ref, first_ref, sums_ref):
    _, height, columns = base_ref.shape
    end, outside, _ = first_end()

    def chunk(j, carry):
        here = pl.ds(pl.multiple_of(j * LANES, LANES), LANES)
        first = jnp.where(outside, 0.0, first_ref[:, here].astype(jnp.float32))
        for r in range(height // SUBLANES):
            rows = slice(r * SUBLANES, (r + 1) * SUBLANES)
            terms = plane_terms(volume_ref, face_ref, square_ref, lit_ref, first[rows], end, rows, here)
            for c in range(3):
                sums_ref[c, rows, here] = base_ref[c, rows, here] + terms[c]
        return carry

    lax.fori_loop(0, columns // LANES, chunk, 0, unroll=4)


def add_first_plane(volume, base, face, square, lit, first):
    return pl.pallas_call(
        first_plane_kernel,
        in_specs=[WHOLE] * 6,
        out_specs=WHOLE,
        out_shape=jax.ShapeDtypeStruct((3, *base.shape[1:]), jnp.float32),
        compiler_params=pltpu.CompilerParams(vmem_limit_bytes=8 * 1024 * 1024),
        cost_estimate=pl.CostEstimate(flops=base.size * 20, bytes_accessed=base.size * 12, transcendentals=base.size // 4),
    )(volume, base, face, square, lit, first)


def edge_kernel(
    share, volume_ref, sums_ref, base_ref, face_ref, square_ref, lit_ref, grad_ref, strip_ref, first_ref, rows_near_ref, second_ref, rows_far_ref, *out_refs
):
    _, slices, height, columns = volume_ref.shape
    tiles = height // SUBLANES
    tile = (SUBLANES, LANES)
    row = lax.broadcasted_iota(jnp.int32, tile, 0)
    first_row, last_row, upper = row == 0, row == SUBLANES - 1, row < SUBLANES // 2
    level = lax.broadcasted_iota(jnp.int32, (slices, LANES), 0)
    front, back = level == 0, level == slices - 1
    odd, odd_row = parity("depth") == 1, parity("rows") == 1
    front_came_first = odd == odd_row
    front_end, back_end = ends("depth")
    top_end, bottom_end = ends("rows")
    end, _, outside = first_end()

    def chunk(j, carry):
        here = pl.ds(pl.multiple_of(j * LANES, LANES), LANES)
        rows_near = rows_near_ref[:, here].astype(jnp.float32)[:slices]
        rows_far = rows_far_ref[:, here].astype(jnp.float32)
        above = jnp.where(top_end, 0.0, jnp.where(odd_row, rows_near, rows_far))
        below = jnp.where(bottom_end, 0.0, jnp.where(odd_row, rows_far, rows_near))
        first = first_ref[:, here].astype(jnp.float32)
        second = second_ref[:, here].astype(jnp.float32)
        before = jnp.where(front_end, 0.0, jnp.where(front_came_first, first, second))
        after = jnp.where(back_end, 0.0, jnp.where(front_came_first, second, first))
        last = jnp.where(outside, 0.0, second)
        extra = []
        for q, edge in enumerate((0, height - 1)):
            inner = grad_ref[q, 1, :, here]
            grad_rows = below - inner if q else inner - above
            grad_cols = grad_ref[q, 2, :, here]
            grad_depth = grad_ref[q, 0, :, here] + jnp.where(
                back, after[edge : edge + 1], jnp.where(front, -before[edge : edge + 1], 0.0)
            )
            shading = shade(
                grad_depth,
                LIGHT_ROWS * grad_rows + LIGHT_COLS * grad_cols,
                grad_rows * grad_rows + grad_cols * grad_cols,
            )
            extra.append([strip_ref[q, c, :, here] * shading for c in range(3)])
        extra = [row_sums(extra[0][c], extra[1][c]) for c in range(3)]
        for r in range(tiles):
            rows = slice(r * SUBLANES, (r + 1) * SUBLANES)
            terms = plane_terms(volume_ref, face_ref, square_ref, lit_ref, last[rows], 1 - end, rows, here)
            planes = [sums_ref[c, rows, here] + terms[c] for c in range(3)] + [base_ref[3, rows, here]]
            for c in range(3):
                if r == 0:
                    planes[c] = planes[c] + jnp.where(first_row, extra[c][0], 0.0)
                if r == tiles - 1:
                    planes[c] = planes[c] + jnp.where(last_row, extra[c][1], 0.0)
            if len(out_refs) == 1:
                for i, first in enumerate(range(0, SUBLANES, share)):
                    block = jnp.concatenate([plane[first : first + share] for plane in planes], axis=0)
                    out_refs[0][r * (SUBLANES // share) + i, :, here] = block.astype(jnp.bfloat16)
            else:
                halves = [(planes[c], pltpu.roll(planes[c + 1], SUBLANES // 2, 0)) for c in (0, 2)]
                even = jnp.concatenate([jnp.where(upper, own, turned) for own, turned in halves], axis=0)
                uneven = jnp.concatenate([jnp.where(upper, turned, own) for own, turned in halves], axis=0)
                blocks_ref, _ = out_refs
                blocks_ref[r, 0, :, here] = even
                blocks_ref[r, 1, :, here] = uneven
        return carry

    lax.fori_loop(0, columns // LANES, chunk, 0, unroll=8)
    if len(out_refs) > 1:
        blocks_ref, give_ref = out_refs
        chip, core, mask = route()
        given = (blocks_ref[chip, 1 - core], blocks_ref[chip ^ 3, core], blocks_ref[chip ^ mask ^ 3, 0], blocks_ref[chip ^ mask ^ 3, 1])
        for i, block in enumerate(given):
            give_ref[i] = block.astype(jnp.bfloat16)


def add_edges(volume, sums, interior, halos, depth_count, paired):
    _, slices, height, columns = volume.shape
    share = height // depth_count
    if paired:
        block = (4 * share, columns)
        shapes = [
            jax.ShapeDtypeStruct((depth_count // 2, 2, *block), jnp.float32),
            jax.ShapeDtypeStruct((4, *block), jnp.bfloat16),
        ]
    else:
        shapes = [jax.ShapeDtypeStruct((depth_count, 4 * share, columns), jnp.bfloat16)]
    return pl.pallas_call(
        functools.partial(edge_kernel, share),
        in_specs=[WHOLE] * 12,
        out_specs=[WHOLE] * len(shapes),
        out_shape=shapes,
        compiler_params=pltpu.CompilerParams(vmem_limit_bytes=24 * 1024 * 1024),
    )(volume, sums, *interior, *halos)


def served(depth):
    chip, core = depth // 2, depth % 2
    return 1 + (core ^ (chip & 1) ^ (chip >> 1))


def route():
    position = lax.axis_index("depth")
    return position // 2, position % 2, served(position)


def over(nearer, farther, uneven):
    share = nearer.shape[0] // 4
    clear = 1.0 - jnp.where(uneven, nearer[2 * share : 3 * share], nearer[3 * share :])
    return nearer + jnp.concatenate([clear] * 4, axis=0) * farther


def merge_kernel(blocks_ref, other_ref, own_ref, cross_ref, side_ref):
    chip, core, mask = route()
    odd = core == 1

    def merged(keep, i, uneven):
        other = other_ref[i].astype(jnp.float32)
        return over(jnp.where(odd, other, keep), jnp.where(odd, keep, other), uneven)

    own_ref[...] = merged(blocks_ref[chip, core], 0, odd)
    for i, p in enumerate((1 - core, core)):
        side_ref[i] = merged(blocks_ref[chip ^ mask, p], 2 + p, p == 1).astype(jnp.bfloat16)
    cross_ref[...] = merged(blocks_ref[chip ^ 3, 1 - core], 1, jnp.logical_not(odd)).astype(jnp.bfloat16)


def merge(blocks, other):
    rows, columns = other.shape[1:]
    return pl.pallas_call(
        merge_kernel,
        in_specs=[WHOLE] * 2,
        out_specs=[WHOLE] * 3,
        out_shape=[
            jax.ShapeDtypeStruct((rows, columns), jnp.float32),
            jax.ShapeDtypeStruct((rows, columns), jnp.bfloat16),
            jax.ShapeDtypeStruct((2, rows, columns), jnp.bfloat16),
        ],
        compiler_params=pltpu.CompilerParams(vmem_limit_bytes=8 * 1024 * 1024),
    )(blocks, other)


def pass_kernel(side_ref, out_ref):
    out_ref[...] = side_ref[1]


def pass_on(side):
    return pl.pallas_call(
        pass_kernel,
        in_specs=[WHOLE],
        out_specs=WHOLE,
        out_shape=jax.ShapeDtypeStruct(side.shape[1:], side.dtype),
        compiler_params=pltpu.CompilerParams(vmem_limit_bytes=4 * 1024 * 1024),
    )(side)


def gather_kernel(side_ref, cross_ref, passed_ref, own_ref, out_ref, plane_ref, sems):
    _, share, columns = out_ref.shape
    chip, core, mask = route()
    odd, serves_x = core == 1, mask == 1
    half = columns // 2
    copies = []
    for h in range(2):
        here = pl.ds(h * half, half)
        side, passed = side_ref[0, :, here].astype(jnp.float32), passed_ref[:, here].astype(jnp.float32)
        parts = [
            own_ref[:, here],
            jnp.where(serves_x, side, passed),
            jnp.where(serves_x, passed, side),
            cross_ref[:, here].astype(jnp.float32),
        ]
        step = 1
        while len(parts) > 1:
            swap = (chip & step) != 0
            parts = [
                over(jnp.where(swap, parts[i + 1], parts[i]), jnp.where(swap, parts[i], parts[i + 1]), odd)
                for i in range(0, len(parts), 2)
            ]
            step *= 2
        planes = [parts[0][c * share : (c + 1) * share] for c in range(4)]
        for c in range(4):
            plane_ref[c, :, here] = jnp.where(odd, planes[c ^ 1], planes[c])
        copies.append(pltpu.make_async_copy(plane_ref.at[:, :, here], out_ref.at[:, :, here], sems.at[h]))
        copies[h].start()
    for copy in copies:
        copy.wait()


def gather(parts, share):
    columns = parts[-1].shape[1]
    return pl.pallas_call(
        gather_kernel,
        in_specs=[WHOLE] * len(parts),
        out_specs=pl.BlockSpec(memory_space=pl.ANY),
        out_shape=jax.ShapeDtypeStruct((4, share, columns), jnp.float32),
        scratch_shapes=[pltpu.VMEM((4, share, columns), jnp.float32), pltpu.SemaphoreType.DMA((2,))],
        compiler_params=pltpu.CompilerParams(vmem_limit_bytes=4 * 1024 * 1024),
    )(*parts)


def finish_kernel(parts_ref, out_ref):
    count = parts_ref.shape[0]
    _, share, columns = out_ref.shape
    remaining = jnp.ones((share, columns), jnp.float32)
    sums = [jnp.zeros((share, columns), jnp.float32) for _ in range(3)]
    for k in range(count):
        part = parts_ref[k].astype(jnp.float32)
        for c in range(3):
            sums[c] = sums[c] + remaining * part[c * share : (c + 1) * share]
        remaining = remaining - remaining * part[3 * share :]
    for c in range(3):
        out_ref[c] = sums[c]
    out_ref[3] = 1.0 - remaining


def finish(parts, share):
    columns = parts.shape[2]
    return pl.pallas_call(
        finish_kernel,
        in_specs=[WHOLE],
        out_specs=WHOLE,
        out_shape=jax.ShapeDtypeStruct((4, share, columns), jnp.float32),
        compiler_params=pltpu.CompilerParams(vmem_limit_bytes=4 * 1024 * 1024),
    )(parts)


def swapped(values, kinds):
    depth_count, row_count = lax.axis_size("depth"), lax.axis_size("rows")
    perm = []
    for d in range(depth_count):
        for r in range(row_count):
            kind = kinds[r % 2]
            e, q = d, r
            if kind == "near slab":
                e = d ^ 1
            elif kind == "far slab":
                e = d + 1 if d % 2 else d - 1
                e = depth_count - 1 - d if not 0 <= e < depth_count else e
            else:
                q = r ^ 1 if kind == "near row" else (r + 1 if r % 2 else r - 1)
                if not 0 <= q < row_count:
                    e, q = d ^ 1, r
            perm.append((d * row_count + r, e * row_count + q))
    return lax.ppermute(values, ("depth", "rows"), perm)


def exchanged(values, mask):
    masks = [mask(d) if callable(mask) else mask for d in range(lax.axis_size("depth"))]
    return lax.ppermute(values, "depth", [(d, d ^ m) for d, m in enumerate(masks)])


def body(volume, color_map, alpha_map):
    depth_count = lax.axis_size("depth")
    share = volume.shape[2] // depth_count
    first, rows_near, second, rows_far = cut_edges(volume)
    first = swapped(first, ("far slab", "near slab"))
    rows_near = swapped(rows_near, ("near row", "near row"))
    second = swapped(second, ("near slab", "far slab"))
    rows_far = swapped(rows_far, ("far row", "far row"))
    interior = march_interior(volume, color_map, alpha_map, depth_count)
    halos = (first, rows_near, second, rows_far)
    paired = depth_count == 8 and 2 * share == SUBLANES
    sums = add_first_plane(volume, *interior[:4], first)
    outs = add_edges(volume, sums, interior, halos, depth_count, paired)
    if not paired:
        return finish(lax.all_to_all(outs[0], "depth", 0, 0, tiled=True), share)
    blocks, give = outs
    own, cross, side = merge(blocks, exchanged(give, 1))
    side = exchanged(side, lambda d: 2 * served(d) + 1)
    cross = exchanged(cross, 7)
    return gather((side, cross, exchanged(pass_on(side), 1), own), share)


def solution(mesh):
    in_specs = (P(None, "depth", "rows", None), P(), P())
    out_specs = P(None, ("rows", "depth"), None)
    return jax.shard_map(body, mesh=mesh, in_specs=in_specs, out_specs=out_specs, check_vma=False)
```

```python
import functools

import jax
import jax.numpy as jnp
from jax import lax
from jax.experimental import pallas as pl
from jax.experimental.pallas import tpu as pltpu
from jax.sharding import PartitionSpec as P

AMBIENT = 0.3
DIFFUSE = 0.7
LIGHT_DEPTH = 0.48 * DIFFUSE
LIGHT_ROWS = 0.6 * DIFFUSE
LIGHT_COLS = 0.64 * DIFFUSE
OPACITY = 4.0
LANES = 128
SUBLANES = 8
WHOLE = pl.BlockSpec(memory_space=pltpu.VMEM)


def parity(axis):
    return lax.axis_index(axis) % 2


def ends(axis):
    position = lax.axis_index(axis)
    return position == 0, position == lax.axis_size(axis) - 1


def edges_kernel(volume_ref, first_out, rows_near_out, second_out, rows_far_out, strip_ref, plane_ref, sems):
    _, slices, height, columns = volume_ref.shape
    odd, odd_row = parity("depth"), parity("rows")
    far_first = 1 - odd_row
    last_first = odd ^ far_first ^ 1
    tiles = height // SUBLANES

    def plane_copies(i, s):
        for t in range(tiles):
            rows = pl.ds(t * SUBLANES, SUBLANES)
            yield pltpu.make_async_copy(volume_ref.at[0, s, rows], plane_ref.at[i, rows], sems.at[i, t])

    def strip_copy(i, row):
        return pltpu.make_async_copy(volume_ref.at[0, :, row], strip_ref.at[i], sems.at[2, i])

    copies = [
        list(plane_copies(0, last_first * (slices - 1))),
        [strip_copy(0, (1 - odd_row) * (height - 1))],
        list(plane_copies(1, (1 - last_first) * (slices - 1))),
        [strip_copy(1, odd_row * (height - 1))],
    ]
    for group in copies:
        for copy in group:
            copy.start()

    def arrive(group):
        for copy in group:
            copy.wait()

    def narrow(values):
        return values.astype(jnp.float32).astype(jnp.bfloat16)

    def padded(strip):
        return narrow(jnp.concatenate([strip, jnp.zeros((height - slices, columns), jnp.int32)], axis=0))

    arrive(copies[0])
    first_out[...] = narrow(plane_ref[0])
    arrive(copies[1])
    rows_near_out[...] = padded(strip_ref[0])
    arrive(copies[2])
    second_out[...] = narrow(plane_ref[1])
    arrive(copies[3])
    rows_far_out[...] = narrow(strip_ref[1])


def cut_edges(volume):
    _, slices, height, columns = volume.shape
    plane = jax.ShapeDtypeStruct((height, columns), jnp.bfloat16)
    strip = jax.ShapeDtypeStruct((slices, columns), jnp.bfloat16)
    return pl.pallas_call(
        edges_kernel,
        in_specs=[pl.BlockSpec(memory_space=pl.ANY)],
        out_specs=[WHOLE] * 4,
        out_shape=[plane, plane, plane, strip],
        scratch_shapes=[
            pltpu.VMEM((2, slices, columns), jnp.int32),
            pltpu.VMEM((2, height, columns), jnp.int32),
            pltpu.SemaphoreType.DMA((3, max(2, height // SUBLANES))),
        ],
        compiler_params=pltpu.CompilerParams(vmem_limit_bytes=52 * 1024 * 1024),
    )(volume)


def pick(entries, places):
    dims = lax.GatherDimensionNumbers(
        offset_dims=(),
        collapsed_slice_dims=(1,),
        start_index_map=(1,),
        operand_batching_dims=(0,),
        start_indices_batching_dims=(0,),
    )
    return lax.gather(entries, places[..., None], dims, (1, 1), mode=lax.GatherScatterMode.PROMISE_IN_BOUNDS)


def shade(grad_depth, facing, squares):
    facing = facing + LIGHT_DEPTH * grad_depth
    squares = squares + grad_depth * grad_depth
    return AMBIENT + jnp.abs(facing) * lax.rsqrt(jnp.maximum(squares, 4.0))


def interior_kernel(
    opacity_scale,
    volume_ref,
    color_ref,
    alpha_ref,
    base_ref,
    face_ref,
    square_ref,
    lit_ref,
    grad_ref,
    strip_ref,
    pair_ref,
    held_ref,
):
    _, slices, height, columns = volume_ref.shape
    tiles = height // SUBLANES
    chunks = columns // LANES
    tile = (SUBLANES, LANES)
    strip = (slices, LANES)

    packed = color_ref[0:1, :] + color_ref[1:2, :] * 256 + color_ref[2:3, :] * 65536
    color_low, color_high = packed[:, :LANES], packed[:, LANES:]
    alpha_both = alpha_ref[0:1, :LANES] + alpha_ref[0:1, LANES:] * 256

    def colors(value, tables):
        low, high = tables
        place = value & (LANES - 1)
        color = jnp.where(value < LANES, pick(low, place), pick(high, place))
        parts = (color & 255, lax.shift_right_logical(color, 8) & 255, lax.shift_right_logical(color, 16))
        return [part.astype(jnp.float32) for part in parts]

    def opacity(level, table):
        entry = pick(table, level & (LANES - 1))
        entry = lax.shift_right_logical(entry, lax.shift_right_logical(level & LANES, 4)) & 255
        return entry.astype(jnp.float32) * opacity_scale

    tile_colors = [jnp.broadcast_to(t, tile) for t in (color_low, color_high)]
    tile_alpha = jnp.broadcast_to(alpha_both, tile)
    strip_colors = [jnp.broadcast_to(t, strip) for t in (color_low, color_high)]

    def masks(shape):
        lane = lax.broadcasted_iota(jnp.int32, shape, 1)
        row = lax.broadcasted_iota(jnp.int32, shape, 0)
        return lane == 0, lane == LANES - 1, row == 0, row == shape[0] - 1

    first_lane, last_lane, first_row, last_row = masks(tile)
    strip_first_lane, strip_last_lane, front, back = masks(strip)

    pairs = slices // 2
    top = SUBLANES

    def clear(j, carry):
        pair_ref[j] = jnp.zeros(pair_ref.shape[1:], jnp.int32)
        return carry

    clear(0, 0)
    clear(chunks + 1, 0)
    margin = jnp.zeros((pairs, SUBLANES, LANES), jnp.int32)

    def pack(j, carry):
        here = pl.ds(pl.multiple_of(j * LANES, LANES), LANES)
        pair_ref[j + 1, :, :top] = margin
        pair_ref[j + 1, :, top + height :] = margin
        for p in range(pairs):
            pair_ref[j + 1, p, top : top + height] = volume_ref[0, p, :, here] + lax.shift_left(
                volume_ref[0, p + pairs, :, here], 16
            )
        return carry

    lax.fori_loop(0, chunks, pack, 0)

    def split(difference):
        low = lax.shift_right_arithmetic(lax.shift_left(difference, 16), 16)
        high = lax.shift_right_arithmetic(difference + 32768, 16)
        return low.astype(jnp.float32), high.astype(jnp.float32)

    def across(left_value, value, right_value, first, last):
        west = pltpu.roll(jnp.where(last, left_value, value), 1, 1)
        east = pltpu.roll(jnp.where(first, right_value, value), LANES - 1, 1)
        return split(east - west)

    def chunk(j, carry):
        here = pl.ds(pl.multiple_of(j * LANES, LANES), LANES)

        for r in range(tiles):
            rows = slice(r * SUBLANES, (r + 1) * SUBLANES)
            values = [volume_ref[0, s, rows, here] for s in range(slices)]

            def words(c, p, offset=0):
                return pair_ref[c, p, top + r * SUBLANES + offset : top + (r + 1) * SUBLANES + offset, :]

            down, right = [], []
            for p in range(pairs):
                down.append(split(words(j + 1, p, 1) - words(j + 1, p, -1)))
                right.append(across(words(j, p), words(j + 1, p), words(j + 2, p), first_lane, last_lane))
            remaining = jnp.ones(tile, jnp.float32)
            sums = [jnp.zeros(tile, jnp.float32) for _ in range(3)]
            for s in range(slices):
                value = values[s]
                grad_rows = down[s % pairs][s // pairs]
                grad_cols = right[s % pairs][s // pairs]
                squares = grad_rows * grad_rows + grad_cols * grad_cols
                facing = LIGHT_ROWS * grad_rows + LIGHT_COLS * grad_cols
                weight = remaining * opacity(volume_ref[1, s, rows, here], tile_alpha)
                remaining = remaining - weight
                if r == 0:
                    held_ref[0, s : s + 1, :] = weight[:1]
                    weight = jnp.where(first_row, 0.0, weight)
                if r == tiles - 1:
                    held_ref[1, s : s + 1, :] = weight[SUBLANES - 1 :]
                    weight = jnp.where(last_row, 0.0, weight)
                emitted = colors(value, tile_colors)
                if 0 < s < slices - 1:
                    grad_depth = (values[s + 1] - values[s - 1]).astype(jnp.float32)
                    weight = weight * shade(grad_depth, facing, squares)
                    for c in range(3):
                        sums[c] = sums[c] + emitted[c] * weight
                else:
                    end = int(s > 0)
                    face_ref[end, rows, here] = facing
                    square_ref[end, rows, here] = squares
                    weight = weight * (1.0 / 255.0)
                    for c in range(3):
                        lit_ref[end, c, rows, here] = emitted[c] * weight
            for c in range(3):
                base_ref[c, rows, here] = sums[c] * (1.0 / 255.0)
            base_ref[3, rows, here] = 1.0 - remaining

        for q, (edge, inner) in enumerate(((0, 1), (height - 1, height - 2))):
            value = volume_ref[0, :, edge, here]
            behind = pltpu.roll(jnp.where(back, 0, value), 1, 0)
            ahead = pltpu.roll(jnp.where(front, 0, value), slices - 1, 0)
            grad_ref[q, 0, :, here] = (ahead - behind).astype(jnp.float32)
            grad_ref[q, 1, :, here] = volume_ref[0, :, inner, here].astype(jnp.float32)
            word = pair_ref[j + 1, :, top + edge, :]
            low, high = across(
                pair_ref[j, :, top + edge, :],
                word,
                pair_ref[j + 2, :, top + edge, :],
                strip_first_lane[:pairs],
                strip_last_lane[:pairs],
            )
            grad_ref[q, 2, :pairs, here] = low
            grad_ref[q, 2, pairs:, here] = high
            weight = held_ref[q] * (1.0 / 255.0)
            emitted = colors(value, strip_colors)
            for c in range(3):
                strip_ref[q, c, :, here] = emitted[c] * weight
        return carry

    lax.fori_loop(0, chunks, chunk, 0, unroll=4)


def march_interior(volume, color_map, alpha_map, depth_count):
    _, slices, height, columns = volume.shape
    opacity_scale = OPACITY / (255.0 * slices * depth_count)
    shapes = [
        (4, height, columns),
        (2, height, columns),
        (2, height, columns),
        (2, 3, height, columns),
        (2, 3, slices, columns),
        (2, 3, slices, columns),
    ]
    voxels = slices * height * columns
    return pl.pallas_call(
        functools.partial(interior_kernel, opacity_scale),
        in_specs=[WHOLE] * 3,
        out_specs=[WHOLE] * len(shapes),
        out_shape=[jax.ShapeDtypeStruct(shape, jnp.float32) for shape in shapes],
        scratch_shapes=[
            pltpu.VMEM((columns // LANES + 2, slices // 2, height + 2 * SUBLANES, LANES), jnp.int32),
            pltpu.VMEM((2, slices, LANES), jnp.float32),
        ],
        compiler_params=pltpu.CompilerParams(vmem_limit_bytes=24 * 1024 * 1024),
        cost_estimate=pl.CostEstimate(flops=voxels * 80, bytes_accessed=voxels * 20, transcendentals=voxels),
    )(volume, color_map, alpha_map.reshape(1, -1))


def row_sums(first, second):
    count = first.shape[0]
    if count != SUBLANES:
        return jnp.sum(first, axis=0, keepdims=True), jnp.sum(second, axis=0, keepdims=True)
    upper = lax.broadcasted_iota(jnp.int32, first.shape, 0) < 4
    both = jnp.where(upper, first, second) + pltpu.roll(jnp.where(upper, second, first), 4, 0)
    both = both + pltpu.roll(both, 6, 0)
    both = both + pltpu.roll(both, 7, 0)
    return both, pltpu.roll(both, 3, 0)


def plane_terms(volume_ref, face_ref, square_ref, lit_ref, halo, end, rows, here):
    slices = volume_ref.shape[1]
    inner = volume_ref[0, jnp.where(end == 1, slices - 2, 1), rows, here].astype(jnp.float32)
    grad_depth = jnp.where(end == 1, halo - inner, inner - halo)
    shading = shade(grad_depth, face_ref[end, rows, here], square_ref[end, rows, here])
    return [lit_ref[end, c, rows, here] * shading for c in range(3)]


def first_end():
    front_end, back_end = ends("depth")
    end = jnp.where(parity("depth") == parity("rows"), 0, 1)
    return end, jnp.where(end == 1, back_end, front_end), jnp.where(end == 1, front_end, back_end)


def first_plane_kernel(volume_ref, base_ref, face_ref, square_ref, lit_ref, first_ref, sums_ref):
    _, height, columns = base_ref.shape
    end, outside, _ = first_end()

    def chunk(j, carry):
        here = pl.ds(pl.multiple_of(j * LANES, LANES), LANES)
        first = jnp.where(outside, 0.0, first_ref[:, here].astype(jnp.float32))
        for r in range(height // SUBLANES):
            rows = slice(r * SUBLANES, (r + 1) * SUBLANES)
            terms = plane_terms(volume_ref, face_ref, square_ref, lit_ref, first[rows], end, rows, here)
            for c in range(3):
                sums_ref[c, rows, here] = base_ref[c, rows, here] + terms[c]
        return carry

    lax.fori_loop(0, columns // LANES, chunk, 0, unroll=4)


def add_first_plane(volume, base, face, square, lit, first):
    return pl.pallas_call(
        first_plane_kernel,
        in_specs=[WHOLE] * 6,
        out_specs=WHOLE,
        out_shape=jax.ShapeDtypeStruct((3, *base.shape[1:]), jnp.float32),
        compiler_params=pltpu.CompilerParams(vmem_limit_bytes=8 * 1024 * 1024),
        cost_estimate=pl.CostEstimate(flops=base.size * 20, bytes_accessed=base.size * 12, transcendentals=base.size // 4),
    )(volume, base, face, square, lit, first)


def edge_kernel(
    share, volume_ref, sums_ref, base_ref, face_ref, square_ref, lit_ref, grad_ref, strip_ref, first_ref, rows_near_ref, second_ref, rows_far_ref, *out_refs
):
    _, slices, height, columns = volume_ref.shape
    tiles = height // SUBLANES
    tile = (SUBLANES, LANES)
    row = lax.broadcasted_iota(jnp.int32, tile, 0)
    first_row, last_row, upper = row == 0, row == SUBLANES - 1, row < SUBLANES // 2
    level = lax.broadcasted_iota(jnp.int32, (slices, LANES), 0)
    front, back = level == 0, level == slices - 1
    odd, odd_row = parity("depth") == 1, parity("rows") == 1
    front_came_first = odd == odd_row
    front_end, back_end = ends("depth")
    top_end, bottom_end = ends("rows")
    end, _, outside = first_end()

    def chunk(j, carry):
        here = pl.ds(pl.multiple_of(j * LANES, LANES), LANES)
        rows_near = rows_near_ref[:, here].astype(jnp.float32)[:slices]
        rows_far = rows_far_ref[:, here].astype(jnp.float32)
        above = jnp.where(top_end, 0.0, jnp.where(odd_row, rows_near, rows_far))
        below = jnp.where(bottom_end, 0.0, jnp.where(odd_row, rows_far, rows_near))
        first = first_ref[:, here].astype(jnp.float32)
        second = second_ref[:, here].astype(jnp.float32)
        before = jnp.where(front_end, 0.0, jnp.where(front_came_first, first, second))
        after = jnp.where(back_end, 0.0, jnp.where(front_came_first, second, first))
        last = jnp.where(outside, 0.0, second)
        extra = []
        for q, edge in enumerate((0, height - 1)):
            inner = grad_ref[q, 1, :, here]
            grad_rows = below - inner if q else inner - above
            grad_cols = grad_ref[q, 2, :, here]
            grad_depth = grad_ref[q, 0, :, here] + jnp.where(
                back, after[edge : edge + 1], jnp.where(front, -before[edge : edge + 1], 0.0)
            )
            shading = shade(
                grad_depth,
                LIGHT_ROWS * grad_rows + LIGHT_COLS * grad_cols,
                grad_rows * grad_rows + grad_cols * grad_cols,
            )
            extra.append([strip_ref[q, c, :, here] * shading for c in range(3)])
        extra = [row_sums(extra[0][c], extra[1][c]) for c in range(3)]
        for r in range(tiles):
            rows = slice(r * SUBLANES, (r + 1) * SUBLANES)
            terms = plane_terms(volume_ref, face_ref, square_ref, lit_ref, last[rows], 1 - end, rows, here)
            planes = [sums_ref[c, rows, here] + terms[c] for c in range(3)] + [base_ref[3, rows, here]]
            for c in range(3):
                if r == 0:
                    planes[c] = planes[c] + jnp.where(first_row, extra[c][0], 0.0)
                if r == tiles - 1:
                    planes[c] = planes[c] + jnp.where(last_row, extra[c][1], 0.0)
            if len(out_refs) == 1:
                for i, first in enumerate(range(0, SUBLANES, share)):
                    block = jnp.concatenate([plane[first : first + share] for plane in planes], axis=0)
                    out_refs[0][r * (SUBLANES // share) + i, :, here] = block.astype(jnp.bfloat16)
            else:
                halves = [(planes[c], pltpu.roll(planes[c + 1], SUBLANES // 2, 0)) for c in (0, 2)]
                even = jnp.concatenate([jnp.where(upper, own, turned) for own, turned in halves], axis=0)
                uneven = jnp.concatenate([jnp.where(upper, turned, own) for own, turned in halves], axis=0)
                blocks_ref, _ = out_refs
                blocks_ref[r, 0, :, here] = even
                blocks_ref[r, 1, :, here] = uneven
        return carry

    lax.fori_loop(0, columns // LANES, chunk, 0, unroll=8)
    if len(out_refs) > 1:
        blocks_ref, give_ref = out_refs
        chip, core, mask = route()
        given = (blocks_ref[chip, 1 - core], blocks_ref[chip ^ 3, core], blocks_ref[chip ^ mask ^ 3, 0], blocks_ref[chip ^ mask ^ 3, 1])
        for i, block in enumerate(given):
            give_ref[i] = block.astype(jnp.bfloat16)


def add_edges(volume, sums, interior, halos, depth_count, paired):
    _, slices, height, columns = volume.shape
    share = height // depth_count
    if paired:
        block = (4 * share, columns)
        shapes = [
            jax.ShapeDtypeStruct((depth_count // 2, 2, *block), jnp.float32),
            jax.ShapeDtypeStruct((4, *block), jnp.bfloat16),
        ]
    else:
        shapes = [jax.ShapeDtypeStruct((depth_count, 4 * share, columns), jnp.bfloat16)]
    return pl.pallas_call(
        functools.partial(edge_kernel, share),
        in_specs=[WHOLE] * 12,
        out_specs=[WHOLE] * len(shapes),
        out_shape=shapes,
        compiler_params=pltpu.CompilerParams(vmem_limit_bytes=24 * 1024 * 1024),
    )(volume, sums, *interior, *halos)


def served(depth):
    chip, core = depth // 2, depth % 2
    return 2 - (core ^ (chip & 1) ^ (chip >> 1))


def route():
    position = lax.axis_index("depth")
    return position // 2, position % 2, served(position)


def over(nearer, farther, uneven):
    share = nearer.shape[0] // 4
    clear = 1.0 - jnp.where(uneven, nearer[2 * share : 3 * share], nearer[3 * share :])
    return nearer + jnp.concatenate([clear] * 4, axis=0) * farther


def merge_kernel(blocks_ref, other_ref, own_ref, cross_ref, side_ref):
    chip, core, mask = route()
    odd = core == 1

    def merged(keep, i, uneven):
        other = other_ref[i].astype(jnp.float32)
        return over(jnp.where(odd, other, keep), jnp.where(odd, keep, other), uneven)

    own_ref[...] = merged(blocks_ref[chip, core], 0, odd)
    for i, p in enumerate((1 - core, core)):
        side_ref[i] = merged(blocks_ref[chip ^ mask, p], 2 + p, p == 1).astype(jnp.bfloat16)
    cross_ref[...] = merged(blocks_ref[chip ^ 3, 1 - core], 1, jnp.logical_not(odd)).astype(jnp.bfloat16)


def merge(blocks, other):
    rows, columns = other.shape[1:]
    return pl.pallas_call(
        merge_kernel,
        in_specs=[WHOLE] * 2,
        out_specs=[WHOLE] * 3,
        out_shape=[
            jax.ShapeDtypeStruct((rows, columns), jnp.float32),
            jax.ShapeDtypeStruct((rows, columns), jnp.bfloat16),
            jax.ShapeDtypeStruct((2, rows, columns), jnp.bfloat16),
        ],
        compiler_params=pltpu.CompilerParams(vmem_limit_bytes=8 * 1024 * 1024),
    )(blocks, other)


def pass_kernel(side_ref, out_ref):
    out_ref[...] = side_ref[1]


def pass_on(side):
    return pl.pallas_call(
        pass_kernel,
        in_specs=[WHOLE],
        out_specs=WHOLE,
        out_shape=jax.ShapeDtypeStruct(side.shape[1:], side.dtype),
        compiler_params=pltpu.CompilerParams(vmem_limit_bytes=4 * 1024 * 1024),
    )(side)


def gather_kernel(side_ref, cross_ref, passed_ref, own_ref, out_ref):
    share = out_ref.shape[1]
    chip, core, mask = route()
    odd, serves_x = core == 1, mask == 1
    side, passed = side_ref[0].astype(jnp.float32), passed_ref[...].astype(jnp.float32)
    parts = [
        own_ref[...],
        jnp.where(serves_x, side, passed),
        jnp.where(serves_x, passed, side),
        cross_ref[...].astype(jnp.float32),
    ]
    step = 1
    while len(parts) > 1:
        swap = (chip & step) != 0
        parts = [
            over(jnp.where(swap, parts[i + 1], parts[i]), jnp.where(swap, parts[i], parts[i + 1]), odd)
            for i in range(0, len(parts), 2)
        ]
        step *= 2
    planes = [parts[0][c * share : (c + 1) * share] for c in range(4)]
    for c in range(4):
        out_ref[c] = jnp.where(odd, planes[c ^ 1], planes[c])


def gather(parts, share):
    columns = parts[-1].shape[1]
    return pl.pallas_call(
        gather_kernel,
        in_specs=[WHOLE] * len(parts),
        out_specs=WHOLE,
        out_shape=jax.ShapeDtypeStruct((4, share, columns), jnp.float32),
        compiler_params=pltpu.CompilerParams(vmem_limit_bytes=4 * 1024 * 1024),
    )(*parts)


def finish_kernel(parts_ref, out_ref):
    count = parts_ref.shape[0]
    _, share, columns = out_ref.shape
    remaining = jnp.ones((share, columns), jnp.float32)
    sums = [jnp.zeros((share, columns), jnp.float32) for _ in range(3)]
    for k in range(count):
        part = parts_ref[k].astype(jnp.float32)
        for c in range(3):
            sums[c] = sums[c] + remaining * part[c * share : (c + 1) * share]
        remaining = remaining - remaining * part[3 * share :]
    for c in range(3):
        out_ref[c] = sums[c]
    out_ref[3] = 1.0 - remaining


def finish(parts, share):
    columns = parts.shape[2]
    return pl.pallas_call(
        finish_kernel,
        in_specs=[WHOLE],
        out_specs=WHOLE,
        out_shape=jax.ShapeDtypeStruct((4, share, columns), jnp.float32),
        compiler_params=pltpu.CompilerParams(vmem_limit_bytes=4 * 1024 * 1024),
    )(parts)


def swapped(values, kinds):
    depth_count, row_count = lax.axis_size("depth"), lax.axis_size("rows")
    perm = []
    for d in range(depth_count):
        for r in range(row_count):
            kind = kinds[r % 2]
            e, q = d, r
            if kind == "near slab":
                e = d ^ 1
            elif kind == "far slab":
                e = d + 1 if d % 2 else d - 1
                e = depth_count - 1 - d if not 0 <= e < depth_count else e
            else:
                q = r ^ 1 if kind == "near row" else (r + 1 if r % 2 else r - 1)
                if not 0 <= q < row_count:
                    e, q = d ^ 1, r
            perm.append((d * row_count + r, e * row_count + q))
    return lax.ppermute(values, ("depth", "rows"), perm)


def exchanged(values, mask):
    masks = [mask(d) if callable(mask) else mask for d in range(lax.axis_size("depth"))]
    return lax.ppermute(values, "depth", [(d, d ^ m) for d, m in enumerate(masks)])


def body(volume, color_map, alpha_map):
    depth_count = lax.axis_size("depth")
    share = volume.shape[2] // depth_count
    first, rows_near, second, rows_far = cut_edges(volume)
    first = swapped(first, ("far slab", "near slab"))
    rows_near = swapped(rows_near, ("near row", "near row"))
    second = swapped(second, ("near slab", "far slab"))
    rows_far = swapped(rows_far, ("far row", "far row"))
    interior = march_interior(volume, color_map, alpha_map, depth_count)
    halos = (first, rows_near, second, rows_far)
    paired = depth_count == 8 and 2 * share == SUBLANES
    sums = add_first_plane(volume, *interior[:4], first)
    outs = add_edges(volume, sums, interior, halos, depth_count, paired)
    if not paired:
        return finish(lax.all_to_all(outs[0], "depth", 0, 0, tiled=True), share)
    blocks, give = outs
    own, cross, side = merge(blocks, exchanged(give, 1))
    side = exchanged(side, lambda d: 2 * served(d) + 1)
    cross = exchanged(cross, 7)
    return gather((side, cross, exchanged(pass_on(side), 1), own), share)


def solution(mesh):
    in_specs = (P(None, "depth", "rows", None), P(), P())
    out_specs = P(None, ("rows", "depth"), None)
    return jax.shard_map(body, mesh=mesh, in_specs=in_specs, out_specs=out_specs, check_vma=False)
```

```python
import functools

import jax
import jax.numpy as jnp
from jax import lax
from jax.experimental import pallas as pl
from jax.experimental.pallas import tpu as pltpu
from jax.sharding import PartitionSpec as P

AMBIENT = 0.3
DIFFUSE = 0.7
LIGHT_DEPTH = 0.48 * DIFFUSE
LIGHT_ROWS = 0.6 * DIFFUSE
LIGHT_COLS = 0.64 * DIFFUSE
OPACITY = 4.0
LANES = 128
SUBLANES = 8
WHOLE = pl.BlockSpec(memory_space=pltpu.VMEM)


def parity(axis):
    return lax.axis_index(axis) % 2


def ends(axis):
    position = lax.axis_index(axis)
    return position == 0, position == lax.axis_size(axis) - 1


def edges_kernel(volume_ref, first_out, rows_near_out, second_out, rows_far_out, strip_ref, plane_ref, sems):
    _, slices, height, columns = volume_ref.shape
    odd, odd_row = parity("depth"), parity("rows")
    far_first = 1 - odd_row
    last_first = odd ^ far_first ^ 1
    tiles = height // SUBLANES

    def plane_copies(i, s):
        for t in range(tiles):
            rows = pl.ds(t * SUBLANES, SUBLANES)
            yield pltpu.make_async_copy(volume_ref.at[0, s, rows], plane_ref.at[i, rows], sems.at[i, t])

    def strip_copy(i, row):
        return pltpu.make_async_copy(volume_ref.at[0, :, row], strip_ref.at[i], sems.at[2, i])

    copies = [
        list(plane_copies(0, last_first * (slices - 1))),
        [strip_copy(0, (1 - odd_row) * (height - 1))],
        list(plane_copies(1, (1 - last_first) * (slices - 1))),
        [strip_copy(1, odd_row * (height - 1))],
    ]
    for group in copies:
        for copy in group:
            copy.start()

    def arrive(group):
        for copy in group:
            copy.wait()

    def narrow(values):
        return values.astype(jnp.float32).astype(jnp.bfloat16)

    def padded(strip):
        return narrow(jnp.concatenate([strip, jnp.zeros((height - slices, columns), jnp.int32)], axis=0))

    arrive(copies[0])
    first_out[...] = narrow(plane_ref[0])
    arrive(copies[1])
    rows_near_out[...] = padded(strip_ref[0])
    arrive(copies[2])
    second_out[...] = narrow(plane_ref[1])
    arrive(copies[3])
    rows_far_out[...] = narrow(strip_ref[1])


def cut_edges(volume):
    _, slices, height, columns = volume.shape
    plane = jax.ShapeDtypeStruct((height, columns), jnp.bfloat16)
    strip = jax.ShapeDtypeStruct((slices, columns), jnp.bfloat16)
    return pl.pallas_call(
        edges_kernel,
        in_specs=[pl.BlockSpec(memory_space=pl.ANY)],
        out_specs=[WHOLE] * 4,
        out_shape=[plane, plane, plane, strip],
        scratch_shapes=[
            pltpu.VMEM((2, slices, columns), jnp.int32),
            pltpu.VMEM((2, height, columns), jnp.int32),
            pltpu.SemaphoreType.DMA((3, max(2, height // SUBLANES))),
        ],
        compiler_params=pltpu.CompilerParams(vmem_limit_bytes=52 * 1024 * 1024),
    )(volume)


def pick(entries, places):
    dims = lax.GatherDimensionNumbers(
        offset_dims=(),
        collapsed_slice_dims=(1,),
        start_index_map=(1,),
        operand_batching_dims=(0,),
        start_indices_batching_dims=(0,),
    )
    return lax.gather(entries, places[..., None], dims, (1, 1), mode=lax.GatherScatterMode.PROMISE_IN_BOUNDS)


def shade(grad_depth, facing, squares):
    facing = facing + LIGHT_DEPTH * grad_depth
    squares = squares + grad_depth * grad_depth
    return AMBIENT + jnp.abs(facing) * lax.rsqrt(jnp.maximum(squares, 4.0))


def interior_kernel(
    opacity_scale,
    volume_ref,
    color_ref,
    alpha_ref,
    base_ref,
    face_ref,
    square_ref,
    lit_ref,
    grad_ref,
    strip_ref,
    pair_ref,
    held_ref,
):
    _, slices, height, columns = volume_ref.shape
    tiles = height // SUBLANES
    chunks = columns // LANES
    tile = (SUBLANES, LANES)
    strip = (slices, LANES)

    packed = color_ref[0:1, :] + color_ref[1:2, :] * 256 + color_ref[2:3, :] * 65536
    color_low, color_high = packed[:, :LANES], packed[:, LANES:]
    alpha_both = alpha_ref[0:1, :LANES] + alpha_ref[0:1, LANES:] * 256

    def colors(value, tables):
        low, high = tables
        place = value & (LANES - 1)
        color = jnp.where(value < LANES, pick(low, place), pick(high, place))
        parts = (color & 255, lax.shift_right_logical(color, 8) & 255, lax.shift_right_logical(color, 16))
        return [part.astype(jnp.float32) for part in parts]

    def opacity(level, table):
        entry = pick(table, level & (LANES - 1))
        entry = lax.shift_right_logical(entry, lax.shift_right_logical(level & LANES, 4)) & 255
        return entry.astype(jnp.float32) * opacity_scale

    tile_colors = [jnp.broadcast_to(t, tile) for t in (color_low, color_high)]
    tile_alpha = jnp.broadcast_to(alpha_both, tile)
    strip_colors = [jnp.broadcast_to(t, strip) for t in (color_low, color_high)]

    def masks(shape):
        lane = lax.broadcasted_iota(jnp.int32, shape, 1)
        row = lax.broadcasted_iota(jnp.int32, shape, 0)
        return lane == 0, lane == LANES - 1, row == 0, row == shape[0] - 1

    first_lane, last_lane, first_row, last_row = masks(tile)
    strip_first_lane, strip_last_lane, front, back = masks(strip)

    pairs = slices // 2
    top = SUBLANES

    def clear(j, carry):
        pair_ref[j] = jnp.zeros(pair_ref.shape[1:], jnp.int32)
        return carry

    clear(0, 0)
    clear(chunks + 1, 0)
    margin = jnp.zeros((pairs, SUBLANES, LANES), jnp.int32)

    def pack(j, carry):
        here = pl.ds(pl.multiple_of(j * LANES, LANES), LANES)
        pair_ref[j + 1, :, :top] = margin
        pair_ref[j + 1, :, top + height :] = margin
        for p in range(pairs):
            pair_ref[j + 1, p, top : top + height] = volume_ref[0, p, :, here] + lax.shift_left(
                volume_ref[0, p + pairs, :, here], 16
            )
        return carry

    lax.fori_loop(0, chunks, pack, 0)

    def split(difference):
        low = lax.shift_right_arithmetic(lax.shift_left(difference, 16), 16)
        high = lax.shift_right_arithmetic(difference + 32768, 16)
        return low.astype(jnp.float32), high.astype(jnp.float32)

    def across(left_value, value, right_value, first, last):
        west = pltpu.roll(jnp.where(last, left_value, value), 1, 1)
        east = pltpu.roll(jnp.where(first, right_value, value), LANES - 1, 1)
        return split(east - west)

    def chunk(j, carry):
        here = pl.ds(pl.multiple_of(j * LANES, LANES), LANES)

        for r in range(tiles):
            rows = slice(r * SUBLANES, (r + 1) * SUBLANES)
            values = [volume_ref[0, s, rows, here] for s in range(slices)]

            def words(c, p, offset=0):
                return pair_ref[c, p, top + r * SUBLANES + offset : top + (r + 1) * SUBLANES + offset, :]

            down, right = [], []
            for p in range(pairs):
                down.append(split(words(j + 1, p, 1) - words(j + 1, p, -1)))
                right.append(across(words(j, p), words(j + 1, p), words(j + 2, p), first_lane, last_lane))
            remaining = jnp.ones(tile, jnp.float32)
            sums = [jnp.zeros(tile, jnp.float32) for _ in range(3)]
            for s in range(slices):
                value = values[s]
                grad_rows = down[s % pairs][s // pairs]
                grad_cols = right[s % pairs][s // pairs]
                squares = grad_rows * grad_rows + grad_cols * grad_cols
                facing = LIGHT_ROWS * grad_rows + LIGHT_COLS * grad_cols
                weight = remaining * opacity(volume_ref[1, s, rows, here], tile_alpha)
                remaining = remaining - weight
                if r == 0:
                    held_ref[0, s : s + 1, :] = weight[:1]
                    weight = jnp.where(first_row, 0.0, weight)
                if r == tiles - 1:
                    held_ref[1, s : s + 1, :] = weight[SUBLANES - 1 :]
                    weight = jnp.where(last_row, 0.0, weight)
                emitted = colors(value, tile_colors)
                if 0 < s < slices - 1:
                    grad_depth = (values[s + 1] - values[s - 1]).astype(jnp.float32)
                    weight = weight * shade(grad_depth, facing, squares)
                    for c in range(3):
                        sums[c] = sums[c] + emitted[c] * weight
                else:
                    end = int(s > 0)
                    face_ref[end, rows, here] = facing
                    square_ref[end, rows, here] = squares
                    weight = weight * (1.0 / 255.0)
                    for c in range(3):
                        lit_ref[end, c, rows, here] = emitted[c] * weight
            for c in range(3):
                base_ref[c, rows, here] = sums[c] * (1.0 / 255.0)
            base_ref[3, rows, here] = 1.0 - remaining

        for q, (edge, inner) in enumerate(((0, 1), (height - 1, height - 2))):
            value = volume_ref[0, :, edge, here]
            behind = pltpu.roll(jnp.where(back, 0, value), 1, 0)
            ahead = pltpu.roll(jnp.where(front, 0, value), slices - 1, 0)
            grad_ref[q, 0, :, here] = (ahead - behind).astype(jnp.float32)
            grad_ref[q, 1, :, here] = volume_ref[0, :, inner, here].astype(jnp.float32)
            word = pair_ref[j + 1, :, top + edge, :]
            low, high = across(
                pair_ref[j, :, top + edge, :],
                word,
                pair_ref[j + 2, :, top + edge, :],
                strip_first_lane[:pairs],
                strip_last_lane[:pairs],
            )
            grad_ref[q, 2, :pairs, here] = low
            grad_ref[q, 2, pairs:, here] = high
            weight = held_ref[q] * (1.0 / 255.0)
            emitted = colors(value, strip_colors)
            for c in range(3):
                strip_ref[q, c, :, here] = emitted[c] * weight
        return carry

    lax.fori_loop(0, chunks, chunk, 0, unroll=8)


def march_interior(volume, color_map, alpha_map, depth_count):
    _, slices, height, columns = volume.shape
    opacity_scale = OPACITY / (255.0 * slices * depth_count)
    shapes = [
        (4, height, columns),
        (2, height, columns),
        (2, height, columns),
        (2, 3, height, columns),
        (2, 3, slices, columns),
        (2, 3, slices, columns),
    ]
    voxels = slices * height * columns
    return pl.pallas_call(
        functools.partial(interior_kernel, opacity_scale),
        in_specs=[WHOLE] * 3,
        out_specs=[WHOLE] * len(shapes),
        out_shape=[jax.ShapeDtypeStruct(shape, jnp.float32) for shape in shapes],
        scratch_shapes=[
            pltpu.VMEM((columns // LANES + 2, slices // 2, height + 2 * SUBLANES, LANES), jnp.int32),
            pltpu.VMEM((2, slices, LANES), jnp.float32),
        ],
        compiler_params=pltpu.CompilerParams(vmem_limit_bytes=24 * 1024 * 1024),
        cost_estimate=pl.CostEstimate(flops=voxels * 80, bytes_accessed=voxels * 20, transcendentals=voxels),
    )(volume, color_map, alpha_map.reshape(1, -1))


def row_sums(first, second):
    count = first.shape[0]
    if count != SUBLANES:
        return jnp.sum(first, axis=0, keepdims=True), jnp.sum(second, axis=0, keepdims=True)
    upper = lax.broadcasted_iota(jnp.int32, first.shape, 0) < 4
    both = jnp.where(upper, first, second) + pltpu.roll(jnp.where(upper, second, first), 4, 0)
    both = both + pltpu.roll(both, 6, 0)
    both = both + pltpu.roll(both, 7, 0)
    return both, pltpu.roll(both, 3, 0)


def plane_terms(volume_ref, face_ref, square_ref, lit_ref, halo, end, rows, here):
    slices = volume_ref.shape[1]
    inner = volume_ref[0, jnp.where(end == 1, slices - 2, 1), rows, here].astype(jnp.float32)
    grad_depth = jnp.where(end == 1, halo - inner, inner - halo)
    shading = shade(grad_depth, face_ref[end, rows, here], square_ref[end, rows, here])
    return [lit_ref[end, c, rows, here] * shading for c in range(3)]


def first_end():
    front_end, back_end = ends("depth")
    end = jnp.where(parity("depth") == parity("rows"), 0, 1)
    return end, jnp.where(end == 1, back_end, front_end), jnp.where(end == 1, front_end, back_end)


def first_plane_kernel(volume_ref, base_ref, face_ref, square_ref, lit_ref, first_ref, sums_ref):
    _, height, columns = base_ref.shape
    end, outside, _ = first_end()

    def chunk(j, carry):
        here = pl.ds(pl.multiple_of(j * LANES, LANES), LANES)
        first = jnp.where(outside, 0.0, first_ref[:, here].astype(jnp.float32))
        for r in range(height // SUBLANES):
            rows = slice(r * SUBLANES, (r + 1) * SUBLANES)
            terms = plane_terms(volume_ref, face_ref, square_ref, lit_ref, first[rows], end, rows, here)
            for c in range(3):
                sums_ref[c, rows, here] = base_ref[c, rows, here] + terms[c]
        return carry

    lax.fori_loop(0, columns // LANES, chunk, 0, unroll=8)


def add_first_plane(volume, base, face, square, lit, first):
    return pl.pallas_call(
        first_plane_kernel,
        in_specs=[WHOLE] * 6,
        out_specs=WHOLE,
        out_shape=jax.ShapeDtypeStruct((3, *base.shape[1:]), jnp.float32),
        compiler_params=pltpu.CompilerParams(vmem_limit_bytes=8 * 1024 * 1024),
        cost_estimate=pl.CostEstimate(flops=base.size * 20, bytes_accessed=base.size * 12, transcendentals=base.size // 4),
    )(volume, base, face, square, lit, first)


def edge_kernel(
    share, volume_ref, sums_ref, base_ref, face_ref, square_ref, lit_ref, grad_ref, strip_ref, first_ref, rows_near_ref, second_ref, rows_far_ref, *out_refs
):
    _, slices, height, columns = volume_ref.shape
    tiles = height // SUBLANES
    tile = (SUBLANES, LANES)
    row = lax.broadcasted_iota(jnp.int32, tile, 0)
    first_row, last_row, upper = row == 0, row == SUBLANES - 1, row < SUBLANES // 2
    level = lax.broadcasted_iota(jnp.int32, (slices, LANES), 0)
    front, back = level == 0, level == slices - 1
    odd, odd_row = parity("depth") == 1, parity("rows") == 1
    front_came_first = odd == odd_row
    front_end, back_end = ends("depth")
    top_end, bottom_end = ends("rows")
    end, _, outside = first_end()

    def chunk(j, carry):
        here = pl.ds(pl.multiple_of(j * LANES, LANES), LANES)
        rows_near = rows_near_ref[:, here].astype(jnp.float32)[:slices]
        rows_far = rows_far_ref[:, here].astype(jnp.float32)
        above = jnp.where(top_end, 0.0, jnp.where(odd_row, rows_near, rows_far))
        below = jnp.where(bottom_end, 0.0, jnp.where(odd_row, rows_far, rows_near))
        first = first_ref[:, here].astype(jnp.float32)
        second = second_ref[:, here].astype(jnp.float32)
        before = jnp.where(front_end, 0.0, jnp.where(front_came_first, first, second))
        after = jnp.where(back_end, 0.0, jnp.where(front_came_first, second, first))
        last = jnp.where(outside, 0.0, second)
        extra = []
        for q, edge in enumerate((0, height - 1)):
            inner = grad_ref[q, 1, :, here]
            grad_rows = below - inner if q else inner - above
            grad_cols = grad_ref[q, 2, :, here]
            grad_depth = grad_ref[q, 0, :, here] + jnp.where(
                back, after[edge : edge + 1], jnp.where(front, -before[edge : edge + 1], 0.0)
            )
            shading = shade(
                grad_depth,
                LIGHT_ROWS * grad_rows + LIGHT_COLS * grad_cols,
                grad_rows * grad_rows + grad_cols * grad_cols,
            )
            extra.append([strip_ref[q, c, :, here] * shading for c in range(3)])
        extra = [row_sums(extra[0][c], extra[1][c]) for c in range(3)]
        for r in range(tiles):
            rows = slice(r * SUBLANES, (r + 1) * SUBLANES)
            terms = plane_terms(volume_ref, face_ref, square_ref, lit_ref, last[rows], 1 - end, rows, here)
            planes = [sums_ref[c, rows, here] + terms[c] for c in range(3)] + [base_ref[3, rows, here]]
            for c in range(3):
                if r == 0:
                    planes[c] = planes[c] + jnp.where(first_row, extra[c][0], 0.0)
                if r == tiles - 1:
                    planes[c] = planes[c] + jnp.where(last_row, extra[c][1], 0.0)
            if len(out_refs) == 1:
                for i, first in enumerate(range(0, SUBLANES, share)):
                    block = jnp.concatenate([plane[first : first + share] for plane in planes], axis=0)
                    out_refs[0][r * (SUBLANES // share) + i, :, here] = block.astype(jnp.bfloat16)
            else:
                halves = [(planes[c], pltpu.roll(planes[c + 1], SUBLANES // 2, 0)) for c in (0, 2)]
                even = jnp.concatenate([jnp.where(upper, own, turned) for own, turned in halves], axis=0)
                uneven = jnp.concatenate([jnp.where(upper, turned, own) for own, turned in halves], axis=0)
                blocks_ref, _ = out_refs
                blocks_ref[r, 0, :, here] = even
                blocks_ref[r, 1, :, here] = uneven
        return carry

    lax.fori_loop(0, columns // LANES, chunk, 0, unroll=8)
    if len(out_refs) > 1:
        blocks_ref, give_ref = out_refs
        chip, core, mask = route()
        given = (blocks_ref[chip, 1 - core], blocks_ref[chip ^ 3, core], blocks_ref[chip ^ mask ^ 3, 0], blocks_ref[chip ^ mask ^ 3, 1])
        for i, block in enumerate(given):
            give_ref[i] = block.astype(jnp.bfloat16)


def add_edges(volume, sums, interior, halos, depth_count, paired):
    _, slices, height, columns = volume.shape
    share = height // depth_count
    if paired:
        block = (4 * share, columns)
        shapes = [
            jax.ShapeDtypeStruct((depth_count // 2, 2, *block), jnp.float32),
            jax.ShapeDtypeStruct((4, *block), jnp.bfloat16),
        ]
    else:
        shapes = [jax.ShapeDtypeStruct((depth_count, 4 * share, columns), jnp.bfloat16)]
    return pl.pallas_call(
        functools.partial(edge_kernel, share),
        in_specs=[WHOLE] * 12,
        out_specs=[WHOLE] * len(shapes),
        out_shape=shapes,
        compiler_params=pltpu.CompilerParams(vmem_limit_bytes=24 * 1024 * 1024),
    )(volume, sums, *interior, *halos)


def served(depth):
    chip, core = depth // 2, depth % 2
    return 1 + (core ^ (chip & 1) ^ (chip >> 1))


def route():
    position = lax.axis_index("depth")
    return position // 2, position % 2, served(position)


def over(nearer, farther, uneven):
    share = nearer.shape[0] // 4
    clear = 1.0 - jnp.where(uneven, nearer[2 * share : 3 * share], nearer[3 * share :])
    return nearer + jnp.concatenate([clear] * 4, axis=0) * farther


def merge_kernel(blocks_ref, other_ref, own_ref, cross_ref, side_ref):
    chip, core, mask = route()
    odd = core == 1

    def merged(keep, i, uneven):
        other = other_ref[i].astype(jnp.float32)
        return over(jnp.where(odd, other, keep), jnp.where(odd, keep, other), uneven)

    own_ref[...] = merged(blocks_ref[chip, core], 0, odd)
    for i, p in enumerate((1 - core, core)):
        side_ref[i] = merged(blocks_ref[chip ^ mask, p], 2 + p, p == 1).astype(jnp.bfloat16)
    cross_ref[...] = merged(blocks_ref[chip ^ 3, 1 - core], 1, jnp.logical_not(odd)).astype(jnp.bfloat16)


def merge(blocks, other):
    rows, columns = other.shape[1:]
    return pl.pallas_call(
        merge_kernel,
        in_specs=[WHOLE] * 2,
        out_specs=[WHOLE] * 3,
        out_shape=[
            jax.ShapeDtypeStruct((rows, columns), jnp.float32),
            jax.ShapeDtypeStruct((rows, columns), jnp.bfloat16),
            jax.ShapeDtypeStruct((2, rows, columns), jnp.bfloat16),
        ],
        compiler_params=pltpu.CompilerParams(vmem_limit_bytes=8 * 1024 * 1024),
    )(blocks, other)


def pass_kernel(side_ref, out_ref):
    out_ref[...] = side_ref[1]


def pass_on(side):
    return pl.pallas_call(
        pass_kernel,
        in_specs=[WHOLE],
        out_specs=WHOLE,
        out_shape=jax.ShapeDtypeStruct(side.shape[1:], side.dtype),
        compiler_params=pltpu.CompilerParams(vmem_limit_bytes=4 * 1024 * 1024),
    )(side)


def gather_kernel(side_ref, cross_ref, passed_ref, own_ref, out_ref):
    share = out_ref.shape[1]
    chip, core, mask = route()
    odd, serves_x = core == 1, mask == 1
    side, passed = side_ref[0].astype(jnp.float32), passed_ref[...].astype(jnp.float32)
    parts = [
        own_ref[...],
        jnp.where(serves_x, side, passed),
        jnp.where(serves_x, passed, side),
        cross_ref[...].astype(jnp.float32),
    ]
    step = 1
    while len(parts) > 1:
        swap = (chip & step) != 0
        parts = [
            over(jnp.where(swap, parts[i + 1], parts[i]), jnp.where(swap, parts[i], parts[i + 1]), odd)
            for i in range(0, len(parts), 2)
        ]
        step *= 2
    planes = [parts[0][c * share : (c + 1) * share] for c in range(4)]
    for c in range(4):
        out_ref[c] = jnp.where(odd, planes[c ^ 1], planes[c])


def gather(parts, share):
    columns = parts[-1].shape[1]
    return pl.pallas_call(
        gather_kernel,
        in_specs=[WHOLE] * len(parts),
        out_specs=WHOLE,
        out_shape=jax.ShapeDtypeStruct((4, share, columns), jnp.float32),
        compiler_params=pltpu.CompilerParams(vmem_limit_bytes=4 * 1024 * 1024),
    )(*parts)


def finish_kernel(parts_ref, out_ref):
    count = parts_ref.shape[0]
    _, share, columns = out_ref.shape
    remaining = jnp.ones((share, columns), jnp.float32)
    sums = [jnp.zeros((share, columns), jnp.float32) for _ in range(3)]
    for k in range(count):
        part = parts_ref[k].astype(jnp.float32)
        for c in range(3):
            sums[c] = sums[c] + remaining * part[c * share : (c + 1) * share]
        remaining = remaining - remaining * part[3 * share :]
    for c in range(3):
        out_ref[c] = sums[c]
    out_ref[3] = 1.0 - remaining


def finish(parts, share):
    columns = parts.shape[2]
    return pl.pallas_call(
        finish_kernel,
        in_specs=[WHOLE],
        out_specs=WHOLE,
        out_shape=jax.ShapeDtypeStruct((4, share, columns), jnp.float32),
        compiler_params=pltpu.CompilerParams(vmem_limit_bytes=4 * 1024 * 1024),
    )(parts)


def swapped(values, kinds):
    depth_count, row_count = lax.axis_size("depth"), lax.axis_size("rows")
    perm = []
    for d in range(depth_count):
        for r in range(row_count):
            kind = kinds[r % 2]
            e, q = d, r
            if kind == "near slab":
                e = d ^ 1
            elif kind == "far slab":
                e = d + 1 if d % 2 else d - 1
                e = depth_count - 1 - d if not 0 <= e < depth_count else e
            else:
                q = r ^ 1 if kind == "near row" else (r + 1 if r % 2 else r - 1)
                if not 0 <= q < row_count:
                    e, q = d ^ 1, r
            perm.append((d * row_count + r, e * row_count + q))
    return lax.ppermute(values, ("depth", "rows"), perm)


def exchanged(values, mask):
    masks = [mask(d) if callable(mask) else mask for d in range(lax.axis_size("depth"))]
    return lax.ppermute(values, "depth", [(d, d ^ m) for d, m in enumerate(masks)])


def body(volume, color_map, alpha_map):
    depth_count = lax.axis_size("depth")
    share = volume.shape[2] // depth_count
    first, rows_near, second, rows_far = cut_edges(volume)
    first = swapped(first, ("far slab", "near slab"))
    rows_near = swapped(rows_near, ("near row", "near row"))
    second = swapped(second, ("near slab", "far slab"))
    rows_far = swapped(rows_far, ("far row", "far row"))
    interior = march_interior(volume, color_map, alpha_map, depth_count)
    halos = (first, rows_near, second, rows_far)
    paired = depth_count == 8 and 2 * share == SUBLANES
    sums = add_first_plane(volume, *interior[:4], first)
    outs = add_edges(volume, sums, interior, halos, depth_count, paired)
    if not paired:
        return finish(lax.all_to_all(outs[0], "depth", 0, 0, tiled=True), share)
    blocks, give = outs
    own, cross, side = merge(blocks, exchanged(give, 1))
    side = exchanged(side, lambda d: 2 * served(d) + 1)
    cross = exchanged(cross, 7)
    return gather((side, cross, exchanged(pass_on(side), 1), own), share)


def solution(mesh):
    in_specs = (P(None, "depth", "rows", None), P(), P())
    out_specs = P(None, ("rows", "depth"), None)
    return jax.shard_map(body, mesh=mesh, in_specs=in_specs, out_specs=out_specs, check_vma=False)
```

```python
import functools

import jax
import jax.numpy as jnp
from jax import lax
from jax.experimental import pallas as pl
from jax.experimental.pallas import tpu as pltpu
from jax.sharding import PartitionSpec as P

AMBIENT = 0.3
DIFFUSE = 0.7
LIGHT_DEPTH = 0.48 * DIFFUSE
LIGHT_ROWS = 0.6 * DIFFUSE
LIGHT_COLS = 0.64 * DIFFUSE
OPACITY = 4.0
LANES = 128
SUBLANES = 8
WHOLE = pl.BlockSpec(memory_space=pltpu.VMEM)


def parity(axis):
    return lax.axis_index(axis) % 2


def ends(axis):
    position = lax.axis_index(axis)
    return position == 0, position == lax.axis_size(axis) - 1


def edges_kernel(volume_ref, first_out, rows_near_out, second_out, rows_far_out, strip_ref, plane_ref, sems):
    _, slices, height, columns = volume_ref.shape
    odd, odd_row = parity("depth"), parity("rows")
    far_first = 1 - odd_row
    last_first = odd ^ far_first ^ 1
    tiles = height // SUBLANES

    def plane_copies(i, s):
        for t in range(tiles):
            rows = pl.ds(t * SUBLANES, SUBLANES)
            yield pltpu.make_async_copy(volume_ref.at[0, s, rows], plane_ref.at[i, rows], sems.at[i, t])

    def strip_copy(i, row):
        return pltpu.make_async_copy(volume_ref.at[0, :, row], strip_ref.at[i], sems.at[2, i])

    copies = [
        list(plane_copies(0, last_first * (slices - 1))),
        [strip_copy(0, (1 - odd_row) * (height - 1))],
        list(plane_copies(1, (1 - last_first) * (slices - 1))),
        [strip_copy(1, odd_row * (height - 1))],
    ]
    for group in copies:
        for copy in group:
            copy.start()

    def arrive(group):
        for copy in group:
            copy.wait()

    def narrow(values):
        return values.astype(jnp.float32).astype(jnp.bfloat16)

    def padded(strip):
        return narrow(jnp.concatenate([strip, jnp.zeros((height - slices, columns), jnp.int32)], axis=0))

    arrive(copies[0])
    first_out[...] = narrow(plane_ref[0])
    arrive(copies[1])
    rows_near_out[...] = padded(strip_ref[0])
    arrive(copies[2])
    second_out[...] = narrow(plane_ref[1])
    arrive(copies[3])
    rows_far_out[...] = narrow(strip_ref[1])


def cut_edges(volume):
    _, slices, height, columns = volume.shape
    plane = jax.ShapeDtypeStruct((height, columns), jnp.bfloat16)
    strip = jax.ShapeDtypeStruct((slices, columns), jnp.bfloat16)
    return pl.pallas_call(
        edges_kernel,
        in_specs=[pl.BlockSpec(memory_space=pl.ANY)],
        out_specs=[WHOLE] * 4,
        out_shape=[plane, plane, plane, strip],
        scratch_shapes=[
            pltpu.VMEM((2, slices, columns), jnp.int32),
            pltpu.VMEM((2, height, columns), jnp.int32),
            pltpu.SemaphoreType.DMA((3, max(2, height // SUBLANES))),
        ],
        compiler_params=pltpu.CompilerParams(vmem_limit_bytes=52 * 1024 * 1024),
    )(volume)


def pick(entries, places):
    dims = lax.GatherDimensionNumbers(
        offset_dims=(),
        collapsed_slice_dims=(1,),
        start_index_map=(1,),
        operand_batching_dims=(0,),
        start_indices_batching_dims=(0,),
    )
    return lax.gather(entries, places[..., None], dims, (1, 1), mode=lax.GatherScatterMode.PROMISE_IN_BOUNDS)


def shade(grad_depth, facing, squares):
    facing = facing + LIGHT_DEPTH * grad_depth
    squares = squares + grad_depth * grad_depth
    return AMBIENT + jnp.abs(facing) * lax.rsqrt(jnp.maximum(squares, 4.0))


def interior_kernel(
    opacity_scale,
    volume_ref,
    color_ref,
    alpha_ref,
    base_ref,
    face_ref,
    square_ref,
    lit_ref,
    grad_ref,
    strip_ref,
    pair_ref,
    held_ref,
):
    _, slices, height, columns = volume_ref.shape
    tiles = height // SUBLANES
    chunks = columns // LANES
    tile = (SUBLANES, LANES)
    strip = (slices, LANES)

    packed = color_ref[0:1, :] + color_ref[1:2, :] * 256 + color_ref[2:3, :] * 65536
    color_low, color_high = packed[:, :LANES], packed[:, LANES:]
    alpha_both = alpha_ref[0:1, :LANES] + alpha_ref[0:1, LANES:] * 256

    def colors(value, tables):
        low, high = tables
        place = value & (LANES - 1)
        color = jnp.where(value < LANES, pick(low, place), pick(high, place))
        parts = (color & 255, lax.shift_right_logical(color, 8) & 255, lax.shift_right_logical(color, 16))
        return [part.astype(jnp.float32) for part in parts]

    def opacity(level, table):
        entry = pick(table, level & (LANES - 1))
        entry = lax.shift_right_logical(entry, lax.shift_right_logical(level & LANES, 4)) & 255
        return entry.astype(jnp.float32) * opacity_scale

    tile_colors = [jnp.broadcast_to(t, tile) for t in (color_low, color_high)]
    tile_alpha = jnp.broadcast_to(alpha_both, tile)
    strip_colors = [jnp.broadcast_to(t, strip) for t in (color_low, color_high)]

    def masks(shape):
        lane = lax.broadcasted_iota(jnp.int32, shape, 1)
        row = lax.broadcasted_iota(jnp.int32, shape, 0)
        return lane == 0, lane == LANES - 1, row == 0, row == shape[0] - 1

    first_lane, last_lane, first_row, last_row = masks(tile)
    strip_first_lane, strip_last_lane, front, back = masks(strip)

    pairs = slices // 2
    top = SUBLANES

    def clear(j, carry):
        pair_ref[j] = jnp.zeros(pair_ref.shape[1:], jnp.int32)
        return carry

    clear(0, 0)
    clear(chunks + 1, 0)
    margin = jnp.zeros((pairs, SUBLANES, LANES), jnp.int32)

    def pack(j, carry):
        here = pl.ds(pl.multiple_of(j * LANES, LANES), LANES)
        pair_ref[j + 1, :, :top] = margin
        pair_ref[j + 1, :, top + height :] = margin
        for p in range(pairs):
            pair_ref[j + 1, p, top : top + height] = volume_ref[0, p, :, here] + lax.shift_left(
                volume_ref[0, p + pairs, :, here], 16
            )
        return carry

    lax.fori_loop(0, chunks, pack, 0)

    def split(difference):
        low = lax.shift_right_arithmetic(lax.shift_left(difference, 16), 16)
        high = lax.shift_right_arithmetic(difference + 32768, 16)
        return low.astype(jnp.float32), high.astype(jnp.float32)

    def across(left_value, value, right_value, first, last):
        west = pltpu.roll(jnp.where(last, left_value, value), 1, 1)
        east = pltpu.roll(jnp.where(first, right_value, value), LANES - 1, 1)
        return split(east - west)

    def chunk(j, carry):
        here = pl.ds(pl.multiple_of(j * LANES, LANES), LANES)

        for r in range(tiles):
            rows = slice(r * SUBLANES, (r + 1) * SUBLANES)
            values = [volume_ref[0, s, rows, here] for s in range(slices)]

            def words(c, p, offset=0):
                return pair_ref[c, p, top + r * SUBLANES + offset : top + (r + 1) * SUBLANES + offset, :]

            down, right = [], []
            for p in range(pairs):
                down.append(split(words(j + 1, p, 1) - words(j + 1, p, -1)))
                right.append(across(words(j, p), words(j + 1, p), words(j + 2, p), first_lane, last_lane))
            remaining = jnp.ones(tile, jnp.float32)
            sums = [jnp.zeros(tile, jnp.float32) for _ in range(3)]
            for s in range(slices):
                value = values[s]
                grad_rows = down[s % pairs][s // pairs]
                grad_cols = right[s % pairs][s // pairs]
                squares = grad_rows * grad_rows + grad_cols * grad_cols
                facing = LIGHT_ROWS * grad_rows + LIGHT_COLS * grad_cols
                weight = remaining * opacity(volume_ref[1, s, rows, here], tile_alpha)
                remaining = remaining - weight
                if r == 0:
                    held_ref[0, s : s + 1, :] = weight[:1]
                    weight = jnp.where(first_row, 0.0, weight)
                if r == tiles - 1:
                    held_ref[1, s : s + 1, :] = weight[SUBLANES - 1 :]
                    weight = jnp.where(last_row, 0.0, weight)
                emitted = colors(value, tile_colors)
                if 0 < s < slices - 1:
                    grad_depth = (values[s + 1] - values[s - 1]).astype(jnp.float32)
                    weight = weight * shade(grad_depth, facing, squares)
                    for c in range(3):
                        sums[c] = sums[c] + emitted[c] * weight
                else:
                    end = int(s > 0)
                    face_ref[end, rows, here] = facing
                    square_ref[end, rows, here] = squares
                    weight = weight * (1.0 / 255.0)
                    for c in range(3):
                        lit_ref[end, c, rows, here] = emitted[c] * weight
            for c in range(3):
                base_ref[c, rows, here] = sums[c] * (1.0 / 255.0)
            base_ref[3, rows, here] = 1.0 - remaining

        for q, (edge, inner) in enumerate(((0, 1), (height - 1, height - 2))):
            value = volume_ref[0, :, edge, here]
            behind = pltpu.roll(jnp.where(back, 0, value), 1, 0)
            ahead = pltpu.roll(jnp.where(front, 0, value), slices - 1, 0)
            grad_ref[q, 0, :, here] = (ahead - behind).astype(jnp.float32)
            grad_ref[q, 1, :, here] = volume_ref[0, :, inner, here].astype(jnp.float32)
            word = pair_ref[j + 1, :, top + edge, :]
            low, high = across(
                pair_ref[j, :, top + edge, :],
                word,
                pair_ref[j + 2, :, top + edge, :],
                strip_first_lane[:pairs],
                strip_last_lane[:pairs],
            )
            grad_ref[q, 2, :pairs, here] = low
            grad_ref[q, 2, pairs:, here] = high
            weight = held_ref[q] * (1.0 / 255.0)
            emitted = colors(value, strip_colors)
            for c in range(3):
                strip_ref[q, c, :, here] = emitted[c] * weight
        return carry

    lax.fori_loop(0, chunks, chunk, 0, unroll=8)


def march_interior(volume, color_map, alpha_map, depth_count):
    _, slices, height, columns = volume.shape
    opacity_scale = OPACITY / (255.0 * slices * depth_count)
    shapes = [
        (4, height, columns),
        (2, height, columns),
        (2, height, columns),
        (2, 3, height, columns),
        (2, 3, slices, columns),
        (2, 3, slices, columns),
    ]
    voxels = slices * height * columns
    return pl.pallas_call(
        functools.partial(interior_kernel, opacity_scale),
        in_specs=[WHOLE] * 3,
        out_specs=[WHOLE] * len(shapes),
        out_shape=[jax.ShapeDtypeStruct(shape, jnp.float32) for shape in shapes],
        scratch_shapes=[
            pltpu.VMEM((columns // LANES + 2, slices // 2, height + 2 * SUBLANES, LANES), jnp.int32),
            pltpu.VMEM((2, slices, LANES), jnp.float32),
        ],
        compiler_params=pltpu.CompilerParams(vmem_limit_bytes=24 * 1024 * 1024),
        cost_estimate=pl.CostEstimate(flops=voxels * 80, bytes_accessed=voxels * 20, transcendentals=voxels),
    )(volume, color_map, alpha_map.reshape(1, -1))


def row_sums(first, second):
    count = first.shape[0]
    if count != SUBLANES:
        return jnp.sum(first, axis=0, keepdims=True), jnp.sum(second, axis=0, keepdims=True)
    upper = lax.broadcasted_iota(jnp.int32, first.shape, 0) < 4
    both = jnp.where(upper, first, second) + pltpu.roll(jnp.where(upper, second, first), 4, 0)
    both = both + pltpu.roll(both, 6, 0)
    both = both + pltpu.roll(both, 7, 0)
    return both, pltpu.roll(both, 3, 0)


def plane_terms(volume_ref, face_ref, square_ref, lit_ref, halo, end, rows, here):
    slices = volume_ref.shape[1]
    inner = volume_ref[0, jnp.where(end == 1, slices - 2, 1), rows, here].astype(jnp.float32)
    grad_depth = jnp.where(end == 1, halo - inner, inner - halo)
    shading = shade(grad_depth, face_ref[end, rows, here], square_ref[end, rows, here])
    return [lit_ref[end, c, rows, here] * shading for c in range(3)]


def first_end():
    front_end, back_end = ends("depth")
    end = jnp.where(parity("depth") == parity("rows"), 0, 1)
    return end, jnp.where(end == 1, back_end, front_end), jnp.where(end == 1, front_end, back_end)


def first_plane_kernel(volume_ref, base_ref, face_ref, square_ref, lit_ref, first_ref, sums_ref):
    _, height, columns = base_ref.shape
    end, outside, _ = first_end()

    def chunk(j, carry):
        here = pl.ds(pl.multiple_of(j * LANES, LANES), LANES)
        first = jnp.where(outside, 0.0, first_ref[:, here].astype(jnp.float32))
        for r in range(height // SUBLANES):
            rows = slice(r * SUBLANES, (r + 1) * SUBLANES)
            terms = plane_terms(volume_ref, face_ref, square_ref, lit_ref, first[rows], end, rows, here)
            for c in range(3):
                sums_ref[c, rows, here] = base_ref[c, rows, here] + terms[c]
        return carry

    lax.fori_loop(0, columns // LANES, chunk, 0, unroll=8)


def add_first_plane(volume, base, face, square, lit, first):
    return pl.pallas_call(
        first_plane_kernel,
        in_specs=[WHOLE] * 6,
        out_specs=WHOLE,
        out_shape=jax.ShapeDtypeStruct((3, *base.shape[1:]), jnp.float32),
        compiler_params=pltpu.CompilerParams(vmem_limit_bytes=8 * 1024 * 1024),
        cost_estimate=pl.CostEstimate(flops=base.size * 20, bytes_accessed=base.size * 12, transcendentals=base.size // 4),
    )(volume, base, face, square, lit, first)


def edge_kernel(
    share, volume_ref, sums_ref, base_ref, face_ref, square_ref, lit_ref, grad_ref, strip_ref, first_ref, rows_near_ref, second_ref, rows_far_ref, *out_refs
):
    _, slices, height, columns = volume_ref.shape
    tiles = height // SUBLANES
    tile = (SUBLANES, LANES)
    row = lax.broadcasted_iota(jnp.int32, tile, 0)
    first_row, last_row, upper = row == 0, row == SUBLANES - 1, row < SUBLANES // 2
    level = lax.broadcasted_iota(jnp.int32, (slices, LANES), 0)
    front, back = level == 0, level == slices - 1
    odd, odd_row = parity("depth") == 1, parity("rows") == 1
    chip = lax.axis_index("depth") // 2
    front_came_first = odd == odd_row
    front_end, back_end = ends("depth")
    top_end, bottom_end = ends("rows")
    end, _, outside = first_end()

    def chunk(j, carry):
        here = pl.ds(pl.multiple_of(j * LANES, LANES), LANES)
        rows_near = rows_near_ref[:, here].astype(jnp.float32)[:slices]
        rows_far = rows_far_ref[:, here].astype(jnp.float32)
        above = jnp.where(top_end, 0.0, jnp.where(odd_row, rows_near, rows_far))
        below = jnp.where(bottom_end, 0.0, jnp.where(odd_row, rows_far, rows_near))
        first = first_ref[:, here].astype(jnp.float32)
        second = second_ref[:, here].astype(jnp.float32)
        before = jnp.where(front_end, 0.0, jnp.where(front_came_first, first, second))
        after = jnp.where(back_end, 0.0, jnp.where(front_came_first, second, first))
        last = jnp.where(outside, 0.0, second)
        extra = []
        for q, edge in enumerate((0, height - 1)):
            inner = grad_ref[q, 1, :, here]
            grad_rows = below - inner if q else inner - above
            grad_cols = grad_ref[q, 2, :, here]
            grad_depth = grad_ref[q, 0, :, here] + jnp.where(
                back, after[edge : edge + 1], jnp.where(front, -before[edge : edge + 1], 0.0)
            )
            shading = shade(
                grad_depth,
                LIGHT_ROWS * grad_rows + LIGHT_COLS * grad_cols,
                grad_rows * grad_rows + grad_cols * grad_cols,
            )
            extra.append([strip_ref[q, c, :, here] * shading for c in range(3)])
        extra = [row_sums(extra[0][c], extra[1][c]) for c in range(3)]
        for r in range(tiles):
            rows = slice(r * SUBLANES, (r + 1) * SUBLANES)
            terms = plane_terms(volume_ref, face_ref, square_ref, lit_ref, last[rows], 1 - end, rows, here)
            planes = [sums_ref[c, rows, here] + terms[c] for c in range(3)] + [base_ref[3, rows, here]]
            for c in range(3):
                if r == 0:
                    planes[c] = planes[c] + jnp.where(first_row, extra[c][0], 0.0)
                if r == tiles - 1:
                    planes[c] = planes[c] + jnp.where(last_row, extra[c][1], 0.0)
            if len(out_refs) == 1:
                for i, first in enumerate(range(0, SUBLANES, share)):
                    block = jnp.concatenate([plane[first : first + share] for plane in planes], axis=0)
                    out_refs[0][r * (SUBLANES // share) + i, :, here] = block.astype(jnp.bfloat16)
            else:
                halves = [(planes[c], pltpu.roll(planes[c + 1], SUBLANES // 2, 0)) for c in (0, 2)]
                even = jnp.concatenate([jnp.where(upper, own, turned) for own, turned in halves], axis=0)
                uneven = jnp.concatenate([jnp.where(upper, turned, own) for own, turned in halves], axis=0)
                keep_ref, give_ref = out_refs
                keep_even = odd != (chip == r)
                keep_ref[r, :, here] = jnp.where(keep_even, even, uneven)
                give_ref[r, :, here] = jnp.where(keep_even, uneven, even).astype(jnp.bfloat16)
        return carry

    lax.fori_loop(0, columns // LANES, chunk, 0, unroll=8)


def add_edges(volume, sums, interior, halos, depth_count, paired):
    _, slices, height, columns = volume.shape
    share = height // depth_count
    if paired:
        half = (depth_count // 2, 4 * share, columns)
        shapes = [jax.ShapeDtypeStruct(half, jnp.float32), jax.ShapeDtypeStruct(half, jnp.bfloat16)]
    else:
        shapes = [jax.ShapeDtypeStruct((depth_count, 4 * share, columns), jnp.bfloat16)]
    return pl.pallas_call(
        functools.partial(edge_kernel, share),
        in_specs=[WHOLE] * 12,
        out_specs=[WHOLE] * len(shapes),
        out_shape=shapes,
        compiler_params=pltpu.CompilerParams(vmem_limit_bytes=24 * 1024 * 1024),
    )(volume, sums, *interior, *halos)


def over(nearer, farther, uneven):
    share = nearer.shape[0] // 4
    clear = 1.0 - jnp.where(uneven, nearer[2 * share : 3 * share], nearer[3 * share :])
    return nearer + jnp.concatenate([clear] * 4, axis=0) * farther


def merge_kernel(keep_ref, other_ref, *out_refs):
    position = lax.axis_index("depth")
    odd, chip = position % 2 == 1, position // 2
    for k, out_ref in enumerate(out_refs):
        keep = keep_ref[chip ^ k]
        other = other_ref[chip ^ k].astype(jnp.float32)
        uneven = jnp.logical_not(odd) if k else odd
        block = over(jnp.where(odd, other, keep), jnp.where(odd, keep, other), uneven)
        out_ref[...] = block.astype(out_ref.dtype)


def merge(keep, other):
    chips, rows, columns = keep.shape
    shapes = [jax.ShapeDtypeStruct((rows, columns), jnp.bfloat16 if k else jnp.float32) for k in range(chips)]
    return pl.pallas_call(
        merge_kernel,
        in_specs=[WHOLE] * 2,
        out_specs=[WHOLE] * chips,
        out_shape=shapes,
        compiler_params=pltpu.CompilerParams(vmem_limit_bytes=8 * 1024 * 1024),
    )(keep, other)


def gather_kernel(*refs):
    *part_refs, out_ref = refs
    part_refs.reverse()
    count = len(part_refs)
    share = out_ref.shape[1]
    position = lax.axis_index("depth")
    odd, chip = position % 2 == 1, position // 2
    parts = [part_ref[...].astype(jnp.float32) for part_ref in part_refs]
    step = 1
    while step < count:
        swap = (chip & step) != 0
        parts = [
            over(jnp.where(swap, parts[i + 1], parts[i]), jnp.where(swap, parts[i], parts[i + 1]), odd)
            for i in range(0, len(parts), 2)
        ]
        step *= 2
    planes = [parts[0][c * share : (c + 1) * share] for c in range(4)]
    for c in range(4):
        out_ref[c] = jnp.where(odd, planes[c ^ 1], planes[c])


def gather(parts, share):
    columns = parts[0].shape[1]
    return pl.pallas_call(
        gather_kernel,
        in_specs=[WHOLE] * len(parts),
        out_specs=WHOLE,
        out_shape=jax.ShapeDtypeStruct((4, share, columns), jnp.float32),
        compiler_params=pltpu.CompilerParams(vmem_limit_bytes=4 * 1024 * 1024),
    )(*parts)


def finish_kernel(parts_ref, out_ref):
    count = parts_ref.shape[0]
    _, share, columns = out_ref.shape
    remaining = jnp.ones((share, columns), jnp.float32)
    sums = [jnp.zeros((share, columns), jnp.float32) for _ in range(3)]
    for k in range(count):
        part = parts_ref[k].astype(jnp.float32)
        for c in range(3):
            sums[c] = sums[c] + remaining * part[c * share : (c + 1) * share]
        remaining = remaining - remaining * part[3 * share :]
    for c in range(3):
        out_ref[c] = sums[c]
    out_ref[3] = 1.0 - remaining


def finish(parts, share):
    columns = parts.shape[2]
    return pl.pallas_call(
        finish_kernel,
        in_specs=[WHOLE],
        out_specs=WHOLE,
        out_shape=jax.ShapeDtypeStruct((4, share, columns), jnp.float32),
        compiler_params=pltpu.CompilerParams(vmem_limit_bytes=4 * 1024 * 1024),
    )(parts)


def swapped(values, kinds):
    depth_count, row_count = lax.axis_size("depth"), lax.axis_size("rows")
    perm = []
    for d in range(depth_count):
        for r in range(row_count):
            kind = kinds[r % 2]
            e, q = d, r
            if kind == "near slab":
                e = d ^ 1
            elif kind == "far slab":
                e = d + 1 if d % 2 else d - 1
                e = depth_count - 1 - d if not 0 <= e < depth_count else e
            else:
                q = r ^ 1 if kind == "near row" else (r + 1 if r % 2 else r - 1)
                if not 0 <= q < row_count:
                    e, q = d ^ 1, r
            perm.append((d * row_count + r, e * row_count + q))
    return lax.ppermute(values, ("depth", "rows"), perm)


def exchanged(values, mask):
    return lax.ppermute(values, "depth", [(d, d ^ mask) for d in range(lax.axis_size("depth"))])


def body(volume, color_map, alpha_map):
    depth_count = lax.axis_size("depth")
    share = volume.shape[2] // depth_count
    first, rows_near, second, rows_far = cut_edges(volume)
    first = swapped(first, ("far slab", "near slab"))
    rows_near = swapped(rows_near, ("near row", "near row"))
    second = swapped(second, ("near slab", "far slab"))
    rows_far = swapped(rows_far, ("far row", "far row"))
    interior = march_interior(volume, color_map, alpha_map, depth_count)
    halos = (first, rows_near, second, rows_far)
    paired = depth_count == 8 and 2 * share == SUBLANES
    sums = add_first_plane(volume, *interior[:4], first)
    outs = add_edges(volume, sums, interior, halos, depth_count, paired)
    if not paired:
        return finish(lax.all_to_all(outs[0], "depth", 0, 0, tiled=True), share)
    keep, give = outs
    own, *sends = merge(keep, exchanged(give, 1))
    received = [exchanged(send, 2 * k + 1) for k, send in reversed(list(enumerate(sends, 1)))]
    return gather((*received, own), share)


def solution(mesh):
    in_specs = (P(None, "depth", "rows", None), P(), P())
    out_specs = P(None, ("rows", "depth"), None)
    return jax.shard_map(body, mesh=mesh, in_specs=in_specs, out_specs=out_specs, check_vma=False)
```
